32 devices in a mesh: row: 8 (over z, y), col: 4 (over x, core).
Axes of the slice: x: 2, y: 2, z: 4, core: 2. Of those that a mesh axis runs over, the one named last changes fastest.
Arguments:
- latents: float32 [16384, 16], P('row'), may hold values from -6 to 6
- noise: float32 [16384, 16], P('row'), may hold values from -6 to 6
- timesteps: int32 [64], P('row'), may hold values from 0 to 999
- labels: int32 [64], P('row'), may hold values from 0 to 999
- loss_mask: int32 [16384], P('row'), may hold values from 0 to 1
- weights_in: float32 [2, 768, 13, 768], P(None, 'row', None, 'col'), may hold values from -0.21875 to 0.21875
- weights_out: float32 [2, 5, 768, 768], P(None, None, 'col', 'row'), may hold values from -0.4375 to 0.4375
- time_mlp: float32 [1024, 768], P('row', 'col'), may hold values from -0.375 to 0.375
- embed_table: float32 [1016, 768], P(None, 'col'), may hold values from -1.5 to 1.5
- final_layer: float32 [768, 1552], replicated, may hold values from -0.21875 to 0.21875
- bias_table: float32 [31, 768], P(None, 'col'), may hold values from -1.3 to 1.8
- final_bias: float32 [1552], replicated, may hold values from -1.75 to 1.75
- momentum_in: float32 [2, 768, 13, 768], P(None, 'row', None, 'col'), may hold values from -0.00012207031 to 0.00012207031
- momentum_out: float32 [2, 5, 768, 768], P(None, None, 'col', 'row'), may hold values from -0.00012207031 to 0.00012207031
- momentum_time: float32 [1024, 768], P('row', 'col'), may hold values from -0.00012207031 to 0.00012207031
- momentum_embed: float32 [1016, 768], P(None, 'col'), may hold values from -0.00012207031 to 0.00012207031
- momentum_final: float32 [768, 1552], replicated, may hold values from -0.00012207031 to 0.00012207031
- momentum_bias: float32 [31, 768], P(None, 'col'), may hold values from -0.00012207031 to 0.00012207031
- momentum_final_bias: float32 [1552], replicated, may hold values from -0.00012207031 to 0.00012207031
- variance_in: float32 [2, 768, 13, 768], P(None, 'row', None, 'col'), may hold values from 4.1635993e-11 to 1.6654397e-10
- variance_out: float32 [2, 5, 768, 768], P(None, None, 'col', 'row'), may hold values from 4.1635993e-11 to 1.6654397e-10
- variance_time: float32 [1024, 768], P('row', 'col'), may hold values from 4.1635993e-11 to 1.6654397e-10
- variance_embed: float32 [1016, 768], P(None, 'col'), may hold values from 4.1635996e-12 to 1.6654398e-11
- variance_final: float32 [768, 1552], replicated, may hold values from 4.1635993e-11 to 1.6654397e-10
- variance_bias: float32 [31, 768], P(None, 'col'), may hold values from 4.1635993e-11 to 1.6654397e-10
- variance_final_bias: float32 [1552], replicated, may hold values from 4.1635993e-11 to 1.6654397e-10
Outputs:
- loss_sum: float32 [], replicated
- token_count: float32 [], replicated
- grad_norm: float32 [], replicated
- new_weights_in: float32 [2, 768, 13, 768], P(None, 'row', None, 'col')
- new_momentum_in: float32 [2, 768, 13, 768], P(None, 'row', None, 'col')
- new_variance_in: float32 [2, 768, 13, 768], P(None, 'row', None, 'col')
- new_weights_out: float32 [2, 5, 768, 768], P(None, None, 'col', 'row')
- new_momentum_out: float32 [2, 5, 768, 768], P(None, None, 'col', 'row')
- new_variance_out: float32 [2, 5, 768, 768], P(None, None, 'col', 'row')
- new_time_mlp: float32 [1024, 768], P('row', 'col')
- new_momentum_time: float32 [1024, 768], P('row', 'col')
- new_variance_time: float32 [1024, 768], P('row', 'col')
- new_embed_table: float32 [1016, 768], P(None, 'col')
- new_momentum_embed: float32 [1016, 768], P(None, 'col')
- new_variance_embed: float32 [1016, 768], P(None, 'col')
- new_final_layer: float32 [768, 1552], replicated
- new_momentum_final: float32 [768, 1552], replicated
- new_variance_final: float32 [768, 1552], replicated
- new_bias_table: float32 [31, 768], P(None, 'col')
- new_momentum_bias: float32 [31, 768], P(None, 'col')
- new_variance_bias: float32 [31, 768], P(None, 'col')
- new_final_bias: float32 [1552], replicated
- new_momentum_final_bias: float32 [1552], replicated
- new_variance_final_bias: float32 [1552], replicated
The draws below stay inside these ranges and needn't reach their ends.
All inputs are finite; a program needn't handle non-finite values.
Results may differ from the reference program's by a relative error of at most 0.012.
Values may be sent and summed in bfloat16 or wider, within the bound.
No kernel may reach another device: no remote copies, remote signals or barrier semaphores. Data moves between devices by JAX's collectives and lax.ppermute only.
A program may use at most 256 MiB of HBM per device.

```python
import math
import jax
import jax.numpy as jnp
from jax import lax

D = 768
HEAD_DIM = 64
FF = 3072
CLASSES = 1000
FREQ = 256
PATCH = 16
LEN = 256
LAYERS = 2
STEPS_T = 1000
STEP = 10
BATCH = 64
TOKENS = 16384
NPARAM = 24017680


def draw_loss_mask(key, part):
    token_place = jnp.arange(TOKENS, dtype=jnp.int32)
    limit = 250 + 500 * (token_place // LEN) // (TOKENS // LEN)
    return (jax.random.randint(key, (TOKENS,), 0, 1000) < limit).astype(jnp.int32)


def draw_bias_table(key, part):
    row_total = LAYERS * 14 + 3
    spread = jnp.clip(jax.random.normal(key, (row_total, D), jnp.float32), -4.0, 4.0)
    ramp = 3.0 ** (jnp.arange(D, dtype=jnp.float32) / D)
    row_index = jnp.arange(row_total)
    kind_index = row_index % 14
    inside = row_index < LAYERS * 14
    scale_rows = inside & ((kind_index == 1) | (kind_index == 4))
    gate_rows = inside & ((kind_index == 2) | (kind_index == 5))
    drawn = 0.3 * spread
    scaled = 0.6 * ramp[None, :] - 1.0 + 0.05 * spread
    gated = 0.5 * ramp[None, :] + 0.05 * spread
    return jnp.where(scale_rows[:, None], scaled, jnp.where(gate_rows[:, None], gated, drawn))


def set_ends(drawn, key, least, largest):
    place = [jax.random.randint(jax.random.fold_in(key, axis), (), 0, length) for axis, length in enumerate(drawn.shape)]
    widest = drawn.shape.index(max(drawn.shape))
    beside = place[:widest] + [(place[widest] + 1) % drawn.shape[widest]] + place[widest + 1:]
    return drawn.at[tuple(place)].set(least).at[tuple(beside)].set(largest)


def steps_of(stream_key, shape, split, smallest, largest):
    factor_of = 1.0
    for axis_at, blocks in split:
        steps = jax.random.uniform(jax.random.fold_in(jax.random.fold_in(stream_key, 6), axis_at), (blocks,), jnp.float32, smallest / len(split), largest / len(split))
        factor_of = factor_of * jnp.repeat(jnp.exp(steps), shape[axis_at] // blocks).reshape((-1,) + (1,) * (len(shape) - 1 - axis_at))
    return factor_of


def scatter_about(key, shape, deviation, reach, shards=(), kind=jnp.bfloat16):
    array = deviation * jax.random.normal(key, shape, jnp.float32)
    if shards:
        array = array * steps_of(key, shape, shards, -0.22, 0.18)
    return jnp.clip(array, -reach, reach).astype(kind)


def setup_inputs(seed: int = 0) -> dict:
    splits = jax.random.split(jax.random.key(seed), 27)
    latents = scatter_about(splits[0], (TOKENS, PATCH), 1.0, 6.0, ((0, 8),), jnp.float32)
    noise = scatter_about(splits[1], (TOKENS, PATCH), 1.0, 6.0, ((0, 8),), jnp.float32)
    timesteps = set_ends(jax.random.randint(splits[2], (BATCH,), 0, STEPS_T), jax.random.fold_in(splits[2], 1), 0, STEPS_T - 1).astype(jnp.int32)
    labels = set_ends(jax.random.randint(splits[3], (BATCH,), 0, CLASSES), jax.random.fold_in(splits[3], 1), 0, CLASSES - 1).astype(jnp.int32)
    loss_mask = draw_loss_mask(jax.random.fold_in(splits[26], 71), 0)
    weights_in = scatter_about(splits[5], (LAYERS, D, 9 + FF // D, D), D ** -0.5, 0.21875, ((1, 8), (3, 4)), jnp.float32)
    weights_out = scatter_about(splits[6], (LAYERS, 1 + FF // D, D, D), (D // 4) ** -0.5, 0.4375, ((2, 4), (3, 8)), jnp.float32)
    time_mlp = scatter_about(splits[7], (FREQ + D, D), FREQ ** -0.5, 0.375, ((0, 8), (1, 4)), jnp.float32)
    embed_table = scatter_about(splits[8], (CLASSES + PATCH, D), 0.25, 1.5, ((1, 4),), jnp.float32)
    final_layer = scatter_about(splits[9], (D, 2 * D + PATCH), D ** -0.5, 0.21875, (), jnp.float32)
    bias_table = draw_bias_table(jax.random.fold_in(splits[26], 71), 0)
    final_bias = scatter_about(splits[11], (2 * D + PATCH,), 0.3, 1.75, (), jnp.float32)
    momentum_in = scatter_about(splits[12], (LAYERS, D, 9 + FF // D, D), (0.11 / NPARAM ** 0.5), 0.00012207031, ((1, 8), (3, 4)), jnp.float32)
    momentum_out = scatter_about(splits[13], (LAYERS, 1 + FF // D, D, D), (0.11 / NPARAM ** 0.5), 0.00012207031, ((2, 4), (3, 8)), jnp.float32)
    momentum_time = scatter_about(splits[14], (FREQ + D, D), (0.11 / NPARAM ** 0.5), 0.00012207031, ((0, 8), (1, 4)), jnp.float32)
    momentum_embed = scatter_about(splits[15], (CLASSES + PATCH, D), (0.11 / NPARAM ** 0.5), 0.00012207031, ((1, 4),), jnp.float32)
    momentum_final = scatter_about(splits[16], (D, 2 * D + PATCH), (0.11 / NPARAM ** 0.5), 0.00012207031, (), jnp.float32)
    momentum_bias = scatter_about(splits[17], (LAYERS * 14 + 3, D), (0.11 / NPARAM ** 0.5), 0.00012207031, ((1, 4),), jnp.float32)
    momentum_final_bias = scatter_about(splits[18], (2 * D + PATCH,), (0.11 / NPARAM ** 0.5), 0.00012207031, (), jnp.float32)
    variance_in = jnp.clip(jnp.exp(math.log(1.665439730569318e-10) - 1.3862944 * jax.random.uniform(splits[19], (LAYERS, D, 9 + FF // D, D), jnp.float32) ** steps_of(splits[19], (LAYERS, D, 9 + FF // D, D), ((1, 8), (3, 4)), -0.2, 0.2)), 4.163599326423295e-11, 1.665439730569318e-10)
    variance_out = jnp.clip(jnp.exp(math.log(1.665439730569318e-10) - 1.3862944 * jax.random.uniform(splits[20], (LAYERS, 1 + FF // D, D, D), jnp.float32) ** steps_of(splits[20], (LAYERS, 1 + FF // D, D, D), ((2, 4), (3, 8)), -0.2, 0.2)), 4.163599326423295e-11, 1.665439730569318e-10)
    variance_time = jnp.clip(jnp.exp(math.log(1.665439730569318e-10) - 1.3862944 * jax.random.uniform(splits[21], (FREQ + D, D), jnp.float32) ** steps_of(splits[21], (FREQ + D, D), ((0, 8), (1, 4)), -0.2, 0.2)), 4.163599326423295e-11, 1.665439730569318e-10)
    variance_embed = jnp.clip(jnp.exp(math.log(1.6654398346527266e-11) - 1.3862944 * jax.random.uniform(splits[22], (CLASSES + PATCH, D), jnp.float32) ** steps_of(splits[22], (CLASSES + PATCH, D), ((1, 4),), -0.2, 0.2)), 4.1635995866318165e-12, 1.6654398346527266e-11)
    variance_final = jnp.clip(jnp.exp(jax.random.uniform(splits[23], (D, 2 * D + PATCH), jnp.float32, math.log(4.163599326423295e-11), math.log(1.665439730569318e-10))), 4.163599326423295e-11, 1.665439730569318e-10)
    variance_bias = jnp.clip(jnp.exp(math.log(1.665439730569318e-10) - 1.3862944 * jax.random.uniform(splits[24], (LAYERS * 14 + 3, D), jnp.float32) ** steps_of(splits[24], (LAYERS * 14 + 3, D), ((1, 4),), -0.2, 0.2)), 4.163599326423295e-11, 1.665439730569318e-10)
    variance_final_bias = jnp.clip(jnp.exp(jax.random.uniform(splits[25], (2 * D + PATCH,), jnp.float32, math.log(4.163599326423295e-11), math.log(1.665439730569318e-10))), 4.163599326423295e-11, 1.665439730569318e-10)
    return {"latents": latents, "noise": noise, "timesteps": timesteps, "labels": labels, "loss_mask": loss_mask, "weights_in": weights_in, "weights_out": weights_out, "time_mlp": time_mlp, "embed_table": embed_table, "final_layer": final_layer, "bias_table": bias_table, "final_bias": final_bias, "momentum_in": momentum_in, "momentum_out": momentum_out, "momentum_time": momentum_time, "momentum_embed": momentum_embed, "momentum_final": momentum_final, "momentum_bias": momentum_bias, "momentum_final_bias": momentum_final_bias, "variance_in": variance_in, "variance_out": variance_out, "variance_time": variance_time, "variance_embed": variance_embed, "variance_final": variance_final, "variance_bias": variance_bias, "variance_final_bias": variance_final_bias}


HIGHEST = lax.Precision.HIGHEST
EPS_NORM = 1e-06
CLIP_NORM = 1.0
RATE = 0.05
RATE_BIAS = 0.25
BETA_ONE = 0.9
BETA_TWO = 0.999
DECAY = 0.01
ADAM_EPS = 1e-08

@jax.custom_vjp
def low(v):
    return lax.optimization_barrier(v.astype(jnp.bfloat16)).astype(jnp.float32)

@jax.custom_vjp
def low_back(v):
    return v

def low_keep(v):
    return (low(v), None)

def low_pass(kept, grad):
    return (grad,)

def back_keep(v):
    return (v, None)

def back_low(kept, grad):
    return (low(grad),)
low.defvjp(low_keep, low_pass)
low_back.defvjp(back_keep, back_low)

def matmul(spec, left, right):
    return jnp.einsum(spec, left, right, precision=HIGHEST)

def layer_norm(values):
    center = lax.optimization_barrier(jnp.mean(values, axis=-1, keepdims=True))
    spread = lax.optimization_barrier(jnp.mean((values - center) ** 2, axis=-1, keepdims=True))
    return (values - center) * lax.rsqrt(spread + EPS_NORM)

def positions(token_place, feature_index, model_width):
    half_width = model_width // 2
    freq_index = (feature_index % half_width).astype(jnp.float32)
    freq_rate = jnp.exp(-math.log(10000.0) * freq_index / half_width)
    angle_grid = token_place.astype(jnp.float32)[:, None] * freq_rate[None, :]
    return jnp.where(feature_index[None, :] < half_width, jnp.sin(angle_grid), jnp.cos(angle_grid))

def attention_group(triple):
    query = triple[:, :, 0]
    keys_part = triple[:, :, 1]
    values_part = triple[:, :, 2]
    scores = low_back(matmul('sqhd,skhd->shqk', query, keys_part) * HEAD_DIM ** (-0.5))
    attention_probs = jax.nn.softmax(scores, axis=-1)
    return low(low_back(matmul('shqk,skhd->sqhd', low(attention_probs), values_part)))

def forward(weights_in, weights_out, time_mlp, embed_table, final_layer, bias_table, final_bias, noisy_input, freq_feats, one_hot, position, noise_target, loss_weights):
    bias_base = LAYERS * 14
    batch_size = noisy_input.shape[0]
    head_count = D // HEAD_DIM
    time_low = low(time_mlp)
    embed_low = low(embed_table)
    final_low = low(final_layer)
    first_time = low_back(matmul('sf,fd->sd', low(freq_feats), time_low[:FREQ])) + bias_table[bias_base]
    second_time = low_back(matmul('sd,de->se', low(jax.nn.silu(first_time)), time_low[FREQ:])) + bias_table[bias_base + 1]
    condition = second_time + matmul('sc,cd->sd', one_hot, embed_low[:CLASSES])
    cond_act = low(jax.nn.silu(condition))
    residual = low_back(matmul('stp,pd->std', low(noisy_input), embed_low[CLASSES:])) + bias_table[bias_base + 2] + position[None]
    group_size = math.gcd(batch_size, max(1, 4096 // LEN))
    for layer_index in range(LAYERS):
        wide_in = low(weights_in[layer_index])
        wide_out = low(weights_out[layer_index])
        layer_rows = bias_table[layer_index * 14:(layer_index + 1) * 14]
        modes = low_back(matmul('sd,dke->ske', cond_act, wide_in[:, :6])) + layer_rows[None, :6]
        normed = low(layer_norm(residual) * (1.0 + modes[:, None, 1]) + modes[:, None, 0])
        triple = low_back(matmul('std,dke->stke', normed, wide_in[:, 6:9]))
        triple = low(triple + jnp.stack([layer_rows[6], jnp.zeros_like(layer_rows[6]), layer_rows[7]]))
        grouped = triple.reshape(batch_size // group_size, group_size, LEN, 3, head_count, HEAD_DIM)
        attended = lax.map(jax.checkpoint(attention_group), grouped).reshape(batch_size, LEN, D)
        branch = low_back(matmul('std,de->ste', attended, wide_out[0])) + layer_rows[12]
        residual = residual + modes[:, None, 2] * branch
        normed = low(layer_norm(residual) * (1.0 + modes[:, None, 4]) + modes[:, None, 3])
        hidden = low_back(matmul('std,dke->stke', normed, wide_in[:, 9:])) + layer_rows[8:12]
        activated = low(jax.nn.gelu(hidden, approximate=True))
        branch = low_back(matmul('stkd,kde->ste', activated, wide_out[1:])) + layer_rows[13]
        residual = residual + modes[:, None, 5] * branch
    final_mod = low_back(matmul('sd,de->se', cond_act, final_low[:, :2 * D])) + final_bias[:2 * D]
    normed = low(layer_norm(residual) * (1.0 + final_mod[:, None, D:]) + final_mod[:, None, :D])
    predicted = low_back(matmul('std,dp->stp', normed, final_low[:, 2 * D:])) + final_bias[2 * D:]
    error = predicted - noise_target
    return jnp.sum(loss_weights[:, :, None] * error * error)

def adam_update(weight, gradient, moment, second, clip_factor, step_rate):
    gradient = gradient * clip_factor
    moment = BETA_ONE * moment + (1.0 - BETA_ONE) * gradient
    second = BETA_TWO * second + (1.0 - BETA_TWO) * gradient * gradient
    update = moment / (1.0 - BETA_ONE ** STEP) / (jnp.sqrt(second / (1.0 - BETA_TWO ** STEP)) + ADAM_EPS)
    return (weight - step_rate * (update + DECAY * weight), moment, second)

def reference(latents, noise, timesteps, labels, loss_mask, weights_in, weights_out, time_mlp, embed_table, final_layer, bias_table, final_bias, momentum_in, momentum_out, momentum_time, momentum_embed, momentum_final, momentum_bias, momentum_final_bias, variance_in, variance_out, variance_time, variance_embed, variance_final, variance_bias, variance_final_bias):
    batch_size = timesteps.shape[0]
    steps_value = timesteps.astype(jnp.float32)
    alpha_bar = jnp.cos((steps_value / STEPS_T + 0.008) / 1.008 * (math.pi / 2)) ** 2
    clean = latents.reshape(batch_size, LEN, PATCH)
    noise_target = noise.reshape(batch_size, LEN, PATCH)
    noisy_input = jnp.sqrt(alpha_bar)[:, None, None] * clean + jnp.sqrt(1.0 - alpha_bar)[:, None, None] * noise_target
    half_freq = FREQ // 2
    freq_rate = jnp.exp(-math.log(10000.0) * jnp.arange(half_freq, dtype=jnp.float32) / half_freq)
    angle_grid = steps_value[:, None] * freq_rate[None, :]
    freq_feats = jnp.concatenate([jnp.cos(angle_grid), jnp.sin(angle_grid)], axis=1)
    one_hot = (labels[:, None] == jnp.arange(CLASSES, dtype=jnp.int32)[None, :]).astype(jnp.float32)
    position = positions(jnp.arange(LEN, dtype=jnp.int32), jnp.arange(D, dtype=jnp.int32), D)
    loss_weights = loss_mask.reshape(batch_size, LEN).astype(jnp.float32)
    params = (weights_in, weights_out, time_mlp, embed_table, final_layer, bias_table, final_bias)

    def objective(*values):
        return forward(*values, noisy_input, freq_feats, one_hot, position, noise_target, loss_weights)
    loss_value, pullback = jax.vjp(objective, *params)
    grads = pullback(jnp.ones((), jnp.float32))
    squares = jnp.zeros((), jnp.float32)
    for gradient in grads:
        squares = squares + jnp.sum(gradient * gradient)
    grad_norm = jnp.sqrt(squares)
    clip_factor = jnp.minimum(1.0, CLIP_NORM / (grad_norm + 1e-06))
    moments = (momentum_in, momentum_out, momentum_time, momentum_embed, momentum_final, momentum_bias, momentum_final_bias)
    seconds = (variance_in, variance_out, variance_time, variance_embed, variance_final, variance_bias, variance_final_bias)
    step_rates = (RATE, RATE, RATE, RATE, RATE, RATE_BIAS, RATE_BIAS)
    results = [loss_value, jnp.sum(loss_weights), grad_norm]
    for weight, gradient, moment, second, step_rate in zip(params, grads, moments, seconds, step_rates):
        results.extend(adam_update(weight, gradient, moment, second, clip_factor, step_rate))
    return tuple(results)
```

```python
import functools
import math

import jax
import jax.numpy as jnp
import numpy as np
from jax import lax
from jax.experimental import pallas as pl
from jax.experimental.pallas import tpu as pltpu
from jax.sharding import PartitionSpec as P

HEAD_DIM = 64
CLASSES = 1000
FREQ = 256
PATCH = 16
LEN = 256
STEPS_T = 1000
STEP = 10

HIGHEST = lax.Precision.HIGHEST
EPS_NORM = 1e-06
CLIP_NORM = 1.0
RATE = 0.05
RATE_BIAS = 0.25
BETA_ONE = 0.9
BETA_TWO = 0.999
DECAY = 0.01
ADAM_EPS = 1e-08

F32 = jnp.float32
BF16 = jnp.bfloat16
MIB = 1024 * 1024
ANY = pl.BlockSpec(memory_space=pl.ANY)
SMEM = pl.BlockSpec(memory_space=pltpu.SMEM)
NT = (((1,), (1,)), ((), ()))
TN = (((0,), (0,)), ((), ()))


def dot_nt(a, b):
    return lax.dot_general(a, b, NT, preferred_element_type=F32)


def dot_tn(a, b):
    return lax.dot_general(a, b, TN, preferred_element_type=F32)


def dot_nn(a, b):
    return jnp.dot(a, b, preferred_element_type=F32)


class Place:
    def __init__(self, row_block):
        self.rows = lax.axis_size("row")
        self.cols = lax.axis_size("col")
        self.row = lax.axis_index("row")
        self.col = lax.axis_index("col")
        self.direct = self.rows == 8 and self.cols == 4 and row_block % 32 == 0
        self.z = self.row // 2
        self.y = self.row % 2
        self.x = self.col // 2
        self.core = self.col % 2
        if self.direct:
            self.col_order = [
                (self.x ^ kx) * 2 + (self.core ^ kc) for kx in (0, 1) for kc in (0, 1)
            ]
            self.row_offsets = jnp.stack(
                [
                    (((self.z + 4 - kz) % 4) * 2 + (self.y ^ ky)) * row_block
                    for ky in (0, 1)
                    for kz in range(4)
                ]
            ).astype(jnp.int32)
        else:
            self.col_order = [jnp.int32(c) for c in range(self.cols)]
            self.row_offsets = jnp.zeros((8,), jnp.int32)
        self.offsets = jnp.concatenate(
            [self.row_offsets, jnp.stack(self.col_order).astype(jnp.int32)]
        )

    def found_at(self):
        device = jnp.arange(self.rows * self.cols, dtype=jnp.int32)
        if not self.direct:
            return device
        row, col = device // 4, device % 4
        kz = (self.z + 4 - row // 2) % 4
        ky = (row % 2) ^ self.y
        kx = (col // 2) ^ self.x
        kc = (col % 2) ^ self.core
        return ((kc * 2 + kx) * 2 + ky) * 4 + kz


def swap_x(v):
    return lax.ppermute(v, "col", [(c, c ^ 2) for c in range(4)])


def swap_core(v):
    return lax.ppermute(v, "col", [(c, c ^ 1) for c in range(4)])


def swap_y(v):
    return lax.ppermute(v, "row", [(r, r ^ 1) for r in range(8)])


def turn_z(v, k):
    return lax.ppermute(v, "row", [(r, (r // 2 + k) % 4 * 2 + r % 2) for r in range(8)])


def pair(index, own, other):
    first = index == 0
    return jnp.stack([jnp.where(first, own, other), jnp.where(first, other, own)])


def gather_z(place, own):
    got = [own] + [turn_z(own, k) for k in (1, 2, 3)]
    ring = jnp.stack([got[3], got[2], got[1], got[0], got[3], got[2], got[1]])
    return lax.dynamic_slice_in_dim(ring, 3 - place.z, 4, 0)


def gather_cols(place, own):
    if not place.direct:
        return lax.all_gather(own, "col")
    both = pair(place.core, own, swap_core(own))
    return pair(place.x, both, swap_x(both)).reshape((4,) + own.shape)


def gather_all(place, own):
    if not place.direct:
        return lax.all_gather(lax.all_gather(own, "col"), "row")
    by_z = gather_z(place, own)
    by_x = pair(place.x, by_z, swap_x(by_z))
    by_y = pair(place.y, by_x, swap_y(by_x))
    every = pair(place.core, by_y, swap_core(by_y))
    rank = own.ndim
    every = jnp.transpose(every, (3, 1, 2, 0) + tuple(range(4, 4 + rank)))
    return every.reshape((8, 4) + own.shape)


def gather_near(place, own):
    if not place.direct:
        return lax.all_gather(own, ("row", "col"))
    every = jnp.stack([own] + [turn_z(own, k) for k in (1, 2, 3)])
    every = jnp.concatenate([every, swap_y(every)])
    every = jnp.concatenate([every, swap_x(every)])
    return jnp.concatenate([every, swap_core(every)])


def sum_all(place, own):
    if not place.direct:
        return lax.psum(own, ("row", "col"))
    parts = own.reshape((4, own.shape[0] // 4) + own.shape[1:])
    total = lax.dynamic_index_in_dim(parts, place.z, 0, False)
    for k in (1, 2, 3):
        total = total + turn_z(
            lax.dynamic_index_in_dim(parts, (place.z + k) % 4, 0, False), k
        )
    total = total + swap_core(total)
    total = total + swap_x(total)
    total = total + swap_y(total)
    return gather_z(place, total).reshape(own.shape)


def sum_scalar(place, value):
    if not place.direct:
        return lax.psum(value, ("row", "col"))
    total = jnp.broadcast_to(value, (8, 128))
    total = total + swap_core(total)
    total = total + swap_x(total)
    total = total + swap_y(total)
    total = total + lax.ppermute(total, "row", [(r, r ^ 2) for r in range(8)])
    total = total + lax.ppermute(total, "row", [(r, r ^ 4) for r in range(8)])
    return total[0, 0]


def scatter_modes(place, partial):
    rows, cols = place.rows, place.cols
    samples, count, width = partial.shape
    mine = samples // (rows * cols)
    if not place.direct:
        summed = lax.psum_scatter(partial, "row", scatter_dimension=0, tiled=True)
        spread = lax.all_gather(summed, "col")
        spread = lax.dynamic_slice_in_dim(spread, place.col * mine, mine, 1)
        return jnp.transpose(spread, (1, 2, 0, 3)).reshape(mine, count, cols * width)
    by_y = partial.reshape(4, 2, samples // 8, count, width)
    own = lax.dynamic_index_in_dim(by_y, place.y, 1, False)
    own = own + swap_y(lax.dynamic_index_in_dim(by_y, 1 - place.y, 1, False))
    total = lax.dynamic_index_in_dim(own, place.z, 0, False)
    for k in (1, 2, 3):
        total = total + turn_z(lax.dynamic_index_in_dim(own, (place.z + k) % 4, 0, False), k)
    by_x = total.reshape(2, 2, mine, count, width)
    own = lax.dynamic_index_in_dim(by_x, place.x, 0, False)
    got = swap_x(lax.dynamic_index_in_dim(by_x, 1 - place.x, 0, False))
    both = pair(place.x, own, got)
    own = lax.dynamic_index_in_dim(both, place.core, 1, False)
    got = swap_core(lax.dynamic_index_in_dim(both, 1 - place.core, 1, False))
    every = pair(place.core, own, got)
    return jnp.transpose(every, (2, 3, 1, 0, 4)).reshape(mine, count, cols * width)


def weight_tables(place, kind, block):
    cols = place.cols
    if not place.direct:
        return [
            [[(m * cols + c, 0, 0, 0, block * place.rows)] for c in range(cols)]
            for m in range(2 if kind == "mlp" else 1)
        ]
    part = block if kind == "mlp" else block // 2
    first, second = [], []
    for kx in (0, 1):
        for kc in (0, 1):
            one, two = [], []
            for ky in (0, 1):
                for kz in range(4):
                    one.append((kc * 4 + ky, kx * 4 + kz, ky * 4 + kz, 0, part))
                    two.append(
                        (
                            kc * 4 + 2 + kx,
                            ky * 4 + kz,
                            ky * 4 + kz,
                            0 if kind == "mlp" else part,
                            part,
                        )
                    )
            first.append(one)
            second.append(two)
    if kind == "mlp":
        return [first, second]
    return [[one + two for one, two in zip(first, second)]]


class Stages:
    def __init__(self):
        self.last = None

    def run(self, moves, works=()):
        operands = ([v for _, v in moves], [w[1:] for w in works])
        if self.last is not None:
            operands, _ = lax.optimization_barrier((operands, self.last))
        moved = [move(v) for (move, _), v in zip(moves, operands[0])]
        done = [w[0](*v) for w, v in zip(works, operands[1])]
        self.last = (moved, done)
        return moved, done


def turn(k):
    return lambda v: turn_z(v, k)


def add_low(a, b):
    return (a.astype(F32) + b.astype(F32)).astype(BF16)


class Spread:
    def __init__(self, own):
        self.own = own

    def turns(self, ks):
        return [(turn(k), self.own) for k in ks]

    def turned(self, one, two, three):
        got = [self.own, one, two, three]
        self.z_a = jnp.stack([t[0] for t in got])
        self.z_b = jnp.stack([t[1] for t in got])

    def first(self):
        return [(swap_x, self.z_a), (swap_y, self.z_b)]

    def second(self, x_a, y_b):
        self.p_a = jnp.concatenate([self.z_a, x_a])
        self.p_b = jnp.concatenate([self.z_b, y_b])
        return [(swap_y, self.p_a), (swap_x, self.p_b)]

    def cores(self):
        return [(swap_core, self.p_a), (swap_core, self.p_b)]

    def late_cores(self, q_a, q_b):
        self.q_a, self.q_b = q_a, q_b
        return [(swap_core, q_a), (swap_core, q_b)]

    def buffers(self, cores, late_cores):
        return [self.p_a, self.q_a, self.p_b, self.q_b] + [
            cores[0],
            late_cores[0],
            cores[1],
            late_cores[1],
        ]


class Gathered:
    def __init__(self, buffers):
        self.own, other = buffers[:4], buffers[4:]
        self.cores = [(swap_core, v) for v in other]

    def first(self, got):
        p_a, q_a, p_b, q_b = [add_low(a, b) for a, b in zip(self.own, got)]
        self.p_a, self.p_b = p_a, p_b
        return [(swap_y, q_a), (swap_x, q_b)]

    def second(self, got):
        self.p_a = add_low(self.p_a, got[0])
        self.p_b = add_low(self.p_b, got[1])
        return [(swap_x, self.p_a[4:]), (swap_y, self.p_b[4:])]

    def third(self, got):
        z_a = add_low(self.p_a[:4], got[0])
        z_b = add_low(self.p_b[:4], got[1])
        self.z = [jnp.stack([z_a[k], z_b[k]]) for k in range(4)]

    def turns(self, ks):
        return [(turn(4 - k), self.z[k]) for k in ks]

    def total(self, got):
        total = self.z[0].astype(F32)
        for v in got:
            total = total + v.astype(F32)
        return total


def plain_gather(place, kind, own):
    parts = own if kind == "mlp" else own.reshape(1, -1, own.shape[2])
    every = lax.all_gather(lax.all_gather(parts, "row", axis=1, tiled=True), "col")
    return [every[c, m][None] for m in range(parts.shape[0]) for c in range(place.cols)]


def plain_scatter(place, buffers):
    count = len(buffers) // place.cols
    stacked = jnp.stack(
        [
            jnp.stack([buffers[m * place.cols + c][0] for m in range(count)])
            for c in range(place.cols)
        ]
    )
    summed = lax.psum_scatter(stacked.astype(F32), "row", scatter_dimension=2, tiled=True)
    return lax.psum_scatter(summed, "col", scatter_dimension=0, tiled=False)


def normal(v):
    center = jnp.mean(v, axis=-1, keepdims=True)
    moved = v - center
    inverse = lax.rsqrt(jnp.mean(moved * moved, axis=-1, keepdims=True) + EPS_NORM)
    return moved * inverse, inverse


def start_loads(table, offsets, buffers, target, sems):
    for c, entries in enumerate(table):
        for buf, block, at, add, rows in entries:
            begin = pl.multiple_of(offsets[at] + add, 16) if rows < target.shape[1] else 0
            pltpu.make_async_copy(
                buffers[buf].at[block], target.at[c, pl.ds(begin, rows), :], sems.at[c]
            ).start()


def start_stores(entries, offsets, source, buffers, sem):
    for buf, block, at, add, rows in entries:
        begin = pl.multiple_of(offsets[at] + add, 16) if rows < source.shape[0] else 0
        pltpu.make_async_copy(
            source.at[pl.ds(begin, rows), :], buffers[buf].at[block], sem
        ).start()


def wait_all(ref, sem):
    pltpu.make_async_copy(ref, ref, sem).wait()


def row_of(shared_ref, at):
    return jnp.concatenate(
        [shared_ref[c, at : at + 1, :] for c in range(shared_ref.shape[0])], axis=1
    )


def attention_forward_body(table, n_buf, base, offsets, x_ref, mod_ref, shared_ref, *refs):
    buffers = refs[:n_buf]
    out_ref, h_ref, qkv_ref, p_ref, o_ref, a_ref, w_ref, sems = refs[n_buf:]
    c = pl.program_id(0)
    samples = mod_ref.shape[0]

    @pl.when(c == 0)
    def _():
        start_loads(table, offsets, buffers, w_ref, sems)
        for s in range(samples):
            rows = pl.ds(s * LEN, LEN)
            n, _ = normal(x_ref[rows, :])
            h_ref[rows, :] = (n * (1.0 + mod_ref[s, 1:2]) + mod_ref[s, 0:1]).astype(BF16)
        a_ref[...] = jnp.zeros_like(a_ref)

    wait_all(w_ref.at[c], sems.at[c])
    width = shared_ref.shape[-1]
    col = offsets[8 + c]
    query_bias = shared_ref[col, base + 6 : base + 7, :]
    value_bias = shared_ref[col, base + 7 : base + 8, :]
    bias = jnp.concatenate([query_bias, jnp.zeros_like(query_bias), value_bias], axis=1)
    triple = dot_nn(h_ref[...], w_ref[c, :, : 3 * width]) + bias
    qkv_ref[0] = triple.astype(BF16)
    for s in range(samples):
        rows = pl.ds(s * LEN, LEN)
        pieces = []
        for j in range(width // HEAD_DIM):
            q = qkv_ref[0, rows, j * HEAD_DIM : (j + 1) * HEAD_DIM]
            k = qkv_ref[0, rows, width + j * HEAD_DIM : width + (j + 1) * HEAD_DIM]
            v = qkv_ref[0, rows, 2 * width + j * HEAD_DIM : 2 * width + (j + 1) * HEAD_DIM]
            scores = dot_nt(q, k) * HEAD_DIM ** (-0.5)
            powers = jnp.exp(scores - jnp.max(scores, axis=-1, keepdims=True))
            probs = (powers / jnp.sum(powers, axis=-1, keepdims=True)).astype(BF16)
            p_ref[0, j, s] = probs
            pieces.append(dot_nn(probs, v).astype(BF16))
        o_ref[0, rows, :] = jnp.concatenate(pieces, axis=1)
    a_ref[...] += dot_nt(o_ref[0], w_ref[c, :, 3 * width :])

    @pl.when(c == pl.num_programs(0) - 1)
    def _():
        a_ref[...] += row_of(shared_ref, base + 12)
        for s in range(samples):
            rows = pl.ds(s * LEN, LEN)
            out_ref[rows, :] = x_ref[rows, :] + mod_ref[s, 2:3] * a_ref[rows, :]


def mlp_forward_body(tables, n_buf, base, offsets, x_ref, mod_ref, shared_ref, *refs):
    buffers = refs[:n_buf]
    out_ref, h_ref, u_ref, m_ref, wi_ref, wo_ref, sems_i, sems_o = refs[n_buf:]
    c = pl.program_id(0)
    samples = mod_ref.shape[0]

    @pl.when(c == 0)
    def _():
        start_loads(tables[0], offsets, buffers, wi_ref, sems_i)
        start_loads(tables[1], offsets, buffers, wo_ref, sems_o)
        for s in range(samples):
            rows = pl.ds(s * LEN, LEN)
            n, _ = normal(x_ref[rows, :])
            h_ref[rows, :] = (n * (1.0 + mod_ref[s, 1:2]) + mod_ref[s, 0:1]).astype(BF16)
        m_ref[...] = jnp.zeros_like(m_ref)

    wait_all(wi_ref.at[c], sems_i.at[c])
    col = offsets[8 + c]
    blocks = wi_ref.shape[-1] // shared_ref.shape[-1]
    bias = jnp.concatenate(
        [shared_ref[col, base + 8 + k : base + 9 + k, :] for k in range(blocks)], axis=1
    )
    hidden = dot_nn(h_ref[...], wi_ref[c]) + bias
    u_ref[0] = hidden
    active = jax.nn.gelu(hidden, approximate=True).astype(BF16)
    wait_all(wo_ref.at[c], sems_o.at[c])
    m_ref[...] += dot_nt(active, wo_ref[c])

    @pl.when(c == pl.num_programs(0) - 1)
    def _():
        m_ref[...] += row_of(shared_ref, base + 13)
        for s in range(samples):
            rows = pl.ds(s * LEN, LEN)
            out_ref[rows, :] = x_ref[rows, :] + mod_ref[s, 2:3] * m_ref[rows, :]


def norm_backward(s, x_ref, mod_ref, dx_ref, dh_ref, out_ref, dmod_ref):
    rows = pl.ds(s * LEN, LEN)
    n, inverse = normal(x_ref[rows, :])
    dh = dh_ref[rows, :]
    dmod_ref[s, 0:1] = jnp.sum(dh, axis=0, keepdims=True)
    dmod_ref[s, 1:2] = jnp.sum(dh * n, axis=0, keepdims=True)
    dn = dh * (1.0 + mod_ref[s, 1:2])
    back = inverse * (
        dn
        - jnp.mean(dn, axis=-1, keepdims=True)
        - n * jnp.mean(dn * n, axis=-1, keepdims=True)
    )
    if dx_ref is None:
        out_ref[rows, :] = back
    else:
        out_ref[rows, :] = dx_ref[rows, :] + back


def branch_gradient(dx_ref, mod_ref, branch_ref, dmod_ref, sum_ref, low_ref):
    total = None
    for s in range(mod_ref.shape[0]):
        rows = pl.ds(s * LEN, LEN)
        dx = dx_ref[rows, :]
        dmod_ref[s, 2:3] = jnp.sum(dx * branch_ref[rows, :], axis=0, keepdims=True)
        db = mod_ref[s, 2:3] * dx
        low_ref[rows, :] = db.astype(BF16)
        part = jnp.sum(db, axis=0, keepdims=True)
        total = part if total is None else total + part
    sum_ref[...] = total


def gelu_slope(u):
    k = math.sqrt(2.0 / math.pi)
    square = u * u
    t = jnp.tanh(k * (u + 0.044715 * square * u))
    half = 0.5 * (1.0 + t)
    slope = half + 0.5 * u * (1.0 - t * t) * (k * (1.0 + 3 * 0.044715 * square))
    return u * half, slope


def mlp_backward_body(
    tables, n_buf, offsets, dx_ref, x_ref, mod_ref, m_ref, h_ref, u_ref, *refs
):
    buffers = refs[:n_buf]
    out_ref, dmod_ref, dbias_ref, dtail_ref = refs[n_buf : n_buf + 4]
    grads = refs[n_buf + 4 : 2 * n_buf + 4]
    wi_ref, wo_ref, low_ref, dh_ref, gi_ref, go_ref, sems_i, sems_o, sems_gi, sems_go = refs[
        2 * n_buf + 4 :
    ]
    c = pl.program_id(0)
    count = len(tables[0])
    samples = mod_ref.shape[0]

    @pl.when(c == 0)
    def _():
        start_loads(tables[1], offsets, buffers, wo_ref, sems_o)
        start_loads(tables[0], offsets, buffers, wi_ref, sems_i)
        branch_gradient(dx_ref, mod_ref, m_ref, dmod_ref, dtail_ref, low_ref)
        dh_ref[...] = jnp.zeros_like(dh_ref)

    slot = lax.rem(c, 2)

    @pl.when(c >= 2)
    def _():
        wait_all(gi_ref.at[slot], sems_gi.at[slot])
        wait_all(go_ref.at[slot], sems_go.at[slot])

    wait_all(wo_ref.at[c], sems_o.at[c])
    active, slope = gelu_slope(u_ref[0])
    low = low_ref[...]
    go_ref[slot] = dot_tn(low, active.astype(BF16)).astype(BF16)
    for cc in range(count):

        @pl.when(c == cc)
        def _(cc=cc):
            start_stores(tables[1][cc], offsets, go_ref.at[slot], grads, sems_go.at[slot])

    du = dot_nn(low, wo_ref[c]) * slope
    dbias_ref[offsets[8 + c]] = jnp.sum(du, axis=0, keepdims=True)
    du = du.astype(BF16)
    gi_ref[slot] = dot_tn(h_ref[...], du).astype(BF16)
    for cc in range(count):

        @pl.when(c == cc)
        def _(cc=cc):
            start_stores(tables[0][cc], offsets, gi_ref.at[slot], grads, sems_gi.at[slot])

    wait_all(wi_ref.at[c], sems_i.at[c])
    dh_ref[...] += dot_nt(du, wi_ref[c])

    @pl.when(c == count - 1)
    def _():
        for s in range(samples):
            norm_backward(s, x_ref, mod_ref, dx_ref, dh_ref, out_ref, dmod_ref)
        for k in range(2):
            wait_all(gi_ref.at[k], sems_gi.at[k])
            wait_all(go_ref.at[k], sems_go.at[k])


def attention_backward_body(
    table, n_buf, offsets, dx_ref, x_ref, mod_ref, a_ref, h_ref, qkv_ref, p_ref, o_ref, *refs
):
    buffers = refs[:n_buf]
    out_ref, dmod_ref, dbias_ref, dtail_ref = refs[n_buf : n_buf + 4]
    grads = refs[n_buf + 4 : 2 * n_buf + 4]
    w_ref, low_ref, dh_ref, d_ref, g_ref, sems, sems_g = refs[2 * n_buf + 4 :]
    c = pl.program_id(0)
    count = len(table)
    samples = mod_ref.shape[0]
    width = qkv_ref.shape[-1] // 3
    factor = HEAD_DIM ** (-0.5)

    @pl.when(c == 0)
    def _():
        start_loads(table, offsets, buffers, w_ref, sems)
        branch_gradient(dx_ref, mod_ref, a_ref, dmod_ref, dtail_ref, low_ref)
        dh_ref[...] = jnp.zeros_like(dh_ref)

    slot = lax.rem(c, 2)

    @pl.when(c >= 2)
    def _():
        wait_all(g_ref.at[slot], sems_g.at[slot])

    wait_all(w_ref.at[c], sems.at[c])
    do_all = dot_nn(low_ref[...], w_ref[c, :, 3 * width :]).astype(BF16)
    sums = [None] * (width // HEAD_DIM)
    for s in range(samples):
        rows = pl.ds(s * LEN, LEN)
        dqs, dks, dvs = [], [], []
        for j in range(width // HEAD_DIM):
            q = qkv_ref[0, rows, j * HEAD_DIM : (j + 1) * HEAD_DIM]
            k = qkv_ref[0, rows, width + j * HEAD_DIM : width + (j + 1) * HEAD_DIM]
            v = qkv_ref[0, rows, 2 * width + j * HEAD_DIM : 2 * width + (j + 1) * HEAD_DIM]
            o = o_ref[0, rows, j * HEAD_DIM : (j + 1) * HEAD_DIM]
            do = do_all[s * LEN : (s + 1) * LEN, j * HEAD_DIM : (j + 1) * HEAD_DIM]
            probs = p_ref[0, j, s]
            dp = dot_nt(do, v)
            delta = jnp.sum(do.astype(F32) * o.astype(F32), axis=-1, keepdims=True)
            ds = (probs.astype(F32) * (dp - delta)).astype(BF16)
            dqs.append(dot_nn(ds, k) * factor)
            dks.append(dot_tn(ds, q) * factor)
            dvs.append(dot_tn(probs, do))
        joined = jnp.concatenate(dqs + dks + dvs, axis=1)
        part = jnp.sum(joined, axis=0, keepdims=True)
        sums = part if s == 0 else sums + part
        d_ref[rows, :] = joined.astype(BF16)
    dbias_ref[offsets[8 + c]] = sums
    grad_in = dot_tn(h_ref[...], d_ref[...])
    grad_out = dot_tn(low_ref[...], o_ref[0])
    g_ref[slot] = jnp.concatenate([grad_in, grad_out], axis=1).astype(BF16)
    for cc in range(count):

        @pl.when(c == cc)
        def _(cc=cc):
            start_stores(table[cc], offsets, g_ref.at[slot], grads, sems_g.at[slot])

    dh_ref[...] += dot_nt(d_ref[...], w_ref[c, :, : 3 * width])

    @pl.when(c == count - 1)
    def _():
        for s in range(samples):
            norm_backward(s, x_ref, mod_ref, dx_ref, dh_ref, out_ref, dmod_ref)
        for k in range(2):
            wait_all(g_ref.at[k], sems_g.at[k])


def final_body(
    x_ref, mod_ref, head_ref, bias_ref, noise_ref, mask_ref,
    dx_ref, loss_ref, dhead_ref, dbias_ref, dmod_ref, h_ref, dh_ref,
):
    samples = mod_ref.shape[0]
    for s in range(samples):
        rows = pl.ds(s * LEN, LEN)
        n, _ = normal(x_ref[rows, :])
        h_ref[rows, :] = (n * (1.0 + mod_ref[s, 1:2]) + mod_ref[s, 0:1]).astype(BF16)
    predicted = dot_nt(h_ref[...], head_ref[...]) + bias_ref[...]
    error = predicted - noise_ref[...]
    masked = mask_ref[...] * error
    loss_ref[...] = jnp.sum(masked * error, axis=0, keepdims=True)
    dpred = 2.0 * masked
    dbias_ref[...] = jnp.sum(dpred, axis=0, keepdims=True)
    low = dpred.astype(BF16)
    dhead_ref[...] = dot_tn(low, h_ref[...])
    dh_ref[...] = dot_nn(low, head_ref[...])
    for s in range(samples):
        norm_backward(s, x_ref, mod_ref, None, dh_ref, dx_ref, dmod_ref)


def whole_block(shape):
    rank = len(shape)
    return pl.BlockSpec(shape, lambda c: (0,) * rank, pipeline_mode=pl.Buffered(1))


def whole_out(shape):
    rank = len(shape)
    return pl.BlockSpec(shape, lambda c: (0,) * rank)


def block_of(shape):
    rank = len(shape)
    return pl.BlockSpec((1,) + tuple(shape[1:]), lambda c: (c,) + (0,) * (rank - 1))


def params(mib):
    return pltpu.CompilerParams(
        dimension_semantics=("arbitrary",), vmem_limit_bytes=mib * MIB
    )


def cost(flops, nbytes, exps=0):
    return pl.CostEstimate(flops=int(flops), bytes_accessed=int(nbytes), transcendentals=int(exps))


def shaped(shape, dtype):
    return jax.ShapeDtypeStruct(tuple(shape), dtype)


def attention_forward(place, block, base, buffers, x, mods, shared):
    table = weight_tables(place, "attn", block)[0]
    count = len(table)
    tokens, width = x.shape
    samples = mods.shape[0]
    narrow = shared.shape[-1]
    heads = narrow // HEAD_DIM
    outs = [
        shaped((tokens, width), F32),
        shaped((tokens, width), BF16),
        shaped((count, tokens, 3 * narrow), BF16),
        shaped((count, heads, samples, LEN, LEN), BF16),
        shaped((count, tokens, narrow), BF16),
        shaped((tokens, width), F32),
    ]
    return pl.pallas_call(
        functools.partial(attention_forward_body, table, len(buffers), base),
        grid=(count,),
        in_specs=[SMEM, whole_block(x.shape), whole_block(mods.shape), whole_block(shared.shape)]
        + [ANY] * len(buffers),
        out_specs=[whole_out(outs[0].shape), whole_out(outs[1].shape)]
        + [block_of(o.shape) for o in outs[2:5]]
        + [whole_out(outs[5].shape)],
        out_shape=outs,
        scratch_shapes=[
            pltpu.VMEM((count, width, 4 * narrow), BF16),
            pltpu.SemaphoreType.DMA((count,)),
        ],
        compiler_params=params(58),
        cost_estimate=cost(
            2 * tokens * width * width * 4 + 4 * tokens * LEN * width,
            8 * width * width + 30 * tokens * width,
            tokens * LEN * width // HEAD_DIM,
        ),
        name="attention_forward",
    )(place.offsets, x, mods, shared, *buffers)


def mlp_forward(place, block, base, buffers, x, mods, shared):
    tables = weight_tables(place, "mlp", block)
    count = len(tables[0])
    tokens, width = x.shape
    wide = buffers[0].shape[-1]
    outs = [
        shaped((tokens, width), F32),
        shaped((tokens, width), BF16),
        shaped((count, tokens, wide), F32),
        shaped((tokens, width), F32),
    ]
    return pl.pallas_call(
        functools.partial(mlp_forward_body, tables, len(buffers), base),
        grid=(count,),
        in_specs=[SMEM, whole_block(x.shape), whole_block(mods.shape), whole_block(shared.shape)]
        + [ANY] * len(buffers),
        out_specs=[whole_out(outs[0].shape), whole_out(outs[1].shape), block_of(outs[2].shape)]
        + [whole_out(outs[3].shape)],
        out_shape=outs,
        scratch_shapes=[
            pltpu.VMEM((count, width, wide), BF16),
            pltpu.VMEM((count, width, wide), BF16),
            pltpu.SemaphoreType.DMA((count,)),
            pltpu.SemaphoreType.DMA((count,)),
        ],
        compiler_params=params(58),
        cost_estimate=cost(
            2 * tokens * width * wide * count * 2,
            4 * width * wide * count + 30 * tokens * width,
            tokens * wide * count,
        ),
        name="mlp_forward",
    )(place.offsets, x, mods, shared, *buffers)


def mlp_backward(place, block, buffers, dx, x, mods, m, h, u):
    tables = weight_tables(place, "mlp", block)
    count = len(tables[0])
    tokens, width = x.shape
    wide = u.shape[-1]
    outs = [
        shaped((tokens, width), F32),
        shaped(mods.shape, F32),
        shaped((count, 1, wide), F32),
        shaped((1, width), F32),
    ] + [shaped(b.shape, BF16) for b in buffers]
    out = pl.pallas_call(
        functools.partial(mlp_backward_body, tables, len(buffers)),
        grid=(count,),
        in_specs=[SMEM, whole_block(x.shape), whole_block(x.shape), whole_block(mods.shape)]
        + [whole_block(m.shape), whole_block(h.shape), block_of(u.shape)]
        + [ANY] * len(buffers),
        out_specs=[whole_out(x.shape), whole_out(mods.shape), whole_out(outs[2].shape)]
        + [whole_out((1, width))]
        + [ANY] * len(buffers),
        out_shape=outs,
        scratch_shapes=[
            pltpu.VMEM((count, width, wide), BF16),
            pltpu.VMEM((count, width, wide), BF16),
            pltpu.VMEM((tokens, width), BF16),
            pltpu.VMEM((tokens, width), F32),
            pltpu.VMEM((2, width, wide), BF16),
            pltpu.VMEM((2, width, wide), BF16),
            pltpu.SemaphoreType.DMA((count,)),
            pltpu.SemaphoreType.DMA((count,)),
            pltpu.SemaphoreType.DMA((2,)),
            pltpu.SemaphoreType.DMA((2,)),
        ],
        compiler_params=params(58),
        cost_estimate=cost(
            4 * 2 * tokens * width * wide * count,
            8 * width * wide * count + 40 * tokens * width,
            tokens * wide * count,
        ),
        name="mlp_backward",
    )(place.offsets, dx, x, mods, m, h, u, *buffers)
    return out[:4], out[4:]


def attention_backward(place, block, buffers, dx, x, mods, a, h, qkv, p, o):
    table = weight_tables(place, "attn", block)[0]
    count = len(table)
    tokens, width = x.shape
    narrow = o.shape[-1]
    outs = [
        shaped((tokens, width), F32),
        shaped(mods.shape, F32),
        shaped((count, 1, 3 * narrow), F32),
        shaped((1, width), F32),
    ] + [shaped(b.shape, BF16) for b in buffers]
    out = pl.pallas_call(
        functools.partial(attention_backward_body, table, len(buffers)),
        grid=(count,),
        in_specs=[SMEM, whole_block(x.shape), whole_block(x.shape), whole_block(mods.shape)]
        + [whole_block(a.shape), whole_block(h.shape)]
        + [block_of(qkv.shape), block_of(p.shape), block_of(o.shape)]
        + [ANY] * len(buffers),
        out_specs=[whole_out(x.shape), whole_out(mods.shape), whole_out(outs[2].shape)]
        + [whole_out((1, width))]
        + [ANY] * len(buffers),
        out_shape=outs,
        scratch_shapes=[
            pltpu.VMEM((count, width, 4 * narrow), BF16),
            pltpu.VMEM((tokens, width), BF16),
            pltpu.VMEM((tokens, width), F32),
            pltpu.VMEM((tokens, 3 * narrow), BF16),
            pltpu.VMEM((2, width, 4 * narrow), BF16),
            pltpu.SemaphoreType.DMA((count,)),
            pltpu.SemaphoreType.DMA((2,)),
        ],
        compiler_params=params(58),
        cost_estimate=cost(
            4 * tokens * width * width * 4 + 10 * tokens * LEN * width,
            16 * width * width + 40 * tokens * width,
        ),
        name="attention_backward",
    )(place.offsets, dx, x, mods, a, h, qkv, p, o, *buffers)
    return out[:4], out[4:]


def final_step(x, mods, head, bias, noise, mask):
    tokens, width = x.shape
    vmem = pl.BlockSpec(memory_space=pltpu.VMEM)
    return pl.pallas_call(
        final_body,
        in_specs=[vmem] * 6,
        out_specs=[vmem] * 5,
        out_shape=[
            shaped((tokens, width), F32),
            shaped((1, PATCH), F32),
            shaped((PATCH, width), F32),
            shaped((1, PATCH), F32),
            shaped(mods.shape, F32),
        ],
        scratch_shapes=[pltpu.VMEM((tokens, width), BF16), pltpu.VMEM((tokens, width), F32)],
        compiler_params=pltpu.CompilerParams(vmem_limit_bytes=32 * MIB),
        cost_estimate=cost(6 * tokens * width * PATCH, 12 * tokens * width),
        name="final_step",
    )(x, mods, head, bias, noise, mask)


def pack_body(in_ref, out_ref, attn_ref, mlp_ref, mode_ref):
    blocks = out_ref.shape[1] - 1
    for k in range(6):
        mode_ref[0, k] = in_ref[0, k].astype(BF16)
    attn = [in_ref[0, 6 + k] for k in range(3)] + [out_ref[0, 0].T]
    attn_ref[0] = jnp.concatenate(attn, axis=1).astype(BF16)
    first = [in_ref[0, 9 + k] for k in range(blocks)]
    mlp_ref[0, 0] = jnp.concatenate(first, axis=1).astype(BF16)
    second = [out_ref[0, 1 + k].T for k in range(blocks)]
    mlp_ref[0, 1] = jnp.concatenate(second, axis=1).astype(BF16)


def pack_weights(weights_in, weights_out):
    layers, kinds, block, narrow = weights_in.shape
    blocks = weights_out.shape[1] - 1
    outs = [
        shaped((layers, block, 4 * narrow), BF16),
        shaped((layers, 2, block, blocks * narrow), BF16),
        shaped((layers, 6, block, narrow), BF16),
    ]
    return pl.pallas_call(
        pack_body,
        grid=(layers,),
        in_specs=[block_of(weights_in.shape), block_of(weights_out.shape)],
        out_specs=[block_of(o.shape) for o in outs],
        out_shape=outs,
        compiler_params=params(32),
        name="pack_weights",
    )(weights_in, weights_out)


def embed_body(base, noisy_ref, shared_ref, table_ref, out_ref):
    patch = jnp.concatenate(
        [
            shared_ref[c, base + 3 : base + 3 + PATCH, :]
            for c in range(shared_ref.shape[0])
        ],
        axis=1,
    ).astype(BF16)
    constant = row_of(shared_ref, base + 2) + table_ref[...]
    for s in range(noisy_ref.shape[0] // LEN):
        rows = pl.ds(s * LEN, LEN)
        out_ref[rows, :] = dot_nn(noisy_ref[rows, :], patch) + constant


def embed_tokens(base, noisy, shared, table):
    vmem = pl.BlockSpec(memory_space=pltpu.VMEM)
    return pl.pallas_call(
        functools.partial(embed_body, base),
        in_specs=[vmem] * 3,
        out_specs=vmem,
        out_shape=shaped((noisy.shape[0], table.shape[1]), F32),
        compiler_params=pltpu.CompilerParams(vmem_limit_bytes=32 * MIB),
        name="embed_tokens",
    )(noisy, shared, table)


def modes_backward_body(with_final, *refs):
    if with_final:
        near_ref, at_ref, rows_ref, pick_ref, mode_ref, act_ref, final_ref = refs[:7]
        block_ref, partial_ref, square_ref, grad_ref, cond_ref, shared_ref = refs[7:]
    else:
        near_ref, at_ref, rows_ref, pick_ref, mode_ref = refs[:5]
        block_ref, partial_ref, square_ref = refs[5:]
    near = near_ref[...]
    at = at_ref[...]
    where = lax.broadcasted_iota(jnp.int32, (at.shape[0], near.shape[0]), 1)

    def rows_at(step, offset):
        spread = (where == at[:, 0:1] + at[:, 1:2] * step + offset).astype(BF16)
        return dot_nn(spread, near).astype(BF16)

    total = None
    squares = jnp.zeros((1, 1), F32)
    for k in range(6):
        low = rows_at(3, 6 * (k // 3) + k % 3)
        low = dot_nn(low, pick_ref[...]).astype(BF16)
        grad = dot_tn(rows_ref[...], low)
        block_ref[k] = grad
        squares = squares + jnp.sum(grad * grad, keepdims=True)
        part = dot_nt(low, mode_ref[k])
        total = part if total is None else total + part
    partial_ref[...] = total
    if with_final:
        width = act_ref.shape[1]
        shift, scale = rows_at(2, 12), rows_at(2, 13)
        shared_squares = jnp.zeros((1, 1), F32)
        for k, low in enumerate((shift, scale)):
            grad = dot_tn(low, act_ref[...])
            grad_ref[k * width : (k + 1) * width, :] = grad
            shared_squares = shared_squares + jnp.sum(grad * grad, keepdims=True)
        cond_ref[...] = dot_nn(shift, final_ref[:width, :]) + dot_nn(
            scale, final_ref[width : 2 * width, :]
        )
        shared_ref[...] = shared_squares
    square_ref[...] = squares


def modes_backward(near, at, cond_rows, pick, mode_low, act=None, final=None):
    vmem = pl.BlockSpec(memory_space=pltpu.VMEM)
    samples, block = cond_rows.shape
    width = near.shape[2]
    narrow = mode_low.shape[2]
    outs = [shaped((6, block, narrow), F32), shaped((samples, block), F32), shaped((1, 1), F32)]
    operands = [near.reshape(-1, width), at, cond_rows, pick, mode_low]
    if act is not None:
        outs += [shaped((2 * width, width), F32), shaped((samples, width), F32)]
        outs += [shaped((1, 1), F32)]
        operands += [act, final]
    return pl.pallas_call(
        functools.partial(modes_backward_body, act is not None),
        in_specs=[vmem] * len(operands),
        out_specs=[vmem] * len(outs),
        out_shape=outs,
        compiler_params=pltpu.CompilerParams(vmem_limit_bytes=48 * MIB),
        name="modes_backward",
    )(*operands)


def collect_body(layers, *refs):
    out_ref = refs[-1]
    at = 0
    out_ref[...] = jnp.zeros_like(out_ref)
    take = list(refs[:-1])
    for _ in range(layers):
        dmod_a, dmod_b, dbias_a, dbias_b, dtail_a, dtail_b = [take.pop(0) for _ in range(6)]
        for k, source in enumerate((dmod_a, dmod_b)):
            total = source[0]
            for s in range(1, source.shape[0]):
                total = total + source[s]
            out_ref[at + 3 * k : at + 3 * k + 3, :] = total
        for c in range(dbias_b.shape[0]):
            out_ref[at + 6 + c : at + 7 + c, : dbias_b.shape[2]] = dbias_b[c]
            out_ref[at + 10 + c : at + 11 + c, : dbias_a.shape[2]] = dbias_a[c]
        out_ref[at + 14 : at + 15, :] = dtail_a[...]
        out_ref[at + 15 : at + 16, :] = dtail_b[...]
        at += 16
    head, head_bias, loss, mask, dfinal, dx, noisy, first, second, row = take
    out_ref[at : at + PATCH, :] = head[...]
    out_ref[at + PATCH : at + 2 * PATCH, :] = dot_tn(noisy[...], dx[...].astype(BF16))
    at += 2 * PATCH
    out_ref[at : at + 1, :] = jnp.sum(dx[...], axis=0, keepdims=True)
    total = dfinal[0]
    for s in range(1, dfinal.shape[0]):
        total = total + dfinal[s]
    out_ref[at + 1 : at + 3, :] = total
    out_ref[at + 3 : at + 4, 0:PATCH] = head_bias[...]
    out_ref[at + 4 : at + 5, 0:PATCH] = loss[...]
    out_ref[at + 5 : at + 6, 0:1] = jnp.sum(mask[...], keepdims=True)
    at += 16
    cond = first[...] + second[...]
    block, width = cond.shape[1], out_ref.shape[1]
    lane = lax.broadcasted_iota(jnp.int32, (block, width), 1)
    sub = lax.broadcasted_iota(jnp.int32, (block, width), 0)
    spread = (lane == sub + row[0] * block).astype(F32)
    out_ref[at : at + cond.shape[0], :] = jnp.dot(
        cond, spread, precision=HIGHEST, preferred_element_type=F32
    )


def collect(layers, parts, row, height, width):
    vmem = pl.BlockSpec(memory_space=pltpu.VMEM)
    return pl.pallas_call(
        functools.partial(collect_body, layers),
        in_specs=[vmem] * len(parts) + [SMEM],
        out_specs=vmem,
        out_shape=shaped((height, width), F32),
        compiler_params=pltpu.CompilerParams(vmem_limit_bytes=48 * MIB),
        name="collect_small",
    )(*parts, row)


def adam(weight, gradient, moment, second, clip, rate):
    gradient = gradient * clip
    moment = BETA_ONE * moment + (1.0 - BETA_ONE) * gradient
    second = BETA_TWO * second + (1.0 - BETA_TWO) * gradient * gradient
    update = (
        moment / (1.0 - BETA_ONE**STEP) / (jnp.sqrt(second / (1.0 - BETA_TWO**STEP)) + ADAM_EPS)
    )
    return weight - rate * (update + DECAY * weight), moment, second


def adam_blocks_body(clip_ref, mode_ref, attn_ref, mlp_ref, *refs):
    wi, mi, vi, wo, mo, vo = refs[:6]
    out_i, out_o = refs[6:9], refs[9:12]
    clip = clip_ref[0]
    narrow = wi.shape[3]
    for k in range(wi.shape[1]):
        if k < 6:
            grad = mode_ref[0, k]
        elif k < 9:
            grad = attn_ref[0, :, (k - 6) * narrow : (k - 5) * narrow]
        else:
            grad = mlp_ref[0, 0, :, (k - 9) * narrow : (k - 8) * narrow]
        new = adam(wi[0, k], grad, mi[0, k], vi[0, k], clip, RATE)
        for ref, value in zip(out_i, new):
            ref[0, k] = value
    for k in range(wo.shape[1]):
        if k == 0:
            grad = attn_ref[0, :, 3 * narrow :]
        else:
            grad = mlp_ref[0, 1, :, (k - 1) * narrow : k * narrow]
        new = adam(wo[0, k], grad.T, mo[0, k], vo[0, k], clip, RATE)
        for ref, value in zip(out_o, new):
            ref[0, k] = value


def adam_blocks(clip, modes, attn, mlp, ins, outs):
    arrays = [modes, attn, mlp] + list(ins) + list(outs)
    results = [shaped(v.shape, F32) for v in list(ins) + list(outs)]
    return pl.pallas_call(
        adam_blocks_body,
        grid=(ins[0].shape[0],),
        in_specs=[SMEM] + [block_of(v.shape) for v in arrays],
        out_specs=[block_of(v.shape) for v in results],
        out_shape=results,
        compiler_params=params(58),
        name="adam_blocks",
    )(clip, *arrays)


def adam_final_body(clip_ref, grad_ref, head_ref, w, m, v, *outs):
    clip = clip_ref[0]
    step = pl.program_id(0)
    last = pl.num_programs(0) - 1

    def update(rows, gradient):
        new = adam(w[rows, :], gradient, m[rows, :], v[rows, :], clip, RATE)
        for ref, value in zip(outs, new):
            ref[rows, :] = value

    height = w.shape[0]
    update(slice(0, height - PATCH), grad_ref[0 : height - PATCH, :])
    tail = slice(height - PATCH, height)

    @pl.when(step < last)
    def _():
        update(tail, grad_ref[tail, :])

    @pl.when(step == last)
    def _():
        update(tail, head_ref[...])


def adam_final(clip, grad, head, w, m, v):
    height, width = w.shape
    steps = 2
    block = pl.BlockSpec((height // steps, width), lambda c: (c, 0))
    padded = jnp.concatenate([grad, head], axis=0)
    return pl.pallas_call(
        adam_final_body,
        grid=(steps,),
        in_specs=[SMEM, block, whole_block(head.shape), block, block, block],
        out_specs=[block] * 3,
        out_shape=[shaped(w.shape, F32)] * 3,
        compiler_params=params(58),
        name="adam_final",
    )(clip, padded, head, w, m, v)


def adam_rest_body(rates, clip_ref, *refs):
    clip = clip_ref[0]
    count = len(rates)
    ins, outs = refs[: 4 * count], refs[4 * count :]
    for k, rate in enumerate(rates):
        w, g, m, v = [r[...] for r in ins[4 * k : 4 * k + 4]]
        for ref, value in zip(outs[3 * k : 3 * k + 3], adam(w, g, m, v, clip, rate)):
            ref[...] = value


def adam_rest(clip, groups):
    vmem = pl.BlockSpec(memory_space=pltpu.VMEM)
    arrays, results, rates = [], [], []
    for w, g, m, v, rate in groups:
        arrays += [w, g, m, v]
        results += [shaped(w.shape, F32)] * 3
        rates.append(rate)
    return pl.pallas_call(
        functools.partial(adam_rest_body, tuple(rates)),
        in_specs=[SMEM] + [vmem] * len(arrays),
        out_specs=[vmem] * len(results),
        out_shape=results,
        compiler_params=pltpu.CompilerParams(vmem_limit_bytes=48 * MIB),
        name="adam_rest",
    )(clip, *arrays)


def silu_slope(values):
    sigmoid_part = jax.nn.sigmoid(values)
    return sigmoid_part * (1.0 + values * (1.0 - sigmoid_part))


def squared(values):
    return jnp.sum(values * values)


def position_table(width):
    half = width // 2
    rate = np.exp(-math.log(10000.0) * (np.arange(width) % half) / half)
    angle = np.arange(LEN)[:, None] * rate[None, :]
    table = np.where(np.arange(width)[None, :] < half, np.sin(angle), np.cos(angle))
    return table.astype(np.float32)


def on_device(
    latents,
    noise,
    timesteps,
    labels,
    loss_mask,
    weights_in,
    weights_out,
    time_mlp,
    embed_table,
    final_layer,
    bias_table,
    final_bias,
    momentum_in,
    momentum_out,
    momentum_time,
    momentum_embed,
    momentum_final,
    momentum_bias,
    momentum_final_bias,
    variance_in,
    variance_out,
    variance_time,
    variance_embed,
    variance_final,
    variance_bias,
    variance_final_bias,
):
    layers, block, _, narrow = weights_in.shape
    place = Place(block)
    rows, cols = place.rows, place.cols
    width = final_layer.shape[0]
    row_samples = timesteps.shape[0]
    samples = row_samples // cols
    every_sample = row_samples * rows
    tokens = samples * LEN
    base = layers * 14
    hidden_blocks = weights_out.shape[1] - 1

    def my_cols(v, axis):
        return lax.dynamic_slice_in_dim(v, place.col * narrow, narrow, axis)

    in_view = [jnp.transpose(v, (0, 2, 1, 3)) for v in (weights_in, momentum_in, variance_in)]
    attn_low, mlp_low, mode_low = pack_weights(in_view[0], weights_out)
    pieces = []
    for layer in range(layers):
        attn = attn_low[layer]
        if place.direct:
            attn = attn.reshape(2, block // 2, attn.shape[1])
        pieces.append(attn)
        pieces.append(mlp_low[layer])

    embed_low = embed_table.astype(BF16)
    one_hot_row = (labels[:, None] == jnp.arange(CLASSES, dtype=jnp.int32)[None, :]).astype(BF16)
    class_rows = jnp.dot(
        one_hot_row, embed_low[:CLASSES], preferred_element_type=F32
    ).astype(BF16)
    whole_numbers = jnp.concatenate(
        [timesteps // 32, timesteps % 32, labels // 32, labels % 32]
    ).astype(BF16)
    time_rows = time_mlp.shape[0]
    flat = jnp.concatenate(
        [
            time_mlp.astype(BF16).T.reshape(-1),
            class_rows.reshape(-1),
            whole_numbers,
        ]
    )
    size = -(-flat.shape[0] // 2048) * 2048
    flat = jnp.concatenate([flat, jnp.zeros((size - flat.shape[0],), BF16)])
    gathered = gather_all(place, flat.reshape(-1, 128)).reshape(rows, cols, size)
    time_size = narrow * time_rows
    time_blocks = gathered[:, :, :time_size].reshape(rows, cols, narrow, time_rows)
    class_size = row_samples * narrow
    class_part = gathered[:, :, time_size : time_size + class_size]
    class_part = class_part.reshape(rows, cols, row_samples, narrow)
    class_part = jnp.swapaxes(class_part, 1, 2).reshape(every_sample, width).astype(F32)
    numbers = gathered[:, 0, time_size + class_size : time_size + class_size + 4 * row_samples]
    numbers = numbers.astype(jnp.int32).reshape(rows, 4, row_samples)
    all_steps = (numbers[:, 0] * 32 + numbers[:, 1]).reshape(-1)
    all_labels = (numbers[:, 2] * 32 + numbers[:, 3]).reshape(-1)
    time_full = jnp.transpose(time_blocks, (0, 3, 1, 2)).reshape(rows * time_rows, width)

    shared = gather_cols(
        place, jnp.concatenate([bias_table, embed_low[CLASSES:].astype(F32)], axis=0)
    )
    bias_full = jnp.swapaxes(shared, 0, 1).reshape(-1, width)

    half_freq = FREQ // 2
    freq_rate = jnp.asarray(
        np.exp(-math.log(10000.0) * np.arange(half_freq) / half_freq).astype(np.float32)
    )
    angle_grid = all_steps.astype(F32)[:, None] * freq_rate[None, :]
    freq_low = jnp.concatenate([jnp.cos(angle_grid), jnp.sin(angle_grid)], axis=1).astype(BF16)
    first_time = (
        jnp.dot(freq_low, time_full[:FREQ], preferred_element_type=F32) + bias_full[base]
    )
    first_act = jax.nn.silu(first_time).astype(BF16)
    condition = (
        jnp.dot(first_act, time_full[FREQ:], preferred_element_type=F32)
        + bias_full[base + 1]
        + class_part
    )
    cond_act = jax.nn.silu(condition).astype(BF16)

    cond_rows = lax.dynamic_slice_in_dim(cond_act, place.row * block, block, 1)
    partial = jnp.einsum("sd,lkde->slke", cond_rows, mode_low, preferred_element_type=F32)
    modes = scatter_modes(place, partial.reshape(every_sample, layers * 6, narrow))
    modes = modes.reshape(samples, layers, 6, width) + jnp.stack(
        [bias_full[14 * layer : 14 * layer + 6] for layer in range(layers)]
    )
    final_view = [v.T for v in (final_layer, momentum_final, variance_final)]
    final_low = final_view[0].astype(BF16)
    own_start = place.row * row_samples + place.col * samples
    cond_own = lax.dynamic_slice_in_dim(cond_act, own_start, samples, 0)
    final_mod = (
        jnp.einsum("sd,ed->se", cond_own, final_low[: 2 * width], preferred_element_type=F32)
        + final_bias[: 2 * width]
    ).reshape(samples, 2, width)

    own_tokens = place.col * tokens
    latents = lax.dynamic_slice_in_dim(latents, own_tokens, tokens, 0)
    noise = lax.dynamic_slice_in_dim(noise, own_tokens, tokens, 0)
    mask = lax.dynamic_slice_in_dim(loss_mask, own_tokens, tokens, 0).astype(F32)
    steps_own = lax.dynamic_slice_in_dim(timesteps, place.col * samples, samples, 0).astype(F32)
    alpha_bar = jnp.cos((steps_own / STEPS_T + 0.008) / 1.008 * (math.pi / 2)) ** 2
    keep_part = jnp.repeat(jnp.sqrt(alpha_bar), LEN)[:, None]
    noise_part = jnp.repeat(jnp.sqrt(1.0 - alpha_bar), LEN)[:, None]
    noisy = (keep_part * latents + noise_part * noise).astype(BF16)
    residual = embed_tokens(base, noisy, shared, jnp.asarray(position_table(width)))

    def attn_step(layer):
        def work(buffers, x, mods):
            return attention_forward(place, block, 14 * layer, buffers, x, mods, shared)

        return work

    def mlp_step(layer):
        def work(buffers, x, mods):
            return mlp_forward(place, block, 14 * layer, buffers, x, mods, shared)

        return work

    def attn_back(buffers, *operands):
        return attention_backward(place, block, buffers, *operands)

    def mlp_back(buffers, *operands):
        return mlp_backward(place, block, buffers, *operands)

    head_low = final_low[2 * width :]

    def last_step(x):
        return final_step(
            x, final_mod, head_low, final_bias[2 * width :][None], noise, mask[:, None]
        )

    mods_a = [modes[:, layer, 0:3] for layer in range(layers)]
    mods_b = [modes[:, layer, 3:6] for layer in range(layers)]
    buffers = [None] * (2 * layers)
    fore_a, fore_b = [None] * layers, [None] * layers
    entry = [None] * layers
    back_a, back_b = [None] * layers, [None] * layers
    summed = [None] * (2 * layers)
    if place.direct and layers == 2:
        stages = Stages()
        spread = [Spread(v) for v in pieces]
        a0, b0, a1, b1 = spread
        (t1, t3, t2), _ = stages.run(a0.turns((1, 3, 2)))
        a0.turned(t1, t2, t3)
        got, _ = stages.run(a0.first() + b0.turns((1, 3)))
        t1, t3 = got[2:]
        got, _ = stages.run(a0.second(*got[:2]) + b0.turns((2,)) + a0.cores())
        b0.turned(t1, got[2], t3)
        cores = got[3:]
        got, _ = stages.run(b0.first() + a1.turns((1, 3)) + a0.late_cores(*got[:2]))
        buffers[0] = a0.buffers(cores, got[4:])
        t1, t3 = got[2:4]
        got, _ = stages.run(b0.second(*got[:2]) + a1.turns((2,)) + b0.cores())
        a1.turned(t1, got[2], t3)
        cores = got[3:]
        got, (fore_a[0],) = stages.run(
            a1.first() + b1.turns((1, 3)) + b0.late_cores(*got[:2]),
            [(attn_step(0), buffers[0], residual, mods_a[0])],
        )
        buffers[1] = b0.buffers(cores, got[4:])
        t1, t3 = got[2:4]
        got, (fore_b[0],) = stages.run(
            a1.second(*got[:2]) + b1.turns((2,)) + a1.cores(),
            [(mlp_step(0), buffers[1], fore_a[0][0], mods_b[0])],
        )
        b1.turned(t1, got[2], t3)
        cores = got[3:]
        got, _ = stages.run(b1.first() + a1.late_cores(*got[:2]))
        buffers[2] = a1.buffers(cores, got[2:])
        got, (fore_a[1],) = stages.run(
            b1.second(*got[:2]) + b1.cores(),
            [(attn_step(1), buffers[2], fore_b[0][0], mods_a[1])],
        )
        cores = got[2:]
        got, _ = stages.run(b1.late_cores(*got[:2]))
        buffers[3] = b1.buffers(cores, got)
        _, (fore_b[1],) = stages.run([], [(mlp_step(1), buffers[3], fore_a[1][0], mods_b[1])])
        entry = [residual, fore_b[0][0]]
        last = last_step(fore_b[1][0])

        def back_b_work(layer, grad):
            out, h, u, m = fore_b[layer]
            return (mlp_back, buffers[2 * layer + 1], grad, fore_a[layer][0], mods_b[layer], m, h, u)

        def back_a_work(layer, grad):
            out, h, qkv, p, o, a = fore_a[layer]
            return (
                attn_back, buffers[2 * layer], grad, entry[layer], mods_a[layer], a, h, qkv, p, o,
            )

        _, ((back_b[1], grads),) = stages.run([], [back_b_work(1, last[0])])
        gb1 = Gathered(grads)
        core_b1, ((back_a[1], grads),) = stages.run(gb1.cores, [back_a_work(1, back_b[1][0])])
        ga1 = Gathered(grads)
        got, ((back_b[0], grads),) = stages.run(
            gb1.first(core_b1) + ga1.cores, [back_b_work(0, back_a[1][0])]
        )
        core_a1 = got[2:]
        gb0 = Gathered(grads)
        got, _ = stages.run(gb1.second(got[:2]) + gb0.cores)
        gb1.third(got[:2])
        core_b0 = got[2:]
        got, ((back_a[0], grads),) = stages.run(
            gb0.first(core_b0) + gb1.turns((1, 3)), [back_a_work(0, back_b[0][0])]
        )
        turned_b1 = got[2:]
        ga0 = Gathered(grads)
        got, _ = stages.run(gb0.second(got[:2]) + gb1.turns((2,)) + ga0.cores)
        summed[3] = gb1.total(turned_b1 + got[2:3])
        core_a0 = got[3:]
        gb0.third(got[:2])
        got, _ = stages.run(ga1.first(core_a1) + gb0.turns((1, 3)))
        turned_b0 = got[2:]
        got, _ = stages.run(ga1.second(got[:2]) + ga0.first(core_a0) + gb0.turns((2,)))
        summed[1] = gb0.total(turned_b0 + got[4:])
        ga1.third(got[:2])
        got, _ = stages.run(ga0.second(got[2:4]) + ga1.turns((1, 3, 2)))
        summed[2] = ga1.total(got[2:])
        ga0.third(got[:2])
        got, _ = stages.run(ga0.turns((1, 3, 2)))
        summed[0] = ga0.total(got)
    else:
        grad = residual
        for layer in range(layers):
            buffers[2 * layer] = plain_gather(place, "attn", pieces[2 * layer][None])
            buffers[2 * layer + 1] = plain_gather(place, "mlp", pieces[2 * layer + 1])
            entry[layer] = grad
            fore_a[layer] = attn_step(layer)(buffers[2 * layer], grad, mods_a[layer])
            grad = fore_a[layer][0]
            fore_b[layer] = mlp_step(layer)(buffers[2 * layer + 1], grad, mods_b[layer])
            grad = fore_b[layer][0]
        last = last_step(grad)
        grad = last[0]
        for layer in reversed(range(layers)):
            out, h, u, m = fore_b[layer]
            back_b[layer], grads = mlp_back(
                buffers[2 * layer + 1], grad, fore_a[layer][0], mods_b[layer], m, h, u
            )
            summed[2 * layer + 1] = plain_scatter(place, grads)
            grad = back_b[layer][0]
            out, h, qkv, p, o, a = fore_a[layer]
            back_a[layer], grads = attn_back(
                buffers[2 * layer], grad, entry[layer], mods_a[layer], a, h, qkv, p, o
            )
            summed[2 * layer] = plain_scatter(place, grads)
            grad = back_a[layer][0]

    _, loss_parts, grad_head, grad_head_bias, grad_final_mod = last
    found = place.found_at()
    sample = jnp.arange(every_sample, dtype=jnp.int32)
    at = jnp.stack([found[sample // samples] * 16, sample % samples], axis=1)
    feature = jnp.arange(width, dtype=jnp.int32)[:, None]
    picked = jnp.arange(narrow, dtype=jnp.int32)[None, :] + place.col * narrow
    pick = (feature == picked).astype(BF16)
    mode_blocks, partials = [None] * layers, []
    own_squares = jnp.zeros((), F32)
    for layer in reversed(range(layers)):
        parts = [back_a[layer][1].reshape(-1, width), back_b[layer][1].reshape(-1, width)]
        top = layer == layers - 1
        if top:
            parts.append(grad_final_mod.reshape(-1, width))
        parts = jnp.concatenate(parts, axis=0).astype(BF16)
        parts = jnp.concatenate([parts, jnp.zeros((16 - parts.shape[0], width), BF16)], axis=0)
        near = gather_near(place, parts)
        got = modes_backward(
            near, at, cond_rows, pick, mode_low[layer], *((cond_act, final_low) if top else ())
        )
        mode_blocks[layer] = got[0]
        partials.append(got[1])
        own_squares = own_squares + got[2][0, 0]
        if top:
            final_grad, cond_final, final_squares = got[3:]
    while len(partials) > 2:
        partials[-2:] = [partials[-2] + partials[-1]]
    small = []
    for layer in range(layers):
        _, dmod_a, dbias_a, dtail_a = back_a[layer]
        _, dmod_b, dbias_b, dtail_b = back_b[layer]
        small += [dmod_a, dmod_b, dbias_a, dbias_b, dtail_a, dtail_b]
    start = 16 * layers + 2 * PATCH
    height = -(-(start + 16 + every_sample) // 32) * 32
    small += [
        grad_head,
        grad_head_bias,
        loss_parts,
        mask[:, None],
        grad_final_mod,
        back_a[0][0],
        noisy,
    ] + partials
    small = collect(layers, small, place.row[None].astype(jnp.int32), height, width)
    small = sum_all(place, small)
    head_grad = small[start - 2 * PATCH : start - PATCH]
    patch_grad = small[start - PATCH : start]
    final_bias_grad = jnp.concatenate(
        [small[start + 1], small[start + 2], small[start + 3, :PATCH]]
    )
    loss_total = jnp.sum(small[start + 4, :PATCH])
    count_total = small[start + 5, 0]
    grad_cond = small[start + 16 : start + 16 + every_sample] + cond_final

    grad_condition = grad_cond * silu_slope(condition)
    one_hot = (all_labels[:, None] == jnp.arange(CLASSES, dtype=jnp.int32)[None, :]).astype(F32)
    grad_classes = jnp.einsum(
        "sd,sc->dc", my_cols(grad_condition, 1), one_hot, precision=HIGHEST
    )
    condition_low = grad_condition.astype(BF16)
    grad_first = jnp.einsum(
        "se,de->sd", condition_low, time_full[FREQ:], preferred_element_type=F32
    ) * silu_slope(first_time)
    first_low = grad_first.astype(BF16)
    time_inputs = lax.dynamic_slice_in_dim(
        jnp.concatenate([freq_low, first_act], axis=1), place.row * time_rows, time_rows, 1
    )
    time_outputs = my_cols(
        jnp.where((place.row + 1) * time_rows <= FREQ, first_low, condition_low), 1
    )
    time_grad = jnp.einsum("sd,se->ed", time_inputs, time_outputs, preferred_element_type=F32)

    own_rows, shared_squares = [], jnp.zeros((), F32)
    for layer in range(layers):
        rows_at = small[16 * layer : 16 * layer + 16]
        own = my_cols(rows_at, 1)
        mlp_rows = lax.dynamic_index_in_dim(rows_at[6:10], place.col, 0, False)
        attn_rows = lax.dynamic_index_in_dim(rows_at[10:14], place.col, 0, False)
        attn_rows = attn_rows[: 3 * narrow].reshape(3, narrow)
        own_rows += [own[:6], attn_rows[0:1], attn_rows[2:3]]
        own_rows += [mlp_rows[: hidden_blocks * narrow].reshape(hidden_blocks, narrow), own[14:16]]
        counted = rows_at[10:14, : 3 * narrow].reshape(4, 3, narrow)[:, 0::2]
        shared_squares = (
            shared_squares + squared(rows_at[:10]) + squared(counted) + squared(rows_at[14:])
        )
    time_bias = jnp.stack([jnp.sum(grad_first, axis=0), jnp.sum(grad_condition, axis=0)])
    patch_bias = small[start : start + 1]
    own_rows += [my_cols(time_bias, 1), my_cols(patch_bias, 1)]
    bias_grad = jnp.concatenate(own_rows, axis=0)
    shared_squares = (
        shared_squares
        + squared(time_bias)
        + squared(small[start - 2 * PATCH : start + 3])
        + squared(small[start + 3, :PATCH])
        + final_squares[0, 0]
    )
    own_squares = own_squares + squared(time_grad) + squared(grad_classes) / rows
    for value in summed:
        own_squares = own_squares + squared(value)
    grad_norm = jnp.sqrt(sum_scalar(place, own_squares) + shared_squares)
    clip_factor = jnp.minimum(1.0, CLIP_NORM / (grad_norm + 1e-06))
    clip = clip_factor[None]

    results = [loss_total, count_total, grad_norm]
    attn_sums = jnp.stack([summed[2 * k].reshape(block, 4 * narrow) for k in range(layers)])
    mlp_sums = jnp.stack([summed[2 * k + 1] for k in range(layers)])
    new_blocks = adam_blocks(
        clip,
        jnp.stack(mode_blocks),
        attn_sums,
        mlp_sums,
        in_view,
        [weights_out, momentum_out, variance_out],
    )
    results += [jnp.transpose(v, (0, 2, 1, 3)) for v in new_blocks[:3]] + list(new_blocks[3:])
    embed_grad = jnp.concatenate([grad_classes, my_cols(patch_grad, 1).T], axis=1)
    rest = adam_rest(
        clip,
        [
            (time_mlp.T, time_grad, momentum_time.T, variance_time.T, RATE),
            (embed_table.T, embed_grad, momentum_embed.T, variance_embed.T, RATE),
            (bias_table, bias_grad, momentum_bias, variance_bias, RATE_BIAS),
            (
                final_bias[None],
                final_bias_grad[None],
                momentum_final_bias[None],
                variance_final_bias[None],
                RATE_BIAS,
            ),
        ],
    )
    results += [v.T for v in rest[:6]]
    results += [v.T for v in adam_final(clip, final_grad, head_grad, *final_view)]
    results += list(rest[6:9]) + [v[0] for v in rest[9:]]
    return tuple(results)


def solution(mesh):
    tokens, latents = P("row", None), P("row")
    weights = (
        P(None, "row", None, "col"),
        P(None, None, "col", "row"),
        P("row", "col"),
        P(None, "col"),
        P(),
        P(None, "col"),
        P(),
    )
    updated = []
    for spec in weights:
        updated += [spec] * 3
    return jax.shard_map(
        on_device,
        mesh=mesh,
        in_specs=(tokens, tokens, latents, latents, latents) + weights * 3,
        out_specs=(P(), P(), P()) + tuple(updated),
        check_vma=False,
    )
```

```python
import functools
import math

import jax
import jax.numpy as jnp
import numpy as np
from jax import lax
from jax.experimental import pallas as pl
from jax.experimental.pallas import tpu as pltpu
from jax.sharding import PartitionSpec as P

HEAD_DIM = 64
CLASSES = 1000
FREQ = 256
PATCH = 16
LEN = 256
STEPS_T = 1000
STEP = 10

HIGHEST = lax.Precision.HIGHEST
EPS_NORM = 1e-06
CLIP_NORM = 1.0
RATE = 0.05
RATE_BIAS = 0.25
BETA_ONE = 0.9
BETA_TWO = 0.999
DECAY = 0.01
ADAM_EPS = 1e-08

F32 = jnp.float32
BF16 = jnp.bfloat16
MIB = 1024 * 1024
ANY = pl.BlockSpec(memory_space=pl.ANY)
SMEM = pl.BlockSpec(memory_space=pltpu.SMEM)
NT = (((1,), (1,)), ((), ()))
TN = (((0,), (0,)), ((), ()))


def dot_nt(a, b):
    return lax.dot_general(a, b, NT, preferred_element_type=F32)


def dot_tn(a, b):
    return lax.dot_general(a, b, TN, preferred_element_type=F32)


def dot_nn(a, b):
    return jnp.dot(a, b, preferred_element_type=F32)


class Place:
    def __init__(self, row_block):
        self.rows = lax.axis_size("row")
        self.cols = lax.axis_size("col")
        self.row = lax.axis_index("row")
        self.col = lax.axis_index("col")
        self.direct = self.rows == 8 and self.cols == 4 and row_block % 32 == 0
        self.z = self.row // 2
        self.y = self.row % 2
        self.x = self.col // 2
        self.core = self.col % 2
        self.half = row_block // 2
        self.table = self.route_table() if self.direct else jnp.zeros((8,), jnp.int32)

    def route_table(self):
        z, y, x, core = self.z, self.y, self.x, self.core
        e = jnp.arange(64, dtype=jnp.int32)
        owner = core ^ (e // 32)
        later, first, kc, kz = e // 16 % 2, e // 8 % 2, e // 4 % 2, e % 4
        kx = jnp.where(owner == 0, first, later)
        ky = jnp.where(owner == 0, later, first)
        cols = (x ^ kx) * 2 + (owner ^ kc)
        rows = ((z + 4 - kz) % 4 * 2 + (y ^ ky)) * 2 * self.half + owner * self.half
        e = jnp.arange(16, dtype=jnp.int32)
        col, owner, ky = e // 4, core ^ (e // 2 % 2), e % 2
        kx = (col // 2) ^ x
        later = jnp.where(owner == 0, ky, kx)
        first = jnp.where(owner == 0, kx, ky)
        slots = jnp.stack([later, first, (col % 2) ^ owner], axis=1).reshape(-1)
        owner, ky, kz = core ^ (e // 8), e // 4 % 2, e % 4
        outs = ((z + 4 - kz) % 4 * 2 + (y ^ ky)) * 2 * self.half + owner * self.half
        return jnp.concatenate([cols, rows, slots, outs]).astype(jnp.int32)

    def found_at(self):
        device = jnp.arange(self.rows * self.cols, dtype=jnp.int32)
        if not self.direct:
            return device
        row, col = device // 4, device % 4
        kz = (self.z + 4 - row // 2) % 4
        ky = (row % 2) ^ self.y
        kx = (col // 2) ^ self.x
        kc = (col % 2) ^ self.core
        return ((kc * 2 + kx) * 2 + ky) * 4 + kz


def swap_x(v):
    return lax.ppermute(v, "col", [(c, c ^ 2) for c in range(4)])


def swap_core(v):
    return lax.ppermute(v, "col", [(c, c ^ 1) for c in range(4)])


def swap_y(v):
    return lax.ppermute(v, "row", [(r, r ^ 1) for r in range(8)])


def swap_first(v):
    pairs = [(d, d ^ 2 if d % 2 == 0 else d ^ 4) for d in range(32)]
    return lax.ppermute(v, ("row", "col"), pairs)


def swap_second(v):
    pairs = [(d, d ^ 4 if d % 2 == 0 else d ^ 2) for d in range(32)]
    return lax.ppermute(v, ("row", "col"), pairs)


def turn_z(v, k):
    return lax.ppermute(v, "row", [(r, (r // 2 + k) % 4 * 2 + r % 2) for r in range(8)])


def pair(index, own, other):
    first = index == 0
    return jnp.stack([jnp.where(first, own, other), jnp.where(first, other, own)])


def gather_z(place, own):
    got = [own] + [turn_z(own, k) for k in (1, 2, 3)]
    ring = jnp.stack([got[3], got[2], got[1], got[0], got[3], got[2], got[1]])
    return lax.dynamic_slice_in_dim(ring, 3 - place.z, 4, 0)


def gather_cols(place, own):
    if not place.direct:
        return lax.all_gather(own, "col")
    both = pair(place.core, own, swap_core(own))
    return pair(place.x, both, swap_x(both)).reshape((4,) + own.shape)


def near_z(own):
    return jnp.stack([own] + [turn_z(own, k) for k in (1, 2, 3)])


def near_y(every):
    return jnp.concatenate([every, swap_y(every)])


def near_rows(own):
    return near_y(near_z(own))


def near_x(every):
    return jnp.concatenate([every, swap_x(every)])


def near_core(every):
    return jnp.concatenate([every, swap_core(every)])


def near_cols(every):
    return near_core(near_x(every))


def gather_near(place, own):
    if not place.direct:
        return lax.all_gather(own, ("row", "col"))
    return near_cols(near_rows(own))


def sum_along_z(place, own):
    parts = own.reshape((4, own.shape[0] // 4) + own.shape[1:])
    total = lax.dynamic_index_in_dim(parts, place.z, 0, False)
    for k in (1, 2, 3):
        total = total + turn_z(
            lax.dynamic_index_in_dim(parts, (place.z + k) % 4, 0, False), k
        )
    return total


def sum_with(swap):
    return lambda total: total + swap(total)


def sum_spread(place, total):
    every = gather_z(place, total)
    return every.reshape((-1,) + total.shape[1:])


def sum_scalar(place, value):
    if not place.direct:
        return lax.psum(value, ("row", "col"))
    total = jnp.broadcast_to(value, (8, 128))
    total = total + swap_core(total)
    total = total + swap_x(total)
    total = total + swap_y(total)
    total = total + lax.ppermute(total, "row", [(r, r ^ 2) for r in range(8)])
    total = total + lax.ppermute(total, "row", [(r, r ^ 4) for r in range(8)])
    return total[0, 0]


def scatter_plain(place, partial, mine):
    _, count, narrow = partial.shape
    summed = lax.psum_scatter(partial, "row", scatter_dimension=0, tiled=True)
    spread = lax.all_gather(summed, "col")
    spread = lax.dynamic_slice_in_dim(spread, place.col * mine, mine, 1)
    return jnp.transpose(spread, (1, 2, 0, 3)).reshape(mine, count, place.cols * narrow)


def scatter_y(place, partial):
    samples, count, narrow = partial.shape
    by_y = partial.reshape(4, 2, samples // 8, count, narrow)
    own = lax.dynamic_index_in_dim(by_y, place.y, 1, False)
    return own + swap_y(lax.dynamic_index_in_dim(by_y, 1 - place.y, 1, False))


def scatter_z(place, own):
    total = lax.dynamic_index_in_dim(own, place.z, 0, False)
    for k in (1, 2, 3):
        total = total + turn_z(lax.dynamic_index_in_dim(own, (place.z + k) % 4, 0, False), k)
    return total


def scatter_x(place, total, mine):
    _, count, narrow = total.shape
    by_x = total.reshape(2, 2, mine, count, narrow)
    own = lax.dynamic_index_in_dim(by_x, place.x, 0, False)
    got = swap_x(lax.dynamic_index_in_dim(by_x, 1 - place.x, 0, False))
    return pair(place.x, own, got)


def scatter_core(place, both):
    _, _, mine, count, narrow = both.shape
    own = lax.dynamic_index_in_dim(both, place.core, 1, False)
    got = swap_core(lax.dynamic_index_in_dim(both, 1 - place.core, 1, False))
    every = pair(place.core, own, got)
    return jnp.transpose(every, (2, 3, 1, 0, 4)).reshape(mine, count, 4 * narrow)


class Route:
    def __init__(self, place, buffers):
        self.direct = place.direct
        self.half = place.half
        self.cols = place.cols
        self.count = len(buffers)
        if self.direct:
            matrices = buffers[0].shape[2]
            self.outs = [(2, 8, 2, matrices) + buffers[0].shape[3:]] * 2
        else:
            self.outs = [buffers[0].shape]

    def load(self, table, buffers, matrix, target, sems):
        if not self.direct:
            for c in range(self.cols):
                pltpu.make_async_copy(buffers[0].at[matrix, c], target.at[c], sems.at[c]).start()
            return
        for e in range(64):
            first, kc, kz = e // 8 % 2, e // 4 % 2, e % 4
            row = pl.multiple_of(table[64 + e], 16)
            pltpu.make_async_copy(
                buffers[e // 16].at[first * 4 + kz, kc, matrix],
                target.at[table[e], pl.ds(row, self.half), :],
                sems.at[table[e]],
            ).start()

    def store(self, table, c, matrix, source, grads, sem):
        if not self.direct:
            pltpu.make_async_copy(source, grads[0].at[matrix, c], sem).start()
            return
        for owner in range(2):
            for ky in range(2):
                at = 128 + ((c * 2 + owner) * 2 + ky) * 3
                for kz in range(4):
                    row = pl.multiple_of(table[176 + (owner * 2 + ky) * 4 + kz], 16)
                    pltpu.make_async_copy(
                        source.at[pl.ds(row, self.half), :],
                        grads[owner].at[
                            table[at], table[at + 1] * 4 + kz, table[at + 2], matrix
                        ],
                        sem,
                    ).start()


class Stages:
    def __init__(self):
        self.last = None

    def run(self, moves, works=()):
        operands = ([v for _, v in moves], [w[1:] for w in works])
        if self.last is not None:
            operands, _ = lax.optimization_barrier((operands, self.last))
        moved = [move(v) for (move, _), v in zip(moves, operands[0])]
        done = [w[0](*v) for w, v in zip(works, operands[1])]
        self.last = (moved, done)
        return moved, done


def turn(k):
    return lambda v: turn_z(v, k)


class Spread:
    def __init__(self, kept, got):
        self.own = jnp.stack([kept, got])

    def turns(self, ks):
        return [(turn(k), self.own) for k in ks]

    def turned(self, one, two, three):
        self.z = jnp.stack([self.own, one, two, three])

    def first(self):
        return [(swap_first, self.z)]

    def second(self, got):
        self.p = jnp.concatenate([self.z, got])
        return [(swap_second, self.p)]

    def core(self):
        return [(swap_core, self.p)]

    def late_core(self, q):
        self.q = q
        return [(swap_core, q)]

    def buffers(self, core, late_core):
        return [self.p, self.q, core, late_core]


def add_up(*parts):
    total = parts[0].astype(F32)
    for part in parts[1:]:
        total = total + part.astype(F32)
    return total


class Gathered:
    def __init__(self, buffers):
        self.own = buffers[0]
        self.core = [(swap_core, buffers[1])]

    def first(self, got):
        self.got = got
        return [(swap_second, add_up(self.own[1], got[1]).astype(BF16))]

    def second(self, got):
        self.parts = (self.own[0], self.got[0], got)
        return [(swap_first, add_up(*[v[4:] for v in self.parts]).astype(BF16))]

    def third(self, got):
        self.z = [add_up(*[v[k] for v in self.parts], got[k]).astype(BF16) for k in range(4)]

    def turns(self, ks=(1, 3, 2)):
        return [(turn(4 - k), self.z[k]) for k in ks]

    def total(self, got):
        return add_up(self.z[0], *got)


def plain_gather(parts):
    every = lax.all_gather(lax.all_gather(parts, "row", axis=1, tiled=True), "col")
    return jnp.swapaxes(every, 0, 1)


def plain_scatter(grads):
    summed = lax.psum_scatter(grads.astype(F32), "row", scatter_dimension=2, tiled=True)
    return lax.psum_scatter(summed, "col", scatter_dimension=1, tiled=False)


def normal(v):
    center = jnp.mean(v, axis=-1, keepdims=True)
    moved = v - center
    inverse = lax.rsqrt(jnp.mean(moved * moved, axis=-1, keepdims=True) + EPS_NORM)
    return moved * inverse, inverse


def wait_all(ref, sem):
    pltpu.make_async_copy(ref, ref, sem).wait()


def row_of(shared_ref, at):
    return jnp.concatenate(
        [shared_ref[c, at : at + 1, :] for c in range(shared_ref.shape[0])], axis=1
    )


def attention_forward_body(route, base, table, x_ref, mod_ref, shared_ref, *refs):
    n_buf = route.count
    buffers = refs[:n_buf]
    out_ref, h_ref, qkv_ref, p_ref, o_ref, a_ref, w_ref, sems = refs[n_buf:]
    c = pl.program_id(0)
    samples = mod_ref.shape[0]

    @pl.when(c == 0)
    def _():
        route.load(table, buffers, 0, w_ref, sems)
        for s in range(samples):
            rows = pl.ds(s * LEN, LEN)
            n, _ = normal(x_ref[rows, :])
            h_ref[rows, :] = (n * (1.0 + mod_ref[s, 1:2]) + mod_ref[s, 0:1]).astype(BF16)
        a_ref[...] = jnp.zeros_like(a_ref)

    wait_all(w_ref.at[c], sems.at[c])
    width = shared_ref.shape[-1]
    query_bias = shared_ref[c, base + 6 : base + 7, :]
    value_bias = shared_ref[c, base + 7 : base + 8, :]
    bias = jnp.concatenate([query_bias, jnp.zeros_like(query_bias), value_bias], axis=1)
    triple = dot_nn(h_ref[...], w_ref[c, :, : 3 * width]) + bias
    qkv_ref[0] = triple.astype(BF16)
    for s in range(samples):
        rows = pl.ds(s * LEN, LEN)
        pieces = []
        for j in range(width // HEAD_DIM):
            q = qkv_ref[0, rows, j * HEAD_DIM : (j + 1) * HEAD_DIM]
            k = qkv_ref[0, rows, width + j * HEAD_DIM : width + (j + 1) * HEAD_DIM]
            v = qkv_ref[0, rows, 2 * width + j * HEAD_DIM : 2 * width + (j + 1) * HEAD_DIM]
            scores = dot_nt(q, k) * HEAD_DIM ** (-0.5)
            powers = jnp.exp(scores - jnp.max(scores, axis=-1, keepdims=True))
            probs = (powers / jnp.sum(powers, axis=-1, keepdims=True)).astype(BF16)
            p_ref[0, j, s] = probs
            pieces.append(dot_nn(probs, v).astype(BF16))
        o_ref[0, rows, :] = jnp.concatenate(pieces, axis=1)
    a_ref[...] += dot_nt(o_ref[0], w_ref[c, :, 3 * width :])

    @pl.when(c == pl.num_programs(0) - 1)
    def _():
        a_ref[...] += row_of(shared_ref, base + 12)
        for s in range(samples):
            rows = pl.ds(s * LEN, LEN)
            out_ref[rows, :] = x_ref[rows, :] + mod_ref[s, 2:3] * a_ref[rows, :]


def mlp_forward_body(route, base, table, x_ref, mod_ref, shared_ref, *refs):
    n_buf = route.count
    buffers = refs[:n_buf]
    out_ref, h_ref, u_ref, m_ref, wi_ref, wo_ref, sems_i, sems_o = refs[n_buf:]
    c = pl.program_id(0)
    samples = mod_ref.shape[0]

    @pl.when(c == 0)
    def _():
        route.load(table, buffers, 0, wi_ref, sems_i)
        route.load(table, buffers, 1, wo_ref, sems_o)
        for s in range(samples):
            rows = pl.ds(s * LEN, LEN)
            n, _ = normal(x_ref[rows, :])
            h_ref[rows, :] = (n * (1.0 + mod_ref[s, 1:2]) + mod_ref[s, 0:1]).astype(BF16)
        m_ref[...] = jnp.zeros_like(m_ref)

    wait_all(wi_ref.at[c], sems_i.at[c])
    blocks = wi_ref.shape[-1] // shared_ref.shape[-1]
    bias = jnp.concatenate(
        [shared_ref[c, base + 8 + k : base + 9 + k, :] for k in range(blocks)], axis=1
    )
    hidden = dot_nn(h_ref[...], wi_ref[c]) + bias
    u_ref[0] = hidden
    active = jax.nn.gelu(hidden, approximate=True).astype(BF16)
    wait_all(wo_ref.at[c], sems_o.at[c])
    m_ref[...] += dot_nt(active, wo_ref[c])

    @pl.when(c == pl.num_programs(0) - 1)
    def _():
        m_ref[...] += row_of(shared_ref, base + 13)
        for s in range(samples):
            rows = pl.ds(s * LEN, LEN)
            out_ref[rows, :] = x_ref[rows, :] + mod_ref[s, 2:3] * m_ref[rows, :]


def norm_backward(s, x_ref, mod_ref, dx_ref, dh_ref, out_ref, dmod_ref):
    rows = pl.ds(s * LEN, LEN)
    n, inverse = normal(x_ref[rows, :])
    dh = dh_ref[rows, :]
    dmod_ref[s, 0:1] = jnp.sum(dh, axis=0, keepdims=True)
    dmod_ref[s, 1:2] = jnp.sum(dh * n, axis=0, keepdims=True)
    dn = dh * (1.0 + mod_ref[s, 1:2])
    back = inverse * (
        dn
        - jnp.mean(dn, axis=-1, keepdims=True)
        - n * jnp.mean(dn * n, axis=-1, keepdims=True)
    )
    if dx_ref is None:
        out_ref[rows, :] = back
    else:
        out_ref[rows, :] = dx_ref[rows, :] + back


def branch_gradient(dx_ref, mod_ref, branch_ref, dmod_ref, sum_ref, low_ref):
    total = None
    for s in range(mod_ref.shape[0]):
        rows = pl.ds(s * LEN, LEN)
        dx = dx_ref[rows, :]
        dmod_ref[s, 2:3] = jnp.sum(dx * branch_ref[rows, :], axis=0, keepdims=True)
        db = mod_ref[s, 2:3] * dx
        low_ref[rows, :] = db.astype(BF16)
        part = jnp.sum(db, axis=0, keepdims=True)
        total = part if total is None else total + part
    sum_ref[...] = total


def gelu_slope(u):
    k = math.sqrt(2.0 / math.pi)
    square = u * u
    t = jnp.tanh(k * (u + 0.044715 * square * u))
    half = 0.5 * (1.0 + t)
    slope = half + 0.5 * u * (1.0 - t * t) * (k * (1.0 + 3 * 0.044715 * square))
    return u * half, slope


def mlp_backward_body(
    route, table, dx_ref, x_ref, mod_ref, m_ref, h_ref, u_ref, *refs
):
    n_buf, n_out = route.count, len(route.outs)
    buffers = refs[:n_buf]
    out_ref, dmod_ref, dbias_ref, dtail_ref = refs[n_buf : n_buf + 4]
    grads = refs[n_buf + 4 : n_buf + n_out + 4]
    wi_ref, wo_ref, low_ref, dh_ref, gi_ref, go_ref, sems_i, sems_o, sems_gi, sems_go = refs[
        n_buf + n_out + 4 :
    ]
    c = pl.program_id(0)
    count = route.cols
    samples = mod_ref.shape[0]

    @pl.when(c == 0)
    def _():
        route.load(table, buffers, 1, wo_ref, sems_o)
        route.load(table, buffers, 0, wi_ref, sems_i)
        branch_gradient(dx_ref, mod_ref, m_ref, dmod_ref, dtail_ref, low_ref)
        dh_ref[...] = jnp.zeros_like(dh_ref)

    slot = lax.rem(c, 2)

    @pl.when(c >= 2)
    def _():
        wait_all(gi_ref.at[slot], sems_gi.at[slot])
        wait_all(go_ref.at[slot], sems_go.at[slot])

    wait_all(wo_ref.at[c], sems_o.at[c])
    active, slope = gelu_slope(u_ref[0])
    low = low_ref[...]
    go_ref[slot] = dot_tn(low, active.astype(BF16)).astype(BF16)
    route.store(table, c, 1, go_ref.at[slot], grads, sems_go.at[slot])
    du = dot_nn(low, wo_ref[c]) * slope
    dbias_ref[c] = jnp.sum(du, axis=0, keepdims=True)
    du = du.astype(BF16)
    gi_ref[slot] = dot_tn(h_ref[...], du).astype(BF16)
    route.store(table, c, 0, gi_ref.at[slot], grads, sems_gi.at[slot])
    wait_all(wi_ref.at[c], sems_i.at[c])
    dh_ref[...] += dot_nt(du, wi_ref[c])

    @pl.when(c == count - 1)
    def _():
        for s in range(samples):
            norm_backward(s, x_ref, mod_ref, dx_ref, dh_ref, out_ref, dmod_ref)
        for k in range(2):
            wait_all(gi_ref.at[k], sems_gi.at[k])
            wait_all(go_ref.at[k], sems_go.at[k])


def attention_backward_body(
    route, table, dx_ref, x_ref, mod_ref, a_ref, h_ref, qkv_ref, p_ref, o_ref, *refs
):
    n_buf, n_out = route.count, len(route.outs)
    buffers = refs[:n_buf]
    out_ref, dmod_ref, dbias_ref, dtail_ref = refs[n_buf : n_buf + 4]
    grads = refs[n_buf + 4 : n_buf + n_out + 4]
    w_ref, low_ref, dh_ref, d_ref, g_ref, sems, sems_g = refs[n_buf + n_out + 4 :]
    c = pl.program_id(0)
    count = route.cols
    samples = mod_ref.shape[0]
    width = qkv_ref.shape[-1] // 3
    factor = HEAD_DIM ** (-0.5)

    @pl.when(c == 0)
    def _():
        route.load(table, buffers, 0, w_ref, sems)
        branch_gradient(dx_ref, mod_ref, a_ref, dmod_ref, dtail_ref, low_ref)
        dh_ref[...] = jnp.zeros_like(dh_ref)

    slot = lax.rem(c, 2)

    @pl.when(c >= 2)
    def _():
        wait_all(g_ref.at[slot], sems_g.at[slot])

    wait_all(w_ref.at[c], sems.at[c])
    do_all = dot_nn(low_ref[...], w_ref[c, :, 3 * width :]).astype(BF16)
    sums = [None] * (width // HEAD_DIM)
    for s in range(samples):
        rows = pl.ds(s * LEN, LEN)
        dqs, dks, dvs = [], [], []
        for j in range(width // HEAD_DIM):
            q = qkv_ref[0, rows, j * HEAD_DIM : (j + 1) * HEAD_DIM]
            k = qkv_ref[0, rows, width + j * HEAD_DIM : width + (j + 1) * HEAD_DIM]
            v = qkv_ref[0, rows, 2 * width + j * HEAD_DIM : 2 * width + (j + 1) * HEAD_DIM]
            o = o_ref[0, rows, j * HEAD_DIM : (j + 1) * HEAD_DIM]
            do = do_all[s * LEN : (s + 1) * LEN, j * HEAD_DIM : (j + 1) * HEAD_DIM]
            probs = p_ref[0, j, s]
            dp = dot_nt(do, v)
            delta = jnp.sum(do.astype(F32) * o.astype(F32), axis=-1, keepdims=True)
            ds = (probs.astype(F32) * (dp - delta)).astype(BF16)
            dqs.append(dot_nn(ds, k) * factor)
            dks.append(dot_tn(ds, q) * factor)
            dvs.append(dot_tn(probs, do))
        joined = jnp.concatenate(dqs + dks + dvs, axis=1)
        part = jnp.sum(joined, axis=0, keepdims=True)
        sums = part if s == 0 else sums + part
        d_ref[rows, :] = joined.astype(BF16)
    dbias_ref[c] = sums
    grad_in = dot_tn(h_ref[...], d_ref[...])
    grad_out = dot_tn(low_ref[...], o_ref[0])
    g_ref[slot] = jnp.concatenate([grad_in, grad_out], axis=1).astype(BF16)
    route.store(table, c, 0, g_ref.at[slot], grads, sems_g.at[slot])
    dh_ref[...] += dot_nt(d_ref[...], w_ref[c, :, : 3 * width])

    @pl.when(c == count - 1)
    def _():
        for s in range(samples):
            norm_backward(s, x_ref, mod_ref, dx_ref, dh_ref, out_ref, dmod_ref)
        for k in range(2):
            wait_all(g_ref.at[k], sems_g.at[k])


def final_body(
    x_ref, mod_ref, head_ref, bias_ref, noise_ref, mask_ref,
    dx_ref, loss_ref, dhead_ref, dbias_ref, dmod_ref, h_ref, dh_ref,
):
    samples = mod_ref.shape[0]
    for s in range(samples):
        rows = pl.ds(s * LEN, LEN)
        n, _ = normal(x_ref[rows, :])
        h_ref[rows, :] = (n * (1.0 + mod_ref[s, 1:2]) + mod_ref[s, 0:1]).astype(BF16)
    predicted = dot_nt(h_ref[...], head_ref[...]) + bias_ref[...]
    error = predicted - noise_ref[...]
    masked = mask_ref[...] * error
    loss_ref[...] = jnp.sum(masked * error, axis=0, keepdims=True)
    dpred = 2.0 * masked
    dbias_ref[...] = jnp.sum(dpred, axis=0, keepdims=True)
    low = dpred.astype(BF16)
    dhead_ref[...] = dot_tn(low, h_ref[...])
    dh_ref[...] = dot_nn(low, head_ref[...])
    for s in range(samples):
        norm_backward(s, x_ref, mod_ref, None, dh_ref, dx_ref, dmod_ref)


def whole_block(shape):
    rank = len(shape)
    return pl.BlockSpec(shape, lambda c: (0,) * rank, pipeline_mode=pl.Buffered(1))


def whole_out(shape):
    rank = len(shape)
    return pl.BlockSpec(shape, lambda c: (0,) * rank)


def block_of(shape):
    rank = len(shape)
    return pl.BlockSpec((1,) + tuple(shape[1:]), lambda c: (c,) + (0,) * (rank - 1))


def params(mib):
    return pltpu.CompilerParams(
        dimension_semantics=("arbitrary",), vmem_limit_bytes=mib * MIB
    )


def cost(flops, nbytes, exps=0):
    return pl.CostEstimate(flops=int(flops), bytes_accessed=int(nbytes), transcendentals=int(exps))


def shaped(shape, dtype):
    return jax.ShapeDtypeStruct(tuple(shape), dtype)


def attention_forward(place, base, buffers, x, mods, shared):
    route = Route(place, buffers)
    count = place.cols
    tokens, width = x.shape
    samples = mods.shape[0]
    narrow = shared.shape[-1]
    heads = narrow // HEAD_DIM
    outs = [
        shaped((tokens, width), F32),
        shaped((tokens, width), BF16),
        shaped((count, tokens, 3 * narrow), BF16),
        shaped((count, heads, samples, LEN, LEN), BF16),
        shaped((count, tokens, narrow), BF16),
        shaped((tokens, width), F32),
    ]
    return pl.pallas_call(
        functools.partial(attention_forward_body, route, base),
        grid=(count,),
        in_specs=[SMEM, whole_block(x.shape), whole_block(mods.shape), whole_block(shared.shape)]
        + [ANY] * len(buffers),
        out_specs=[whole_out(outs[0].shape), whole_out(outs[1].shape)]
        + [block_of(o.shape) for o in outs[2:5]]
        + [whole_out(outs[5].shape)],
        out_shape=outs,
        scratch_shapes=[
            pltpu.VMEM((count, width, 4 * narrow), BF16),
            pltpu.SemaphoreType.DMA((count,)),
        ],
        compiler_params=params(58),
        cost_estimate=cost(
            2 * tokens * width * width * 4 + 4 * tokens * LEN * width,
            8 * width * width + 30 * tokens * width,
            tokens * LEN * width // HEAD_DIM,
        ),
        name="attention_forward",
    )(place.table, x, mods, shared, *buffers)


def mlp_forward(place, base, buffers, x, mods, shared):
    route = Route(place, buffers)
    count = place.cols
    tokens, width = x.shape
    wide = buffers[0].shape[-1]
    outs = [
        shaped((tokens, width), F32),
        shaped((tokens, width), BF16),
        shaped((count, tokens, wide), F32),
        shaped((tokens, width), F32),
    ]
    return pl.pallas_call(
        functools.partial(mlp_forward_body, route, base),
        grid=(count,),
        in_specs=[SMEM, whole_block(x.shape), whole_block(mods.shape), whole_block(shared.shape)]
        + [ANY] * len(buffers),
        out_specs=[whole_out(outs[0].shape), whole_out(outs[1].shape), block_of(outs[2].shape)]
        + [whole_out(outs[3].shape)],
        out_shape=outs,
        scratch_shapes=[
            pltpu.VMEM((count, width, wide), BF16),
            pltpu.VMEM((count, width, wide), BF16),
            pltpu.SemaphoreType.DMA((count,)),
            pltpu.SemaphoreType.DMA((count,)),
        ],
        compiler_params=params(58),
        cost_estimate=cost(
            2 * tokens * width * wide * count * 2,
            4 * width * wide * count + 30 * tokens * width,
            tokens * wide * count,
        ),
        name="mlp_forward",
    )(place.table, x, mods, shared, *buffers)


def mlp_backward(place, buffers, dx, x, mods, m, h, u):
    route = Route(place, buffers)
    count = place.cols
    tokens, width = x.shape
    wide = u.shape[-1]
    outs = [
        shaped((tokens, width), F32),
        shaped(mods.shape, F32),
        shaped((count, 1, wide), F32),
        shaped((1, width), F32),
    ] + [shaped(v, BF16) for v in route.outs]
    out = pl.pallas_call(
        functools.partial(mlp_backward_body, route),
        grid=(count,),
        in_specs=[SMEM, whole_block(x.shape), whole_block(x.shape), whole_block(mods.shape)]
        + [whole_block(m.shape), whole_block(h.shape), block_of(u.shape)]
        + [ANY] * len(buffers),
        out_specs=[whole_out(x.shape), whole_out(mods.shape), whole_out(outs[2].shape)]
        + [whole_out((1, width))]
        + [ANY] * len(route.outs),
        out_shape=outs,
        scratch_shapes=[
            pltpu.VMEM((count, width, wide), BF16),
            pltpu.VMEM((count, width, wide), BF16),
            pltpu.VMEM((tokens, width), BF16),
            pltpu.VMEM((tokens, width), F32),
            pltpu.VMEM((2, width, wide), BF16),
            pltpu.VMEM((2, width, wide), BF16),
            pltpu.SemaphoreType.DMA((count,)),
            pltpu.SemaphoreType.DMA((count,)),
            pltpu.SemaphoreType.DMA((2,)),
            pltpu.SemaphoreType.DMA((2,)),
        ],
        compiler_params=params(58),
        cost_estimate=cost(
            4 * 2 * tokens * width * wide * count,
            8 * width * wide * count + 40 * tokens * width,
            tokens * wide * count,
        ),
        name="mlp_backward",
    )(place.table, dx, x, mods, m, h, u, *buffers)
    return out[:4], out[4:]


def attention_backward(place, buffers, dx, x, mods, a, h, qkv, p, o):
    route = Route(place, buffers)
    count = place.cols
    tokens, width = x.shape
    narrow = o.shape[-1]
    outs = [
        shaped((tokens, width), F32),
        shaped(mods.shape, F32),
        shaped((count, 1, 3 * narrow), F32),
        shaped((1, width), F32),
    ] + [shaped(v, BF16) for v in route.outs]
    out = pl.pallas_call(
        functools.partial(attention_backward_body, route),
        grid=(count,),
        in_specs=[SMEM, whole_block(x.shape), whole_block(x.shape), whole_block(mods.shape)]
        + [whole_block(a.shape), whole_block(h.shape)]
        + [block_of(qkv.shape), block_of(p.shape), block_of(o.shape)]
        + [ANY] * len(buffers),
        out_specs=[whole_out(x.shape), whole_out(mods.shape), whole_out(outs[2].shape)]
        + [whole_out((1, width))]
        + [ANY] * len(route.outs),
        out_shape=outs,
        scratch_shapes=[
            pltpu.VMEM((count, width, 4 * narrow), BF16),
            pltpu.VMEM((tokens, width), BF16),
            pltpu.VMEM((tokens, width), F32),
            pltpu.VMEM((tokens, 3 * narrow), BF16),
            pltpu.VMEM((2, width, 4 * narrow), BF16),
            pltpu.SemaphoreType.DMA((count,)),
            pltpu.SemaphoreType.DMA((2,)),
        ],
        compiler_params=params(58),
        cost_estimate=cost(
            4 * tokens * width * width * 4 + 10 * tokens * LEN * width,
            16 * width * width + 40 * tokens * width,
        ),
        name="attention_backward",
    )(place.table, dx, x, mods, a, h, qkv, p, o, *buffers)
    return out[:4], out[4:]


def final_step(x, mods, head, bias, noise, mask):
    tokens, width = x.shape
    vmem = pl.BlockSpec(memory_space=pltpu.VMEM)
    return pl.pallas_call(
        final_body,
        in_specs=[vmem] * 6,
        out_specs=[vmem] * 5,
        out_shape=[
            shaped((tokens, width), F32),
            shaped((1, PATCH), F32),
            shaped((PATCH, width), F32),
            shaped((1, PATCH), F32),
            shaped(mods.shape, F32),
        ],
        scratch_shapes=[pltpu.VMEM((tokens, width), BF16), pltpu.VMEM((tokens, width), F32)],
        compiler_params=pltpu.CompilerParams(vmem_limit_bytes=32 * MIB),
        cost_estimate=cost(6 * tokens * width * PATCH, 12 * tokens * width),
        name="final_step",
    )(x, mods, head, bias, noise, mask)


def pack_body(in_ref, out_ref, block_ref, mode_ref):
    blocks = out_ref.shape[1] - 1
    for k in range(6):
        mode_ref[0, k] = in_ref[0, k].astype(BF16)
    attn = [in_ref[0, 6 + k] for k in range(3)] + [out_ref[0, 0].T]
    block_ref[0] = jnp.concatenate(attn, axis=1).astype(BF16)
    first = [in_ref[0, 9 + k] for k in range(blocks)]
    block_ref[1] = jnp.concatenate(first, axis=1).astype(BF16)
    second = [out_ref[0, 1 + k].T for k in range(blocks)]
    block_ref[2] = jnp.concatenate(second, axis=1).astype(BF16)


def pack_weights(weights_in, weights_out):
    layers, kinds, block, narrow = weights_in.shape
    outs = [
        shaped((3 * layers, block, 4 * narrow), BF16),
        shaped((layers, 6, block, narrow), BF16),
    ]
    return pl.pallas_call(
        pack_body,
        grid=(layers,),
        in_specs=[block_of(weights_in.shape), block_of(weights_out.shape)],
        out_specs=[
            pl.BlockSpec((3, block, 4 * narrow), lambda c: (c, 0, 0)),
            block_of(outs[1].shape),
        ],
        out_shape=outs,
        compiler_params=params(32),
        name="pack_weights",
    )(weights_in, weights_out)


def embed_body(base, noisy_ref, shared_ref, table_ref, out_ref):
    patch = jnp.concatenate(
        [
            shared_ref[c, base + 3 : base + 3 + PATCH, :]
            for c in range(shared_ref.shape[0])
        ],
        axis=1,
    ).astype(BF16)
    constant = row_of(shared_ref, base + 2) + table_ref[...]
    for s in range(noisy_ref.shape[0] // LEN):
        rows = pl.ds(s * LEN, LEN)
        out_ref[rows, :] = dot_nn(noisy_ref[rows, :], patch) + constant


def embed_tokens(base, noisy, shared, table):
    vmem = pl.BlockSpec(memory_space=pltpu.VMEM)
    return pl.pallas_call(
        functools.partial(embed_body, base),
        in_specs=[vmem] * 3,
        out_specs=vmem,
        out_shape=shaped((noisy.shape[0], table.shape[1]), F32),
        compiler_params=pltpu.CompilerParams(vmem_limit_bytes=32 * MIB),
        name="embed_tokens",
    )(noisy, shared, table)


def silu_slope(values):
    sigmoid_part = jax.nn.sigmoid(values)
    return sigmoid_part * (1.0 + values * (1.0 - sigmoid_part))


TIME_BLOCK = 128
CLASS_AT, FREQ_AT, LABEL_AT = 192, 208, 224


def condition_body(base, found, near_ref, shared_ref, *refs):
    cond_ref, act_ref, first_ref, first_act_ref, freq_ref, label_ref, class_ref, wave_ref = refs
    cols, _, narrow = shared_ref.shape
    rows = near_ref.shape[0] // cols
    steps = FREQ // TIME_BLOCK
    for r in range(rows):
        at = slice(r * 8, r * 8 + 8)
        for c in range(cols):
            block = near_ref[found[r * cols + c], CLASS_AT:, :].astype(F32)
            joined = jnp.concatenate([block[:8], block[8:16, : narrow - 128]], axis=1)
            class_ref[at, c * narrow : (c + 1) * narrow] = joined
            if c == 0:
                wave_ref[at, :TIME_BLOCK] = block[16:24]
                wave_ref[at, TIME_BLOCK:] = block[24:32]
                label_ref[at, :] = block[32:40] * 32.0 + block[40:48]
    freq = wave_ref[...].astype(BF16)
    freq_ref[...] = freq

    def product(left, first_row, count):
        parts = []
        for c in range(cols):
            total = None
            for k in range(count):
                block = near_ref[found[(first_row + k) * cols + c], :CLASS_AT, :]
                part = dot_nt(left[:, k * TIME_BLOCK : (k + 1) * TIME_BLOCK], block)
                total = part if total is None else total + part
            parts.append(total)
        return jnp.concatenate(parts, axis=1)

    first = product(freq, 0, steps) + row_of(shared_ref, base)
    first_ref[...] = first
    first_act = (first * jax.nn.sigmoid(first)).astype(BF16)
    first_act_ref[...] = first_act
    cond = product(first_act, steps, rows - steps) + row_of(shared_ref, base + 1)
    cond = cond + class_ref[...]
    cond_ref[...] = cond
    act_ref[...] = (cond * jax.nn.sigmoid(cond)).astype(BF16)


def condition_step(base, found, near, shared, samples, width):
    vmem = pl.BlockSpec(memory_space=pltpu.VMEM)
    outs = [
        shaped((samples, width), F32),
        shaped((samples, width), BF16),
        shaped((samples, width), F32),
        shaped((samples, width), BF16),
        shaped((samples, FREQ), BF16),
        shaped((samples, 128), F32),
    ]
    return pl.pallas_call(
        functools.partial(condition_body, base),
        in_specs=[SMEM, vmem, vmem],
        out_specs=[vmem] * len(outs),
        out_shape=outs,
        scratch_shapes=[pltpu.VMEM((samples, width), F32), pltpu.VMEM((samples, FREQ), F32)],
        compiler_params=pltpu.CompilerParams(vmem_limit_bytes=32 * MIB),
        name="condition_step",
    )(found, near, shared)


def condition_back_body(
    layers, blocks, found, spot, small_ref, part_ref, final_ref, square_ref, cond_ref, first_ref,
    input_ref, label_ref, pick_ref, near_ref, time_ref, embed_ref, bias_ref, own_ref, shared_ref,
    grad_ref,
):
    row, col = spot[0], spot[1]
    samples, width = cond_ref.shape
    narrow = pick_ref.shape[1]
    cols = width // narrow
    rows = near_ref.shape[0] // cols
    steps = FREQ // TIME_BLOCK
    start = 16 * layers + 2 * PATCH
    pick = pick_ref[...]
    pick_wide = pick.astype(F32)

    def own_cols(v):
        return jnp.dot(v, pick_wide, precision=HIGHEST, preferred_element_type=F32)

    def squares(v):
        return jnp.sum(v * v, keepdims=True)

    block_rows = part_ref.shape[2]
    for r in range(rows):
        part = part_ref[found[r * cols + col]]
        grad_ref[:, r * block_rows : (r + 1) * block_rows] = part
    grad_cond = (grad_ref[...] + final_ref[...]) * silu_slope(cond_ref[...])
    low = grad_cond.astype(BF16)
    parts = []
    for r in range(steps, rows):
        total = None
        for c in range(cols):
            block = near_ref[found[r * cols + c], :CLASS_AT, :]
            part = dot_nn(low[:, c * narrow : (c + 1) * narrow], block)
            total = part if total is None else total + part
        parts.append(total)
    grad_first = jnp.concatenate(parts, axis=1) * silu_slope(first_ref[...])
    is_first = (row < steps).astype(F32)
    outputs = grad_first.astype(BF16).astype(F32) * is_first + low.astype(F32) * (1.0 - is_first)
    outputs = dot_nn(outputs.astype(BF16), pick).astype(BF16)
    time_grad = dot_tn(outputs, input_ref[...])
    time_ref[...] = time_grad
    hot = lax.broadcasted_iota(jnp.int32, (samples, CLASSES), 1).astype(F32)
    hot = (hot == label_ref[:, 0:1]).astype(F32)
    class_grad = lax.dot_general(
        own_cols(grad_cond), hot, TN, precision=HIGHEST, preferred_element_type=F32
    )
    patch = own_cols(small_ref[start - PATCH : start, :])
    embed_ref[...] = jnp.concatenate([class_grad, patch.T], axis=1)
    own_ref[...] = squares(time_grad) + squares(class_grad) * (1.0 / rows)
    time_bias = jnp.concatenate(
        [jnp.sum(grad_first, axis=0, keepdims=True), jnp.sum(grad_cond, axis=0, keepdims=True)],
        axis=0,
    )
    total = square_ref[...] + squares(time_bias) + squares(small_ref[start - 2 * PATCH : start + 3, :])
    total = total + squares(small_ref[start + 3 : start + 4, :PATCH])
    own = own_cols(small_ref[: start + 16, :])
    lines = []
    for layer in range(layers):
        at = 16 * layer
        total = total + squares(small_ref[at : at + 6 + cols, :])
        total = total + squares(small_ref[at + 10 : at + 10 + cols, :narrow])
        total = total + squares(small_ref[at + 10 : at + 10 + cols, 2 * narrow : 3 * narrow])
        total = total + squares(small_ref[at + 14 : at + 16, :])
        attn = small_ref[pl.ds(at + 10 + col, 1), :]
        mlp = small_ref[pl.ds(at + 6 + col, 1), :]
        lines += [own[at : at + 6], attn[:, :narrow], attn[:, 2 * narrow : 3 * narrow]]
        lines += [mlp[:, k * narrow : (k + 1) * narrow] for k in range(blocks)]
        lines += [own[at + 14 : at + 16]]
    lines += [own_cols(time_bias), own[start : start + 1]]
    bias_ref[...] = jnp.concatenate(lines, axis=0)
    shared_ref[...] = total


def condition_back(
    layers, blocks, found, spot, small, part, final, squares, cond, first, inputs, labels, pick, near
):
    vmem = pl.BlockSpec(memory_space=pltpu.VMEM)
    narrow = pick.shape[1]
    outs = [
        shaped((narrow, TIME_BLOCK), F32),
        shaped((narrow, CLASSES + PATCH), F32),
        shaped((14 * layers + 3, narrow), F32),
        shaped((1, 1), F32),
        shaped((1, 1), F32),
    ]
    operands = [small, part, final, squares, cond, first, inputs, labels, pick, near]
    return pl.pallas_call(
        functools.partial(condition_back_body, layers, blocks),
        in_specs=[SMEM, SMEM] + [vmem] * len(operands),
        out_specs=[vmem] * len(outs),
        out_shape=outs,
        scratch_shapes=[pltpu.VMEM(cond.shape, F32)],
        compiler_params=pltpu.CompilerParams(vmem_limit_bytes=48 * MIB),
        name="condition_back",
    )(found, spot, *operands)


def modes_backward_body(
    layers, near_ref, at_ref, rows_ref, pick_ref, mode_ref, act_ref, final_ref,
    block_ref, part_ref, square_ref, grad_ref, cond_ref, shared_ref,
):
    near = near_ref[...]
    at = at_ref[...]
    samples = at.shape[0]
    where = lax.broadcasted_iota(jnp.int32, (samples, near.shape[0]), 1)
    cols, narrow = mode_ref.shape[0], mode_ref.shape[4]
    spreads = []
    for layer in range(layers):
        for k in range(6):
            offset = 12 * layer + 6 * (k // 3) + k % 3
            spreads.append((where == at[:, 0:1] + at[:, 1:2] * 3 + offset).astype(BF16))
    for k in range(2):
        spreads.append((where == at[:, 0:1] + at[:, 1:2] * 2 + 12 * layers + k).astype(BF16))
    rows = dot_nn(jnp.concatenate(spreads, axis=0), near).astype(BF16)
    mine = dot_nn(rows[: 6 * layers * samples], pick_ref[...]).astype(BF16)

    total = None
    squares = jnp.zeros((1, 1), F32)
    for layer in range(layers):
        for k in range(6):
            at_row = (6 * layer + k) * samples
            low = rows[at_row : at_row + samples]
            grad = dot_tn(rows_ref[...], mine[at_row : at_row + samples])
            block_ref[layer, k] = grad
            squares = squares + jnp.sum(grad * grad, keepdims=True)
            full = jnp.concatenate([mode_ref[c, layer, k] for c in range(cols)], axis=1)
            part = dot_nt(low, full)
            total = part if total is None else total + part
    part_ref[...] = total
    square_ref[...] = squares
    width = act_ref.shape[1]
    at_row = 6 * layers * samples
    shift, scale = rows[at_row : at_row + samples], rows[at_row + samples :]
    squares = jnp.zeros((1, 1), F32)
    for k, low in enumerate((shift, scale)):
        grad = dot_tn(low, act_ref[...])
        grad_ref[k * width : (k + 1) * width, :] = grad
        squares = squares + jnp.sum(grad * grad, keepdims=True)
    cond_ref[...] = dot_nn(shift, final_ref[:width, :]) + dot_nn(
        scale, final_ref[width : 2 * width, :]
    )
    shared_ref[...] = squares


def modes_backward(near, at, cond_rows, pick, mode_full, act, final):
    vmem = pl.BlockSpec(memory_space=pltpu.VMEM)
    samples, block = cond_rows.shape
    width = near.shape[2]
    layers, narrow = mode_full.shape[1], mode_full.shape[4]
    outs = [
        shaped((layers, 6, block, narrow), F32),
        shaped((samples, block), F32),
        shaped((1, 1), F32),
        shaped((2 * width, width), F32),
        shaped((samples, width), F32),
        shaped((1, 1), F32),
    ]
    operands = [near.reshape(-1, width), at, cond_rows, pick, mode_full, act, final]
    return pl.pallas_call(
        functools.partial(modes_backward_body, layers),
        in_specs=[vmem] * len(operands),
        out_specs=[vmem] * len(outs),
        out_shape=outs,
        compiler_params=pltpu.CompilerParams(vmem_limit_bytes=56 * MIB),
        name="modes_backward",
    )(*operands)


def modes_backward_plain(near, cond_rows, mode_full, act, final, col):
    layers, narrow, width = mode_full.shape[1], mode_full.shape[4], near.shape[2]
    devices = near.shape[0]
    samples = act.shape[0] // devices
    low = near[:, : 12 * layers].reshape(devices, layers, 2, samples, 3, width)
    low = jnp.transpose(low, (1, 2, 4, 0, 3, 5)).reshape(layers, 6, devices * samples, width)
    mine = lax.dynamic_slice_in_dim(low, col * narrow, narrow, 3)
    block = jnp.einsum("sd,lkse->lkde", cond_rows, mine, preferred_element_type=F32)
    full = jnp.transpose(mode_full, (1, 2, 3, 0, 4)).reshape(layers, 6, -1, width)
    part = jnp.einsum("lkse,lkde->sd", low, full, preferred_element_type=F32)
    ends = near[:, 12 * layers : 12 * layers + 2 * samples].reshape(-1, 2, width)
    grad = jnp.einsum("ske,sd->ked", ends, act, preferred_element_type=F32)
    cond = jnp.einsum(
        "ske,ked->sd", ends, final[: 2 * width].reshape(2, width, width), preferred_element_type=F32
    )
    grad = grad.reshape(2 * width, width)
    return block, part, squared(block)[None, None], grad, cond, squared(grad)[None, None]


def collect_body(layers, *refs):
    out_ref = refs[-1]
    at = 0
    out_ref[...] = jnp.zeros_like(out_ref)
    take = list(refs[:-1])
    for _ in range(layers):
        dmod_a, dmod_b, dbias_a, dbias_b, dtail_a, dtail_b = [take.pop(0) for _ in range(6)]
        for k, source in enumerate((dmod_a, dmod_b)):
            total = source[0]
            for s in range(1, source.shape[0]):
                total = total + source[s]
            out_ref[at + 3 * k : at + 3 * k + 3, :] = total
        for c in range(dbias_b.shape[0]):
            out_ref[at + 6 + c : at + 7 + c, : dbias_b.shape[2]] = dbias_b[c]
            out_ref[at + 10 + c : at + 11 + c, : dbias_a.shape[2]] = dbias_a[c]
        out_ref[at + 14 : at + 15, :] = dtail_a[...]
        out_ref[at + 15 : at + 16, :] = dtail_b[...]
        at += 16
    head, head_bias, loss, mask, dfinal, dx, noisy = take
    out_ref[at : at + PATCH, :] = head[...]
    out_ref[at + PATCH : at + 2 * PATCH, :] = dot_tn(noisy[...], dx[...].astype(BF16))
    at += 2 * PATCH
    out_ref[at : at + 1, :] = jnp.sum(dx[...], axis=0, keepdims=True)
    total = dfinal[0]
    for s in range(1, dfinal.shape[0]):
        total = total + dfinal[s]
    out_ref[at + 1 : at + 3, :] = total
    out_ref[at + 3 : at + 4, 0:PATCH] = head_bias[...]
    out_ref[at + 4 : at + 5, 0:PATCH] = loss[...]
    out_ref[at + 5 : at + 6, 0:1] = jnp.sum(mask[...], keepdims=True)


def collect(layers, parts, height, width):
    vmem = pl.BlockSpec(memory_space=pltpu.VMEM)
    return pl.pallas_call(
        functools.partial(collect_body, layers),
        in_specs=[vmem] * len(parts),
        out_specs=vmem,
        out_shape=shaped((height, width), F32),
        compiler_params=pltpu.CompilerParams(vmem_limit_bytes=48 * MIB),
        name="collect_small",
    )(*parts)


def adam(weight, gradient, moment, second, clip, rate):
    gradient = gradient * clip
    moment = BETA_ONE * moment + (1.0 - BETA_ONE) * gradient
    second = BETA_TWO * second + (1.0 - BETA_TWO) * gradient * gradient
    update = (
        moment / (1.0 - BETA_ONE**STEP) / (jnp.sqrt(second / (1.0 - BETA_TWO**STEP)) + ADAM_EPS)
    )
    return weight - rate * (update + DECAY * weight), moment, second


def adam_blocks_body(layers, halves, clip_ref, spot, *refs):
    clip = clip_ref[0]
    per = 5 if halves else 3
    sums = [refs[per * layer : per * layer + per] for layer in range(layers)]
    refs = refs[per * layers :]
    wi, mi, vi, wo, mo, vo = refs[:6]
    out_i, out_o = refs[6:9], refs[9:12]
    total_ref = refs[12]
    narrow = wi.shape[3]

    def fill(layer):
        group = sums[layer]
        for k in range(3):
            if not halves:
                total_ref[k] = group[1][0] if k == 0 else group[2][k - 1]
                continue
            half = total_ref.shape[1] // 2
            mine, other = group[1:3] if k == 0 else group[3:5]
            at = 0 if k == 0 else k - 1
            core = spot[1] % 2
            total_ref[k, pl.ds(pl.multiple_of(core * half, 8), half), :] = mine[0, at]
            total_ref[k, pl.ds(pl.multiple_of((1 - core) * half, 8), half), :] = other[at]

    def update(layer, mode_ref):
        for k in range(wi.shape[1]):
            if k < 6:
                grad = mode_ref[layer, k]
            elif k < 9:
                grad = total_ref[0, :, (k - 6) * narrow : (k - 5) * narrow]
            else:
                grad = total_ref[1, :, (k - 9) * narrow : (k - 8) * narrow]
            new = adam(wi[0, k], grad, mi[0, k], vi[0, k], clip, RATE)
            for ref, value in zip(out_i, new):
                ref[0, k] = value
        for k in range(wo.shape[1]):
            if k == 0:
                grad = total_ref[0, :, 3 * narrow :]
            else:
                grad = total_ref[2, :, (k - 1) * narrow : k * narrow]
            new = adam(wo[0, k], grad.T, mo[0, k], vo[0, k], clip, RATE)
            for ref, value in zip(out_o, new):
                ref[0, k] = value

    for layer in range(layers):

        @pl.when(pl.program_id(0) == layer)
        def _(layer=layer):
            fill(layer)
            update(layer, sums[layer][0])


def adam_blocks(clip, spot, sums, ins, outs):
    arrays = list(ins) + list(outs)
    grads = [v for group in sums for v in group]
    halves = len(sums[0]) == 5
    results = [shaped(v.shape, F32) for v in arrays]
    block, narrow = ins[0].shape[2:]
    return pl.pallas_call(
        functools.partial(adam_blocks_body, len(sums), halves),
        grid=(ins[0].shape[0],),
        in_specs=[SMEM, SMEM]
        + [whole_block(v.shape) for v in grads]
        + [block_of(v.shape) for v in arrays],
        out_specs=[block_of(v.shape) for v in results],
        out_shape=results,
        scratch_shapes=[pltpu.VMEM((3, block, 4 * narrow), F32)],
        compiler_params=params(58),
        name="adam_blocks",
    )(clip, spot, *grads, *arrays)


def adam_final_body(clip_ref, grad_ref, head_ref, w, m, v, *outs):
    clip = clip_ref[0]
    step = pl.program_id(0)
    last = pl.num_programs(0) - 1

    @pl.when(step < last)
    def _():
        new = adam(w[...], grad_ref[...], m[...], v[...], clip, RATE)
        for ref, value in zip(outs, new):
            ref[...] = value

    @pl.when(step == last)
    def _():
        rows = slice(0, PATCH)
        new = adam(w[rows, :], head_ref[...], m[rows, :], v[rows, :], clip, RATE)
        for ref, value in zip(outs, new):
            ref[rows, :] = value


def adam_final(clip, grad, head, w, m, v):
    width = w.shape[1]
    height = 256
    steps = grad.shape[0] // height
    part = pl.BlockSpec((height, width), lambda c: (c, 0))
    grad_part = pl.BlockSpec((height, width), lambda c: (jnp.minimum(c, steps - 1), 0))
    return pl.pallas_call(
        adam_final_body,
        grid=(steps + 1,),
        in_specs=[SMEM, grad_part, whole_block(head.shape)] + [part] * 3,
        out_specs=[part] * 3,
        out_shape=[shaped(w.shape, F32)] * 3,
        compiler_params=params(58),
        name="adam_final",
    )(clip, grad, head, w, m, v)


def adam_rest_body(rates, clip_ref, *refs):
    clip = clip_ref[0]
    count = len(rates)
    ins, outs = refs[: 4 * count], refs[4 * count :]
    for k, rate in enumerate(rates):
        w, g, m, v = [r[...] for r in ins[4 * k : 4 * k + 4]]
        for ref, value in zip(outs[3 * k : 3 * k + 3], adam(w, g, m, v, clip, rate)):
            ref[...] = value


def adam_rest(clip, groups):
    vmem = pl.BlockSpec(memory_space=pltpu.VMEM)
    arrays, results, rates = [], [], []
    for w, g, m, v, rate in groups:
        arrays += [w, g, m, v]
        results += [shaped(w.shape, F32)] * 3
        rates.append(rate)
    return pl.pallas_call(
        functools.partial(adam_rest_body, tuple(rates)),
        in_specs=[SMEM] + [vmem] * len(arrays),
        out_specs=[vmem] * len(results),
        out_shape=results,
        compiler_params=pltpu.CompilerParams(vmem_limit_bytes=58 * MIB),
        name="adam_rest",
    )(clip, *arrays)


def squared(values):
    return jnp.sum(values * values)


def position_table(width):
    half = width // 2
    rate = np.exp(-math.log(10000.0) * (np.arange(width) % half) / half)
    angle = np.arange(LEN)[:, None] * rate[None, :]
    table = np.where(np.arange(width)[None, :] < half, np.sin(angle), np.cos(angle))
    return table.astype(np.float32)


def on_device(
    latents,
    noise,
    timesteps,
    labels,
    loss_mask,
    weights_in,
    weights_out,
    time_mlp,
    embed_table,
    final_layer,
    bias_table,
    final_bias,
    momentum_in,
    momentum_out,
    momentum_time,
    momentum_embed,
    momentum_final,
    momentum_bias,
    momentum_final_bias,
    variance_in,
    variance_out,
    variance_time,
    variance_embed,
    variance_final,
    variance_bias,
    variance_final_bias,
):
    layers, block, _, narrow = weights_in.shape
    place = Place(block)
    rows, cols = place.rows, place.cols
    width = final_layer.shape[0]
    row_samples = timesteps.shape[0]
    samples = row_samples // cols
    every_sample = row_samples * rows
    tokens = samples * LEN
    base = layers * 14
    hidden_blocks = weights_out.shape[1] - 1

    def my_cols(v, axis):
        return lax.dynamic_slice_in_dim(v, place.col * narrow, narrow, axis)

    in_view = [jnp.transpose(v, (0, 2, 1, 3)) for v in (weights_in, momentum_in, variance_in)]
    packed, mode_low = pack_weights(in_view[0], weights_out)

    embed_low = embed_table.astype(BF16)
    one_hot_row = (labels[:, None] == jnp.arange(CLASSES, dtype=jnp.int32)[None, :]).astype(BF16)
    class_rows = jnp.dot(
        one_hot_row, embed_low[:CLASSES], preferred_element_type=F32
    ).astype(BF16)
    half_freq = FREQ // 2
    freq_rate = jnp.asarray(
        np.exp(-math.log(10000.0) * np.arange(half_freq) / half_freq).astype(np.float32)
    )
    angle_grid = timesteps.astype(F32)[:, None] * freq_rate[None, :]
    freq_row = jnp.concatenate([jnp.cos(angle_grid), jnp.sin(angle_grid)], axis=1).astype(BF16)
    time_rows = time_mlp.shape[0]
    mine = jnp.concatenate([bias_table, embed_low[CLASSES:].astype(F32)], axis=0)
    final_view = [v.T for v in (final_layer, momentum_final, variance_final)]
    final_low = final_view[0].astype(BF16)
    found = place.found_at()
    sample = jnp.arange(every_sample, dtype=jnp.int32)
    mode_height = -(-(12 * layers + 4) // 16) * 16
    at = jnp.stack([found[sample // samples] * mode_height, sample % samples], axis=1)
    feature = jnp.arange(width, dtype=jnp.int32)[:, None]
    picked = jnp.arange(narrow, dtype=jnp.int32)[None, :] + place.col * narrow
    pick = (feature == picked).astype(BF16)
    spot = jnp.stack([place.row, place.col]).astype(jnp.int32)

    def partial_modes(cond_act):
        cond_rows = lax.dynamic_slice_in_dim(cond_act, place.row * block, block, 1)
        partial = jnp.einsum("sd,lkde->slke", cond_rows, mode_low, preferred_element_type=F32)
        return cond_rows, partial.reshape(every_sample, layers * 6, narrow)

    def own_modes(total, shared, cond_act):
        bias_full = jnp.swapaxes(shared, 0, 1).reshape(-1, width)
        modes = total.reshape(samples, layers, 6, width) + jnp.stack(
            [bias_full[14 * layer : 14 * layer + 6] for layer in range(layers)]
        )
        own_start = place.row * row_samples + place.col * samples
        cond_own = lax.dynamic_slice_in_dim(cond_act, own_start, samples, 0)
        final_mod = (
            jnp.einsum("sd,ed->se", cond_own, final_low[: 2 * width], preferred_element_type=F32)
            + final_bias[: 2 * width]
        ).reshape(samples, 2, width)
        mods_a = [modes[:, layer, 0:3] for layer in range(layers)]
        mods_b = [modes[:, layer, 3:6] for layer in range(layers)]
        return mods_a, mods_b, final_mod

    own_tokens = place.col * tokens
    latents = lax.dynamic_slice_in_dim(latents, own_tokens, tokens, 0)
    noise = lax.dynamic_slice_in_dim(noise, own_tokens, tokens, 0)
    mask = lax.dynamic_slice_in_dim(loss_mask, own_tokens, tokens, 0).astype(F32)
    steps_own = lax.dynamic_slice_in_dim(timesteps, place.col * samples, samples, 0).astype(F32)
    alpha_bar = jnp.cos((steps_own / STEPS_T + 0.008) / 1.008 * (math.pi / 2)) ** 2
    keep_part = jnp.repeat(jnp.sqrt(alpha_bar), LEN)[:, None]
    noise_part = jnp.repeat(jnp.sqrt(1.0 - alpha_bar), LEN)[:, None]
    noisy = (keep_part * latents + noise_part * noise).astype(BF16)
    position = jnp.asarray(position_table(width))

    def attn_step(layer):
        def work(buffers, x, mods, shared):
            return attention_forward(place, 14 * layer, buffers, x, mods, shared)

        return work

    def mlp_step(layer):
        def work(buffers, x, mods, shared):
            return mlp_forward(place, 14 * layer, buffers, x, mods, shared)

        return work

    def attn_back(buffers, *operands):
        return attention_backward(place, buffers, *operands)

    def mlp_back(buffers, *operands):
        return mlp_backward(place, buffers, *operands)

    head_low = final_low[2 * width :]

    def last_step(x, final_mod):
        return final_step(
            x, final_mod, head_low, final_bias[2 * width :][None], noise, mask[:, None]
        )

    def mode_parts(back_a, back_b, grad_final_mod):
        parts = []
        for layer in range(layers):
            parts += [back_a[layer][1], back_b[layer][1]]
        parts = [v.reshape(-1, width) for v in parts + [grad_final_mod]]
        spare = mode_height - sum(v.shape[0] for v in parts)
        return jnp.concatenate(parts + [jnp.zeros((spare, width), F32)], axis=0).astype(BF16)

    start = 16 * layers + 2 * PATCH
    height = -(-(start + 16) // 32) * 32

    def collected(back_a, back_b, last):
        small = []
        for layer in range(layers):
            _, dmod_a, dbias_a, dtail_a = back_a[layer]
            _, dmod_b, dbias_b, dtail_b = back_b[layer]
            small += [dmod_a, dmod_b, dbias_a, dbias_b, dtail_a, dtail_b]
        _, loss_parts, grad_head, grad_head_bias, grad_final_mod = last
        small += [grad_head, grad_head_bias, loss_parts, mask[:, None], grad_final_mod]
        small += [back_a[0][0], noisy]
        return collect(layers, small, height, width)

    buffers = [None] * (2 * layers)
    fore_a, fore_b = [None] * layers, [None] * layers
    entry = [None] * layers
    back_a, back_b = [None] * layers, [None] * layers
    summed = [None] * (2 * layers)
    if place.direct and layers == 2:
        stages = Stages()
        halves = packed.reshape(3 * layers, 2, place.half, packed.shape[2])
        kept = lax.dynamic_index_in_dim(halves, place.core, 1, False)
        sent = lax.dynamic_index_in_dim(halves, 1 - place.core, 1, False)
        (got,), _ = stages.run([(swap_core, sent)])
        a0, b0, a1, b1 = [
            Spread(kept[k : k + n], got[k : k + n]) for k, n in ((0, 1), (1, 2), (3, 1), (4, 2))
        ]
        wide = jnp.broadcast_to
        own_block = jnp.concatenate(
            [
                time_mlp.astype(BF16).T,
                class_rows[:, :128],
                jnp.pad(class_rows[:, 128:], ((0, 0), (0, 256 - narrow))),
                freq_row[:, :128],
                freq_row[:, 128:],
                wide((labels // 32).astype(BF16)[:, None], (row_samples, 128)),
                wide((labels % 32).astype(BF16)[:, None], (row_samples, 128)),
            ],
            axis=0,
        )
        (t1, t3, t2), (near, shared) = stages.run(
            a0.turns((1, 3, 2)),
            [(near_rows, own_block), (functools.partial(gather_cols, place), mine)],
        )
        a0.turned(t1, t2, t3)

        got, (near, residual) = stages.run(
            a0.first() + b0.turns((1, 3)),
            [
                (near_x, near),
                (functools.partial(embed_tokens, base), noisy, shared, position),
            ],
        )
        t1, t3 = got[1:]

        def condition_work(near, shared, found):
            near = near_core(near)
            got = condition_step(base, found, near, shared, every_sample, width)
            return near, got, partial_modes(got[1])

        got, ((near, conditions, (cond_rows, partial)),) = stages.run(
            a0.second(got[0]) + b0.turns((2,)) + a0.core(),
            [(condition_work, near, shared, found)],
        )
        condition, cond_act, first_time, first_act, freq_low, all_labels = conditions
        b0.turned(t1, got[1], t3)
        core = got[2]
        got, (total,) = stages.run(
            b0.first() + a1.turns((1, 3)) + a0.late_core(got[0]),
            [(functools.partial(scatter_y, place), partial)],
        )
        buffers[0] = a0.buffers(core, got[3])
        t1, t3 = got[1:3]

        def scatter_work(total):
            return scatter_x(place, scatter_z(place, total), samples)

        got, (total,) = stages.run(
            b0.second(got[0]) + a1.turns((2,)) + b0.core(), [(scatter_work, total)]
        )
        a1.turned(t1, got[1], t3)
        core = got[2]

        def modes_work(total, shared, cond_act):
            return own_modes(scatter_core(place, total), shared, cond_act)

        got, ((mods_a, mods_b, final_mod),) = stages.run(
            a1.first() + b1.turns((1, 3)) + b0.late_core(got[0]),
            [(modes_work, total, shared, cond_act)],
        )
        buffers[1] = b0.buffers(core, got[3])
        t1, t3 = got[1:3]
        got, (fore_a[0],) = stages.run(
            a1.second(got[0]) + b1.turns((2,)) + a1.core(),
            [(attn_step(0), buffers[0], residual, mods_a[0], shared)],
        )
        b1.turned(t1, got[1], t3)
        core = got[2]
        got, (fore_b[0],) = stages.run(
            b1.first() + a1.late_core(got[0]),
            [(mlp_step(0), buffers[1], fore_a[0][0], mods_b[0], shared)],
        )
        buffers[2] = a1.buffers(core, got[1])
        got, (fore_a[1],) = stages.run(
            b1.second(got[0]) + b1.core(),
            [(attn_step(1), buffers[2], fore_b[0][0], mods_a[1], shared)],
        )
        core = got[1]
        got, _ = stages.run(b1.late_core(got[0]))
        buffers[3] = b1.buffers(core, got[0])
        got, (fore_b[1],) = stages.run(
            [(swap_x, mode_low)], [(mlp_step(1), buffers[3], fore_a[1][0], mods_b[1], shared)]
        )
        mode_half = pair(place.x, mode_low, got[0])
        entry = [residual, fore_b[0][0]]
        last = last_step(fore_b[1][0], final_mod)

        def back_b_work(layer, grad):
            out, h, u, m = fore_b[layer]
            return (mlp_back, buffers[2 * layer + 1], grad, fore_a[layer][0], mods_b[layer], m, h, u)

        def back_a_work(layer, grad):
            out, h, qkv, p, o, a = fore_a[layer]
            return (
                attn_back, buffers[2 * layer], grad, entry[layer], mods_a[layer], a, h, qkv, p, o,
            )

        got, ((back_b[1], grads),) = stages.run(
            [(swap_core, mode_half)], [back_b_work(1, last[0])]
        )
        mode_full = jnp.swapaxes(pair(place.core, mode_half, got[0]), 0, 1)
        mode_full = mode_full.reshape((4,) + mode_low.shape)
        gb1 = Gathered(grads)
        got, ((back_a[1], grads),) = stages.run(gb1.core, [back_a_work(1, back_b[1][0])])
        ga1 = Gathered(grads)
        got, ((back_b[0], grads),) = stages.run(
            gb1.first(got[0]) + ga1.core, [back_b_work(0, back_a[1][0])]
        )
        core_a1 = got[1]
        gb0 = Gathered(grads)
        got, ((back_a[0], grads),) = stages.run(
            gb1.second(got[0]) + ga1.first(core_a1) + gb0.core, [back_a_work(0, back_b[0][0])]
        )
        gb1.third(got[0])
        ga0 = Gathered(grads)

        def sum_work(back_a, back_b, last):
            return sum_along_z(place, collected(back_a, back_b, last))

        moded = mode_parts(back_a, back_b, last[4])
        t2_a1 = ga1.second(got[1])
        got, (near_modes, small) = stages.run(
            gb0.first(got[2]) + gb1.turns((1, 3)) + ga0.core,
            [(near_z, moded), (sum_work, back_a, back_b, last)],
        )
        turned_b1 = got[1:3]
        t2_b0 = gb0.second(got[0])
        got, (near_modes, small) = stages.run(
            ga0.first(got[3]) + t2_a1 + gb1.turns((2,)),
            [(near_y, near_modes), (sum_with(swap_core), small)],
        )
        total_b1 = gb1.total(turned_b1 + got[2:])
        ga1.third(got[1])
        t2_a0 = ga0.second(got[0])
        got, (near_modes, small) = stages.run(
            t2_b0 + ga1.turns((1, 3)), [(near_x, near_modes), (sum_with(swap_x), small)]
        )
        turned_a1 = got[1:]
        gb0.third(got[0])
        got, (near_modes, small) = stages.run(
            t2_a0 + ga1.turns((2,)) + gb0.turns((1, 3)),
            [(near_core, near_modes), (sum_with(swap_y), small)],
        )
        total_a1 = ga1.total(turned_a1 + got[1:2])
        turned_b0 = got[2:]
        ga0.third(got[0])

        def modes_back_work(near):
            return modes_backward(near, at, cond_rows, pick, mode_full, cond_act, final_low)

        got, (moded, small) = stages.run(
            gb0.turns((2,)),
            [(modes_back_work, near_modes), (functools.partial(sum_spread, place), small)],
        )
        total_b0 = gb0.total(turned_b0 + got)
        time_inputs = lax.dynamic_slice_in_dim(
            jnp.concatenate([freq_low, first_act], axis=1), place.row * time_rows, time_rows, 1
        )
        turned_a0, (part,) = stages.run(ga0.turns((1, 3)), [(near_z, moded[1])])
        got, (part,) = stages.run(ga0.turns((2,)), [(near_y, part)])
        total_a0 = ga0.total(turned_a0 + got)
        ends = condition_back(
            layers, hidden_blocks, found, spot, small, part, moded[4], moded[5], condition,
            first_time, time_inputs, all_labels, pick, near,
        )
        late = swap_core(
            jnp.concatenate([total_b1[1], total_b0[1], total_a1[1], total_a0[1]])
        )
        summed = [total_a0, total_b0, total_a1, total_b1]
        sums = [
            (moded[0], total_a0, late[5:6], total_b0, late[2:4]),
            (moded[0], total_a1, late[4:5], total_b1, late[0:2]),
        ]
        time_grad, embed_grad, bias_grad, own_part, shared_part = ends
        own_squares = own_part[0, 0] + moded[2][0, 0]
        shared_squares = shared_part[0, 0]
        final_grad = moded[3]
    else:
        shared = gather_cols(place, mine)
        time_full = lax.all_gather(time_mlp.astype(BF16), "row", axis=0, tiled=True)
        time_full = lax.all_gather(time_full, "col", axis=1, tiled=True)
        class_full = lax.all_gather(class_rows, "col", axis=1, tiled=True)
        class_full = lax.all_gather(class_full, "row", axis=0, tiled=True).astype(F32)
        freq_low = lax.all_gather(freq_row, "row", axis=0, tiled=True)
        all_labels = lax.all_gather(labels, "row", axis=0, tiled=True)
        bias_full = jnp.swapaxes(shared, 0, 1).reshape(-1, width)
        first_time = (
            jnp.dot(freq_low, time_full[:FREQ], preferred_element_type=F32) + bias_full[base]
        )
        first_act = jax.nn.silu(first_time).astype(BF16)
        condition = (
            jnp.dot(first_act, time_full[FREQ:], preferred_element_type=F32)
            + bias_full[base + 1]
            + class_full
        )
        cond_act = jax.nn.silu(condition).astype(BF16)
        cond_rows, partial = partial_modes(cond_act)
        mods_a, mods_b, final_mod = own_modes(
            scatter_plain(place, partial, samples), shared, cond_act
        )
        grad = embed_tokens(base, noisy, shared, position)
        for layer in range(layers):
            buffers[2 * layer] = [plain_gather(packed[3 * layer : 3 * layer + 1])]
            buffers[2 * layer + 1] = [plain_gather(packed[3 * layer + 1 : 3 * layer + 3])]
            entry[layer] = grad
            fore_a[layer] = attn_step(layer)(buffers[2 * layer], grad, mods_a[layer], shared)
            grad = fore_a[layer][0]
            fore_b[layer] = mlp_step(layer)(buffers[2 * layer + 1], grad, mods_b[layer], shared)
            grad = fore_b[layer][0]
        last = last_step(grad, final_mod)
        grad = last[0]
        for layer in reversed(range(layers)):
            out, h, u, m = fore_b[layer]
            back_b[layer], grads = mlp_back(
                buffers[2 * layer + 1], grad, fore_a[layer][0], mods_b[layer], m, h, u
            )
            summed[2 * layer + 1] = plain_scatter(grads[0])
            grad = back_b[layer][0]
            out, h, qkv, p, o, a = fore_a[layer]
            back_a[layer], grads = attn_back(
                buffers[2 * layer], grad, entry[layer], mods_a[layer], a, h, qkv, p, o
            )
            summed[2 * layer] = plain_scatter(grads[0])
            grad = back_a[layer][0]
        mode_full = lax.all_gather(mode_low, "col")
        near = gather_near(place, mode_parts(back_a, back_b, last[4]))
        moded = modes_backward_plain(
            near, cond_rows, mode_full, cond_act, final_low, place.col
        )
        mode_blocks, part, square, final_grad, cond_final, final_squares = moded
        own_squares = square[0, 0]
        small = lax.psum(collected(back_a, back_b, last), ("row", "col"))
        grad_cond = lax.all_gather(part, "row", axis=1, tiled=True) + cond_final
        grad_condition = grad_cond * silu_slope(condition)
        one_hot = (all_labels[:, None] == jnp.arange(CLASSES, dtype=jnp.int32)[None, :]).astype(F32)
        grad_classes = jnp.einsum(
            "sd,sc->dc", my_cols(grad_condition, 1), one_hot, precision=HIGHEST
        )
        condition_low = grad_condition.astype(BF16)
        grad_first = jnp.einsum(
            "se,de->sd", condition_low, time_full[FREQ:], preferred_element_type=F32
        ) * silu_slope(first_time)
        time_inputs = lax.dynamic_slice_in_dim(
            jnp.concatenate([freq_low, first_act], axis=1), place.row * time_rows, time_rows, 1
        )
        time_outputs = jnp.where(
            (place.row + 1) * time_rows <= FREQ, grad_first.astype(BF16), condition_low
        )
        time_grad = jnp.einsum(
            "sd,se->ed", time_inputs, my_cols(time_outputs, 1), preferred_element_type=F32
        )
        own_rows, shared_squares = [], jnp.zeros((), F32)
        for layer in range(layers):
            rows_at = small[16 * layer : 16 * layer + 16]
            own = my_cols(rows_at, 1)
            mlp_rows = lax.dynamic_index_in_dim(rows_at[6:10], place.col, 0, False)
            attn_rows = lax.dynamic_index_in_dim(rows_at[10:14], place.col, 0, False)
            attn_rows = attn_rows[: 3 * narrow].reshape(3, narrow)
            own_rows += [own[:6], attn_rows[0:1], attn_rows[2:3]]
            own_rows += [mlp_rows.reshape(hidden_blocks, narrow), own[14:16]]
            counted = rows_at[10:14, : 3 * narrow].reshape(4, 3, narrow)[:, 0::2]
            shared_squares = (
                shared_squares + squared(rows_at[:10]) + squared(counted) + squared(rows_at[14:])
            )
        time_bias = jnp.stack([jnp.sum(grad_first, axis=0), jnp.sum(grad_condition, axis=0)])
        own_rows += [my_cols(time_bias, 1), my_cols(small[start : start + 1], 1)]
        bias_grad = jnp.concatenate(own_rows, axis=0)
        shared_squares = (
            shared_squares
            + squared(time_bias)
            + squared(small[start - 2 * PATCH : start + 3])
            + squared(small[start + 3, :PATCH])
            + final_squares[0, 0]
        )
        own_squares = own_squares + squared(time_grad) + squared(grad_classes) / rows
        sums = [(mode_blocks, summed[2 * k], summed[2 * k + 1]) for k in range(layers)]
        patch_grad = my_cols(small[start - PATCH : start], 1)
        embed_grad = jnp.concatenate([grad_classes, patch_grad.T], axis=1)

    head_grad = small[start - 2 * PATCH : start - PATCH]
    final_bias_grad = jnp.concatenate(
        [small[start + 1], small[start + 2], small[start + 3, :PATCH]]
    )
    loss_total = jnp.sum(small[start + 4, :PATCH])
    count_total = small[start + 5, 0]
    for value in summed:
        own_squares = own_squares + squared(value)
    grad_norm = jnp.sqrt(sum_scalar(place, own_squares) + shared_squares)
    clip_factor = jnp.minimum(1.0, CLIP_NORM / (grad_norm + 1e-06))
    clip = clip_factor[None]

    results = [loss_total, count_total, grad_norm]
    new_blocks = adam_blocks(clip, spot, sums, in_view, [weights_out, momentum_out, variance_out])
    results += [jnp.transpose(v, (0, 2, 1, 3)) for v in new_blocks[:3]] + list(new_blocks[3:])
    rest = adam_rest(
        clip,
        [
            (time_mlp.T, time_grad, momentum_time.T, variance_time.T, RATE),
            (embed_table.T, embed_grad, momentum_embed.T, variance_embed.T, RATE),
            (bias_table, bias_grad, momentum_bias, variance_bias, RATE_BIAS),
        ],
    )
    results += [v.T for v in rest[:6]]
    results += [v.T for v in adam_final(clip, final_grad, head_grad, *final_view)]
    results += list(rest[6:9])
    results += adam(
        final_bias, final_bias_grad, momentum_final_bias, variance_final_bias, clip_factor,
        RATE_BIAS,
    )
    return tuple(results)


def solution(mesh):
    tokens, latents = P("row", None), P("row")
    weights = (
        P(None, "row", None, "col"),
        P(None, None, "col", "row"),
        P("row", "col"),
        P(None, "col"),
        P(),
        P(None, "col"),
        P(),
    )
    updated = []
    for spec in weights:
        updated += [spec] * 3
    return jax.shard_map(
        on_device,
        mesh=mesh,
        in_specs=(tokens, tokens, latents, latents, latents) + weights * 3,
        out_specs=(P(), P(), P()) + tuple(updated),
        check_vma=False,
    )
```

```python
import functools
import math

import jax
import jax.numpy as jnp
import numpy as np
from jax import lax
from jax.experimental import pallas as pl
from jax.experimental.pallas import tpu as pltpu
from jax.sharding import PartitionSpec as P

HEAD_DIM = 64
CLASSES = 1000
FREQ = 256
PATCH = 16
LEN = 256
STEPS_T = 1000
STEP = 10

HIGHEST = lax.Precision.HIGHEST
EPS_NORM = 1e-06
CLIP_NORM = 1.0
RATE = 0.05
RATE_BIAS = 0.25
BETA_ONE = 0.9
BETA_TWO = 0.999
DECAY = 0.01
ADAM_EPS = 1e-08

F32 = jnp.float32
BF16 = jnp.bfloat16
MIB = 1024 * 1024
ANY = pl.BlockSpec(memory_space=pl.ANY)
SMEM = pl.BlockSpec(memory_space=pltpu.SMEM)
NT = (((1,), (1,)), ((), ()))
TN = (((0,), (0,)), ((), ()))


def dot_nt(a, b):
    return lax.dot_general(a, b, NT, preferred_element_type=F32)


def dot_tn(a, b):
    return lax.dot_general(a, b, TN, preferred_element_type=F32)


def dot_nn(a, b):
    return jnp.dot(a, b, preferred_element_type=F32)


def along(k):
    return k % 2 * 2 + k // 2


class Place:
    def __init__(self, row_block):
        self.rows = lax.axis_size("row")
        self.cols = lax.axis_size("col")
        self.row = lax.axis_index("row")
        self.col = lax.axis_index("col")
        self.direct = self.rows == 8 and self.cols == 4 and row_block % 32 == 0
        self.z = self.row // 2
        self.y = self.row % 2
        self.x = self.col // 2
        self.core = self.col % 2
        self.half = row_block // 2
        self.table = self.route_table() if self.direct else jnp.zeros((8,), jnp.int32)

    def route_table(self):
        z, y, x, core = self.z, self.y, self.x, self.core
        e = jnp.arange(64, dtype=jnp.int32)
        owner = core ^ (e // 32)
        later, first, kc, kz = e // 16 % 2, e // 8 % 2, e // 4 % 2, e % 4
        kx = jnp.where(owner == 0, first, later)
        ky = jnp.where(owner == 0, later, first)
        cols = (x ^ kx) * 2 + (owner ^ kc)
        rows = ((z ^ along(kz)) * 2 + (y ^ ky)) * 2 * self.half + owner * self.half
        e = jnp.arange(16, dtype=jnp.int32)
        col, owner, ky = e // 4, core ^ (e // 2 % 2), e % 2
        kx = (col // 2) ^ x
        later = jnp.where(owner == 0, ky, kx)
        first = jnp.where(owner == 0, kx, ky)
        slots = jnp.stack([later, first, (col % 2) ^ owner], axis=1).reshape(-1)
        owner, ky, kz = core ^ (e // 8), e // 4 % 2, e % 4
        outs = ((z ^ along(kz)) * 2 + (y ^ ky)) * 2 * self.half + owner * self.half
        step = jnp.arange(4, dtype=jnp.int32)
        order = (x ^ (step % 2)) * 2 + (core ^ (step // 2))
        return jnp.concatenate([cols, rows, slots, outs, order, core[None]]).astype(jnp.int32)

    def found_at(self):
        device = jnp.arange(self.rows * self.cols, dtype=jnp.int32)
        if not self.direct:
            return device
        row, col = device // 4, device % 4
        kz = along(row // 2 ^ self.z)
        ky = (row % 2) ^ self.y
        kx = (col // 2) ^ self.x
        kc = (col % 2) ^ self.core
        return ((kc * 2 + kx) * 2 + ky) * 4 + kz


def swap_x(v):
    return lax.ppermute(v, "col", [(c, c ^ 2) for c in range(4)])


def swap_core(v):
    return lax.ppermute(v, "col", [(c, c ^ 1) for c in range(4)])


def swap_y(v):
    return lax.ppermute(v, "row", [(r, r ^ 1) for r in range(8)])


def swap_first(v):
    pairs = [(d, d ^ 2 if d % 2 == 0 else d ^ 4) for d in range(32)]
    return lax.ppermute(v, ("row", "col"), pairs)


def swap_second(v):
    pairs = [(d, d ^ 4 if d % 2 == 0 else d ^ 2) for d in range(32)]
    return lax.ppermute(v, ("row", "col"), pairs)


def swap_far(v):
    return lax.ppermute(v, "row", [(r, r ^ 4) for r in range(8)])


def swap_near(v):
    return lax.ppermute(v, "row", [(r, r ^ 2) for r in range(8)])


def swap_beyond(v):
    return lax.ppermute(v, "row", [(r, r ^ 6) for r in range(8)])


def pair(index, own, other):
    first = index == 0
    return jnp.stack([jnp.where(first, own, other), jnp.where(first, other, own)])


def gather_cols(place, own):
    if not place.direct:
        return lax.all_gather(own, "col")
    both = pair(place.core, own, swap_core(own))
    return pair(place.x, both, swap_x(both)).reshape((4,) + own.shape)


def near_z(own):
    both = jnp.stack([own, swap_far(own)])
    return jnp.concatenate([both, swap_near(both)])


def near_z_at_once(own):
    return jnp.stack([own, swap_far(own), swap_near(own), swap_beyond(own)])


def near_y(every):
    return jnp.concatenate([every, swap_y(every)])


def near_rows(own):
    return near_y(near_z(own))


def near_x(every):
    return jnp.concatenate([every, swap_x(every)])


def near_core(every):
    return jnp.concatenate([every, swap_core(every)])


def near_cols(every):
    return near_core(near_x(every))


def gather_near(place, own):
    if not place.direct:
        return lax.all_gather(own, ("row", "col"))
    return near_cols(near_rows(own))


def sum_parts(place, parts):
    z = place.z

    def two(at):
        return jnp.stack([lax.dynamic_index_in_dim(parts, k, 0, False) for k in (at, at ^ 2)])

    total = two(z) + swap_near(two(z ^ 1))
    return total[0] + swap_far(total[1])


def sum_along_z(place, own):
    return sum_parts(place, own.reshape((4, own.shape[0] // 4) + own.shape[1:]))


def sum_with(swap):
    return lambda total: total + swap(total)


def sum_spread(place, total):
    far = pair(place.z // 2, total, swap_far(total))
    every = pair(place.z % 2, far, swap_near(far))
    return jnp.swapaxes(every, 0, 1).reshape((-1,) + total.shape[1:])


def sum_scalar(place, value):
    if not place.direct:
        return lax.psum(value, ("row", "col"))
    total = jnp.broadcast_to(value, (8, 128))
    for swap in (swap_far, swap_near, swap_y, swap_x, swap_core):
        total = total + swap(total)
    return total[0, 0]


def scatter_plain(place, partial, mine):
    _, count, narrow = partial.shape
    summed = lax.psum_scatter(partial, "row", scatter_dimension=0, tiled=True)
    spread = lax.all_gather(summed, "col")
    spread = lax.dynamic_slice_in_dim(spread, place.col * mine, mine, 1)
    return jnp.transpose(spread, (1, 2, 0, 3)).reshape(mine, count, place.cols * narrow)


def scatter_y(place, partial):
    samples, count, narrow = partial.shape
    by_y = partial.reshape(4, 2, samples // 8, count, narrow)
    own = lax.dynamic_index_in_dim(by_y, place.y, 1, False)
    return own + swap_y(lax.dynamic_index_in_dim(by_y, 1 - place.y, 1, False))


def scatter_z(place, own):
    return sum_parts(place, own)


def scatter_x(place, total, mine):
    _, count, narrow = total.shape
    by_x = total.reshape(2, 2, mine, count, narrow)
    own = lax.dynamic_index_in_dim(by_x, place.x, 0, False)
    got = swap_x(lax.dynamic_index_in_dim(by_x, 1 - place.x, 0, False))
    return pair(place.x, own, got)


def scatter_core(place, both):
    _, _, mine, count, narrow = both.shape
    own = lax.dynamic_index_in_dim(both, place.core, 1, False)
    got = swap_core(lax.dynamic_index_in_dim(both, 1 - place.core, 1, False))
    every = pair(place.core, own, got)
    return jnp.transpose(every, (2, 3, 1, 0, 4)).reshape(mine, count, 4 * narrow)


class Route:
    def __init__(self, place, buffers):
        self.direct = place.direct
        self.half = place.half
        self.cols = place.cols
        self.count = len(buffers)
        if self.direct:
            matrices = buffers[0].shape[2]
            self.outs = [(2, 8, 2, matrices) + buffers[0].shape[3:]] * 2
        else:
            self.outs = [buffers[0].shape]

    def column(self, table, step):
        return table[192 + step] if self.direct else step

    def load(self, table, buffers, moves):
        if not self.direct:
            for c in range(self.cols):
                for matrix, target, sems in moves:
                    pltpu.make_async_copy(
                        buffers[0].at[matrix, c], target.at[c], sems.at[c]
                    ).start()
            return
        for core in range(2):

            @pl.when(table[196] == core)
            def _(core=core):
                entries = []
                for e in range(64):
                    owner, later, first, kc = core ^ (e // 32), e // 16 % 2, e // 8 % 2, e // 4 % 2
                    kx = first if owner == 0 else later
                    entries.append(((owner ^ kc ^ core) * 2 + kx, e))
                for step in range(4):
                    for matrix, target, sems in moves:
                        for at, e in entries:
                            if at != step:
                                continue
                            row = pl.multiple_of(table[64 + e], 16)
                            pltpu.make_async_copy(
                                buffers[e // 16].at[e // 8 % 2 * 4 + e % 4, e // 4 % 2, matrix],
                                target.at[step, pl.ds(row, self.half), :],
                                sems.at[step],
                            ).start()

    def store(self, table, c, matrix, source, grads, sem):
        if not self.direct:
            pltpu.make_async_copy(source, grads[0].at[matrix, c], sem).start()
            return
        for owner in range(2):
            for ky in range(2):
                at = 128 + ((c * 2 + owner) * 2 + ky) * 3
                for kz in range(4):
                    row = pl.multiple_of(table[176 + (owner * 2 + ky) * 4 + kz], 16)
                    pltpu.make_async_copy(
                        source.at[pl.ds(row, self.half), :],
                        grads[owner].at[
                            table[at], table[at + 1] * 4 + kz, table[at + 2], matrix
                        ],
                        sem,
                    ).start()


class Stages:
    def __init__(self):
        self.last = None

    def run(self, moves, works=(), late=()):
        operands = ([v for _, v in moves], [w[1:] for w in works], [v for _, v in late])
        if self.last is not None:
            operands, _ = lax.optimization_barrier((operands, self.last))
        moved = [move(v) for (move, _), v in zip(moves, operands[0])]
        done = [w[0](*v) for w, v in zip(works, operands[1])]
        if late:
            held, _ = lax.optimization_barrier((operands[2], done))
            moved += [move(v) for (move, _), v in zip(late, held)]
        self.last = (moved, done)
        return moved, done


class Spread:
    def __init__(self, kept, got):
        self.own = jnp.stack([kept, got])

    def far(self):
        return [(swap_far, self.own)]

    def near(self, got):
        self.two = jnp.stack([self.own, got])
        return [(swap_near, self.two)]

    def at_once(self):
        return [(swap_far, self.own), (swap_near, self.own), (swap_beyond, self.own)]

    def along_at_once(self, got):
        self.z = jnp.stack([self.own] + list(got))

    def along(self, got):
        self.z = jnp.concatenate([self.two, got])

    def first(self):
        return [(swap_first, self.z)]

    def second(self, got):
        self.p = jnp.concatenate([self.z, got])
        return [(swap_second, self.p)]

    def core(self):
        return [(swap_core, self.p)]

    def late_core(self, q):
        self.q = q
        return [(swap_core, q)]

    def buffers(self, core, late_core):
        return [self.p, self.q, core, late_core]


def add_up(*parts):
    total = parts[0].astype(F32)
    for part in parts[1:]:
        total = total + part.astype(F32)
    return total


class Gathered:
    def __init__(self, buffers):
        self.own = buffers[0]
        self.core = [(swap_core, buffers[1])]

    def first(self, got):
        self.got = got
        return [(swap_second, add_up(self.own[1], got[1]).astype(BF16))]

    def second(self, got):
        self.parts = (self.own[0], self.got[0], got)
        return [(swap_first, add_up(*[v[4:] for v in self.parts]).astype(BF16))]

    def near(self, got):
        self.parts = self.parts + (got,)
        return [(swap_near, add_up(*[v[2:4] for v in self.parts]).astype(BF16))]

    def far(self, got):
        self.last = got
        return [(swap_far, add_up(*[v[1] for v in self.parts], got[1]).astype(BF16))]

    def total(self, got):
        return add_up(*[v[0] for v in self.parts], self.last[0], got)


def plain_gather(parts):
    every = lax.all_gather(lax.all_gather(parts, "row", axis=1, tiled=True), "col")
    return jnp.swapaxes(every, 0, 1)


def plain_scatter(grads):
    summed = lax.psum_scatter(grads.astype(F32), "row", scatter_dimension=2, tiled=True)
    return lax.psum_scatter(summed, "col", scatter_dimension=1, tiled=False)


def normal(v):
    center = jnp.mean(v, axis=-1, keepdims=True)
    moved = v - center
    inverse = lax.rsqrt(jnp.mean(moved * moved, axis=-1, keepdims=True) + EPS_NORM)
    return moved * inverse, inverse


def wait_all(ref, sem):
    pltpu.make_async_copy(ref, ref, sem).wait()


def row_of(shared_ref, at):
    return jnp.concatenate(
        [shared_ref[c, at : at + 1, :] for c in range(shared_ref.shape[0])], axis=1
    )


def attention_forward_body(route, base, table, x_ref, mod_ref, shared_ref, *refs):
    n_buf = route.count
    buffers = refs[:n_buf]
    out_ref, h_ref, qkv_ref, p_ref, o_ref, a_ref, w_ref, sems = refs[n_buf:]
    c = pl.program_id(0)
    samples = mod_ref.shape[0]

    @pl.when(c == 0)
    def _():
        route.load(table, buffers, [(0, w_ref, sems)])
        for s in range(samples):
            rows = pl.ds(s * LEN, LEN)
            n, _ = normal(x_ref[rows, :])
            h_ref[rows, :] = (n * (1.0 + mod_ref[s, 1:2]) + mod_ref[s, 0:1]).astype(BF16)
        a_ref[...] = jnp.zeros_like(a_ref)

    wait_all(w_ref.at[c], sems.at[c])
    width = shared_ref.shape[-1]
    col = route.column(table, c)
    query_bias = shared_ref[col, base + 6 : base + 7, :]
    value_bias = shared_ref[col, base + 7 : base + 8, :]
    bias = jnp.concatenate([query_bias, jnp.zeros_like(query_bias), value_bias], axis=1)
    triple = dot_nn(h_ref[...], w_ref[c, :, : 3 * width]) + bias
    qkv_ref[0] = triple.astype(BF16)
    triple = triple.astype(BF16)
    heads = width // HEAD_DIM

    def part(s, k, j):
        at = k * width + j * HEAD_DIM
        return triple[s * LEN : (s + 1) * LEN, at : at + HEAD_DIM]

    each = [(s, j) for s in range(samples) for j in range(heads)]
    scores = [dot_nt(part(s, 1, j), part(s, 0, j)) * HEAD_DIM ** (-0.5) for s, j in each]
    probs = []
    for score in scores:
        powers = jnp.exp(score - jnp.max(score, axis=0, keepdims=True))
        probs.append((powers * (1.0 / jnp.sum(powers, axis=0, keepdims=True))).astype(BF16))
    for (s, j), prob in zip(each, probs):
        p_ref[0, j, s] = prob
    outs = [dot_tn(prob, part(s, 2, j)).astype(BF16) for (s, j), prob in zip(each, probs)]
    for s in range(samples):
        o_ref[0, pl.ds(s * LEN, LEN), :] = jnp.concatenate(
            outs[s * heads : (s + 1) * heads], axis=1
        )
    a_ref[...] += dot_nt(o_ref[0], w_ref[c, :, 3 * width :])

    @pl.when(c == pl.num_programs(0) - 1)
    def _():
        a_ref[...] += row_of(shared_ref, base + 12)
        for s in range(samples):
            rows = pl.ds(s * LEN, LEN)
            out_ref[rows, :] = x_ref[rows, :] + mod_ref[s, 2:3] * a_ref[rows, :]


def mlp_forward_body(route, base, table, x_ref, mod_ref, shared_ref, *refs):
    n_buf = route.count
    buffers = refs[:n_buf]
    out_ref, h_ref, u_ref, m_ref, wi_ref, wo_ref, sems_i, sems_o = refs[n_buf:]
    c = pl.program_id(0)
    samples = mod_ref.shape[0]

    @pl.when(c == 0)
    def _():
        route.load(table, buffers, [(0, wi_ref, sems_i), (1, wo_ref, sems_o)])
        for s in range(samples):
            rows = pl.ds(s * LEN, LEN)
            n, _ = normal(x_ref[rows, :])
            h_ref[rows, :] = (n * (1.0 + mod_ref[s, 1:2]) + mod_ref[s, 0:1]).astype(BF16)
        m_ref[...] = jnp.zeros_like(m_ref)

    wait_all(wi_ref.at[c], sems_i.at[c])
    col = route.column(table, c)
    blocks = wi_ref.shape[-1] // shared_ref.shape[-1]
    bias = jnp.concatenate(
        [shared_ref[col, base + 8 + k : base + 9 + k, :] for k in range(blocks)], axis=1
    )
    hidden = dot_nn(h_ref[...], wi_ref[c]) + bias
    u_ref[0] = hidden
    active = jax.nn.gelu(hidden, approximate=True).astype(BF16)
    wait_all(wo_ref.at[c], sems_o.at[c])
    m_ref[...] += dot_nt(active, wo_ref[c])

    @pl.when(c == pl.num_programs(0) - 1)
    def _():
        m_ref[...] += row_of(shared_ref, base + 13)
        for s in range(samples):
            rows = pl.ds(s * LEN, LEN)
            out_ref[rows, :] = x_ref[rows, :] + mod_ref[s, 2:3] * m_ref[rows, :]


def norm_backward(s, x_ref, mod_ref, dx_ref, dh_ref, out_ref, dmod_ref):
    rows = pl.ds(s * LEN, LEN)
    n, inverse = normal(x_ref[rows, :])
    dh = dh_ref[rows, :]
    dmod_ref[s, 0:1] = jnp.sum(dh, axis=0, keepdims=True)
    dmod_ref[s, 1:2] = jnp.sum(dh * n, axis=0, keepdims=True)
    dn = dh * (1.0 + mod_ref[s, 1:2])
    back = inverse * (
        dn
        - jnp.mean(dn, axis=-1, keepdims=True)
        - n * jnp.mean(dn * n, axis=-1, keepdims=True)
    )
    if dx_ref is None:
        out_ref[rows, :] = back
    else:
        out_ref[rows, :] = dx_ref[rows, :] + back


def branch_gradient(dx_ref, mod_ref, branch_ref, dmod_ref, sum_ref, low_ref):
    total = None
    for s in range(mod_ref.shape[0]):
        rows = pl.ds(s * LEN, LEN)
        dx = dx_ref[rows, :]
        dmod_ref[s, 2:3] = jnp.sum(dx * branch_ref[rows, :], axis=0, keepdims=True)
        db = mod_ref[s, 2:3] * dx
        low_ref[rows, :] = db.astype(BF16)
        part = jnp.sum(db, axis=0, keepdims=True)
        total = part if total is None else total + part
    sum_ref[...] = total


def gelu_slope(u):
    k = math.sqrt(2.0 / math.pi)
    square = u * u
    t = jnp.tanh(k * (u + 0.044715 * square * u))
    half = 0.5 * (1.0 + t)
    slope = half + 0.5 * u * (1.0 - t * t) * (k * (1.0 + 3 * 0.044715 * square))
    return u * half, slope


def mlp_backward_body(
    route, table, dx_ref, x_ref, mod_ref, m_ref, h_ref, u_ref, *refs
):
    n_buf, n_out = route.count, len(route.outs)
    buffers = refs[:n_buf]
    out_ref, dmod_ref, dbias_ref, dtail_ref = refs[n_buf : n_buf + 4]
    grads = refs[n_buf + 4 : n_buf + n_out + 4]
    wi_ref, wo_ref, low_ref, dh_ref, gi_ref, go_ref, sems_i, sems_o, sems_gi, sems_go = refs[
        n_buf + n_out + 4 :
    ]
    c = pl.program_id(0)
    count = route.cols
    samples = mod_ref.shape[0]

    @pl.when(c == 0)
    def _():
        route.load(table, buffers, [(1, wo_ref, sems_o), (0, wi_ref, sems_i)])
        branch_gradient(dx_ref, mod_ref, m_ref, dmod_ref, dtail_ref, low_ref)
        dh_ref[...] = jnp.zeros_like(dh_ref)

    slot = lax.rem(c, 2)

    @pl.when(c >= 2)
    def _():
        wait_all(gi_ref.at[slot], sems_gi.at[slot])
        wait_all(go_ref.at[slot], sems_go.at[slot])

    wait_all(wo_ref.at[c], sems_o.at[c])
    active, slope = gelu_slope(u_ref[0])
    low = low_ref[...]
    go_ref[slot] = dot_tn(low, active.astype(BF16)).astype(BF16)
    route.store(table, route.column(table, c), 1, go_ref.at[slot], grads, sems_go.at[slot])
    du = dot_nn(low, wo_ref[c]) * slope
    dbias_ref[route.column(table, c)] = jnp.sum(du, axis=0, keepdims=True)
    du = du.astype(BF16)
    gi_ref[slot] = dot_tn(h_ref[...], du).astype(BF16)
    route.store(table, route.column(table, c), 0, gi_ref.at[slot], grads, sems_gi.at[slot])
    wait_all(wi_ref.at[c], sems_i.at[c])
    dh_ref[...] += dot_nt(du, wi_ref[c])

    @pl.when(c == count - 1)
    def _():
        for s in range(samples):
            norm_backward(s, x_ref, mod_ref, dx_ref, dh_ref, out_ref, dmod_ref)
        for k in range(2):
            wait_all(gi_ref.at[k], sems_gi.at[k])
            wait_all(go_ref.at[k], sems_go.at[k])


def attention_backward_body(
    route, table, dx_ref, x_ref, mod_ref, a_ref, h_ref, qkv_ref, p_ref, o_ref, *refs
):
    n_buf, n_out = route.count, len(route.outs)
    buffers = refs[:n_buf]
    out_ref, dmod_ref, dbias_ref, dtail_ref = refs[n_buf : n_buf + 4]
    grads = refs[n_buf + 4 : n_buf + n_out + 4]
    w_ref, low_ref, dh_ref, d_ref, g_ref, sems, sems_g = refs[n_buf + n_out + 4 :]
    c = pl.program_id(0)
    count = route.cols
    samples = mod_ref.shape[0]
    width = qkv_ref.shape[-1] // 3
    factor = HEAD_DIM ** (-0.5)

    @pl.when(c == 0)
    def _():
        route.load(table, buffers, [(0, w_ref, sems)])
        branch_gradient(dx_ref, mod_ref, a_ref, dmod_ref, dtail_ref, low_ref)
        dh_ref[...] = jnp.zeros_like(dh_ref)

    slot = lax.rem(c, 2)

    @pl.when(c >= 2)
    def _():
        wait_all(g_ref.at[slot], sems_g.at[slot])

    wait_all(w_ref.at[c], sems.at[c])
    do_all = dot_nn(low_ref[...], w_ref[c, :, 3 * width :]).astype(BF16)
    heads = width // HEAD_DIM
    each = [(s, j) for s in range(samples) for j in range(heads)]

    def part(s, k, j):
        at = k * width + j * HEAD_DIM
        return qkv_ref[0, pl.ds(s * LEN, LEN), at : at + HEAD_DIM]

    def given(s, j):
        return do_all[s * LEN : (s + 1) * LEN, j * HEAD_DIM : (j + 1) * HEAD_DIM]

    dps = [dot_nt(part(s, 2, j), given(s, j)) for s, j in each]
    dss = []
    for (s, j), dp in zip(each, dps):
        probs = p_ref[0, j, s].astype(F32)
        delta = jnp.sum(probs * dp, axis=0, keepdims=True)
        dss.append((probs * (dp - delta)).astype(BF16))
    dqs = [dot_tn(ds, part(s, 1, j)) * factor for (s, j), ds in zip(each, dss)]
    dks = [dot_nn(ds, part(s, 0, j)) * factor for (s, j), ds in zip(each, dss)]
    dvs = [dot_nn(p_ref[0, j, s], given(s, j)) for s, j in each]
    sums = None
    for s in range(samples):
        at = slice(s * heads, (s + 1) * heads)
        joined = jnp.concatenate(dqs[at] + dks[at] + dvs[at], axis=1)
        total = jnp.sum(joined, axis=0, keepdims=True)
        sums = total if s == 0 else sums + total
        d_ref[pl.ds(s * LEN, LEN), :] = joined.astype(BF16)
    dbias_ref[route.column(table, c)] = sums
    grad_in = dot_tn(h_ref[...], d_ref[...])
    grad_out = dot_tn(low_ref[...], o_ref[0])
    g_ref[slot] = jnp.concatenate([grad_in, grad_out], axis=1).astype(BF16)
    route.store(table, route.column(table, c), 0, g_ref.at[slot], grads, sems_g.at[slot])
    dh_ref[...] += dot_nt(d_ref[...], w_ref[c, :, : 3 * width])

    @pl.when(c == count - 1)
    def _():
        for s in range(samples):
            norm_backward(s, x_ref, mod_ref, dx_ref, dh_ref, out_ref, dmod_ref)
        for k in range(2):
            wait_all(g_ref.at[k], sems_g.at[k])


def final_body(
    x_ref, mod_ref, head_ref, bias_ref, noise_ref, mask_ref,
    dx_ref, loss_ref, dhead_ref, dbias_ref, dmod_ref, h_ref, dh_ref,
):
    samples = mod_ref.shape[0]
    for s in range(samples):
        rows = pl.ds(s * LEN, LEN)
        n, _ = normal(x_ref[rows, :])
        h_ref[rows, :] = (n * (1.0 + mod_ref[s, 1:2]) + mod_ref[s, 0:1]).astype(BF16)
    predicted = dot_nt(h_ref[...], head_ref[...]) + bias_ref[...]
    error = predicted - noise_ref[...]
    masked = mask_ref[...] * error
    loss_ref[...] = jnp.sum(masked * error, axis=0, keepdims=True)
    dpred = 2.0 * masked
    dbias_ref[...] = jnp.sum(dpred, axis=0, keepdims=True)
    low = dpred.astype(BF16)
    dhead_ref[...] = dot_tn(low, h_ref[...])
    dh_ref[...] = dot_nn(low, head_ref[...])
    for s in range(samples):
        norm_backward(s, x_ref, mod_ref, None, dh_ref, dx_ref, dmod_ref)


def whole_block(shape):
    rank = len(shape)
    return pl.BlockSpec(shape, lambda c: (0,) * rank, pipeline_mode=pl.Buffered(1))


def whole_out(shape):
    rank = len(shape)
    return pl.BlockSpec(shape, lambda c: (0,) * rank)


def block_of(shape):
    rank = len(shape)
    return pl.BlockSpec((1,) + tuple(shape[1:]), lambda c: (c,) + (0,) * (rank - 1))


def params(mib):
    return pltpu.CompilerParams(
        dimension_semantics=("arbitrary",), vmem_limit_bytes=mib * MIB
    )


def cost(flops, nbytes, exps=0):
    return pl.CostEstimate(flops=int(flops), bytes_accessed=int(nbytes), transcendentals=int(exps))


def shaped(shape, dtype):
    return jax.ShapeDtypeStruct(tuple(shape), dtype)


def attention_forward(place, base, buffers, x, mods, shared):
    route = Route(place, buffers)
    count = place.cols
    tokens, width = x.shape
    samples = mods.shape[0]
    narrow = shared.shape[-1]
    heads = narrow // HEAD_DIM
    outs = [
        shaped((tokens, width), F32),
        shaped((tokens, width), BF16),
        shaped((count, tokens, 3 * narrow), BF16),
        shaped((count, heads, samples, LEN, LEN), BF16),
        shaped((count, tokens, narrow), BF16),
        shaped((tokens, width), F32),
    ]
    return pl.pallas_call(
        functools.partial(attention_forward_body, route, base),
        grid=(count,),
        in_specs=[SMEM, whole_block(x.shape), whole_block(mods.shape), whole_block(shared.shape)]
        + [ANY] * len(buffers),
        out_specs=[whole_out(outs[0].shape), whole_out(outs[1].shape)]
        + [block_of(o.shape) for o in outs[2:5]]
        + [whole_out(outs[5].shape)],
        out_shape=outs,
        scratch_shapes=[
            pltpu.VMEM((count, width, 4 * narrow), BF16),
            pltpu.SemaphoreType.DMA((count,)),
        ],
        compiler_params=params(58),
        cost_estimate=cost(
            2 * tokens * width * width * 4 + 4 * tokens * LEN * width,
            8 * width * width + 30 * tokens * width,
            tokens * LEN * width // HEAD_DIM,
        ),
        name="attention_forward",
    )(place.table, x, mods, shared, *buffers)


def mlp_forward(place, base, buffers, x, mods, shared):
    route = Route(place, buffers)
    count = place.cols
    tokens, width = x.shape
    wide = buffers[0].shape[-1]
    outs = [
        shaped((tokens, width), F32),
        shaped((tokens, width), BF16),
        shaped((count, tokens, wide), F32),
        shaped((tokens, width), F32),
    ]
    return pl.pallas_call(
        functools.partial(mlp_forward_body, route, base),
        grid=(count,),
        in_specs=[SMEM, whole_block(x.shape), whole_block(mods.shape), whole_block(shared.shape)]
        + [ANY] * len(buffers),
        out_specs=[whole_out(outs[0].shape), whole_out(outs[1].shape), block_of(outs[2].shape)]
        + [whole_out(outs[3].shape)],
        out_shape=outs,
        scratch_shapes=[
            pltpu.VMEM((count, width, wide), BF16),
            pltpu.VMEM((count, width, wide), BF16),
            pltpu.SemaphoreType.DMA((count,)),
            pltpu.SemaphoreType.DMA((count,)),
        ],
        compiler_params=params(58),
        cost_estimate=cost(
            2 * tokens * width * wide * count * 2,
            4 * width * wide * count + 30 * tokens * width,
            tokens * wide * count,
        ),
        name="mlp_forward",
    )(place.table, x, mods, shared, *buffers)


def mlp_backward(place, buffers, dx, x, mods, m, h, u):
    route = Route(place, buffers)
    count = place.cols
    tokens, width = x.shape
    wide = u.shape[-1]
    outs = [
        shaped((tokens, width), F32),
        shaped(mods.shape, F32),
        shaped((count, 1, wide), F32),
        shaped((1, width), F32),
    ] + [shaped(v, BF16) for v in route.outs]
    out = pl.pallas_call(
        functools.partial(mlp_backward_body, route),
        grid=(count,),
        in_specs=[SMEM, whole_block(x.shape), whole_block(x.shape), whole_block(mods.shape)]
        + [whole_block(m.shape), whole_block(h.shape), block_of(u.shape)]
        + [ANY] * len(buffers),
        out_specs=[whole_out(x.shape), whole_out(mods.shape), whole_out(outs[2].shape)]
        + [whole_out((1, width))]
        + [ANY] * len(route.outs),
        out_shape=outs,
        scratch_shapes=[
            pltpu.VMEM((count, width, wide), BF16),
            pltpu.VMEM((count, width, wide), BF16),
            pltpu.VMEM((tokens, width), BF16),
            pltpu.VMEM((tokens, width), F32),
            pltpu.VMEM((2, width, wide), BF16),
            pltpu.VMEM((2, width, wide), BF16),
            pltpu.SemaphoreType.DMA((count,)),
            pltpu.SemaphoreType.DMA((count,)),
            pltpu.SemaphoreType.DMA((2,)),
            pltpu.SemaphoreType.DMA((2,)),
        ],
        compiler_params=params(58),
        cost_estimate=cost(
            4 * 2 * tokens * width * wide * count,
            8 * width * wide * count + 40 * tokens * width,
            tokens * wide * count,
        ),
        name="mlp_backward",
    )(place.table, dx, x, mods, m, h, u, *buffers)
    return out[:4], out[4:]


def attention_backward(place, buffers, dx, x, mods, a, h, qkv, p, o):
    route = Route(place, buffers)
    count = place.cols
    tokens, width = x.shape
    narrow = o.shape[-1]
    outs = [
        shaped((tokens, width), F32),
        shaped(mods.shape, F32),
        shaped((count, 1, 3 * narrow), F32),
        shaped((1, width), F32),
    ] + [shaped(v, BF16) for v in route.outs]
    out = pl.pallas_call(
        functools.partial(attention_backward_body, route),
        grid=(count,),
        in_specs=[SMEM, whole_block(x.shape), whole_block(x.shape), whole_block(mods.shape)]
        + [whole_block(a.shape), whole_block(h.shape)]
        + [block_of(qkv.shape), block_of(p.shape), block_of(o.shape)]
        + [ANY] * len(buffers),
        out_specs=[whole_out(x.shape), whole_out(mods.shape), whole_out(outs[2].shape)]
        + [whole_out((1, width))]
        + [ANY] * len(route.outs),
        out_shape=outs,
        scratch_shapes=[
            pltpu.VMEM((count, width, 4 * narrow), BF16),
            pltpu.VMEM((tokens, width), BF16),
            pltpu.VMEM((tokens, width), F32),
            pltpu.VMEM((tokens, 3 * narrow), BF16),
            pltpu.VMEM((2, width, 4 * narrow), BF16),
            pltpu.SemaphoreType.DMA((count,)),
            pltpu.SemaphoreType.DMA((2,)),
        ],
        compiler_params=params(58),
        cost_estimate=cost(
            4 * tokens * width * width * 4 + 10 * tokens * LEN * width,
            16 * width * width + 40 * tokens * width,
        ),
        name="attention_backward",
    )(place.table, dx, x, mods, a, h, qkv, p, o, *buffers)
    return out[:4], out[4:]


def final_step(x, mods, head, bias, noise, mask):
    tokens, width = x.shape
    vmem = pl.BlockSpec(memory_space=pltpu.VMEM)
    return pl.pallas_call(
        final_body,
        in_specs=[vmem] * 6,
        out_specs=[vmem] * 5,
        out_shape=[
            shaped((tokens, width), F32),
            shaped((1, PATCH), F32),
            shaped((PATCH, width), F32),
            shaped((1, PATCH), F32),
            shaped(mods.shape, F32),
        ],
        scratch_shapes=[pltpu.VMEM((tokens, width), BF16), pltpu.VMEM((tokens, width), F32)],
        compiler_params=pltpu.CompilerParams(vmem_limit_bytes=32 * MIB),
        cost_estimate=cost(6 * tokens * width * PATCH, 12 * tokens * width),
        name="final_step",
    )(x, mods, head, bias, noise, mask)


def pack_body(in_ref, out_ref, block_ref, mode_ref):
    blocks = out_ref.shape[1] - 1
    for k in range(6):
        mode_ref[0, k] = in_ref[0, k].astype(BF16)
    attn = [in_ref[0, 6 + k] for k in range(3)] + [out_ref[0, 0].T]
    block_ref[0] = jnp.concatenate(attn, axis=1).astype(BF16)
    first = [in_ref[0, 9 + k] for k in range(blocks)]
    block_ref[1] = jnp.concatenate(first, axis=1).astype(BF16)
    second = [out_ref[0, 1 + k].T for k in range(blocks)]
    block_ref[2] = jnp.concatenate(second, axis=1).astype(BF16)


def pack_weights(weights_in, weights_out):
    layers, kinds, block, narrow = weights_in.shape
    outs = [
        shaped((3 * layers, block, 4 * narrow), BF16),
        shaped((layers, 6, block, narrow), BF16),
    ]
    return pl.pallas_call(
        pack_body,
        grid=(layers,),
        in_specs=[block_of(weights_in.shape), block_of(weights_out.shape)],
        out_specs=[
            pl.BlockSpec((3, block, 4 * narrow), lambda c: (c, 0, 0)),
            block_of(outs[1].shape),
        ],
        out_shape=outs,
        compiler_params=params(32),
        name="pack_weights",
    )(weights_in, weights_out)


def embed_body(base, noisy_ref, shared_ref, table_ref, out_ref):
    patch = jnp.concatenate(
        [
            shared_ref[c, base + 3 : base + 3 + PATCH, :]
            for c in range(shared_ref.shape[0])
        ],
        axis=1,
    ).astype(BF16)
    constant = row_of(shared_ref, base + 2) + table_ref[...]
    for s in range(noisy_ref.shape[0] // LEN):
        rows = pl.ds(s * LEN, LEN)
        out_ref[rows, :] = dot_nn(noisy_ref[rows, :], patch) + constant


def embed_tokens(base, noisy, shared, table):
    vmem = pl.BlockSpec(memory_space=pltpu.VMEM)
    return pl.pallas_call(
        functools.partial(embed_body, base),
        in_specs=[vmem] * 3,
        out_specs=vmem,
        out_shape=shaped((noisy.shape[0], table.shape[1]), F32),
        compiler_params=pltpu.CompilerParams(vmem_limit_bytes=32 * MIB),
        name="embed_tokens",
    )(noisy, shared, table)


def silu_slope(values):
    sigmoid_part = jax.nn.sigmoid(values)
    return sigmoid_part * (1.0 + values * (1.0 - sigmoid_part))


TIME_BLOCK = 128
CLASS_AT, FREQ_AT, LABEL_AT = 192, 208, 224


def condition_body(base, found, near_ref, shared_ref, *refs):
    cond_ref, act_ref, first_ref, first_act_ref, freq_ref, label_ref, class_ref, wave_ref = refs
    cols, _, narrow = shared_ref.shape
    rows = near_ref.shape[0] // cols
    steps = FREQ // TIME_BLOCK
    for r in range(rows):
        at = slice(r * 8, r * 8 + 8)
        for c in range(cols):
            block = near_ref[found[r * cols + c], CLASS_AT:, :].astype(F32)
            joined = jnp.concatenate([block[:8], block[8:16, : narrow - 128]], axis=1)
            class_ref[at, c * narrow : (c + 1) * narrow] = joined
            if c == 0:
                wave_ref[at, :TIME_BLOCK] = block[16:24]
                wave_ref[at, TIME_BLOCK:] = block[24:32]
                label_ref[at, :] = block[32:40] * 32.0 + block[40:48]
    freq = wave_ref[...].astype(BF16)
    freq_ref[...] = freq

    def product(left, first_row, count):
        parts = []
        for c in range(cols):
            total = None
            for k in range(count):
                block = near_ref[found[(first_row + k) * cols + c], :CLASS_AT, :]
                part = dot_nt(left[:, k * TIME_BLOCK : (k + 1) * TIME_BLOCK], block)
                total = part if total is None else total + part
            parts.append(total)
        return jnp.concatenate(parts, axis=1)

    first = product(freq, 0, steps) + row_of(shared_ref, base)
    first_ref[...] = first
    first_act = (first * jax.nn.sigmoid(first)).astype(BF16)
    first_act_ref[...] = first_act
    cond = product(first_act, steps, rows - steps) + row_of(shared_ref, base + 1)
    cond = cond + class_ref[...]
    cond_ref[...] = cond
    act_ref[...] = (cond * jax.nn.sigmoid(cond)).astype(BF16)


def condition_step(base, found, near, shared, samples, width):
    vmem = pl.BlockSpec(memory_space=pltpu.VMEM)
    outs = [
        shaped((samples, width), F32),
        shaped((samples, width), BF16),
        shaped((samples, width), F32),
        shaped((samples, width), BF16),
        shaped((samples, FREQ), BF16),
        shaped((samples, 128), F32),
    ]
    return pl.pallas_call(
        functools.partial(condition_body, base),
        in_specs=[SMEM, vmem, vmem],
        out_specs=[vmem] * len(outs),
        out_shape=outs,
        scratch_shapes=[pltpu.VMEM((samples, width), F32), pltpu.VMEM((samples, FREQ), F32)],
        compiler_params=pltpu.CompilerParams(vmem_limit_bytes=32 * MIB),
        name="condition_step",
    )(found, near, shared)


def condition_back_body(
    layers, blocks, found, spot, small_ref, part_ref, final_ref, square_ref, cond_ref, first_ref,
    input_ref, label_ref, pick_ref, near_ref, time_ref, embed_ref, bias_ref, own_ref, shared_ref,
    grad_ref,
):
    row, col = spot[0], spot[1]
    samples, width = cond_ref.shape
    narrow = pick_ref.shape[1]
    cols = width // narrow
    rows = near_ref.shape[0] // cols
    steps = FREQ // TIME_BLOCK
    start = 16 * layers + 2 * PATCH
    pick = pick_ref[...]
    pick_wide = pick.astype(F32)

    def own_cols(v):
        return jnp.dot(v, pick_wide, precision=HIGHEST, preferred_element_type=F32)

    def squares(v):
        return jnp.sum(v * v, keepdims=True)

    block_rows = part_ref.shape[2]
    for r in range(rows):
        part = part_ref[found[r * cols + col]]
        grad_ref[:, r * block_rows : (r + 1) * block_rows] = part
    grad_cond = (grad_ref[...] + final_ref[...]) * silu_slope(cond_ref[...])
    low = grad_cond.astype(BF16)
    parts = []
    for r in range(steps, rows):
        total = None
        for c in range(cols):
            block = near_ref[found[r * cols + c], :CLASS_AT, :]
            part = dot_nn(low[:, c * narrow : (c + 1) * narrow], block)
            total = part if total is None else total + part
        parts.append(total)
    grad_first = jnp.concatenate(parts, axis=1) * silu_slope(first_ref[...])
    is_first = (row < steps).astype(F32)
    outputs = grad_first.astype(BF16).astype(F32) * is_first + low.astype(F32) * (1.0 - is_first)
    outputs = dot_nn(outputs.astype(BF16), pick).astype(BF16)
    time_grad = dot_tn(outputs, input_ref[...])
    time_ref[...] = time_grad
    hot = lax.broadcasted_iota(jnp.int32, (samples, CLASSES), 1).astype(F32)
    hot = (hot == label_ref[:, 0:1]).astype(F32)
    class_grad = lax.dot_general(
        own_cols(grad_cond), hot, TN, precision=HIGHEST, preferred_element_type=F32
    )
    patch = own_cols(small_ref[start - PATCH : start, :])
    embed_ref[...] = jnp.concatenate([class_grad, patch.T], axis=1)
    own_ref[...] = squares(time_grad) + squares(class_grad) * (1.0 / rows)
    time_bias = jnp.concatenate(
        [jnp.sum(grad_first, axis=0, keepdims=True), jnp.sum(grad_cond, axis=0, keepdims=True)],
        axis=0,
    )
    total = square_ref[...] + squares(time_bias) + squares(small_ref[start - 2 * PATCH : start + 3, :])
    total = total + squares(small_ref[start + 3 : start + 4, :PATCH])
    own = own_cols(small_ref[: start + 16, :])
    lines = []
    for layer in range(layers):
        at = 16 * layer
        total = total + squares(small_ref[at : at + 6 + cols, :])
        total = total + squares(small_ref[at + 10 : at + 10 + cols, :narrow])
        total = total + squares(small_ref[at + 10 : at + 10 + cols, 2 * narrow : 3 * narrow])
        total = total + squares(small_ref[at + 14 : at + 16, :])
        attn = small_ref[pl.ds(at + 10 + col, 1), :]
        mlp = small_ref[pl.ds(at + 6 + col, 1), :]
        lines += [own[at : at + 6], attn[:, :narrow], attn[:, 2 * narrow : 3 * narrow]]
        lines += [mlp[:, k * narrow : (k + 1) * narrow] for k in range(blocks)]
        lines += [own[at + 14 : at + 16]]
    lines += [own_cols(time_bias), own[start : start + 1]]
    bias_ref[...] = jnp.concatenate(lines, axis=0)
    shared_ref[...] = total


def condition_back(
    layers, blocks, found, spot, small, part, final, squares, cond, first, inputs, labels, pick, near
):
    vmem = pl.BlockSpec(memory_space=pltpu.VMEM)
    narrow = pick.shape[1]
    outs = [
        shaped((narrow, TIME_BLOCK), F32),
        shaped((narrow, CLASSES + PATCH), F32),
        shaped((14 * layers + 3, narrow), F32),
        shaped((1, 1), F32),
        shaped((1, 1), F32),
    ]
    operands = [small, part, final, squares, cond, first, inputs, labels, pick, near]
    return pl.pallas_call(
        functools.partial(condition_back_body, layers, blocks),
        in_specs=[SMEM, SMEM] + [vmem] * len(operands),
        out_specs=[vmem] * len(outs),
        out_shape=outs,
        scratch_shapes=[pltpu.VMEM(cond.shape, F32)],
        compiler_params=pltpu.CompilerParams(vmem_limit_bytes=48 * MIB),
        name="condition_back",
    )(found, spot, *operands)


def modes_backward_body(
    layers, near_ref, at_ref, rows_ref, pick_ref, mode_ref, act_ref, final_ref,
    block_ref, part_ref, square_ref, grad_ref, cond_ref, shared_ref,
):
    near = near_ref[...]
    at = at_ref[...]
    samples = at.shape[0]
    where = lax.broadcasted_iota(jnp.int32, (samples, near.shape[0]), 1)
    cols, narrow = mode_ref.shape[0], mode_ref.shape[4]
    spreads = []
    for layer in range(layers):
        for k in range(6):
            offset = 12 * layer + 6 * (k // 3) + k % 3
            spreads.append((where == at[:, 0:1] + at[:, 1:2] * 3 + offset).astype(BF16))
    for k in range(2):
        spreads.append((where == at[:, 0:1] + at[:, 1:2] * 2 + 12 * layers + k).astype(BF16))
    rows = dot_nn(jnp.concatenate(spreads, axis=0), near).astype(BF16)
    mine = dot_nn(rows[: 6 * layers * samples], pick_ref[...]).astype(BF16)

    total = None
    squares = jnp.zeros((1, 1), F32)
    for layer in range(layers):
        for k in range(6):
            at_row = (6 * layer + k) * samples
            low = rows[at_row : at_row + samples]
            grad = dot_tn(rows_ref[...], mine[at_row : at_row + samples])
            block_ref[layer, k] = grad
            squares = squares + jnp.sum(grad * grad, keepdims=True)
            full = jnp.concatenate([mode_ref[c, layer, k] for c in range(cols)], axis=1)
            part = dot_nt(low, full)
            total = part if total is None else total + part
    part_ref[...] = total
    square_ref[...] = squares
    width = act_ref.shape[1]
    at_row = 6 * layers * samples
    shift, scale = rows[at_row : at_row + samples], rows[at_row + samples :]
    squares = jnp.zeros((1, 1), F32)
    for k, low in enumerate((shift, scale)):
        grad = dot_tn(low, act_ref[...])
        grad_ref[k * width : (k + 1) * width, :] = grad
        squares = squares + jnp.sum(grad * grad, keepdims=True)
    cond_ref[...] = dot_nn(shift, final_ref[:width, :]) + dot_nn(
        scale, final_ref[width : 2 * width, :]
    )
    shared_ref[...] = squares


def modes_backward(near, at, cond_rows, pick, mode_full, act, final):
    vmem = pl.BlockSpec(memory_space=pltpu.VMEM)
    samples, block = cond_rows.shape
    width = near.shape[2]
    layers, narrow = mode_full.shape[1], mode_full.shape[4]
    outs = [
        shaped((layers, 6, block, narrow), F32),
        shaped((samples, block), F32),
        shaped((1, 1), F32),
        shaped((2 * width, width), F32),
        shaped((samples, width), F32),
        shaped((1, 1), F32),
    ]
    operands = [near.reshape(-1, width), at, cond_rows, pick, mode_full, act, final]
    return pl.pallas_call(
        functools.partial(modes_backward_body, layers),
        in_specs=[vmem] * len(operands),
        out_specs=[vmem] * len(outs),
        out_shape=outs,
        compiler_params=pltpu.CompilerParams(vmem_limit_bytes=56 * MIB),
        name="modes_backward",
    )(*operands)


def modes_backward_plain(near, cond_rows, mode_full, act, final, col):
    layers, narrow, width = mode_full.shape[1], mode_full.shape[4], near.shape[2]
    devices = near.shape[0]
    samples = act.shape[0] // devices
    low = near[:, : 12 * layers].reshape(devices, layers, 2, samples, 3, width)
    low = jnp.transpose(low, (1, 2, 4, 0, 3, 5)).reshape(layers, 6, devices * samples, width)
    mine = lax.dynamic_slice_in_dim(low, col * narrow, narrow, 3)
    block = jnp.einsum("sd,lkse->lkde", cond_rows, mine, preferred_element_type=F32)
    full = jnp.transpose(mode_full, (1, 2, 3, 0, 4)).reshape(layers, 6, -1, width)
    part = jnp.einsum("lkse,lkde->sd", low, full, preferred_element_type=F32)
    ends = near[:, 12 * layers : 12 * layers + 2 * samples].reshape(-1, 2, width)
    grad = jnp.einsum("ske,sd->ked", ends, act, preferred_element_type=F32)
    cond = jnp.einsum(
        "ske,ked->sd", ends, final[: 2 * width].reshape(2, width, width), preferred_element_type=F32
    )
    grad = grad.reshape(2 * width, width)
    return block, part, squared(block)[None, None], grad, cond, squared(grad)[None, None]


def collect_body(layers, *refs):
    out_ref = refs[-1]
    at = 0
    out_ref[...] = jnp.zeros_like(out_ref)
    take = list(refs[:-1])
    for _ in range(layers):
        dmod_a, dmod_b, dbias_a, dbias_b, dtail_a, dtail_b = [take.pop(0) for _ in range(6)]
        for k, source in enumerate((dmod_a, dmod_b)):
            total = source[0]
            for s in range(1, source.shape[0]):
                total = total + source[s]
            out_ref[at + 3 * k : at + 3 * k + 3, :] = total
        for c in range(dbias_b.shape[0]):
            out_ref[at + 6 + c : at + 7 + c, : dbias_b.shape[2]] = dbias_b[c]
            out_ref[at + 10 + c : at + 11 + c, : dbias_a.shape[2]] = dbias_a[c]
        out_ref[at + 14 : at + 15, :] = dtail_a[...]
        out_ref[at + 15 : at + 16, :] = dtail_b[...]
        at += 16
    head, head_bias, loss, mask, dfinal, dx, noisy = take
    out_ref[at : at + PATCH, :] = head[...]
    out_ref[at + PATCH : at + 2 * PATCH, :] = dot_tn(noisy[...], dx[...].astype(BF16))
    at += 2 * PATCH
    out_ref[at : at + 1, :] = jnp.sum(dx[...], axis=0, keepdims=True)
    total = dfinal[0]
    for s in range(1, dfinal.shape[0]):
        total = total + dfinal[s]
    out_ref[at + 1 : at + 3, :] = total
    out_ref[at + 3 : at + 4, 0:PATCH] = head_bias[...]
    out_ref[at + 4 : at + 5, 0:PATCH] = loss[...]
    out_ref[at + 5 : at + 6, 0:1] = jnp.sum(mask[...], keepdims=True)


def collect(layers, parts, height, width):
    vmem = pl.BlockSpec(memory_space=pltpu.VMEM)
    return pl.pallas_call(
        functools.partial(collect_body, layers),
        in_specs=[vmem] * len(parts),
        out_specs=vmem,
        out_shape=shaped((height, width), F32),
        compiler_params=pltpu.CompilerParams(vmem_limit_bytes=48 * MIB),
        name="collect_small",
    )(*parts)


def adam(weight, gradient, moment, second, clip, rate):
    gradient = gradient * clip
    moment = BETA_ONE * moment + (1.0 - BETA_ONE) * gradient
    second = BETA_TWO * second + (1.0 - BETA_TWO) * gradient * gradient
    update = (
        moment / (1.0 - BETA_ONE**STEP) / (jnp.sqrt(second / (1.0 - BETA_TWO**STEP)) + ADAM_EPS)
    )
    return weight - rate * (update + DECAY * weight), moment, second


def adam_blocks_body(layers, halves, clip_ref, spot, *refs):
    clip = clip_ref[0]
    per = 5 if halves else 3
    sums = [refs[per * layer : per * layer + per] for layer in range(layers)]
    refs = refs[per * layers :]
    wi, mi, vi, wo, mo, vo = refs[:6]
    out_i, out_o = refs[6:9], refs[9:12]
    total_ref = refs[12]
    narrow = wi.shape[3]

    def fill(layer):
        group = sums[layer]
        for k in range(3):
            if not halves:
                total_ref[k] = group[1][0] if k == 0 else group[2][k - 1]
                continue
            half = total_ref.shape[1] // 2
            mine, other = group[1:3] if k == 0 else group[3:5]
            at = 0 if k == 0 else k - 1
            core = spot[1] % 2
            total_ref[k, pl.ds(pl.multiple_of(core * half, 8), half), :] = mine[0, at]
            total_ref[k, pl.ds(pl.multiple_of((1 - core) * half, 8), half), :] = other[at]

    def update(layer, mode_ref):
        for k in range(wi.shape[1]):
            if k < 6:
                grad = mode_ref[layer, k]
            elif k < 9:
                grad = total_ref[0, :, (k - 6) * narrow : (k - 5) * narrow]
            else:
                grad = total_ref[1, :, (k - 9) * narrow : (k - 8) * narrow]
            new = adam(wi[0, k], grad, mi[0, k], vi[0, k], clip, RATE)
            for ref, value in zip(out_i, new):
                ref[0, k] = value
        for k in range(wo.shape[1]):
            if k == 0:
                grad = total_ref[0, :, 3 * narrow :]
            else:
                grad = total_ref[2, :, (k - 1) * narrow : k * narrow]
            new = adam(wo[0, k], grad.T, mo[0, k], vo[0, k], clip, RATE)
            for ref, value in zip(out_o, new):
                ref[0, k] = value

    for layer in range(layers):

        @pl.when(pl.program_id(0) == layer)
        def _(layer=layer):
            fill(layer)
            update(layer, sums[layer][0])


def adam_blocks(clip, spot, sums, ins, outs):
    arrays = list(ins) + list(outs)
    grads = [v for group in sums for v in group]
    halves = len(sums[0]) == 5
    results = [shaped(v.shape, F32) for v in arrays]
    block, narrow = ins[0].shape[2:]
    return pl.pallas_call(
        functools.partial(adam_blocks_body, len(sums), halves),
        grid=(ins[0].shape[0],),
        in_specs=[SMEM, SMEM]
        + [whole_block(v.shape) for v in grads]
        + [block_of(v.shape) for v in arrays],
        out_specs=[block_of(v.shape) for v in results],
        out_shape=results,
        scratch_shapes=[pltpu.VMEM((3, block, 4 * narrow), F32)],
        compiler_params=params(58),
        name="adam_blocks",
    )(clip, spot, *grads, *arrays)


def adam_final_body(clip_ref, grad_ref, head_ref, w, m, v, *outs):
    clip = clip_ref[0]
    step = pl.program_id(0)
    last = pl.num_programs(0) - 1

    @pl.when(step < last)
    def _():
        new = adam(w[...], grad_ref[...], m[...], v[...], clip, RATE)
        for ref, value in zip(outs, new):
            ref[...] = value

    @pl.when(step == last)
    def _():
        rows = slice(0, PATCH)
        new = adam(w[rows, :], head_ref[...], m[rows, :], v[rows, :], clip, RATE)
        for ref, value in zip(outs, new):
            ref[rows, :] = value


def adam_final(clip, grad, head, w, m, v):
    width = w.shape[1]
    height = 256
    steps = grad.shape[0] // height
    part = pl.BlockSpec((height, width), lambda c: (c, 0))
    grad_part = pl.BlockSpec((height, width), lambda c: (jnp.minimum(c, steps - 1), 0))
    return pl.pallas_call(
        adam_final_body,
        grid=(steps + 1,),
        in_specs=[SMEM, grad_part, whole_block(head.shape)] + [part] * 3,
        out_specs=[part] * 3,
        out_shape=[shaped(w.shape, F32)] * 3,
        compiler_params=params(58),
        name="adam_final",
    )(clip, grad, head, w, m, v)


def adam_rest_body(rates, clip_ref, *refs):
    clip = clip_ref[0]
    count = len(rates)
    ins, outs = refs[: 4 * count], refs[4 * count :]
    for k, rate in enumerate(rates):
        w, g, m, v = [r[...] for r in ins[4 * k : 4 * k + 4]]
        for ref, value in zip(outs[3 * k : 3 * k + 3], adam(w, g, m, v, clip, rate)):
            ref[...] = value


def adam_rest(clip, groups):
    vmem = pl.BlockSpec(memory_space=pltpu.VMEM)
    arrays, results, rates = [], [], []
    for w, g, m, v, rate in groups:
        arrays += [w, g, m, v]
        results += [shaped(w.shape, F32)] * 3
        rates.append(rate)
    return pl.pallas_call(
        functools.partial(adam_rest_body, tuple(rates)),
        in_specs=[SMEM] + [vmem] * len(arrays),
        out_specs=[vmem] * len(results),
        out_shape=results,
        compiler_params=pltpu.CompilerParams(vmem_limit_bytes=58 * MIB),
        name="adam_rest",
    )(clip, *arrays)


def squared(values):
    return jnp.sum(values * values)


def position_table(width):
    half = width // 2
    rate = np.exp(-math.log(10000.0) * (np.arange(width) % half) / half)
    angle = np.arange(LEN)[:, None] * rate[None, :]
    table = np.where(np.arange(width)[None, :] < half, np.sin(angle), np.cos(angle))
    return table.astype(np.float32)


def on_device(
    latents,
    noise,
    timesteps,
    labels,
    loss_mask,
    weights_in,
    weights_out,
    time_mlp,
    embed_table,
    final_layer,
    bias_table,
    final_bias,
    momentum_in,
    momentum_out,
    momentum_time,
    momentum_embed,
    momentum_final,
    momentum_bias,
    momentum_final_bias,
    variance_in,
    variance_out,
    variance_time,
    variance_embed,
    variance_final,
    variance_bias,
    variance_final_bias,
):
    layers, block, _, narrow = weights_in.shape
    place = Place(block)
    rows, cols = place.rows, place.cols
    width = final_layer.shape[0]
    row_samples = timesteps.shape[0]
    samples = row_samples // cols
    every_sample = row_samples * rows
    tokens = samples * LEN
    base = layers * 14
    hidden_blocks = weights_out.shape[1] - 1

    def my_cols(v, axis):
        return lax.dynamic_slice_in_dim(v, place.col * narrow, narrow, axis)

    in_view = [jnp.transpose(v, (0, 2, 1, 3)) for v in (weights_in, momentum_in, variance_in)]
    packed, mode_low = pack_weights(in_view[0], weights_out)

    embed_low = embed_table.astype(BF16)
    one_hot_row = (labels[:, None] == jnp.arange(CLASSES, dtype=jnp.int32)[None, :]).astype(BF16)
    class_rows = jnp.dot(
        one_hot_row, embed_low[:CLASSES], preferred_element_type=F32
    ).astype(BF16)
    half_freq = FREQ // 2
    freq_rate = jnp.asarray(
        np.exp(-math.log(10000.0) * np.arange(half_freq) / half_freq).astype(np.float32)
    )
    angle_grid = timesteps.astype(F32)[:, None] * freq_rate[None, :]
    freq_row = jnp.concatenate([jnp.cos(angle_grid), jnp.sin(angle_grid)], axis=1).astype(BF16)
    time_rows = time_mlp.shape[0]
    mine = jnp.concatenate([bias_table, embed_low[CLASSES:].astype(F32)], axis=0)
    final_view = [v.T for v in (final_layer, momentum_final, variance_final)]
    found = place.found_at()
    sample = jnp.arange(every_sample, dtype=jnp.int32)
    mode_height = -(-(12 * layers + 4) // 16) * 16
    at = jnp.stack([found[sample // samples] * mode_height, sample % samples], axis=1)
    feature = jnp.arange(width, dtype=jnp.int32)[:, None]
    picked = jnp.arange(narrow, dtype=jnp.int32)[None, :] + place.col * narrow
    pick = (feature == picked).astype(BF16)
    spot = jnp.stack([place.row, place.col]).astype(jnp.int32)

    def partial_modes(cond_act):
        cond_rows = lax.dynamic_slice_in_dim(cond_act, place.row * block, block, 1)
        partial = jnp.einsum("sd,lkde->slke", cond_rows, mode_low, preferred_element_type=F32)
        return cond_rows, partial.reshape(every_sample, layers * 6, narrow)

    def own_modes(total, shared, cond_act, final_low):
        bias_full = jnp.swapaxes(shared, 0, 1).reshape(-1, width)
        modes = total.reshape(samples, layers, 6, width) + jnp.stack(
            [bias_full[14 * layer : 14 * layer + 6] for layer in range(layers)]
        )
        own_start = place.row * row_samples + place.col * samples
        cond_own = lax.dynamic_slice_in_dim(cond_act, own_start, samples, 0)
        final_mod = (
            jnp.einsum("sd,ed->se", cond_own, final_low[: 2 * width], preferred_element_type=F32)
            + final_bias[: 2 * width]
        ).reshape(samples, 2, width)
        mods_a = [modes[:, layer, 0:3] for layer in range(layers)]
        mods_b = [modes[:, layer, 3:6] for layer in range(layers)]
        return mods_a, mods_b, final_mod

    own_tokens = place.col * tokens
    latents = lax.dynamic_slice_in_dim(latents, own_tokens, tokens, 0)
    noise = lax.dynamic_slice_in_dim(noise, own_tokens, tokens, 0)
    mask = lax.dynamic_slice_in_dim(loss_mask, own_tokens, tokens, 0).astype(F32)
    steps_own = lax.dynamic_slice_in_dim(timesteps, place.col * samples, samples, 0).astype(F32)
    alpha_bar = jnp.cos((steps_own / STEPS_T + 0.008) / 1.008 * (math.pi / 2)) ** 2
    keep_part = jnp.repeat(jnp.sqrt(alpha_bar), LEN)[:, None]
    noise_part = jnp.repeat(jnp.sqrt(1.0 - alpha_bar), LEN)[:, None]
    noisy = (keep_part * latents + noise_part * noise).astype(BF16)
    position = jnp.asarray(position_table(width))

    def attn_step(layer):
        def work(buffers, x, mods, shared):
            return attention_forward(place, 14 * layer, buffers, x, mods, shared)

        return work

    def mlp_step(layer):
        def work(buffers, x, mods, shared):
            return mlp_forward(place, 14 * layer, buffers, x, mods, shared)

        return work

    def attn_back(buffers, *operands):
        return attention_backward(place, buffers, *operands)

    def mlp_back(buffers, *operands):
        return mlp_backward(place, buffers, *operands)

    def last_step(x, final_mod, final_low):
        return final_step(
            x, final_mod, final_low[2 * width :], final_bias[2 * width :][None], noise, mask[:, None]
        )

    def mode_parts(back_a, back_b, grad_final_mod):
        parts = []
        for layer in range(layers):
            parts += [back_a[layer][1], back_b[layer][1]]
        parts = [v.reshape(-1, width) for v in parts + [grad_final_mod]]
        spare = mode_height - sum(v.shape[0] for v in parts)
        return jnp.concatenate(parts + [jnp.zeros((spare, width), F32)], axis=0).astype(BF16)

    start = 16 * layers + 2 * PATCH
    height = -(-(start + 16) // 32) * 32

    def collected(back_a, back_b, last):
        small = []
        for layer in range(layers):
            _, dmod_a, dbias_a, dtail_a = back_a[layer]
            _, dmod_b, dbias_b, dtail_b = back_b[layer]
            small += [dmod_a, dmod_b, dbias_a, dbias_b, dtail_a, dtail_b]
        _, loss_parts, grad_head, grad_head_bias, grad_final_mod = last
        small += [grad_head, grad_head_bias, loss_parts, mask[:, None], grad_final_mod]
        small += [back_a[0][0], noisy]
        return collect(layers, small, height, width)

    buffers = [None] * (2 * layers)
    fore_a, fore_b = [None] * layers, [None] * layers
    entry = [None] * layers
    back_a, back_b = [None] * layers, [None] * layers
    summed = [None] * (2 * layers)
    if place.direct and layers == 2:
        stages = Stages()
        halves = packed.reshape(3 * layers, 2, place.half, packed.shape[2])
        kept = lax.dynamic_index_in_dim(halves, place.core, 1, False)
        sent = lax.dynamic_index_in_dim(halves, 1 - place.core, 1, False)
        (got,), _ = stages.run([(swap_core, sent)])
        a0, b0, a1, b1 = [
            Spread(kept[k : k + n], got[k : k + n]) for k, n in ((0, 1), (1, 2), (3, 1), (4, 2))
        ]
        wide = jnp.broadcast_to
        own_block = jnp.concatenate(
            [
                time_mlp.astype(BF16).T,
                class_rows[:, :128],
                jnp.pad(class_rows[:, 128:], ((0, 0), (0, 256 - narrow))),
                freq_row[:, :128],
                freq_row[:, 128:],
                wide((labels // 32).astype(BF16)[:, None], (row_samples, 128)),
                wide((labels % 32).astype(BF16)[:, None], (row_samples, 128)),
            ],
            axis=0,
        )
        got, (near, shared, final_low) = stages.run(
            a0.at_once(),
            [
                (near_rows, own_block),
                (functools.partial(gather_cols, place), mine),
                (lambda v: v.astype(BF16), final_view[0]),
            ],
        )
        a0.along_at_once(got)
        got, (near, residual) = stages.run(
            a0.first() + b0.far(),
            [
                (near_x, near),
                (functools.partial(embed_tokens, base), noisy, shared, position),
            ],
        )

        def condition_work(near, shared, found):
            near = near_core(near)
            got = condition_step(base, found, near, shared, every_sample, width)
            return near, got, partial_modes(got[1])

        got, ((near, conditions, (cond_rows, partial)),) = stages.run(
            a0.second(got[0]) + b0.near(got[1]),
            [(condition_work, near, shared, found)],
            a0.core(),
        )
        b0.along(got[1])
        condition, cond_act, first_time, first_act, freq_low, all_labels = conditions
        core = got[2]
        got, (total,) = stages.run(
            b0.first() + a1.far() + a0.late_core(got[0]),
            [(functools.partial(scatter_y, place), partial)],
        )
        buffers[0] = a0.buffers(core, got[2])

        two = a1.near(got[1])[0][1]

        def scatter_work(total, two):
            blocks = swap_near(two)
            total, blocks = lax.optimization_barrier((scatter_z(place, total), blocks))
            return blocks, scatter_x(place, total, samples)

        got, ((blocks, total),) = stages.run(
            b0.second(got[0]) + b0.core(), [(scatter_work, total, two)]
        )
        a1.along(blocks)
        core = got[1]

        def modes_work(total, shared, cond_act):
            return own_modes(scatter_core(place, total), shared, cond_act, final_low)

        got, ((mods_a, mods_b, final_mod),) = stages.run(
            b1.far() + b0.late_core(got[0]),
            [(modes_work, total, shared, cond_act)],
            a1.first(),
        )
        buffers[1] = b0.buffers(core, got[1])
        got = [got[2], got[0]]
        got, (fore_a[0],) = stages.run(
            a1.second(got[0]) + b1.near(got[1]) + a1.core(),
            [(attn_step(0), buffers[0], residual, mods_a[0], shared)],
        )
        b1.along(got[1])
        core = got[2]
        got, (fore_b[0],) = stages.run(
            b1.first() + a1.late_core(got[0]),
            [(mlp_step(0), buffers[1], fore_a[0][0], mods_b[0], shared)],
        )
        buffers[2] = a1.buffers(core, got[1])
        got, (fore_a[1],) = stages.run(
            b1.second(got[0]) + b1.core(),
            [(attn_step(1), buffers[2], fore_b[0][0], mods_a[1], shared)],
        )
        core = got[1]
        got, _ = stages.run(b1.late_core(got[0]))
        buffers[3] = b1.buffers(core, got[0])
        got, (fore_b[1],) = stages.run(
            [(swap_x, mode_low)], [(mlp_step(1), buffers[3], fore_a[1][0], mods_b[1], shared)]
        )
        mode_half = pair(place.x, mode_low, got[0])
        entry = [residual, fore_b[0][0]]
        last = last_step(fore_b[1][0], final_mod, final_low)

        def back_b_work(layer, grad):
            out, h, u, m = fore_b[layer]
            return (mlp_back, buffers[2 * layer + 1], grad, fore_a[layer][0], mods_b[layer], m, h, u)

        def back_a_work(layer, grad):
            out, h, qkv, p, o, a = fore_a[layer]
            return (
                attn_back, buffers[2 * layer], grad, entry[layer], mods_a[layer], a, h, qkv, p, o,
            )

        got, ((back_b[1], grads),) = stages.run(
            [(swap_core, mode_half)], [back_b_work(1, last[0])]
        )
        mode_full = jnp.swapaxes(pair(place.core, mode_half, got[0]), 0, 1)
        mode_full = mode_full.reshape((4,) + mode_low.shape)
        gb1 = Gathered(grads)
        got, ((back_a[1], grads),) = stages.run(gb1.core, [back_a_work(1, back_b[1][0])])
        ga1 = Gathered(grads)
        got, ((back_b[0], grads),) = stages.run(
            gb1.first(got[0]) + ga1.core, [back_b_work(0, back_a[1][0])]
        )
        core_a1 = got[1]
        gb0 = Gathered(grads)
        got, ((back_a[0], grads),) = stages.run(
            gb1.second(got[0]) + ga1.first(core_a1) + gb0.core, [back_a_work(0, back_b[0][0])]
        )
        zn_b1 = gb1.near(got[0])
        ga0 = Gathered(grads)

        def sum_work(back_a, back_b, last):
            return sum_along_z(place, collected(back_a, back_b, last))

        moded = mode_parts(back_a, back_b, last[4])
        t2_a1 = ga1.second(got[1])
        got, (near_modes, small) = stages.run(
            gb0.first(got[2]) + ga0.core,
            [(near_z, moded), (sum_work, back_a, back_b, last)],
            zn_b1,
        )
        got = [got[0], got[2], got[1]]
        t2_b0 = gb0.second(got[0])
        got, (near_modes, small) = stages.run(
            ga0.first(got[2]) + t2_a1 + gb1.far(got[1]),
            [(near_y, near_modes), (sum_with(swap_core), small)],
        )
        total_b1 = gb1.total(got[2])
        t2_a0 = ga0.second(got[0])
        got, (near_modes, small) = stages.run(
            t2_b0 + ga1.near(got[1]), [(near_x, near_modes), (sum_with(swap_x), small)]
        )
        got, (near_modes, small) = stages.run(
            gb0.near(got[0]) + ga1.far(got[1]),
            [(near_core, near_modes), (sum_with(swap_y), small)],
            t2_a0,
        )
        got = [got[2], got[1], got[0]]
        total_a1 = ga1.total(got[1])

        def modes_back_work(near):
            return modes_backward(near, at, cond_rows, pick, mode_full, cond_act, final_low)

        got, (moded, small) = stages.run(
            gb0.far(got[2]) + ga0.near(got[0]),
            [(modes_back_work, near_modes), (functools.partial(sum_spread, place), small)],
        )
        total_b0 = gb0.total(got[0])
        time_inputs = lax.dynamic_slice_in_dim(
            jnp.concatenate([freq_low, first_act], axis=1), place.row * time_rows, time_rows, 1
        )
        got, (part,) = stages.run(ga0.far(got[1]), [(near_z_at_once, moded[1])])
        total_a0 = ga0.total(got[0])
        part = near_y(part)
        ends = condition_back(
            layers, hidden_blocks, found, spot, small, part, moded[4], moded[5], condition,
            first_time, time_inputs, all_labels, pick, near,
        )
        late = swap_core(
            jnp.concatenate([total_b1[1], total_b0[1], total_a1[1], total_a0[1]])
        )
        summed = [total_a0, total_b0, total_a1, total_b1]
        sums = [
            (moded[0], total_a0, late[5:6], total_b0, late[2:4]),
            (moded[0], total_a1, late[4:5], total_b1, late[0:2]),
        ]
        time_grad, embed_grad, bias_grad, own_part, shared_part = ends
        own_squares = own_part[0, 0] + moded[2][0, 0]
        shared_squares = shared_part[0, 0]
        final_grad = moded[3]
    else:
        final_low = final_view[0].astype(BF16)
        shared = gather_cols(place, mine)
        time_full = lax.all_gather(time_mlp.astype(BF16), "row", axis=0, tiled=True)
        time_full = lax.all_gather(time_full, "col", axis=1, tiled=True)
        class_full = lax.all_gather(class_rows, "col", axis=1, tiled=True)
        class_full = lax.all_gather(class_full, "row", axis=0, tiled=True).astype(F32)
        freq_low = lax.all_gather(freq_row, "row", axis=0, tiled=True)
        all_labels = lax.all_gather(labels, "row", axis=0, tiled=True)
        bias_full = jnp.swapaxes(shared, 0, 1).reshape(-1, width)
        first_time = (
            jnp.dot(freq_low, time_full[:FREQ], preferred_element_type=F32) + bias_full[base]
        )
        first_act = jax.nn.silu(first_time).astype(BF16)
        condition = (
            jnp.dot(first_act, time_full[FREQ:], preferred_element_type=F32)
            + bias_full[base + 1]
            + class_full
        )
        cond_act = jax.nn.silu(condition).astype(BF16)
        cond_rows, partial = partial_modes(cond_act)
        mods_a, mods_b, final_mod = own_modes(
            scatter_plain(place, partial, samples), shared, cond_act, final_low
        )
        grad = embed_tokens(base, noisy, shared, position)
        for layer in range(layers):
            buffers[2 * layer] = [plain_gather(packed[3 * layer : 3 * layer + 1])]
            buffers[2 * layer + 1] = [plain_gather(packed[3 * layer + 1 : 3 * layer + 3])]
            entry[layer] = grad
            fore_a[layer] = attn_step(layer)(buffers[2 * layer], grad, mods_a[layer], shared)
            grad = fore_a[layer][0]
            fore_b[layer] = mlp_step(layer)(buffers[2 * layer + 1], grad, mods_b[layer], shared)
            grad = fore_b[layer][0]
        last = last_step(grad, final_mod, final_low)
        grad = last[0]
        for layer in reversed(range(layers)):
            out, h, u, m = fore_b[layer]
            back_b[layer], grads = mlp_back(
                buffers[2 * layer + 1], grad, fore_a[layer][0], mods_b[layer], m, h, u
            )
            summed[2 * layer + 1] = plain_scatter(grads[0])
            grad = back_b[layer][0]
            out, h, qkv, p, o, a = fore_a[layer]
            back_a[layer], grads = attn_back(
                buffers[2 * layer], grad, entry[layer], mods_a[layer], a, h, qkv, p, o
            )
            summed[2 * layer] = plain_scatter(grads[0])
            grad = back_a[layer][0]
        mode_full = lax.all_gather(mode_low, "col")
        near = gather_near(place, mode_parts(back_a, back_b, last[4]))
        moded = modes_backward_plain(
            near, cond_rows, mode_full, cond_act, final_low, place.col
        )
        mode_blocks, part, square, final_grad, cond_final, final_squares = moded
        own_squares = square[0, 0]
        small = lax.psum(collected(back_a, back_b, last), ("row", "col"))
        grad_cond = lax.all_gather(part, "row", axis=1, tiled=True) + cond_final
        grad_condition = grad_cond * silu_slope(condition)
        one_hot = (all_labels[:, None] == jnp.arange(CLASSES, dtype=jnp.int32)[None, :]).astype(F32)
        grad_classes = jnp.einsum(
            "sd,sc->dc", my_cols(grad_condition, 1), one_hot, precision=HIGHEST
        )
        condition_low = grad_condition.astype(BF16)
        grad_first = jnp.einsum(
            "se,de->sd", condition_low, time_full[FREQ:], preferred_element_type=F32
        ) * silu_slope(first_time)
        time_inputs = lax.dynamic_slice_in_dim(
            jnp.concatenate([freq_low, first_act], axis=1), place.row * time_rows, time_rows, 1
        )
        time_outputs = jnp.where(
            (place.row + 1) * time_rows <= FREQ, grad_first.astype(BF16), condition_low
        )
        time_grad = jnp.einsum(
            "sd,se->ed", time_inputs, my_cols(time_outputs, 1), preferred_element_type=F32
        )
        own_rows, shared_squares = [], jnp.zeros((), F32)
        for layer in range(layers):
            rows_at = small[16 * layer : 16 * layer + 16]
            own = my_cols(rows_at, 1)
            mlp_rows = lax.dynamic_index_in_dim(rows_at[6:10], place.col, 0, False)
            attn_rows = lax.dynamic_index_in_dim(rows_at[10:14], place.col, 0, False)
            attn_rows = attn_rows[: 3 * narrow].reshape(3, narrow)
            own_rows += [own[:6], attn_rows[0:1], attn_rows[2:3]]
            own_rows += [mlp_rows.reshape(hidden_blocks, narrow), own[14:16]]
            counted = rows_at[10:14, : 3 * narrow].reshape(4, 3, narrow)[:, 0::2]
            shared_squares = (
                shared_squares + squared(rows_at[:10]) + squared(counted) + squared(rows_at[14:])
            )
        time_bias = jnp.stack([jnp.sum(grad_first, axis=0), jnp.sum(grad_condition, axis=0)])
        own_rows += [my_cols(time_bias, 1), my_cols(small[start : start + 1], 1)]
        bias_grad = jnp.concatenate(own_rows, axis=0)
        shared_squares = (
            shared_squares
            + squared(time_bias)
            + squared(small[start - 2 * PATCH : start + 3])
            + squared(small[start + 3, :PATCH])
            + final_squares[0, 0]
        )
        own_squares = own_squares + squared(time_grad) + squared(grad_classes) / rows
        sums = [(mode_blocks, summed[2 * k], summed[2 * k + 1]) for k in range(layers)]
        patch_grad = my_cols(small[start - PATCH : start], 1)
        embed_grad = jnp.concatenate([grad_classes, patch_grad.T], axis=1)

    head_grad = small[start - 2 * PATCH : start - PATCH]
    final_bias_grad = jnp.concatenate(
        [small[start + 1], small[start + 2], small[start + 3, :PATCH]]
    )
    loss_total = jnp.sum(small[start + 4, :PATCH])
    count_total = small[start + 5, 0]
    for value in summed:
        own_squares = own_squares + squared(value)
    grad_norm = jnp.sqrt(sum_scalar(place, own_squares) + shared_squares)
    clip_factor = jnp.minimum(1.0, CLIP_NORM / (grad_norm + 1e-06))
    clip = clip_factor[None]

    results = [loss_total, count_total, grad_norm]
    new_blocks = adam_blocks(clip, spot, sums, in_view, [weights_out, momentum_out, variance_out])
    results += [jnp.transpose(v, (0, 2, 1, 3)) for v in new_blocks[:3]] + list(new_blocks[3:])
    rest = adam_rest(
        clip,
        [
            (time_mlp.T, time_grad, momentum_time.T, variance_time.T, RATE),
            (embed_table.T, embed_grad, momentum_embed.T, variance_embed.T, RATE),
            (bias_table, bias_grad, momentum_bias, variance_bias, RATE_BIAS),
        ],
    )
    results += [v.T for v in rest[:6]]
    results += [v.T for v in adam_final(clip, final_grad, head_grad, *final_view)]
    results += list(rest[6:9])
    results += adam(
        final_bias, final_bias_grad, momentum_final_bias, variance_final_bias, clip_factor,
        RATE_BIAS,
    )
    return tuple(results)


def solution(mesh):
    tokens, latents = P("row", None), P("row")
    weights = (
        P(None, "row", None, "col"),
        P(None, None, "col", "row"),
        P("row", "col"),
        P(None, "col"),
        P(),
        P(None, "col"),
        P(),
    )
    updated = []
    for spec in weights:
        updated += [spec] * 3
    return jax.shard_map(
        on_device,
        mesh=mesh,
        in_specs=(tokens, tokens, latents, latents, latents) + weights * 3,
        out_specs=(P(), P(), P()) + tuple(updated),
        check_vma=False,
    )
```

```python
import functools
import math

import jax
import jax.numpy as jnp
import numpy as np
from jax import lax
from jax.experimental import pallas as pl
from jax.experimental.pallas import tpu as pltpu
from jax.sharding import PartitionSpec as P

HEAD_DIM = 64
CLASSES = 1000
FREQ = 256
PATCH = 16
LEN = 256
STEPS_T = 1000
STEP = 10

HIGHEST = lax.Precision.HIGHEST
EPS_NORM = 1e-06
CLIP_NORM = 1.0
RATE = 0.05
RATE_BIAS = 0.25
BETA_ONE = 0.9
BETA_TWO = 0.999
DECAY = 0.01
ADAM_EPS = 1e-08

F32 = jnp.float32
BF16 = jnp.bfloat16
MIB = 1024 * 1024
ANY = pl.BlockSpec(memory_space=pl.ANY)
SMEM = pl.BlockSpec(memory_space=pltpu.SMEM)
NT = (((1,), (1,)), ((), ()))
TN = (((0,), (0,)), ((), ()))


def dot_nt(a, b):
    return lax.dot_general(a, b, NT, preferred_element_type=F32)


def dot_tn(a, b):
    return lax.dot_general(a, b, TN, preferred_element_type=F32)


def dot_nn(a, b):
    return jnp.dot(a, b, preferred_element_type=F32)


def along(k):
    return k % 2 * 2 + k // 2


class Place:
    def __init__(self, row_block):
        self.rows = lax.axis_size("row")
        self.cols = lax.axis_size("col")
        self.row = lax.axis_index("row")
        self.col = lax.axis_index("col")
        self.direct = self.rows == 8 and self.cols == 4 and row_block % 32 == 0
        self.z = self.row // 2
        self.y = self.row % 2
        self.x = self.col // 2
        self.core = self.col % 2
        self.half = row_block // 2
        self.table = self.route_table() if self.direct else jnp.zeros((8,), jnp.int32)

    def route_table(self):
        z, y, x, core = self.z, self.y, self.x, self.core
        e = jnp.arange(64, dtype=jnp.int32)
        owner = core ^ (e // 32)
        later, first, kc, kz = e // 16 % 2, e // 8 % 2, e // 4 % 2, e % 4
        kx = jnp.where(owner == 0, first, later)
        ky = jnp.where(owner == 0, later, first)
        cols = (x ^ kx) * 2 + (owner ^ kc)
        rows = ((z ^ along(kz)) * 2 + (y ^ ky)) * 2 * self.half + owner * self.half
        e = jnp.arange(16, dtype=jnp.int32)
        col, owner, ky = e // 4, core ^ (e // 2 % 2), e % 2
        kx = (col // 2) ^ x
        later = jnp.where(owner == 0, ky, kx)
        first = jnp.where(owner == 0, kx, ky)
        slots = jnp.stack([later, first, (col % 2) ^ owner], axis=1).reshape(-1)
        owner, ky, kz = core ^ (e // 8), e // 4 % 2, e % 4
        outs = ((z ^ along(kz)) * 2 + (y ^ ky)) * 2 * self.half + owner * self.half
        step = jnp.arange(4, dtype=jnp.int32)
        order = (x ^ (step % 2)) * 2 + (core ^ (step // 2))
        return jnp.concatenate([cols, rows, slots, outs, order, core[None]]).astype(jnp.int32)

    def found_at(self):
        device = jnp.arange(self.rows * self.cols, dtype=jnp.int32)
        if not self.direct:
            return device
        row, col = device // 4, device % 4
        kz = along(row // 2 ^ self.z)
        ky = (row % 2) ^ self.y
        kx = (col // 2) ^ self.x
        kc = (col % 2) ^ self.core
        return ((kc * 2 + kx) * 2 + ky) * 4 + kz


def swap_x(v):
    return lax.ppermute(v, "col", [(c, c ^ 2) for c in range(4)])


def swap_core(v):
    return lax.ppermute(v, "col", [(c, c ^ 1) for c in range(4)])


def swap_y(v):
    return lax.ppermute(v, "row", [(r, r ^ 1) for r in range(8)])


def swap_first(v):
    pairs = [(d, d ^ 2 if d % 2 == 0 else d ^ 4) for d in range(32)]
    return lax.ppermute(v, ("row", "col"), pairs)


def swap_second(v):
    pairs = [(d, d ^ 4 if d % 2 == 0 else d ^ 2) for d in range(32)]
    return lax.ppermute(v, ("row", "col"), pairs)


def swap_far(v):
    return lax.ppermute(v, "row", [(r, r ^ 4) for r in range(8)])


def swap_near(v):
    return lax.ppermute(v, "row", [(r, r ^ 2) for r in range(8)])


def swap_across(v):
    return lax.ppermute(v, ("row", "col"), [(d, d ^ 6) for d in range(32)])


def swap_beyond(v):
    return lax.ppermute(v, "row", [(r, r ^ 6) for r in range(8)])


def pair(index, own, other):
    first = index == 0
    return jnp.stack([jnp.where(first, own, other), jnp.where(first, other, own)])


def gather_cols(place, own):
    if not place.direct:
        return lax.all_gather(own, "col")
    both = pair(place.core, own, swap_core(own))
    return pair(place.x, both, swap_x(both)).reshape((4,) + own.shape)


def near_z(own):
    both = jnp.stack([own, swap_far(own)])
    return jnp.concatenate([both, swap_near(both)])


def near_z_at_once(own):
    return jnp.stack([own, swap_far(own), swap_near(own), swap_beyond(own)])


def near_y(every):
    return jnp.concatenate([every, swap_y(every)])


def near_rows(own):
    return near_y(near_z(own))


def near_x(every):
    return jnp.concatenate([every, swap_x(every)])


def near_core(every):
    return jnp.concatenate([every, swap_core(every)])


def near_cols(every):
    return near_core(near_x(every))


def gather_near(place, own):
    if not place.direct:
        return lax.all_gather(own, ("row", "col"))
    return near_cols(near_rows(own))


def sum_parts(place, parts):
    z = place.z

    def two(at):
        return jnp.stack([lax.dynamic_index_in_dim(parts, k, 0, False) for k in (at, at ^ 2)])

    total = two(z) + swap_near(two(z ^ 1))
    return total[0] + swap_far(total[1])


def sum_along_z(place, own):
    return sum_parts(place, own.reshape((4, own.shape[0] // 4) + own.shape[1:]))


def sum_with(swap):
    return lambda total: total + swap(total)


def sum_spread(place, total):
    far = pair(place.z // 2, total, swap_far(total))
    every = pair(place.z % 2, far, swap_near(far))
    return jnp.swapaxes(every, 0, 1).reshape((-1,) + total.shape[1:])


def sum_scalar(place, value):
    if not place.direct:
        return lax.psum(value, ("row", "col"))
    total = jnp.broadcast_to(value, (8, 128))
    total = total + swap_far(total) + (swap_near(total) + swap_beyond(total))
    total = total + swap_x(total) + (swap_y(total) + swap_across(total))
    total = total + swap_core(total)
    return total[0, 0]


def scatter_plain(place, partial, mine):
    _, count, narrow = partial.shape
    summed = lax.psum_scatter(partial, "row", scatter_dimension=0, tiled=True)
    spread = lax.all_gather(summed, "col")
    spread = lax.dynamic_slice_in_dim(spread, place.col * mine, mine, 1)
    return jnp.transpose(spread, (1, 2, 0, 3)).reshape(mine, count, place.cols * narrow)


def scatter_y(place, partial):
    samples, count, narrow = partial.shape
    by_y = partial.reshape(4, 2, samples // 8, count, narrow)
    own = lax.dynamic_index_in_dim(by_y, place.y, 1, False)
    return own + swap_y(lax.dynamic_index_in_dim(by_y, 1 - place.y, 1, False))


def scatter_z(place, own):
    return sum_parts(place, own)


def scatter_x(place, total, mine):
    _, count, narrow = total.shape
    by_x = total.reshape(2, 2, mine, count, narrow)
    own = lax.dynamic_index_in_dim(by_x, place.x, 0, False)
    got = swap_x(lax.dynamic_index_in_dim(by_x, 1 - place.x, 0, False))
    return pair(place.x, own, got)


def scatter_core(place, both):
    _, _, mine, count, narrow = both.shape
    own = lax.dynamic_index_in_dim(both, place.core, 1, False)
    got = swap_core(lax.dynamic_index_in_dim(both, 1 - place.core, 1, False))
    every = pair(place.core, own, got)
    return jnp.transpose(every, (2, 3, 1, 0, 4)).reshape(mine, count, 4 * narrow)


class Route:
    def __init__(self, place, buffers):
        self.direct = place.direct
        self.half = place.half
        self.cols = place.cols
        self.count = len(buffers)
        if self.direct:
            matrices = buffers[0].shape[2]
            self.outs = [(2, 8, 2, matrices) + buffers[0].shape[3:]] * 2
        else:
            self.outs = [buffers[0].shape]

    def column(self, table, step):
        return table[192 + step] if self.direct else step

    def load(self, table, buffers, moves):
        if not self.direct:
            for c in range(self.cols):
                for matrix, target, sems in moves:
                    pltpu.make_async_copy(
                        buffers[0].at[matrix, c], target.at[c], sems.at[c]
                    ).start()
            return
        for core in range(2):

            @pl.when(table[196] == core)
            def _(core=core):
                entries = []
                for e in range(64):
                    owner, later, first, kc = core ^ (e // 32), e // 16 % 2, e // 8 % 2, e // 4 % 2
                    kx = first if owner == 0 else later
                    entries.append(((owner ^ kc ^ core) * 2 + kx, e))
                for step in range(4):
                    for matrix, target, sems in moves:
                        for at, e in entries:
                            if at != step:
                                continue
                            row = pl.multiple_of(table[64 + e], 16)
                            pltpu.make_async_copy(
                                buffers[e // 16].at[e // 8 % 2 * 4 + e % 4, e // 4 % 2, matrix],
                                target.at[step, pl.ds(row, self.half), :],
                                sems.at[step],
                            ).start()

    def store(self, table, c, matrix, source, grads, sem):
        if not self.direct:
            pltpu.make_async_copy(source, grads[0].at[matrix, c], sem).start()
            return
        for owner in range(2):
            for ky in range(2):
                at = 128 + ((c * 2 + owner) * 2 + ky) * 3
                for kz in range(4):
                    row = pl.multiple_of(table[176 + (owner * 2 + ky) * 4 + kz], 16)
                    pltpu.make_async_copy(
                        source.at[pl.ds(row, self.half), :],
                        grads[owner].at[
                            table[at], table[at + 1] * 4 + kz, table[at + 2], matrix
                        ],
                        sem,
                    ).start()


class Stages:
    def __init__(self):
        self.last = None

    def run(self, moves, works=(), late=()):
        operands = ([v for _, v in moves], [w[1:] for w in works], [v for _, v in late])
        if self.last is not None:
            operands, _ = lax.optimization_barrier((operands, self.last))
        moved = [move(v) for (move, _), v in zip(moves, operands[0])]
        done = [w[0](*v) for w, v in zip(works, operands[1])]
        if late:
            held, _ = lax.optimization_barrier((operands[2], done))
            moved += [move(v) for (move, _), v in zip(late, held)]
        self.last = (moved, done)
        return moved, done


class Spread:
    def __init__(self, kept, got):
        self.own = jnp.stack([kept, got])

    def far(self):
        return [(swap_far, self.own)]

    def near(self, got):
        self.two = jnp.stack([self.own, got])
        return [(swap_near, self.two)]

    def at_once(self):
        return [(swap_far, self.own), (swap_near, self.own), (swap_beyond, self.own)]

    def along_at_once(self, got):
        self.z = jnp.stack([self.own] + list(got))

    def along(self, got):
        self.z = jnp.concatenate([self.two, got])

    def first(self):
        return [(swap_first, self.z)]

    def second(self, got):
        self.p = jnp.concatenate([self.z, got])
        return [(swap_second, self.p)]

    def core(self):
        return [(swap_core, self.p)]

    def late_core(self, q):
        self.q = q
        return [(swap_core, q)]

    def buffers(self, core, late_core):
        return [self.p, self.q, core, late_core]


def add_up(*parts):
    total = parts[0].astype(F32)
    for part in parts[1:]:
        total = total + part.astype(F32)
    return total


class Gathered:
    def __init__(self, buffers):
        self.own = buffers[0]
        self.core = [(swap_core, buffers[1])]

    def first(self, got):
        self.got = got
        return [(swap_second, add_up(self.own[1], got[1]).astype(BF16))]

    def second(self, got):
        self.parts = (self.own[0], self.got[0], got)
        return [(swap_first, add_up(*[v[4:] for v in self.parts]).astype(BF16))]

    def near(self, got):
        self.parts = self.parts + (got,)
        return [(swap_near, add_up(*[v[2:4] for v in self.parts]).astype(BF16))]

    def far(self, got):
        self.last = got
        return [(swap_far, add_up(*[v[1] for v in self.parts], got[1]).astype(BF16))]

    def total(self, got):
        return add_up(*[v[0] for v in self.parts], self.last[0], got)


def plain_gather(parts):
    every = lax.all_gather(lax.all_gather(parts, "row", axis=1, tiled=True), "col")
    return jnp.swapaxes(every, 0, 1)


def plain_scatter(grads):
    summed = lax.psum_scatter(grads.astype(F32), "row", scatter_dimension=2, tiled=True)
    return lax.psum_scatter(summed, "col", scatter_dimension=1, tiled=False)


def normal(v):
    center = jnp.mean(v, axis=-1, keepdims=True)
    moved = v - center
    inverse = lax.rsqrt(jnp.mean(moved * moved, axis=-1, keepdims=True) + EPS_NORM)
    return moved * inverse, inverse


def wait_all(ref, sem):
    pltpu.make_async_copy(ref, ref, sem).wait()


def row_of(shared_ref, at):
    return jnp.concatenate(
        [shared_ref[c, at : at + 1, :] for c in range(shared_ref.shape[0])], axis=1
    )


def attention_forward_body(route, base, table, x_ref, mod_ref, shared_ref, *refs):
    n_buf = route.count
    buffers = refs[:n_buf]
    out_ref, h_ref, qkv_ref, p_ref, o_ref, a_ref, w_ref, sems = refs[n_buf:]
    c = pl.program_id(0)
    samples = mod_ref.shape[0]

    @pl.when(c == 0)
    def _():
        route.load(table, buffers, [(0, w_ref, sems)])
        for s in range(samples):
            rows = pl.ds(s * LEN, LEN)
            n, _ = normal(x_ref[rows, :])
            h_ref[rows, :] = (n * (1.0 + mod_ref[s, 1:2]) + mod_ref[s, 0:1]).astype(BF16)
        a_ref[...] = jnp.zeros_like(a_ref)

    wait_all(w_ref.at[c], sems.at[c])
    width = shared_ref.shape[-1]
    col = route.column(table, c)
    query_bias = shared_ref[col, base + 6 : base + 7, :]
    value_bias = shared_ref[col, base + 7 : base + 8, :]
    bias = jnp.concatenate([query_bias, jnp.zeros_like(query_bias), value_bias], axis=1)
    triple = dot_nn(h_ref[...], w_ref[c, :, : 3 * width]) + bias
    qkv_ref[0] = triple.astype(BF16)
    triple = triple.astype(BF16)
    heads = width // HEAD_DIM

    def part(s, k, j):
        at = k * width + j * HEAD_DIM
        return triple[s * LEN : (s + 1) * LEN, at : at + HEAD_DIM]

    each = [(s, j) for s in range(samples) for j in range(heads)]
    scores = [dot_nt(part(s, 1, j), part(s, 0, j)) * HEAD_DIM ** (-0.5) for s, j in each]
    probs = []
    for score in scores:
        powers = jnp.exp(score - jnp.max(score, axis=0, keepdims=True))
        probs.append((powers * (1.0 / jnp.sum(powers, axis=0, keepdims=True))).astype(BF16))
    for (s, j), prob in zip(each, probs):
        p_ref[0, j, s] = prob
    outs = [dot_tn(prob, part(s, 2, j)).astype(BF16) for (s, j), prob in zip(each, probs)]
    for s in range(samples):
        o_ref[0, pl.ds(s * LEN, LEN), :] = jnp.concatenate(
            outs[s * heads : (s + 1) * heads], axis=1
        )
    a_ref[...] += dot_nt(o_ref[0], w_ref[c, :, 3 * width :])

    @pl.when(c == pl.num_programs(0) - 1)
    def _():
        a_ref[...] += row_of(shared_ref, base + 12)
        for s in range(samples):
            rows = pl.ds(s * LEN, LEN)
            out_ref[rows, :] = x_ref[rows, :] + mod_ref[s, 2:3] * a_ref[rows, :]


def mlp_forward_body(route, base, table, x_ref, mod_ref, shared_ref, *refs):
    n_buf = route.count
    buffers = refs[:n_buf]
    out_ref, h_ref, u_ref, m_ref, wi_ref, wo_ref, sems_i, sems_o = refs[n_buf:]
    c = pl.program_id(0)
    samples = mod_ref.shape[0]

    @pl.when(c == 0)
    def _():
        route.load(table, buffers, [(0, wi_ref, sems_i), (1, wo_ref, sems_o)])
        for s in range(samples):
            rows = pl.ds(s * LEN, LEN)
            n, _ = normal(x_ref[rows, :])
            h_ref[rows, :] = (n * (1.0 + mod_ref[s, 1:2]) + mod_ref[s, 0:1]).astype(BF16)
        m_ref[...] = jnp.zeros_like(m_ref)

    wait_all(wi_ref.at[c], sems_i.at[c])
    col = route.column(table, c)
    blocks = wi_ref.shape[-1] // shared_ref.shape[-1]
    bias = jnp.concatenate(
        [shared_ref[col, base + 8 + k : base + 9 + k, :] for k in range(blocks)], axis=1
    )
    hidden = dot_nn(h_ref[...], wi_ref[c]) + bias
    u_ref[0] = hidden
    active = jax.nn.gelu(hidden, approximate=True).astype(BF16)
    wait_all(wo_ref.at[c], sems_o.at[c])
    m_ref[...] += dot_nt(active, wo_ref[c])

    @pl.when(c == pl.num_programs(0) - 1)
    def _():
        m_ref[...] += row_of(shared_ref, base + 13)
        for s in range(samples):
            rows = pl.ds(s * LEN, LEN)
            out_ref[rows, :] = x_ref[rows, :] + mod_ref[s, 2:3] * m_ref[rows, :]


def norm_backward(s, x_ref, mod_ref, dx_ref, dh_ref, out_ref, dmod_ref):
    rows = pl.ds(s * LEN, LEN)
    n, inverse = normal(x_ref[rows, :])
    dh = dh_ref[rows, :]
    dmod_ref[s, 0:1] = jnp.sum(dh, axis=0, keepdims=True)
    dmod_ref[s, 1:2] = jnp.sum(dh * n, axis=0, keepdims=True)
    dn = dh * (1.0 + mod_ref[s, 1:2])
    back = inverse * (
        dn
        - jnp.mean(dn, axis=-1, keepdims=True)
        - n * jnp.mean(dn * n, axis=-1, keepdims=True)
    )
    if dx_ref is None:
        out_ref[rows, :] = back
    else:
        out_ref[rows, :] = dx_ref[rows, :] + back


def branch_gradient(dx_ref, mod_ref, branch_ref, dmod_ref, sum_ref, low_ref):
    total = None
    for s in range(mod_ref.shape[0]):
        rows = pl.ds(s * LEN, LEN)
        dx = dx_ref[rows, :]
        dmod_ref[s, 2:3] = jnp.sum(dx * branch_ref[rows, :], axis=0, keepdims=True)
        db = mod_ref[s, 2:3] * dx
        low_ref[rows, :] = db.astype(BF16)
        part = jnp.sum(db, axis=0, keepdims=True)
        total = part if total is None else total + part
    sum_ref[...] = total


def gelu_slope(u):
    k = math.sqrt(2.0 / math.pi)
    square = u * u
    t = jnp.tanh(k * (u + 0.044715 * square * u))
    half = 0.5 * (1.0 + t)
    slope = half + 0.5 * u * (1.0 - t * t) * (k * (1.0 + 3 * 0.044715 * square))
    return u * half, slope


def mlp_backward_body(
    route, table, dx_ref, x_ref, mod_ref, m_ref, h_ref, u_ref, *refs
):
    n_buf, n_out = route.count, len(route.outs)
    buffers = refs[:n_buf]
    out_ref, dmod_ref, dbias_ref, dtail_ref = refs[n_buf : n_buf + 4]
    grads = refs[n_buf + 4 : n_buf + n_out + 4]
    wi_ref, wo_ref, low_ref, dh_ref, gi_ref, go_ref, sems_i, sems_o, sems_gi, sems_go = refs[
        n_buf + n_out + 4 :
    ]
    c = pl.program_id(0)
    count = route.cols
    samples = mod_ref.shape[0]

    @pl.when(c == 0)
    def _():
        route.load(table, buffers, [(1, wo_ref, sems_o), (0, wi_ref, sems_i)])
        branch_gradient(dx_ref, mod_ref, m_ref, dmod_ref, dtail_ref, low_ref)
        dh_ref[...] = jnp.zeros_like(dh_ref)

    slot = lax.rem(c, 2)

    @pl.when(c >= 2)
    def _():
        wait_all(gi_ref.at[slot], sems_gi.at[slot])
        wait_all(go_ref.at[slot], sems_go.at[slot])

    wait_all(wo_ref.at[c], sems_o.at[c])
    active, slope = gelu_slope(u_ref[0])
    low = low_ref[...]
    go_ref[slot] = dot_tn(low, active.astype(BF16)).astype(BF16)
    route.store(table, route.column(table, c), 1, go_ref.at[slot], grads, sems_go.at[slot])
    du = dot_nn(low, wo_ref[c]) * slope
    dbias_ref[route.column(table, c)] = jnp.sum(du, axis=0, keepdims=True)
    du = du.astype(BF16)
    gi_ref[slot] = dot_tn(h_ref[...], du).astype(BF16)
    route.store(table, route.column(table, c), 0, gi_ref.at[slot], grads, sems_gi.at[slot])
    wait_all(wi_ref.at[c], sems_i.at[c])
    dh_ref[...] += dot_nt(du, wi_ref[c])

    @pl.when(c == count - 1)
    def _():
        for s in range(samples):
            norm_backward(s, x_ref, mod_ref, dx_ref, dh_ref, out_ref, dmod_ref)
        for k in range(2):
            wait_all(gi_ref.at[k], sems_gi.at[k])
            wait_all(go_ref.at[k], sems_go.at[k])


def attention_backward_body(
    route, table, dx_ref, x_ref, mod_ref, a_ref, h_ref, qkv_ref, p_ref, o_ref, *refs
):
    n_buf, n_out = route.count, len(route.outs)
    buffers = refs[:n_buf]
    out_ref, dmod_ref, dbias_ref, dtail_ref = refs[n_buf : n_buf + 4]
    grads = refs[n_buf + 4 : n_buf + n_out + 4]
    w_ref, low_ref, dh_ref, d_ref, g_ref, sems, sems_g = refs[n_buf + n_out + 4 :]
    c = pl.program_id(0)
    count = route.cols
    samples = mod_ref.shape[0]
    width = qkv_ref.shape[-1] // 3
    factor = HEAD_DIM ** (-0.5)

    @pl.when(c == 0)
    def _():
        route.load(table, buffers, [(0, w_ref, sems)])
        branch_gradient(dx_ref, mod_ref, a_ref, dmod_ref, dtail_ref, low_ref)
        dh_ref[...] = jnp.zeros_like(dh_ref)

    slot = lax.rem(c, 2)

    @pl.when(c >= 2)
    def _():
        wait_all(g_ref.at[slot], sems_g.at[slot])

    wait_all(w_ref.at[c], sems.at[c])
    do_all = dot_nn(low_ref[...], w_ref[c, :, 3 * width :]).astype(BF16)
    heads = width // HEAD_DIM
    each = [(s, j) for s in range(samples) for j in range(heads)]

    def part(s, k, j):
        at = k * width + j * HEAD_DIM
        return qkv_ref[0, pl.ds(s * LEN, LEN), at : at + HEAD_DIM]

    def given(s, j):
        return do_all[s * LEN : (s + 1) * LEN, j * HEAD_DIM : (j + 1) * HEAD_DIM]

    dps = [dot_nt(part(s, 2, j), given(s, j)) for s, j in each]
    dss = []
    for (s, j), dp in zip(each, dps):
        probs = p_ref[0, j, s].astype(F32)
        delta = jnp.sum(probs * dp, axis=0, keepdims=True)
        dss.append((probs * (dp - delta)).astype(BF16))
    dqs = [dot_tn(ds, part(s, 1, j)) * factor for (s, j), ds in zip(each, dss)]
    dks = [dot_nn(ds, part(s, 0, j)) * factor for (s, j), ds in zip(each, dss)]
    dvs = [dot_nn(p_ref[0, j, s], given(s, j)) for s, j in each]
    sums = None
    for s in range(samples):
        at = slice(s * heads, (s + 1) * heads)
        joined = jnp.concatenate(dqs[at] + dks[at] + dvs[at], axis=1)
        total = jnp.sum(joined, axis=0, keepdims=True)
        sums = total if s == 0 else sums + total
        d_ref[pl.ds(s * LEN, LEN), :] = joined.astype(BF16)
    dbias_ref[route.column(table, c)] = sums
    grad_in = dot_tn(h_ref[...], d_ref[...])
    grad_out = dot_tn(low_ref[...], o_ref[0])
    g_ref[slot] = jnp.concatenate([grad_in, grad_out], axis=1).astype(BF16)
    route.store(table, route.column(table, c), 0, g_ref.at[slot], grads, sems_g.at[slot])
    dh_ref[...] += dot_nt(d_ref[...], w_ref[c, :, : 3 * width])

    @pl.when(c == count - 1)
    def _():
        for s in range(samples):
            norm_backward(s, x_ref, mod_ref, dx_ref, dh_ref, out_ref, dmod_ref)
        for k in range(2):
            wait_all(g_ref.at[k], sems_g.at[k])


def final_body(
    x_ref, mod_ref, head_ref, bias_ref, noise_ref, mask_ref,
    dx_ref, loss_ref, dhead_ref, dbias_ref, dmod_ref, h_ref, dh_ref,
):
    samples = mod_ref.shape[0]
    for s in range(samples):
        rows = pl.ds(s * LEN, LEN)
        n, _ = normal(x_ref[rows, :])
        h_ref[rows, :] = (n * (1.0 + mod_ref[s, 1:2]) + mod_ref[s, 0:1]).astype(BF16)
    predicted = dot_nt(h_ref[...], head_ref[...]) + bias_ref[...]
    error = predicted - noise_ref[...]
    masked = mask_ref[...] * error
    loss_ref[...] = jnp.sum(masked * error, axis=0, keepdims=True)
    dpred = 2.0 * masked
    dbias_ref[...] = jnp.sum(dpred, axis=0, keepdims=True)
    low = dpred.astype(BF16)
    dhead_ref[...] = dot_tn(low, h_ref[...])
    dh_ref[...] = dot_nn(low, head_ref[...])
    for s in range(samples):
        norm_backward(s, x_ref, mod_ref, None, dh_ref, dx_ref, dmod_ref)


def whole_block(shape):
    rank = len(shape)
    return pl.BlockSpec(shape, lambda c: (0,) * rank, pipeline_mode=pl.Buffered(1))


def whole_out(shape):
    rank = len(shape)
    return pl.BlockSpec(shape, lambda c: (0,) * rank)


def block_of(shape):
    rank = len(shape)
    return pl.BlockSpec((1,) + tuple(shape[1:]), lambda c: (c,) + (0,) * (rank - 1))


def params(mib):
    return pltpu.CompilerParams(
        dimension_semantics=("arbitrary",), vmem_limit_bytes=mib * MIB
    )


def cost(flops, nbytes, exps=0):
    return pl.CostEstimate(flops=int(flops), bytes_accessed=int(nbytes), transcendentals=int(exps))


def shaped(shape, dtype):
    return jax.ShapeDtypeStruct(tuple(shape), dtype)


def attention_forward(place, base, buffers, x, mods, shared):
    route = Route(place, buffers)
    count = place.cols
    tokens, width = x.shape
    samples = mods.shape[0]
    narrow = shared.shape[-1]
    heads = narrow // HEAD_DIM
    outs = [
        shaped((tokens, width), F32),
        shaped((tokens, width), BF16),
        shaped((count, tokens, 3 * narrow), BF16),
        shaped((count, heads, samples, LEN, LEN), BF16),
        shaped((count, tokens, narrow), BF16),
        shaped((tokens, width), F32),
    ]
    return pl.pallas_call(
        functools.partial(attention_forward_body, route, base),
        grid=(count,),
        in_specs=[SMEM, whole_block(x.shape), whole_block(mods.shape), whole_block(shared.shape)]
        + [ANY] * len(buffers),
        out_specs=[whole_out(outs[0].shape), whole_out(outs[1].shape)]
        + [block_of(o.shape) for o in outs[2:5]]
        + [whole_out(outs[5].shape)],
        out_shape=outs,
        scratch_shapes=[
            pltpu.VMEM((count, width, 4 * narrow), BF16),
            pltpu.SemaphoreType.DMA((count,)),
        ],
        compiler_params=params(58),
        cost_estimate=cost(
            2 * tokens * width * width * 4 + 4 * tokens * LEN * width,
            8 * width * width + 30 * tokens * width,
            tokens * LEN * width // HEAD_DIM,
        ),
        name="attention_forward",
    )(place.table, x, mods, shared, *buffers)


def mlp_forward(place, base, buffers, x, mods, shared):
    route = Route(place, buffers)
    count = place.cols
    tokens, width = x.shape
    wide = buffers[0].shape[-1]
    outs = [
        shaped((tokens, width), F32),
        shaped((tokens, width), BF16),
        shaped((count, tokens, wide), F32),
        shaped((tokens, width), F32),
    ]
    return pl.pallas_call(
        functools.partial(mlp_forward_body, route, base),
        grid=(count,),
        in_specs=[SMEM, whole_block(x.shape), whole_block(mods.shape), whole_block(shared.shape)]
        + [ANY] * len(buffers),
        out_specs=[whole_out(outs[0].shape), whole_out(outs[1].shape), block_of(outs[2].shape)]
        + [whole_out(outs[3].shape)],
        out_shape=outs,
        scratch_shapes=[
            pltpu.VMEM((count, width, wide), BF16),
            pltpu.VMEM((count, width, wide), BF16),
            pltpu.SemaphoreType.DMA((count,)),
            pltpu.SemaphoreType.DMA((count,)),
        ],
        compiler_params=params(58),
        cost_estimate=cost(
            2 * tokens * width * wide * count * 2,
            4 * width * wide * count + 30 * tokens * width,
            tokens * wide * count,
        ),
        name="mlp_forward",
    )(place.table, x, mods, shared, *buffers)


def mlp_backward(place, buffers, dx, x, mods, m, h, u):
    route = Route(place, buffers)
    count = place.cols
    tokens, width = x.shape
    wide = u.shape[-1]
    outs = [
        shaped((tokens, width), F32),
        shaped(mods.shape, F32),
        shaped((count, 1, wide), F32),
        shaped((1, width), F32),
    ] + [shaped(v, BF16) for v in route.outs]
    out = pl.pallas_call(
        functools.partial(mlp_backward_body, route),
        grid=(count,),
        in_specs=[SMEM, whole_block(x.shape), whole_block(x.shape), whole_block(mods.shape)]
        + [whole_block(m.shape), whole_block(h.shape), block_of(u.shape)]
        + [ANY] * len(buffers),
        out_specs=[whole_out(x.shape), whole_out(mods.shape), whole_out(outs[2].shape)]
        + [whole_out((1, width))]
        + [ANY] * len(route.outs),
        out_shape=outs,
        scratch_shapes=[
            pltpu.VMEM((count, width, wide), BF16),
            pltpu.VMEM((count, width, wide), BF16),
            pltpu.VMEM((tokens, width), BF16),
            pltpu.VMEM((tokens, width), F32),
            pltpu.VMEM((2, width, wide), BF16),
            pltpu.VMEM((2, width, wide), BF16),
            pltpu.SemaphoreType.DMA((count,)),
            pltpu.SemaphoreType.DMA((count,)),
            pltpu.SemaphoreType.DMA((2,)),
            pltpu.SemaphoreType.DMA((2,)),
        ],
        compiler_params=params(58),
        cost_estimate=cost(
            4 * 2 * tokens * width * wide * count,
            8 * width * wide * count + 40 * tokens * width,
            tokens * wide * count,
        ),
        name="mlp_backward",
    )(place.table, dx, x, mods, m, h, u, *buffers)
    return out[:4], out[4:]


def attention_backward(place, buffers, dx, x, mods, a, h, qkv, p, o):
    route = Route(place, buffers)
    count = place.cols
    tokens, width = x.shape
    narrow = o.shape[-1]
    outs = [
        shaped((tokens, width), F32),
        shaped(mods.shape, F32),
        shaped((count, 1, 3 * narrow), F32),
        shaped((1, width), F32),
    ] + [shaped(v, BF16) for v in route.outs]
    out = pl.pallas_call(
        functools.partial(attention_backward_body, route),
        grid=(count,),
        in_specs=[SMEM, whole_block(x.shape), whole_block(x.shape), whole_block(mods.shape)]
        + [whole_block(a.shape), whole_block(h.shape)]
        + [block_of(qkv.shape), block_of(p.shape), block_of(o.shape)]
        + [ANY] * len(buffers),
        out_specs=[whole_out(x.shape), whole_out(mods.shape), whole_out(outs[2].shape)]
        + [whole_out((1, width))]
        + [ANY] * len(route.outs),
        out_shape=outs,
        scratch_shapes=[
            pltpu.VMEM((count, width, 4 * narrow), BF16),
            pltpu.VMEM((tokens, width), BF16),
            pltpu.VMEM((tokens, width), F32),
            pltpu.VMEM((tokens, 3 * narrow), BF16),
            pltpu.VMEM((2, width, 4 * narrow), BF16),
            pltpu.SemaphoreType.DMA((count,)),
            pltpu.SemaphoreType.DMA((2,)),
        ],
        compiler_params=params(58),
        cost_estimate=cost(
            4 * tokens * width * width * 4 + 10 * tokens * LEN * width,
            16 * width * width + 40 * tokens * width,
        ),
        name="attention_backward",
    )(place.table, dx, x, mods, a, h, qkv, p, o, *buffers)
    return out[:4], out[4:]


def final_step(x, mods, head, bias, noise, mask):
    tokens, width = x.shape
    vmem = pl.BlockSpec(memory_space=pltpu.VMEM)
    return pl.pallas_call(
        final_body,
        in_specs=[vmem] * 6,
        out_specs=[vmem] * 5,
        out_shape=[
            shaped((tokens, width), F32),
            shaped((1, PATCH), F32),
            shaped((PATCH, width), F32),
            shaped((1, PATCH), F32),
            shaped(mods.shape, F32),
        ],
        scratch_shapes=[pltpu.VMEM((tokens, width), BF16), pltpu.VMEM((tokens, width), F32)],
        compiler_params=pltpu.CompilerParams(vmem_limit_bytes=32 * MIB),
        cost_estimate=cost(6 * tokens * width * PATCH, 12 * tokens * width),
        name="final_step",
    )(x, mods, head, bias, noise, mask)


def pack_body(in_ref, out_ref, block_ref, mode_ref):
    blocks = out_ref.shape[1] - 1
    for k in range(6):
        mode_ref[0, k] = in_ref[0, k].astype(BF16)
    attn = [in_ref[0, 6 + k] for k in range(3)] + [out_ref[0, 0].T]
    block_ref[0] = jnp.concatenate(attn, axis=1).astype(BF16)
    first = [in_ref[0, 9 + k] for k in range(blocks)]
    block_ref[1] = jnp.concatenate(first, axis=1).astype(BF16)
    second = [out_ref[0, 1 + k].T for k in range(blocks)]
    block_ref[2] = jnp.concatenate(second, axis=1).astype(BF16)


def pack_weights(weights_in, weights_out):
    layers, kinds, block, narrow = weights_in.shape
    outs = [
        shaped((3 * layers, block, 4 * narrow), BF16),
        shaped((layers, 6, block, narrow), BF16),
    ]
    return pl.pallas_call(
        pack_body,
        grid=(layers,),
        in_specs=[block_of(weights_in.shape), block_of(weights_out.shape)],
        out_specs=[
            pl.BlockSpec((3, block, 4 * narrow), lambda c: (c, 0, 0)),
            block_of(outs[1].shape),
        ],
        out_shape=outs,
        compiler_params=params(32),
        name="pack_weights",
    )(weights_in, weights_out)


def embed_body(base, noisy_ref, shared_ref, table_ref, out_ref):
    patch = jnp.concatenate(
        [
            shared_ref[c, base + 3 : base + 3 + PATCH, :]
            for c in range(shared_ref.shape[0])
        ],
        axis=1,
    ).astype(BF16)
    constant = row_of(shared_ref, base + 2) + table_ref[...]
    for s in range(noisy_ref.shape[0] // LEN):
        rows = pl.ds(s * LEN, LEN)
        out_ref[rows, :] = dot_nn(noisy_ref[rows, :], patch) + constant


def embed_tokens(base, noisy, shared, table):
    vmem = pl.BlockSpec(memory_space=pltpu.VMEM)
    return pl.pallas_call(
        functools.partial(embed_body, base),
        in_specs=[vmem] * 3,
        out_specs=vmem,
        out_shape=shaped((noisy.shape[0], table.shape[1]), F32),
        compiler_params=pltpu.CompilerParams(vmem_limit_bytes=32 * MIB),
        name="embed_tokens",
    )(noisy, shared, table)


def silu_slope(values):
    sigmoid_part = jax.nn.sigmoid(values)
    return sigmoid_part * (1.0 + values * (1.0 - sigmoid_part))


TIME_BLOCK = 128
CLASS_AT, FREQ_AT, LABEL_AT = 192, 208, 224


def condition_body(base, found, near_ref, shared_ref, *refs):
    cond_ref, act_ref, first_ref, first_act_ref, freq_ref, label_ref, class_ref, wave_ref = refs
    cols, _, narrow = shared_ref.shape
    rows = near_ref.shape[0] // cols
    steps = FREQ // TIME_BLOCK
    for r in range(rows):
        at = slice(r * 8, r * 8 + 8)
        for c in range(cols):
            block = near_ref[found[r * cols + c], CLASS_AT:, :].astype(F32)
            joined = jnp.concatenate([block[:8], block[8:16, : narrow - 128]], axis=1)
            class_ref[at, c * narrow : (c + 1) * narrow] = joined
            if c == 0:
                wave_ref[at, :TIME_BLOCK] = block[16:24]
                wave_ref[at, TIME_BLOCK:] = block[24:32]
                label_ref[at, :] = block[32:40] * 32.0 + block[40:48]
    freq = wave_ref[...].astype(BF16)
    freq_ref[...] = freq

    def product(left, first_row, count):
        parts = []
        for c in range(cols):
            total = None
            for k in range(count):
                block = near_ref[found[(first_row + k) * cols + c], :CLASS_AT, :]
                part = dot_nt(left[:, k * TIME_BLOCK : (k + 1) * TIME_BLOCK], block)
                total = part if total is None else total + part
            parts.append(total)
        return jnp.concatenate(parts, axis=1)

    first = product(freq, 0, steps) + row_of(shared_ref, base)
    first_ref[...] = first
    first_act = (first * jax.nn.sigmoid(first)).astype(BF16)
    first_act_ref[...] = first_act
    cond = product(first_act, steps, rows - steps) + row_of(shared_ref, base + 1)
    cond = cond + class_ref[...]
    cond_ref[...] = cond
    act_ref[...] = (cond * jax.nn.sigmoid(cond)).astype(BF16)


def condition_step(base, found, near, shared, samples, width):
    vmem = pl.BlockSpec(memory_space=pltpu.VMEM)
    outs = [
        shaped((samples, width), F32),
        shaped((samples, width), BF16),
        shaped((samples, width), F32),
        shaped((samples, width), BF16),
        shaped((samples, FREQ), BF16),
        shaped((samples, 128), F32),
    ]
    return pl.pallas_call(
        functools.partial(condition_body, base),
        in_specs=[SMEM, vmem, vmem],
        out_specs=[vmem] * len(outs),
        out_shape=outs,
        scratch_shapes=[pltpu.VMEM((samples, width), F32), pltpu.VMEM((samples, FREQ), F32)],
        compiler_params=pltpu.CompilerParams(vmem_limit_bytes=32 * MIB),
        name="condition_step",
    )(found, near, shared)


def condition_back_body(
    layers, blocks, found, spot, small_ref, part_ref, final_ref, square_ref, cond_ref, first_ref,
    input_ref, label_ref, pick_ref, near_ref, time_ref, embed_ref, bias_ref, own_ref, shared_ref,
    grad_ref,
):
    row, col = spot[0], spot[1]
    samples, width = cond_ref.shape
    narrow = pick_ref.shape[1]
    cols = width // narrow
    rows = near_ref.shape[0] // cols
    steps = FREQ // TIME_BLOCK
    start = 16 * layers + 2 * PATCH
    pick = pick_ref[...]
    pick_wide = pick.astype(F32)

    def own_cols(v):
        return jnp.dot(v, pick_wide, precision=HIGHEST, preferred_element_type=F32)

    def squares(v):
        return jnp.sum(v * v, keepdims=True)

    block_rows = part_ref.shape[2]
    for r in range(rows):
        part = part_ref[found[r * cols + col]]
        grad_ref[:, r * block_rows : (r + 1) * block_rows] = part
    grad_cond = (grad_ref[...] + final_ref[...]) * silu_slope(cond_ref[...])
    low = grad_cond.astype(BF16)
    parts = []
    for r in range(steps, rows):
        total = None
        for c in range(cols):
            block = near_ref[found[r * cols + c], :CLASS_AT, :]
            part = dot_nn(low[:, c * narrow : (c + 1) * narrow], block)
            total = part if total is None else total + part
        parts.append(total)
    grad_first = jnp.concatenate(parts, axis=1) * silu_slope(first_ref[...])
    is_first = (row < steps).astype(F32)
    outputs = grad_first.astype(BF16).astype(F32) * is_first + low.astype(F32) * (1.0 - is_first)
    outputs = dot_nn(outputs.astype(BF16), pick).astype(BF16)
    time_grad = dot_tn(outputs, input_ref[...])
    time_ref[...] = time_grad
    hot = lax.broadcasted_iota(jnp.int32, (samples, CLASSES), 1).astype(F32)
    hot = (hot == label_ref[:, 0:1]).astype(F32)
    class_grad = lax.dot_general(
        own_cols(grad_cond), hot, TN, precision=HIGHEST, preferred_element_type=F32
    )
    patch = own_cols(small_ref[start - PATCH : start, :])
    embed_ref[...] = jnp.concatenate([class_grad, patch.T], axis=1)
    own_ref[...] = squares(time_grad) + squares(class_grad) * (1.0 / rows)
    time_bias = jnp.concatenate(
        [jnp.sum(grad_first, axis=0, keepdims=True), jnp.sum(grad_cond, axis=0, keepdims=True)],
        axis=0,
    )
    total = square_ref[...] + squares(time_bias) + squares(small_ref[start - 2 * PATCH : start + 3, :])
    total = total + squares(small_ref[start + 3 : start + 4, :PATCH])
    own = own_cols(small_ref[: start + 16, :])
    lines = []
    for layer in range(layers):
        at = 16 * layer
        total = total + squares(small_ref[at : at + 6 + cols, :])
        total = total + squares(small_ref[at + 10 : at + 10 + cols, :narrow])
        total = total + squares(small_ref[at + 10 : at + 10 + cols, 2 * narrow : 3 * narrow])
        total = total + squares(small_ref[at + 14 : at + 16, :])
        attn = small_ref[pl.ds(at + 10 + col, 1), :]
        mlp = small_ref[pl.ds(at + 6 + col, 1), :]
        lines += [own[at : at + 6], attn[:, :narrow], attn[:, 2 * narrow : 3 * narrow]]
        lines += [mlp[:, k * narrow : (k + 1) * narrow] for k in range(blocks)]
        lines += [own[at + 14 : at + 16]]
    lines += [own_cols(time_bias), own[start : start + 1]]
    bias_ref[...] = jnp.concatenate(lines, axis=0)
    shared_ref[...] = total


def condition_back(
    layers, blocks, found, spot, small, part, final, squares, cond, first, inputs, labels, pick, near
):
    vmem = pl.BlockSpec(memory_space=pltpu.VMEM)
    narrow = pick.shape[1]
    outs = [
        shaped((narrow, TIME_BLOCK), F32),
        shaped((narrow, CLASSES + PATCH), F32),
        shaped((14 * layers + 3, narrow), F32),
        shaped((1, 1), F32),
        shaped((1, 1), F32),
    ]
    operands = [small, part, final, squares, cond, first, inputs, labels, pick, near]
    return pl.pallas_call(
        functools.partial(condition_back_body, layers, blocks),
        in_specs=[SMEM, SMEM] + [vmem] * len(operands),
        out_specs=[vmem] * len(outs),
        out_shape=outs,
        scratch_shapes=[pltpu.VMEM(cond.shape, F32)],
        compiler_params=pltpu.CompilerParams(vmem_limit_bytes=48 * MIB),
        name="condition_back",
    )(found, spot, *operands)


def modes_backward_body(
    layers, near_ref, at_ref, rows_ref, pick_ref, mode_ref, act_ref, final_ref,
    block_ref, part_ref, square_ref, grad_ref, cond_ref, shared_ref,
):
    near = near_ref[...]
    at = at_ref[...]
    samples = at.shape[0]
    where = lax.broadcasted_iota(jnp.int32, (samples, near.shape[0]), 1)
    cols, narrow = mode_ref.shape[0], mode_ref.shape[4]
    spreads = []
    for layer in range(layers):
        for k in range(6):
            offset = 12 * layer + 6 * (k // 3) + k % 3
            spreads.append((where == at[:, 0:1] + at[:, 1:2] * 3 + offset).astype(BF16))
    for k in range(2):
        spreads.append((where == at[:, 0:1] + at[:, 1:2] * 2 + 12 * layers + k).astype(BF16))
    rows = dot_nn(jnp.concatenate(spreads, axis=0), near).astype(BF16)
    mine = dot_nn(rows[: 6 * layers * samples], pick_ref[...]).astype(BF16)

    total = None
    squares = jnp.zeros((1, 1), F32)
    for layer in range(layers):
        for k in range(6):
            at_row = (6 * layer + k) * samples
            low = rows[at_row : at_row + samples]
            grad = dot_tn(rows_ref[...], mine[at_row : at_row + samples])
            block_ref[layer, k] = grad
            squares = squares + jnp.sum(grad * grad, keepdims=True)
            full = jnp.concatenate([mode_ref[c, layer, k] for c in range(cols)], axis=1)
            part = dot_nt(low, full)
            total = part if total is None else total + part
    part_ref[...] = total
    square_ref[...] = squares
    width = act_ref.shape[1]
    at_row = 6 * layers * samples
    shift, scale = rows[at_row : at_row + samples], rows[at_row + samples :]
    squares = jnp.zeros((1, 1), F32)
    for k, low in enumerate((shift, scale)):
        grad = dot_tn(low, act_ref[...])
        grad_ref[k * width : (k + 1) * width, :] = grad
        squares = squares + jnp.sum(grad * grad, keepdims=True)
    cond_ref[...] = dot_nn(shift, final_ref[:width, :]) + dot_nn(
        scale, final_ref[width : 2 * width, :]
    )
    shared_ref[...] = squares


def modes_backward(near, at, cond_rows, pick, mode_full, act, final):
    vmem = pl.BlockSpec(memory_space=pltpu.VMEM)
    samples, block = cond_rows.shape
    width = near.shape[2]
    layers, narrow = mode_full.shape[1], mode_full.shape[4]
    outs = [
        shaped((layers, 6, block, narrow), F32),
        shaped((samples, block), F32),
        shaped((1, 1), F32),
        shaped((2 * width, width), F32),
        shaped((samples, width), F32),
        shaped((1, 1), F32),
    ]
    operands = [near.reshape(-1, width), at, cond_rows, pick, mode_full, act, final]
    return pl.pallas_call(
        functools.partial(modes_backward_body, layers),
        in_specs=[vmem] * len(operands),
        out_specs=[vmem] * len(outs),
        out_shape=outs,
        compiler_params=pltpu.CompilerParams(vmem_limit_bytes=56 * MIB),
        name="modes_backward",
    )(*operands)


def modes_backward_plain(near, cond_rows, mode_full, act, final, col):
    layers, narrow, width = mode_full.shape[1], mode_full.shape[4], near.shape[2]
    devices = near.shape[0]
    samples = act.shape[0] // devices
    low = near[:, : 12 * layers].reshape(devices, layers, 2, samples, 3, width)
    low = jnp.transpose(low, (1, 2, 4, 0, 3, 5)).reshape(layers, 6, devices * samples, width)
    mine = lax.dynamic_slice_in_dim(low, col * narrow, narrow, 3)
    block = jnp.einsum("sd,lkse->lkde", cond_rows, mine, preferred_element_type=F32)
    full = jnp.transpose(mode_full, (1, 2, 3, 0, 4)).reshape(layers, 6, -1, width)
    part = jnp.einsum("lkse,lkde->sd", low, full, preferred_element_type=F32)
    ends = near[:, 12 * layers : 12 * layers + 2 * samples].reshape(-1, 2, width)
    grad = jnp.einsum("ske,sd->ked", ends, act, preferred_element_type=F32)
    cond = jnp.einsum(
        "ske,ked->sd", ends, final[: 2 * width].reshape(2, width, width), preferred_element_type=F32
    )
    grad = grad.reshape(2 * width, width)
    return block, part, squared(block)[None, None], grad, cond, squared(grad)[None, None]


def collect_body(layers, *refs):
    out_ref = refs[-1]
    at = 0
    out_ref[...] = jnp.zeros_like(out_ref)
    take = list(refs[:-1])
    for _ in range(layers):
        dmod_a, dmod_b, dbias_a, dbias_b, dtail_a, dtail_b = [take.pop(0) for _ in range(6)]
        for k, source in enumerate((dmod_a, dmod_b)):
            total = source[0]
            for s in range(1, source.shape[0]):
                total = total + source[s]
            out_ref[at + 3 * k : at + 3 * k + 3, :] = total
        for c in range(dbias_b.shape[0]):
            out_ref[at + 6 + c : at + 7 + c, : dbias_b.shape[2]] = dbias_b[c]
            out_ref[at + 10 + c : at + 11 + c, : dbias_a.shape[2]] = dbias_a[c]
        out_ref[at + 14 : at + 15, :] = dtail_a[...]
        out_ref[at + 15 : at + 16, :] = dtail_b[...]
        at += 16
    head, head_bias, loss, mask, dfinal, dx, noisy = take
    out_ref[at : at + PATCH, :] = head[...]
    out_ref[at + PATCH : at + 2 * PATCH, :] = dot_tn(noisy[...], dx[...].astype(BF16))
    at += 2 * PATCH
    out_ref[at : at + 1, :] = jnp.sum(dx[...], axis=0, keepdims=True)
    total = dfinal[0]
    for s in range(1, dfinal.shape[0]):
        total = total + dfinal[s]
    out_ref[at + 1 : at + 3, :] = total
    out_ref[at + 3 : at + 4, 0:PATCH] = head_bias[...]
    out_ref[at + 4 : at + 5, 0:PATCH] = loss[...]
    out_ref[at + 5 : at + 6, 0:1] = jnp.sum(mask[...], keepdims=True)


def collect(layers, parts, height, width):
    vmem = pl.BlockSpec(memory_space=pltpu.VMEM)
    return pl.pallas_call(
        functools.partial(collect_body, layers),
        in_specs=[vmem] * len(parts),
        out_specs=vmem,
        out_shape=shaped((height, width), F32),
        compiler_params=pltpu.CompilerParams(vmem_limit_bytes=48 * MIB),
        name="collect_small",
    )(*parts)


def adam(weight, gradient, moment, second, clip, rate):
    gradient = gradient * clip
    moment = BETA_ONE * moment + (1.0 - BETA_ONE) * gradient
    second = BETA_TWO * second + (1.0 - BETA_TWO) * gradient * gradient
    update = (
        moment / (1.0 - BETA_ONE**STEP) / (jnp.sqrt(second / (1.0 - BETA_TWO**STEP)) + ADAM_EPS)
    )
    return weight - rate * (update + DECAY * weight), moment, second


def adam_blocks_body(layers, halves, clip_ref, spot, *refs):
    clip = clip_ref[0]
    per = 5 if halves else 3
    sums = [refs[per * layer : per * layer + per] for layer in range(layers)]
    refs = refs[per * layers :]
    wi, mi, vi, wo, mo, vo = refs[:6]
    out_i, out_o = refs[6:9], refs[9:12]
    total_ref = refs[12]
    narrow = wi.shape[3]

    def fill(layer):
        group = sums[layer]
        for k in range(3):
            if not halves:
                total_ref[k] = group[1][0] if k == 0 else group[2][k - 1]
                continue
            half = total_ref.shape[1] // 2
            mine, other = group[1:3] if k == 0 else group[3:5]
            at = 0 if k == 0 else k - 1
            core = spot[1] % 2
            total_ref[k, pl.ds(pl.multiple_of(core * half, 8), half), :] = mine[0, at]
            total_ref[k, pl.ds(pl.multiple_of((1 - core) * half, 8), half), :] = other[at]

    def update(layer, mode_ref):
        for k in range(wi.shape[1]):
            if k < 6:
                grad = mode_ref[layer, k]
            elif k < 9:
                grad = total_ref[0, :, (k - 6) * narrow : (k - 5) * narrow]
            else:
                grad = total_ref[1, :, (k - 9) * narrow : (k - 8) * narrow]
            new = adam(wi[0, k], grad, mi[0, k], vi[0, k], clip, RATE)
            for ref, value in zip(out_i, new):
                ref[0, k] = value
        for k in range(wo.shape[1]):
            if k == 0:
                grad = total_ref[0, :, 3 * narrow :]
            else:
                grad = total_ref[2, :, (k - 1) * narrow : k * narrow]
            new = adam(wo[0, k], grad.T, mo[0, k], vo[0, k], clip, RATE)
            for ref, value in zip(out_o, new):
                ref[0, k] = value

    for layer in range(layers):

        @pl.when(pl.program_id(0) == layer)
        def _(layer=layer):
            fill(layer)
            update(layer, sums[layer][0])


def adam_blocks(clip, spot, sums, ins, outs):
    arrays = list(ins) + list(outs)
    grads = [v for group in sums for v in group]
    halves = len(sums[0]) == 5
    results = [shaped(v.shape, F32) for v in arrays]
    block, narrow = ins[0].shape[2:]
    return pl.pallas_call(
        functools.partial(adam_blocks_body, len(sums), halves),
        grid=(ins[0].shape[0],),
        in_specs=[SMEM, SMEM]
        + [whole_block(v.shape) for v in grads]
        + [block_of(v.shape) for v in arrays],
        out_specs=[block_of(v.shape) for v in results],
        out_shape=results,
        scratch_shapes=[pltpu.VMEM((3, block, 4 * narrow), F32)],
        compiler_params=params(58),
        name="adam_blocks",
    )(clip, spot, *grads, *arrays)


def adam_final_body(clip_ref, grad_ref, head_ref, w, m, v, *outs):
    clip = clip_ref[0]
    step = pl.program_id(0)
    last = pl.num_programs(0) - 1

    @pl.when(step < last)
    def _():
        new = adam(w[...], grad_ref[...], m[...], v[...], clip, RATE)
        for ref, value in zip(outs, new):
            ref[...] = value

    @pl.when(step == last)
    def _():
        rows = slice(0, PATCH)
        new = adam(w[rows, :], head_ref[...], m[rows, :], v[rows, :], clip, RATE)
        for ref, value in zip(outs, new):
            ref[rows, :] = value


def adam_final(clip, grad, head, w, m, v):
    width = w.shape[1]
    height = 256
    steps = grad.shape[0] // height
    part = pl.BlockSpec((height, width), lambda c: (c, 0))
    grad_part = pl.BlockSpec((height, width), lambda c: (jnp.minimum(c, steps - 1), 0))
    return pl.pallas_call(
        adam_final_body,
        grid=(steps + 1,),
        in_specs=[SMEM, grad_part, whole_block(head.shape)] + [part] * 3,
        out_specs=[part] * 3,
        out_shape=[shaped(w.shape, F32)] * 3,
        compiler_params=params(58),
        name="adam_final",
    )(clip, grad, head, w, m, v)


def adam_rest_body(rates, clip_ref, *refs):
    clip = clip_ref[0]
    count = len(rates)
    ins, outs = refs[: 4 * count], refs[4 * count :]
    for k, rate in enumerate(rates):
        w, g, m, v = [r[...] for r in ins[4 * k : 4 * k + 4]]
        for ref, value in zip(outs[3 * k : 3 * k + 3], adam(w, g, m, v, clip, rate)):
            ref[...] = value


def adam_rest(clip, groups):
    vmem = pl.BlockSpec(memory_space=pltpu.VMEM)
    arrays, results, rates = [], [], []
    for w, g, m, v, rate in groups:
        arrays += [w, g, m, v]
        results += [shaped(w.shape, F32)] * 3
        rates.append(rate)
    return pl.pallas_call(
        functools.partial(adam_rest_body, tuple(rates)),
        in_specs=[SMEM] + [vmem] * len(arrays),
        out_specs=[vmem] * len(results),
        out_shape=results,
        compiler_params=pltpu.CompilerParams(vmem_limit_bytes=58 * MIB),
        name="adam_rest",
    )(clip, *arrays)


def squared(values):
    return jnp.sum(values * values)


def position_table(width):
    half = width // 2
    rate = np.exp(-math.log(10000.0) * (np.arange(width) % half) / half)
    angle = np.arange(LEN)[:, None] * rate[None, :]
    table = np.where(np.arange(width)[None, :] < half, np.sin(angle), np.cos(angle))
    return table.astype(np.float32)


def on_device(
    latents,
    noise,
    timesteps,
    labels,
    loss_mask,
    weights_in,
    weights_out,
    time_mlp,
    embed_table,
    final_layer,
    bias_table,
    final_bias,
    momentum_in,
    momentum_out,
    momentum_time,
    momentum_embed,
    momentum_final,
    momentum_bias,
    momentum_final_bias,
    variance_in,
    variance_out,
    variance_time,
    variance_embed,
    variance_final,
    variance_bias,
    variance_final_bias,
):
    layers, block, _, narrow = weights_in.shape
    place = Place(block)
    rows, cols = place.rows, place.cols
    width = final_layer.shape[0]
    row_samples = timesteps.shape[0]
    samples = row_samples // cols
    every_sample = row_samples * rows
    tokens = samples * LEN
    base = layers * 14
    hidden_blocks = weights_out.shape[1] - 1

    def my_cols(v, axis):
        return lax.dynamic_slice_in_dim(v, place.col * narrow, narrow, axis)

    in_view = [jnp.transpose(v, (0, 2, 1, 3)) for v in (weights_in, momentum_in, variance_in)]
    packed, mode_low = pack_weights(in_view[0], weights_out)

    embed_low = embed_table.astype(BF16)
    one_hot_row = (labels[:, None] == jnp.arange(CLASSES, dtype=jnp.int32)[None, :]).astype(BF16)
    class_rows = jnp.dot(
        one_hot_row, embed_low[:CLASSES], preferred_element_type=F32
    ).astype(BF16)
    half_freq = FREQ // 2
    freq_rate = jnp.asarray(
        np.exp(-math.log(10000.0) * np.arange(half_freq) / half_freq).astype(np.float32)
    )
    angle_grid = timesteps.astype(F32)[:, None] * freq_rate[None, :]
    freq_row = jnp.concatenate([jnp.cos(angle_grid), jnp.sin(angle_grid)], axis=1).astype(BF16)
    time_rows = time_mlp.shape[0]
    mine = jnp.concatenate([bias_table, embed_low[CLASSES:].astype(F32)], axis=0)
    final_view = [v.T for v in (final_layer, momentum_final, variance_final)]
    found = place.found_at()
    sample = jnp.arange(every_sample, dtype=jnp.int32)
    mode_height = -(-(12 * layers + 4) // 16) * 16
    at = jnp.stack([found[sample // samples] * mode_height, sample % samples], axis=1)
    feature = jnp.arange(width, dtype=jnp.int32)[:, None]
    picked = jnp.arange(narrow, dtype=jnp.int32)[None, :] + place.col * narrow
    pick = (feature == picked).astype(BF16)
    spot = jnp.stack([place.row, place.col]).astype(jnp.int32)

    def partial_modes(cond_act):
        cond_rows = lax.dynamic_slice_in_dim(cond_act, place.row * block, block, 1)
        partial = jnp.einsum("sd,lkde->slke", cond_rows, mode_low, preferred_element_type=F32)
        return cond_rows, partial.reshape(every_sample, layers * 6, narrow)

    def own_modes(total, shared, cond_act, final_low):
        bias_full = jnp.swapaxes(shared, 0, 1).reshape(-1, width)
        modes = total.reshape(samples, layers, 6, width) + jnp.stack(
            [bias_full[14 * layer : 14 * layer + 6] for layer in range(layers)]
        )
        own_start = place.row * row_samples + place.col * samples
        cond_own = lax.dynamic_slice_in_dim(cond_act, own_start, samples, 0)
        final_mod = (
            jnp.einsum("sd,ed->se", cond_own, final_low[: 2 * width], preferred_element_type=F32)
            + final_bias[: 2 * width]
        ).reshape(samples, 2, width)
        mods_a = [modes[:, layer, 0:3] for layer in range(layers)]
        mods_b = [modes[:, layer, 3:6] for layer in range(layers)]
        return mods_a, mods_b, final_mod

    own_tokens = place.col * tokens
    latents = lax.dynamic_slice_in_dim(latents, own_tokens, tokens, 0)
    noise = lax.dynamic_slice_in_dim(noise, own_tokens, tokens, 0)
    mask = lax.dynamic_slice_in_dim(loss_mask, own_tokens, tokens, 0).astype(F32)
    steps_own = lax.dynamic_slice_in_dim(timesteps, place.col * samples, samples, 0).astype(F32)
    alpha_bar = jnp.cos((steps_own / STEPS_T + 0.008) / 1.008 * (math.pi / 2)) ** 2
    keep_part = jnp.repeat(jnp.sqrt(alpha_bar), LEN)[:, None]
    noise_part = jnp.repeat(jnp.sqrt(1.0 - alpha_bar), LEN)[:, None]
    noisy = (keep_part * latents + noise_part * noise).astype(BF16)
    position = jnp.asarray(position_table(width))

    def attn_step(layer):
        def work(buffers, x, mods, shared):
            return attention_forward(place, 14 * layer, buffers, x, mods, shared)

        return work

    def mlp_step(layer):
        def work(buffers, x, mods, shared):
            return mlp_forward(place, 14 * layer, buffers, x, mods, shared)

        return work

    def attn_back(buffers, *operands):
        return attention_backward(place, buffers, *operands)

    def mlp_back(buffers, *operands):
        return mlp_backward(place, buffers, *operands)

    def last_step(x, final_mod, final_low):
        return final_step(
            x, final_mod, final_low[2 * width :], final_bias[2 * width :][None], noise, mask[:, None]
        )

    def mode_parts(back_a, back_b, grad_final_mod):
        parts = []
        for layer in range(layers):
            parts += [back_a[layer][1], back_b[layer][1]]
        parts = [v.reshape(-1, width) for v in parts + [grad_final_mod]]
        spare = mode_height - sum(v.shape[0] for v in parts)
        return jnp.concatenate(parts + [jnp.zeros((spare, width), F32)], axis=0).astype(BF16)

    start = 16 * layers + 2 * PATCH
    height = -(-(start + 16) // 32) * 32

    def collected(back_a, back_b, last):
        small = []
        for layer in range(layers):
            _, dmod_a, dbias_a, dtail_a = back_a[layer]
            _, dmod_b, dbias_b, dtail_b = back_b[layer]
            small += [dmod_a, dmod_b, dbias_a, dbias_b, dtail_a, dtail_b]
        _, loss_parts, grad_head, grad_head_bias, grad_final_mod = last
        small += [grad_head, grad_head_bias, loss_parts, mask[:, None], grad_final_mod]
        small += [back_a[0][0], noisy]
        return collect(layers, small, height, width)

    buffers = [None] * (2 * layers)
    fore_a, fore_b = [None] * layers, [None] * layers
    entry = [None] * layers
    back_a, back_b = [None] * layers, [None] * layers
    summed = [None] * (2 * layers)
    if place.direct and layers == 2:
        stages = Stages()
        halves = packed.reshape(3 * layers, 2, place.half, packed.shape[2])
        kept = lax.dynamic_index_in_dim(halves, place.core, 1, False)
        sent = lax.dynamic_index_in_dim(halves, 1 - place.core, 1, False)
        (got,), _ = stages.run([(swap_core, sent)])
        a0, b0, a1, b1 = [
            Spread(kept[k : k + n], got[k : k + n]) for k, n in ((0, 1), (1, 2), (3, 1), (4, 2))
        ]
        wide = jnp.broadcast_to
        own_block = jnp.concatenate(
            [
                time_mlp.astype(BF16).T,
                class_rows[:, :128],
                jnp.pad(class_rows[:, 128:], ((0, 0), (0, 256 - narrow))),
                freq_row[:, :128],
                freq_row[:, 128:],
                wide((labels // 32).astype(BF16)[:, None], (row_samples, 128)),
                wide((labels % 32).astype(BF16)[:, None], (row_samples, 128)),
            ],
            axis=0,
        )
        got, (near, shared) = stages.run(
            a0.at_once(),
            [
                (near_rows, own_block),
                (functools.partial(gather_cols, place), mine),
            ],
        )
        a0.along_at_once(got)
        got, (near, residual) = stages.run(
            a0.first() + b0.far(),
            [
                (near_x, near),
                (functools.partial(embed_tokens, base), noisy, shared, position),
            ],
        )

        def condition_work(near, shared, found):
            near = near_core(near)
            got = condition_step(base, found, near, shared, every_sample, width)
            return near, got, partial_modes(got[1])

        got, ((near, conditions, (cond_rows, partial)),) = stages.run(
            a0.second(got[0]) + b0.near(got[1]),
            [(condition_work, near, shared, found)],
            a0.core(),
        )
        b0.along(got[1])
        condition, cond_act, first_time, first_act, freq_low, all_labels = conditions
        core = got[2]
        got, (total,) = stages.run(
            b0.first() + a1.far() + a0.late_core(got[0]),
            [(functools.partial(scatter_y, place), partial)],
        )
        buffers[0] = a0.buffers(core, got[2])

        two = a1.near(got[1])[0][1]

        def scatter_work(total, two):
            blocks = swap_near(two)
            total, blocks = lax.optimization_barrier((scatter_z(place, total), blocks))
            return blocks, scatter_x(place, total, samples)

        got, ((blocks, total), final_low) = stages.run(
            b0.second(got[0]) + b0.core(),
            [(scatter_work, total, two), (lambda v: v.astype(BF16), final_view[0])],
        )
        a1.along(blocks)
        core = got[1]

        def modes_work(total, shared, cond_act):
            return own_modes(scatter_core(place, total), shared, cond_act, final_low)

        got, ((mods_a, mods_b, final_mod),) = stages.run(
            b1.far() + b0.late_core(got[0]),
            [(modes_work, total, shared, cond_act)],
            a1.first(),
        )
        buffers[1] = b0.buffers(core, got[1])
        got = [got[2], got[0]]
        got, (fore_a[0],) = stages.run(
            a1.second(got[0]) + b1.near(got[1]) + a1.core(),
            [(attn_step(0), buffers[0], residual, mods_a[0], shared)],
        )
        b1.along(got[1])
        core = got[2]
        got, (fore_b[0],) = stages.run(
            b1.first() + a1.late_core(got[0]),
            [(mlp_step(0), buffers[1], fore_a[0][0], mods_b[0], shared)],
        )
        buffers[2] = a1.buffers(core, got[1])
        got, (fore_a[1],) = stages.run(
            b1.second(got[0]) + b1.core(),
            [(attn_step(1), buffers[2], fore_b[0][0], mods_a[1], shared)],
        )
        core = got[1]
        got, _ = stages.run(b1.late_core(got[0]))
        buffers[3] = b1.buffers(core, got[0])
        got, (fore_b[1],) = stages.run(
            [(swap_x, mode_low)], [(mlp_step(1), buffers[3], fore_a[1][0], mods_b[1], shared)]
        )
        mode_half = pair(place.x, mode_low, got[0])
        entry = [residual, fore_b[0][0]]
        last = last_step(fore_b[1][0], final_mod, final_low)

        def back_b_work(layer, grad):
            out, h, u, m = fore_b[layer]
            return (mlp_back, buffers[2 * layer + 1], grad, fore_a[layer][0], mods_b[layer], m, h, u)

        def back_a_work(layer, grad):
            out, h, qkv, p, o, a = fore_a[layer]
            return (
                attn_back, buffers[2 * layer], grad, entry[layer], mods_a[layer], a, h, qkv, p, o,
            )

        got, ((back_b[1], grads),) = stages.run(
            [(swap_core, mode_half)], [back_b_work(1, last[0])]
        )
        mode_full = jnp.swapaxes(pair(place.core, mode_half, got[0]), 0, 1)
        mode_full = mode_full.reshape((4,) + mode_low.shape)
        gb1 = Gathered(grads)
        got, ((back_a[1], grads),) = stages.run(gb1.core, [back_a_work(1, back_b[1][0])])
        ga1 = Gathered(grads)
        got, ((back_b[0], grads),) = stages.run(
            gb1.first(got[0]) + ga1.core, [back_b_work(0, back_a[1][0])]
        )
        core_a1 = got[1]
        gb0 = Gathered(grads)
        got, ((back_a[0], grads),) = stages.run(
            gb1.second(got[0]) + ga1.first(core_a1) + gb0.core, [back_a_work(0, back_b[0][0])]
        )
        zn_b1 = gb1.near(got[0])
        ga0 = Gathered(grads)

        def sum_work(back_a, back_b, last):
            return sum_along_z(place, collected(back_a, back_b, last))

        moded = mode_parts(back_a, back_b, last[4])
        t2_a1 = ga1.second(got[1])
        got, (near_modes, small) = stages.run(
            gb0.first(got[2]) + ga0.core,
            [(near_z, moded), (sum_work, back_a, back_b, last)],
            zn_b1,
        )
        got = [got[0], got[2], got[1]]
        t2_b0 = gb0.second(got[0])
        got, (near_modes, small) = stages.run(
            ga0.first(got[2]) + t2_a1 + gb1.far(got[1]),
            [(near_y, near_modes), (sum_with(swap_core), small)],
        )
        total_b1 = gb1.total(got[2])
        t2_a0 = ga0.second(got[0])
        got, (near_modes, small) = stages.run(
            t2_b0 + ga1.near(got[1]), [(near_x, near_modes), (sum_with(swap_x), small)]
        )
        got, (near_modes, small) = stages.run(
            gb0.near(got[0]) + ga1.far(got[1]),
            [(near_core, near_modes), (sum_with(swap_y), small)],
            t2_a0,
        )
        got = [got[2], got[1], got[0]]
        total_a1 = ga1.total(got[1])

        def modes_back_work(near):
            return modes_backward(near, at, cond_rows, pick, mode_full, cond_act, final_low)

        got, (moded, small) = stages.run(
            gb0.far(got[2]) + ga0.near(got[0]),
            [(modes_back_work, near_modes), (functools.partial(sum_spread, place), small)],
        )
        total_b0 = gb0.total(got[0])
        time_inputs = lax.dynamic_slice_in_dim(
            jnp.concatenate([freq_low, first_act], axis=1), place.row * time_rows, time_rows, 1
        )
        got, (part,) = stages.run(ga0.far(got[1]), [(near_z_at_once, moded[1])])
        total_a0 = ga0.total(got[0])
        part = near_y(part)
        ends = condition_back(
            layers, hidden_blocks, found, spot, small, part, moded[4], moded[5], condition,
            first_time, time_inputs, all_labels, pick, near,
        )
        late = swap_core(
            jnp.concatenate([total_b1[1], total_b0[1], total_a1[1], total_a0[1]])
        )
        summed = [total_a0, total_b0, total_a1, total_b1]
        sums = [
            (moded[0], total_a0, late[5:6], total_b0, late[2:4]),
            (moded[0], total_a1, late[4:5], total_b1, late[0:2]),
        ]
        time_grad, embed_grad, bias_grad, own_part, shared_part = ends
        own_squares = own_part[0, 0] + moded[2][0, 0]
        shared_squares = shared_part[0, 0]
        final_grad = moded[3]
    else:
        final_low = final_view[0].astype(BF16)
        shared = gather_cols(place, mine)
        time_full = lax.all_gather(time_mlp.astype(BF16), "row", axis=0, tiled=True)
        time_full = lax.all_gather(time_full, "col", axis=1, tiled=True)
        class_full = lax.all_gather(class_rows, "col", axis=1, tiled=True)
        class_full = lax.all_gather(class_full, "row", axis=0, tiled=True).astype(F32)
        freq_low = lax.all_gather(freq_row, "row", axis=0, tiled=True)
        all_labels = lax.all_gather(labels, "row", axis=0, tiled=True)
        bias_full = jnp.swapaxes(shared, 0, 1).reshape(-1, width)
        first_time = (
            jnp.dot(freq_low, time_full[:FREQ], preferred_element_type=F32) + bias_full[base]
        )
        first_act = jax.nn.silu(first_time).astype(BF16)
        condition = (
            jnp.dot(first_act, time_full[FREQ:], preferred_element_type=F32)
            + bias_full[base + 1]
            + class_full
        )
        cond_act = jax.nn.silu(condition).astype(BF16)
        cond_rows, partial = partial_modes(cond_act)
        mods_a, mods_b, final_mod = own_modes(
            scatter_plain(place, partial, samples), shared, cond_act, final_low
        )
        grad = embed_tokens(base, noisy, shared, position)
        for layer in range(layers):
            buffers[2 * layer] = [plain_gather(packed[3 * layer : 3 * layer + 1])]
            buffers[2 * layer + 1] = [plain_gather(packed[3 * layer + 1 : 3 * layer + 3])]
            entry[layer] = grad
            fore_a[layer] = attn_step(layer)(buffers[2 * layer], grad, mods_a[layer], shared)
            grad = fore_a[layer][0]
            fore_b[layer] = mlp_step(layer)(buffers[2 * layer + 1], grad, mods_b[layer], shared)
            grad = fore_b[layer][0]
        last = last_step(grad, final_mod, final_low)
        grad = last[0]
        for layer in reversed(range(layers)):
            out, h, u, m = fore_b[layer]
            back_b[layer], grads = mlp_back(
                buffers[2 * layer + 1], grad, fore_a[layer][0], mods_b[layer], m, h, u
            )
            summed[2 * layer + 1] = plain_scatter(grads[0])
            grad = back_b[layer][0]
            out, h, qkv, p, o, a = fore_a[layer]
            back_a[layer], grads = attn_back(
                buffers[2 * layer], grad, entry[layer], mods_a[layer], a, h, qkv, p, o
            )
            summed[2 * layer] = plain_scatter(grads[0])
            grad = back_a[layer][0]
        mode_full = lax.all_gather(mode_low, "col")
        near = gather_near(place, mode_parts(back_a, back_b, last[4]))
        moded = modes_backward_plain(
            near, cond_rows, mode_full, cond_act, final_low, place.col
        )
        mode_blocks, part, square, final_grad, cond_final, final_squares = moded
        own_squares = square[0, 0]
        small = lax.psum(collected(back_a, back_b, last), ("row", "col"))
        grad_cond = lax.all_gather(part, "row", axis=1, tiled=True) + cond_final
        grad_condition = grad_cond * silu_slope(condition)
        one_hot = (all_labels[:, None] == jnp.arange(CLASSES, dtype=jnp.int32)[None, :]).astype(F32)
        grad_classes = jnp.einsum(
            "sd,sc->dc", my_cols(grad_condition, 1), one_hot, precision=HIGHEST
        )
        condition_low = grad_condition.astype(BF16)
        grad_first = jnp.einsum(
            "se,de->sd", condition_low, time_full[FREQ:], preferred_element_type=F32
        ) * silu_slope(first_time)
        time_inputs = lax.dynamic_slice_in_dim(
            jnp.concatenate([freq_low, first_act], axis=1), place.row * time_rows, time_rows, 1
        )
        time_outputs = jnp.where(
            (place.row + 1) * time_rows <= FREQ, grad_first.astype(BF16), condition_low
        )
        time_grad = jnp.einsum(
            "sd,se->ed", time_inputs, my_cols(time_outputs, 1), preferred_element_type=F32
        )
        own_rows, shared_squares = [], jnp.zeros((), F32)
        for layer in range(layers):
            rows_at = small[16 * layer : 16 * layer + 16]
            own = my_cols(rows_at, 1)
            mlp_rows = lax.dynamic_index_in_dim(rows_at[6:10], place.col, 0, False)
            attn_rows = lax.dynamic_index_in_dim(rows_at[10:14], place.col, 0, False)
            attn_rows = attn_rows[: 3 * narrow].reshape(3, narrow)
            own_rows += [own[:6], attn_rows[0:1], attn_rows[2:3]]
            own_rows += [mlp_rows.reshape(hidden_blocks, narrow), own[14:16]]
            counted = rows_at[10:14, : 3 * narrow].reshape(4, 3, narrow)[:, 0::2]
            shared_squares = (
                shared_squares + squared(rows_at[:10]) + squared(counted) + squared(rows_at[14:])
            )
        time_bias = jnp.stack([jnp.sum(grad_first, axis=0), jnp.sum(grad_condition, axis=0)])
        own_rows += [my_cols(time_bias, 1), my_cols(small[start : start + 1], 1)]
        bias_grad = jnp.concatenate(own_rows, axis=0)
        shared_squares = (
            shared_squares
            + squared(time_bias)
            + squared(small[start - 2 * PATCH : start + 3])
            + squared(small[start + 3, :PATCH])
            + final_squares[0, 0]
        )
        own_squares = own_squares + squared(time_grad) + squared(grad_classes) / rows
        sums = [(mode_blocks, summed[2 * k], summed[2 * k + 1]) for k in range(layers)]
        patch_grad = my_cols(small[start - PATCH : start], 1)
        embed_grad = jnp.concatenate([grad_classes, patch_grad.T], axis=1)

    head_grad = small[start - 2 * PATCH : start - PATCH]
    final_bias_grad = jnp.concatenate(
        [small[start + 1], small[start + 2], small[start + 3, :PATCH]]
    )
    loss_total = jnp.sum(small[start + 4, :PATCH])
    count_total = small[start + 5, 0]
    for value in summed:
        own_squares = own_squares + squared(value)
    grad_norm = jnp.sqrt(sum_scalar(place, own_squares) + shared_squares)
    clip_factor = jnp.minimum(1.0, CLIP_NORM / (grad_norm + 1e-06))
    clip = clip_factor[None]

    results = [loss_total, count_total, grad_norm]
    new_blocks = adam_blocks(clip, spot, sums, in_view, [weights_out, momentum_out, variance_out])
    results += [jnp.transpose(v, (0, 2, 1, 3)) for v in new_blocks[:3]] + list(new_blocks[3:])
    rest = adam_rest(
        clip,
        [
            (time_mlp.T, time_grad, momentum_time.T, variance_time.T, RATE),
            (embed_table.T, embed_grad, momentum_embed.T, variance_embed.T, RATE),
            (bias_table, bias_grad, momentum_bias, variance_bias, RATE_BIAS),
        ],
    )
    results += [v.T for v in rest[:6]]
    results += [v.T for v in adam_final(clip, final_grad, head_grad, *final_view)]
    results += list(rest[6:9])
    results += adam(
        final_bias, final_bias_grad, momentum_final_bias, variance_final_bias, clip_factor,
        RATE_BIAS,
    )
    return tuple(results)


def solution(mesh):
    tokens, latents = P("row", None), P("row")
    weights = (
        P(None, "row", None, "col"),
        P(None, None, "col", "row"),
        P("row", "col"),
        P(None, "col"),
        P(),
        P(None, "col"),
        P(),
    )
    updated = []
    for spec in weights:
        updated += [spec] * 3
    return jax.shard_map(
        on_device,
        mesh=mesh,
        in_specs=(tokens, tokens, latents, latents, latents) + weights * 3,
        out_specs=(P(), P(), P()) + tuple(updated),
        check_vma=False,
    )
```

```python
import functools
import math

import jax
import jax.numpy as jnp
import numpy as np
from jax import lax
from jax.experimental import pallas as pl
from jax.experimental.pallas import tpu as pltpu
from jax.sharding import PartitionSpec as P

HEAD_DIM = 64
CLASSES = 1000
FREQ = 256
PATCH = 16
LEN = 256
STEPS_T = 1000
STEP = 10

HIGHEST = lax.Precision.HIGHEST
EPS_NORM = 1e-06
CLIP_NORM = 1.0
RATE = 0.05
RATE_BIAS = 0.25
BETA_ONE = 0.9
BETA_TWO = 0.999
DECAY = 0.01
ADAM_EPS = 1e-08

F32 = jnp.float32
BF16 = jnp.bfloat16
MIB = 1024 * 1024
ANY = pl.BlockSpec(memory_space=pl.ANY)
SMEM = pl.BlockSpec(memory_space=pltpu.SMEM)
NT = (((1,), (1,)), ((), ()))
TN = (((0,), (0,)), ((), ()))


def dot_nt(a, b):
    return lax.dot_general(a, b, NT, preferred_element_type=F32)


def dot_tn(a, b):
    return lax.dot_general(a, b, TN, preferred_element_type=F32)


def dot_nn(a, b):
    return jnp.dot(a, b, preferred_element_type=F32)


def along(k):
    return k % 2 * 2 + k // 2


class Place:
    def __init__(self, row_block):
        self.rows = lax.axis_size("row")
        self.cols = lax.axis_size("col")
        self.row = lax.axis_index("row")
        self.col = lax.axis_index("col")
        self.direct = self.rows == 8 and self.cols == 4 and row_block % 32 == 0
        self.z = self.row // 2
        self.y = self.row % 2
        self.x = self.col // 2
        self.core = self.col % 2
        self.half = row_block // 2
        self.table = self.route_table() if self.direct else jnp.zeros((8,), jnp.int32)

    def route_table(self):
        z, y, x, core = self.z, self.y, self.x, self.core
        e = jnp.arange(64, dtype=jnp.int32)
        owner = core ^ (e // 32)
        later, first, kc, kz = e // 16 % 2, e // 8 % 2, e // 4 % 2, e % 4
        kx = jnp.where(owner == 0, first, later)
        ky = jnp.where(owner == 0, later, first)
        cols = (x ^ kx) * 2 + (owner ^ kc)
        rows = ((z ^ along(kz)) * 2 + (y ^ ky)) * 2 * self.half + owner * self.half
        e = jnp.arange(16, dtype=jnp.int32)
        col, owner, ky = e // 4, core ^ (e // 2 % 2), e % 2
        kx = (col // 2) ^ x
        later = jnp.where(owner == 0, ky, kx)
        first = jnp.where(owner == 0, kx, ky)
        slots = jnp.stack([later, first, (col % 2) ^ owner], axis=1).reshape(-1)
        owner, ky, kz = core ^ (e // 8), e // 4 % 2, e % 4
        outs = ((z ^ along(kz)) * 2 + (y ^ ky)) * 2 * self.half + owner * self.half
        step = jnp.arange(4, dtype=jnp.int32)
        order = (x ^ (step % 2)) * 2 + (core ^ (step // 2))
        return jnp.concatenate([cols, rows, slots, outs, order, core[None]]).astype(jnp.int32)

    def found_at(self):
        device = jnp.arange(self.rows * self.cols, dtype=jnp.int32)
        if not self.direct:
            return device
        row, col = device // 4, device % 4
        kz = along(row // 2 ^ self.z)
        ky = (row % 2) ^ self.y
        kx = (col // 2) ^ self.x
        kc = (col % 2) ^ self.core
        return ((kc * 2 + kx) * 2 + ky) * 4 + kz


def swap_x(v):
    return lax.ppermute(v, "col", [(c, c ^ 2) for c in range(4)])


def swap_core(v):
    return lax.ppermute(v, "col", [(c, c ^ 1) for c in range(4)])


def swap_y(v):
    return lax.ppermute(v, "row", [(r, r ^ 1) for r in range(8)])


def swap_first(v):
    pairs = [(d, d ^ 2 if d % 2 == 0 else d ^ 4) for d in range(32)]
    return lax.ppermute(v, ("row", "col"), pairs)


def swap_second(v):
    pairs = [(d, d ^ 4 if d % 2 == 0 else d ^ 2) for d in range(32)]
    return lax.ppermute(v, ("row", "col"), pairs)


def swap_far(v):
    return lax.ppermute(v, "row", [(r, r ^ 4) for r in range(8)])


def swap_near(v):
    return lax.ppermute(v, "row", [(r, r ^ 2) for r in range(8)])


def swap_across(v):
    return lax.ppermute(v, ("row", "col"), [(d, d ^ 6) for d in range(32)])


def swap_beyond(v):
    return lax.ppermute(v, "row", [(r, r ^ 6) for r in range(8)])


def pair(index, own, other):
    first = index == 0
    return jnp.stack([jnp.where(first, own, other), jnp.where(first, other, own)])


def gather_cols(place, own):
    if not place.direct:
        return lax.all_gather(own, "col")
    both = pair(place.core, own, swap_core(own))
    return pair(place.x, both, swap_x(both)).reshape((4,) + own.shape)


def near_z(own):
    both = jnp.stack([own, swap_far(own)])
    return jnp.concatenate([both, swap_near(both)])


def near_z_at_once(own):
    return jnp.stack([own, swap_far(own), swap_near(own), swap_beyond(own)])


def near_y(every):
    return jnp.concatenate([every, swap_y(every)])


def near_rows(own):
    return near_y(near_z(own))


def near_x(every):
    return jnp.concatenate([every, swap_x(every)])


def near_core(every):
    return jnp.concatenate([every, swap_core(every)])


def near_cols(every):
    return near_core(near_x(every))


def gather_near(place, own):
    if not place.direct:
        return lax.all_gather(own, ("row", "col"))
    return near_cols(near_rows(own))


def sum_parts(place, parts):
    z = place.z

    def two(at):
        return jnp.stack([lax.dynamic_index_in_dim(parts, k, 0, False) for k in (at, at ^ 2)])

    total = two(z) + swap_near(two(z ^ 1))
    return total[0] + swap_far(total[1])


def sum_along_z(place, own):
    return sum_parts(place, own.reshape((4, own.shape[0] // 4) + own.shape[1:]))


def sum_with(swap):
    return lambda total: total + swap(total)


def sum_spread(place, total):
    far = pair(place.z // 2, total, swap_far(total))
    every = pair(place.z % 2, far, swap_near(far))
    return jnp.swapaxes(every, 0, 1).reshape((-1,) + total.shape[1:])


def sum_scalar(place, value):
    if not place.direct:
        return lax.psum(value, ("row", "col"))
    total = jnp.broadcast_to(value, (8, 128))
    total = total + swap_far(total) + (swap_near(total) + swap_beyond(total))
    total = total + swap_x(total) + (swap_y(total) + swap_across(total))
    total = total + swap_core(total)
    return total[0, 0]


def scatter_plain(place, partial, mine):
    _, count, narrow = partial.shape
    summed = lax.psum_scatter(partial, "row", scatter_dimension=0, tiled=True)
    spread = lax.all_gather(summed, "col")
    spread = lax.dynamic_slice_in_dim(spread, place.col * mine, mine, 1)
    return jnp.transpose(spread, (1, 2, 0, 3)).reshape(mine, count, place.cols * narrow)


def scatter_y(place, partial):
    samples, count, narrow = partial.shape
    by_y = partial.reshape(4, 2, samples // 8, count, narrow)
    own = lax.dynamic_index_in_dim(by_y, place.y, 1, False)
    return own + swap_y(lax.dynamic_index_in_dim(by_y, 1 - place.y, 1, False))


def scatter_z(place, own):
    return sum_parts(place, own)


def scatter_x(place, total, mine):
    _, count, narrow = total.shape
    by_x = total.reshape(2, 2, mine, count, narrow)
    own = lax.dynamic_index_in_dim(by_x, place.x, 0, False)
    got = swap_x(lax.dynamic_index_in_dim(by_x, 1 - place.x, 0, False))
    return pair(place.x, own, got)


def scatter_core(place, both):
    _, _, mine, count, narrow = both.shape
    own = lax.dynamic_index_in_dim(both, place.core, 1, False)
    got = swap_core(lax.dynamic_index_in_dim(both, 1 - place.core, 1, False))
    every = pair(place.core, own, got)
    return jnp.transpose(every, (2, 3, 1, 0, 4)).reshape(mine, count, 4 * narrow)


class Route:
    def __init__(self, place, buffers):
        self.direct = place.direct
        self.half = place.half
        self.cols = place.cols
        self.count = len(buffers)
        if self.direct:
            matrices = buffers[0].shape[2]
            self.outs = [(2, 8, 2, matrices) + buffers[0].shape[3:]] * 2
        else:
            self.outs = [buffers[0].shape]

    def column(self, table, step):
        return table[192 + step] if self.direct else step

    def load(self, table, buffers, moves):
        if not self.direct:
            for c in range(self.cols):
                for matrix, target, sems in moves:
                    pltpu.make_async_copy(
                        buffers[0].at[matrix, c], target.at[c], sems.at[c]
                    ).start()
            return
        for core in range(2):

            @pl.when(table[196] == core)
            def _(core=core):
                entries = []
                for e in range(64):
                    owner, later, first, kc = core ^ (e // 32), e // 16 % 2, e // 8 % 2, e // 4 % 2
                    kx = first if owner == 0 else later
                    entries.append(((owner ^ kc ^ core) * 2 + kx, e))
                for step in range(4):
                    for matrix, target, sems in moves:
                        for at, e in entries:
                            if at != step:
                                continue
                            row = pl.multiple_of(table[64 + e], 16)
                            pltpu.make_async_copy(
                                buffers[e // 16].at[e // 8 % 2 * 4 + e % 4, e // 4 % 2, matrix],
                                target.at[step, pl.ds(row, self.half), :],
                                sems.at[step],
                            ).start()

    def store(self, table, c, matrix, source, grads, sem):
        if not self.direct:
            pltpu.make_async_copy(source, grads[0].at[matrix, c], sem).start()
            return
        for owner in range(2):
            for ky in range(2):
                at = 128 + ((c * 2 + owner) * 2 + ky) * 3
                for kz in range(4):
                    row = pl.multiple_of(table[176 + (owner * 2 + ky) * 4 + kz], 16)
                    pltpu.make_async_copy(
                        source.at[pl.ds(row, self.half), :],
                        grads[owner].at[
                            table[at], table[at + 1] * 4 + kz, table[at + 2], matrix
                        ],
                        sem,
                    ).start()


class Stages:
    def __init__(self):
        self.last = None

    def run(self, moves, works=(), late=()):
        operands = ([v for _, v in moves], [w[1:] for w in works], [v for _, v in late])
        if self.last is not None:
            operands, _ = lax.optimization_barrier((operands, self.last))
        moved = [move(v) for (move, _), v in zip(moves, operands[0])]
        done = [w[0](*v) for w, v in zip(works, operands[1])]
        if late:
            held, _ = lax.optimization_barrier((operands[2], done))
            moved += [move(v) for (move, _), v in zip(late, held)]
        self.last = (moved, done)
        return moved, done


class Spread:
    def __init__(self, kept, got):
        self.own = jnp.stack([kept, got])

    def far(self):
        return [(swap_far, self.own)]

    def near(self, got):
        self.two = jnp.stack([self.own, got])
        return [(swap_near, self.two)]

    def at_once(self):
        return [(swap_far, self.own), (swap_near, self.own), (swap_beyond, self.own)]

    def along_at_once(self, got):
        self.z = jnp.stack([self.own] + list(got))

    def along(self, got):
        self.z = jnp.concatenate([self.two, got])

    def first(self):
        return [(swap_first, self.z)]

    def second(self, got):
        self.p = jnp.concatenate([self.z, got])
        return [(swap_second, self.p)]

    def core(self):
        return [(swap_core, self.p)]

    def late_core(self, q):
        self.q = q
        return [(swap_core, q)]

    def buffers(self, core, late_core):
        return [self.p, self.q, core, late_core]


def add_up(*parts):
    total = parts[0].astype(F32)
    for part in parts[1:]:
        total = total + part.astype(F32)
    return total


class Gathered:
    def __init__(self, buffers):
        self.own = buffers[0]
        self.core = [(swap_core, buffers[1])]

    def first(self, got):
        self.got = got
        return [(swap_second, add_up(self.own[1], got[1]).astype(BF16))]

    def second(self, got):
        self.parts = (self.own[0], self.got[0], got)
        return [(swap_first, add_up(*[v[4:] for v in self.parts]).astype(BF16))]

    def near(self, got):
        self.parts = self.parts + (got,)
        return [(swap_near, add_up(*[v[2:4] for v in self.parts]).astype(BF16))]

    def far(self, got):
        self.last = got
        return [(swap_far, add_up(*[v[1] for v in self.parts], got[1]).astype(BF16))]

    def total(self, got):
        return add_up(*[v[0] for v in self.parts], self.last[0], got)


def plain_gather(parts):
    every = lax.all_gather(lax.all_gather(parts, "row", axis=1, tiled=True), "col")
    return jnp.swapaxes(every, 0, 1)


def plain_scatter(grads):
    summed = lax.psum_scatter(grads.astype(F32), "row", scatter_dimension=2, tiled=True)
    return lax.psum_scatter(summed, "col", scatter_dimension=1, tiled=False)


def normal(v):
    center = jnp.mean(v, axis=-1, keepdims=True)
    moved = v - center
    inverse = lax.rsqrt(jnp.mean(moved * moved, axis=-1, keepdims=True) + EPS_NORM)
    return moved * inverse, inverse


def wait_all(ref, sem):
    pltpu.make_async_copy(ref, ref, sem).wait()


def row_of(shared_ref, at):
    return jnp.concatenate(
        [shared_ref[c, at : at + 1, :] for c in range(shared_ref.shape[0])], axis=1
    )


def attention_forward_body(route, base, table, x_ref, mod_ref, shared_ref, *refs):
    n_buf = route.count
    buffers = refs[:n_buf]
    out_ref, h_ref, qkv_ref, p_ref, o_ref, a_ref, w_ref, sems = refs[n_buf:]
    c = pl.program_id(0)
    samples = mod_ref.shape[0]

    @pl.when(c == 0)
    def _():
        route.load(table, buffers, [(0, w_ref, sems)])
        for s in range(samples):
            rows = pl.ds(s * LEN, LEN)
            n, _ = normal(x_ref[rows, :])
            h_ref[rows, :] = (n * (1.0 + mod_ref[s, 1:2]) + mod_ref[s, 0:1]).astype(BF16)
        a_ref[...] = jnp.zeros_like(a_ref)

    wait_all(w_ref.at[c], sems.at[c])
    width = shared_ref.shape[-1]
    col = route.column(table, c)
    query_bias = shared_ref[col, base + 6 : base + 7, :]
    value_bias = shared_ref[col, base + 7 : base + 8, :]
    bias = jnp.concatenate([query_bias, jnp.zeros_like(query_bias), value_bias], axis=1)
    triple = dot_nn(h_ref[...], w_ref[c, :, : 3 * width]) + bias
    qkv_ref[0] = triple.astype(BF16)
    triple = triple.astype(BF16)
    heads = width // HEAD_DIM

    def part(s, k, j):
        at = k * width + j * HEAD_DIM
        return triple[s * LEN : (s + 1) * LEN, at : at + HEAD_DIM]

    each = [(s, j) for s in range(samples) for j in range(heads)]
    scores = [dot_nt(part(s, 1, j), part(s, 0, j)) * HEAD_DIM ** (-0.5) for s, j in each]
    probs = []
    for score in scores:
        powers = jnp.exp(score - jnp.max(score, axis=0, keepdims=True))
        probs.append((powers * (1.0 / jnp.sum(powers, axis=0, keepdims=True))).astype(BF16))
    for (s, j), prob in zip(each, probs):
        p_ref[0, j, s] = prob
    outs = [dot_tn(prob, part(s, 2, j)).astype(BF16) for (s, j), prob in zip(each, probs)]
    for s in range(samples):
        o_ref[0, pl.ds(s * LEN, LEN), :] = jnp.concatenate(
            outs[s * heads : (s + 1) * heads], axis=1
        )
    a_ref[...] += dot_nt(o_ref[0], w_ref[c, :, 3 * width :])

    @pl.when(c == pl.num_programs(0) - 1)
    def _():
        a_ref[...] += row_of(shared_ref, base + 12)
        for s in range(samples):
            rows = pl.ds(s * LEN, LEN)
            out_ref[rows, :] = x_ref[rows, :] + mod_ref[s, 2:3] * a_ref[rows, :]


def mlp_forward_body(route, base, table, x_ref, mod_ref, shared_ref, *refs):
    n_buf = route.count
    buffers = refs[:n_buf]
    out_ref, h_ref, u_ref, m_ref, wi_ref, wo_ref, sems_i, sems_o = refs[n_buf:]
    c = pl.program_id(0)
    samples = mod_ref.shape[0]

    @pl.when(c == 0)
    def _():
        route.load(table, buffers, [(0, wi_ref, sems_i), (1, wo_ref, sems_o)])
        for s in range(samples):
            rows = pl.ds(s * LEN, LEN)
            n, _ = normal(x_ref[rows, :])
            h_ref[rows, :] = (n * (1.0 + mod_ref[s, 1:2]) + mod_ref[s, 0:1]).astype(BF16)
        m_ref[...] = jnp.zeros_like(m_ref)

    wait_all(wi_ref.at[c], sems_i.at[c])
    col = route.column(table, c)
    blocks = wi_ref.shape[-1] // shared_ref.shape[-1]
    bias = jnp.concatenate(
        [shared_ref[col, base + 8 + k : base + 9 + k, :] for k in range(blocks)], axis=1
    )
    hidden = dot_nn(h_ref[...], wi_ref[c]) + bias
    u_ref[0] = hidden
    active = jax.nn.gelu(hidden, approximate=True).astype(BF16)
    wait_all(wo_ref.at[c], sems_o.at[c])
    m_ref[...] += dot_nt(active, wo_ref[c])

    @pl.when(c == pl.num_programs(0) - 1)
    def _():
        m_ref[...] += row_of(shared_ref, base + 13)
        for s in range(samples):
            rows = pl.ds(s * LEN, LEN)
            out_ref[rows, :] = x_ref[rows, :] + mod_ref[s, 2:3] * m_ref[rows, :]


def norm_backward(s, x_ref, mod_ref, dx_ref, dh_ref, out_ref, dmod_ref):
    rows = pl.ds(s * LEN, LEN)
    n, inverse = normal(x_ref[rows, :])
    dh = dh_ref[rows, :]
    dmod_ref[s, 0:1] = jnp.sum(dh, axis=0, keepdims=True)
    dmod_ref[s, 1:2] = jnp.sum(dh * n, axis=0, keepdims=True)
    dn = dh * (1.0 + mod_ref[s, 1:2])
    back = inverse * (
        dn
        - jnp.mean(dn, axis=-1, keepdims=True)
        - n * jnp.mean(dn * n, axis=-1, keepdims=True)
    )
    if dx_ref is None:
        out_ref[rows, :] = back
    else:
        out_ref[rows, :] = dx_ref[rows, :] + back


def branch_gradient(dx_ref, mod_ref, branch_ref, dmod_ref, sum_ref, low_ref):
    total = None
    for s in range(mod_ref.shape[0]):
        rows = pl.ds(s * LEN, LEN)
        dx = dx_ref[rows, :]
        dmod_ref[s, 2:3] = jnp.sum(dx * branch_ref[rows, :], axis=0, keepdims=True)
        db = mod_ref[s, 2:3] * dx
        low_ref[rows, :] = db.astype(BF16)
        part = jnp.sum(db, axis=0, keepdims=True)
        total = part if total is None else total + part
    sum_ref[...] = total


def gelu_slope(u):
    k = math.sqrt(2.0 / math.pi)
    square = u * u
    t = jnp.tanh(k * (u + 0.044715 * square * u))
    half = 0.5 * (1.0 + t)
    slope = half + 0.5 * u * (1.0 - t * t) * (k * (1.0 + 3 * 0.044715 * square))
    return u * half, slope


def mlp_backward_body(
    route, table, dx_ref, x_ref, mod_ref, m_ref, h_ref, u_ref, *refs
):
    n_buf, n_out = route.count, len(route.outs)
    buffers = refs[:n_buf]
    out_ref, dmod_ref, dbias_ref, dtail_ref = refs[n_buf : n_buf + 4]
    grads = refs[n_buf + 4 : n_buf + n_out + 4]
    wi_ref, wo_ref, low_ref, dh_ref, gi_ref, go_ref, sems_i, sems_o, sems_gi, sems_go = refs[
        n_buf + n_out + 4 :
    ]
    c = pl.program_id(0)
    count = route.cols
    samples = mod_ref.shape[0]

    @pl.when(c == 0)
    def _():
        route.load(table, buffers, [(1, wo_ref, sems_o), (0, wi_ref, sems_i)])
        branch_gradient(dx_ref, mod_ref, m_ref, dmod_ref, dtail_ref, low_ref)
        dh_ref[...] = jnp.zeros_like(dh_ref)

    slot = lax.rem(c, 2)

    @pl.when(c >= 2)
    def _():
        wait_all(gi_ref.at[slot], sems_gi.at[slot])
        wait_all(go_ref.at[slot], sems_go.at[slot])

    wait_all(wo_ref.at[c], sems_o.at[c])
    active, slope = gelu_slope(u_ref[0])
    low = low_ref[...]
    go_ref[slot] = dot_tn(low, active.astype(BF16)).astype(BF16)
    route.store(table, route.column(table, c), 1, go_ref.at[slot], grads, sems_go.at[slot])
    du = dot_nn(low, wo_ref[c]) * slope
    dbias_ref[route.column(table, c)] = jnp.sum(du, axis=0, keepdims=True)
    du = du.astype(BF16)
    gi_ref[slot] = dot_tn(h_ref[...], du).astype(BF16)
    route.store(table, route.column(table, c), 0, gi_ref.at[slot], grads, sems_gi.at[slot])
    wait_all(wi_ref.at[c], sems_i.at[c])
    dh_ref[...] += dot_nt(du, wi_ref[c])

    @pl.when(c == count - 1)
    def _():
        for s in range(samples):
            norm_backward(s, x_ref, mod_ref, dx_ref, dh_ref, out_ref, dmod_ref)
        for k in range(2):
            wait_all(gi_ref.at[k], sems_gi.at[k])
            wait_all(go_ref.at[k], sems_go.at[k])


def attention_backward_body(
    route, table, dx_ref, x_ref, mod_ref, a_ref, h_ref, qkv_ref, p_ref, o_ref, *refs
):
    n_buf, n_out = route.count, len(route.outs)
    buffers = refs[:n_buf]
    out_ref, dmod_ref, dbias_ref, dtail_ref = refs[n_buf : n_buf + 4]
    grads = refs[n_buf + 4 : n_buf + n_out + 4]
    w_ref, low_ref, dh_ref, d_ref, g_ref, sems, sems_g = refs[n_buf + n_out + 4 :]
    c = pl.program_id(0)
    count = route.cols
    samples = mod_ref.shape[0]
    width = qkv_ref.shape[-1] // 3
    factor = HEAD_DIM ** (-0.5)

    @pl.when(c == 0)
    def _():
        route.load(table, buffers, [(0, w_ref, sems)])
        branch_gradient(dx_ref, mod_ref, a_ref, dmod_ref, dtail_ref, low_ref)
        dh_ref[...] = jnp.zeros_like(dh_ref)

    slot = lax.rem(c, 2)

    @pl.when(c >= 2)
    def _():
        wait_all(g_ref.at[slot], sems_g.at[slot])

    wait_all(w_ref.at[c], sems.at[c])
    do_all = dot_nn(low_ref[...], w_ref[c, :, 3 * width :]).astype(BF16)
    heads = width // HEAD_DIM
    each = [(s, j) for s in range(samples) for j in range(heads)]

    def part(s, k, j):
        at = k * width + j * HEAD_DIM
        return qkv_ref[0, pl.ds(s * LEN, LEN), at : at + HEAD_DIM]

    def given(s, j):
        return do_all[s * LEN : (s + 1) * LEN, j * HEAD_DIM : (j + 1) * HEAD_DIM]

    dps = [dot_nt(part(s, 2, j), given(s, j)) for s, j in each]
    dss = []
    for (s, j), dp in zip(each, dps):
        probs = p_ref[0, j, s].astype(F32)
        delta = jnp.sum(probs * dp, axis=0, keepdims=True)
        dss.append((probs * (dp - delta)).astype(BF16))
    dqs = [dot_tn(ds, part(s, 1, j)) * factor for (s, j), ds in zip(each, dss)]
    dks = [dot_nn(ds, part(s, 0, j)) * factor for (s, j), ds in zip(each, dss)]
    dvs = [dot_nn(p_ref[0, j, s], given(s, j)) for s, j in each]
    sums = None
    for s in range(samples):
        at = slice(s * heads, (s + 1) * heads)
        joined = jnp.concatenate(dqs[at] + dks[at] + dvs[at], axis=1)
        total = jnp.sum(joined, axis=0, keepdims=True)
        sums = total if s == 0 else sums + total
        d_ref[pl.ds(s * LEN, LEN), :] = joined.astype(BF16)
    dbias_ref[route.column(table, c)] = sums
    grad_in = dot_tn(h_ref[...], d_ref[...])
    grad_out = dot_tn(low_ref[...], o_ref[0])
    g_ref[slot] = jnp.concatenate([grad_in, grad_out], axis=1).astype(BF16)
    route.store(table, route.column(table, c), 0, g_ref.at[slot], grads, sems_g.at[slot])
    dh_ref[...] += dot_nt(d_ref[...], w_ref[c, :, : 3 * width])

    @pl.when(c == count - 1)
    def _():
        for s in range(samples):
            norm_backward(s, x_ref, mod_ref, dx_ref, dh_ref, out_ref, dmod_ref)
        for k in range(2):
            wait_all(g_ref.at[k], sems_g.at[k])


def final_body(
    x_ref, mod_ref, head_ref, bias_ref, noise_ref, mask_ref,
    dx_ref, loss_ref, dhead_ref, dbias_ref, dmod_ref, h_ref, dh_ref,
):
    samples = mod_ref.shape[0]
    for s in range(samples):
        rows = pl.ds(s * LEN, LEN)
        n, _ = normal(x_ref[rows, :])
        h_ref[rows, :] = (n * (1.0 + mod_ref[s, 1:2]) + mod_ref[s, 0:1]).astype(BF16)
    predicted = dot_nt(h_ref[...], head_ref[...]) + bias_ref[...]
    error = predicted - noise_ref[...]
    masked = mask_ref[...] * error
    loss_ref[...] = jnp.sum(masked * error, axis=0, keepdims=True)
    dpred = 2.0 * masked
    dbias_ref[...] = jnp.sum(dpred, axis=0, keepdims=True)
    low = dpred.astype(BF16)
    dhead_ref[...] = dot_tn(low, h_ref[...])
    dh_ref[...] = dot_nn(low, head_ref[...])
    for s in range(samples):
        norm_backward(s, x_ref, mod_ref, None, dh_ref, dx_ref, dmod_ref)


def whole_block(shape):
    rank = len(shape)
    return pl.BlockSpec(shape, lambda c: (0,) * rank, pipeline_mode=pl.Buffered(1))


def whole_out(shape):
    rank = len(shape)
    return pl.BlockSpec(shape, lambda c: (0,) * rank)


def block_of(shape):
    rank = len(shape)
    return pl.BlockSpec((1,) + tuple(shape[1:]), lambda c: (c,) + (0,) * (rank - 1))


def params(mib):
    return pltpu.CompilerParams(
        dimension_semantics=("arbitrary",), vmem_limit_bytes=mib * MIB
    )


def cost(flops, nbytes, exps=0):
    return pl.CostEstimate(flops=int(flops), bytes_accessed=int(nbytes), transcendentals=int(exps))


def shaped(shape, dtype):
    return jax.ShapeDtypeStruct(tuple(shape), dtype)


def attention_forward(place, base, buffers, x, mods, shared):
    route = Route(place, buffers)
    count = place.cols
    tokens, width = x.shape
    samples = mods.shape[0]
    narrow = shared.shape[-1]
    heads = narrow // HEAD_DIM
    outs = [
        shaped((tokens, width), F32),
        shaped((tokens, width), BF16),
        shaped((count, tokens, 3 * narrow), BF16),
        shaped((count, heads, samples, LEN, LEN), BF16),
        shaped((count, tokens, narrow), BF16),
        shaped((tokens, width), F32),
    ]
    return pl.pallas_call(
        functools.partial(attention_forward_body, route, base),
        grid=(count,),
        in_specs=[SMEM, whole_block(x.shape), whole_block(mods.shape), whole_block(shared.shape)]
        + [ANY] * len(buffers),
        out_specs=[whole_out(outs[0].shape), whole_out(outs[1].shape)]
        + [block_of(o.shape) for o in outs[2:5]]
        + [whole_out(outs[5].shape)],
        out_shape=outs,
        scratch_shapes=[
            pltpu.VMEM((count, width, 4 * narrow), BF16),
            pltpu.SemaphoreType.DMA((count,)),
        ],
        compiler_params=params(58),
        cost_estimate=cost(
            2 * tokens * width * width * 4 + 4 * tokens * LEN * width,
            8 * width * width + 30 * tokens * width,
            tokens * LEN * width // HEAD_DIM,
        ),
        name="attention_forward",
    )(place.table, x, mods, shared, *buffers)


def mlp_forward(place, base, buffers, x, mods, shared):
    route = Route(place, buffers)
    count = place.cols
    tokens, width = x.shape
    wide = buffers[0].shape[-1]
    outs = [
        shaped((tokens, width), F32),
        shaped((tokens, width), BF16),
        shaped((count, tokens, wide), F32),
        shaped((tokens, width), F32),
    ]
    return pl.pallas_call(
        functools.partial(mlp_forward_body, route, base),
        grid=(count,),
        in_specs=[SMEM, whole_block(x.shape), whole_block(mods.shape), whole_block(shared.shape)]
        + [ANY] * len(buffers),
        out_specs=[whole_out(outs[0].shape), whole_out(outs[1].shape), block_of(outs[2].shape)]
        + [whole_out(outs[3].shape)],
        out_shape=outs,
        scratch_shapes=[
            pltpu.VMEM((count, width, wide), BF16),
            pltpu.VMEM((count, width, wide), BF16),
            pltpu.SemaphoreType.DMA((count,)),
            pltpu.SemaphoreType.DMA((count,)),
        ],
        compiler_params=params(58),
        cost_estimate=cost(
            2 * tokens * width * wide * count * 2,
            4 * width * wide * count + 30 * tokens * width,
            tokens * wide * count,
        ),
        name="mlp_forward",
    )(place.table, x, mods, shared, *buffers)


def mlp_backward(place, buffers, dx, x, mods, m, h, u):
    route = Route(place, buffers)
    count = place.cols
    tokens, width = x.shape
    wide = u.shape[-1]
    outs = [
        shaped((tokens, width), F32),
        shaped(mods.shape, F32),
        shaped((count, 1, wide), F32),
        shaped((1, width), F32),
    ] + [shaped(v, BF16) for v in route.outs]
    out = pl.pallas_call(
        functools.partial(mlp_backward_body, route),
        grid=(count,),
        in_specs=[SMEM, whole_block(x.shape), whole_block(x.shape), whole_block(mods.shape)]
        + [whole_block(m.shape), whole_block(h.shape), block_of(u.shape)]
        + [ANY] * len(buffers),
        out_specs=[whole_out(x.shape), whole_out(mods.shape), whole_out(outs[2].shape)]
        + [whole_out((1, width))]
        + [ANY] * len(route.outs),
        out_shape=outs,
        scratch_shapes=[
            pltpu.VMEM((count, width, wide), BF16),
            pltpu.VMEM((count, width, wide), BF16),
            pltpu.VMEM((tokens, width), BF16),
            pltpu.VMEM((tokens, width), F32),
            pltpu.VMEM((2, width, wide), BF16),
            pltpu.VMEM((2, width, wide), BF16),
            pltpu.SemaphoreType.DMA((count,)),
            pltpu.SemaphoreType.DMA((count,)),
            pltpu.SemaphoreType.DMA((2,)),
            pltpu.SemaphoreType.DMA((2,)),
        ],
        compiler_params=params(58),
        cost_estimate=cost(
            4 * 2 * tokens * width * wide * count,
            8 * width * wide * count + 40 * tokens * width,
            tokens * wide * count,
        ),
        name="mlp_backward",
    )(place.table, dx, x, mods, m, h, u, *buffers)
    return out[:4], out[4:]


def attention_backward(place, buffers, dx, x, mods, a, h, qkv, p, o):
    route = Route(place, buffers)
    count = place.cols
    tokens, width = x.shape
    narrow = o.shape[-1]
    outs = [
        shaped((tokens, width), F32),
        shaped(mods.shape, F32),
        shaped((count, 1, 3 * narrow), F32),
        shaped((1, width), F32),
    ] + [shaped(v, BF16) for v in route.outs]
    out = pl.pallas_call(
        functools.partial(attention_backward_body, route),
        grid=(count,),
        in_specs=[SMEM, whole_block(x.shape), whole_block(x.shape), whole_block(mods.shape)]
        + [whole_block(a.shape), whole_block(h.shape)]
        + [block_of(qkv.shape), block_of(p.shape), block_of(o.shape)]
        + [ANY] * len(buffers),
        out_specs=[whole_out(x.shape), whole_out(mods.shape), whole_out(outs[2].shape)]
        + [whole_out((1, width))]
        + [ANY] * len(route.outs),
        out_shape=outs,
        scratch_shapes=[
            pltpu.VMEM((count, width, 4 * narrow), BF16),
            pltpu.VMEM((tokens, width), BF16),
            pltpu.VMEM((tokens, width), F32),
            pltpu.VMEM((tokens, 3 * narrow), BF16),
            pltpu.VMEM((2, width, 4 * narrow), BF16),
            pltpu.SemaphoreType.DMA((count,)),
            pltpu.SemaphoreType.DMA((2,)),
        ],
        compiler_params=params(58),
        cost_estimate=cost(
            4 * tokens * width * width * 4 + 10 * tokens * LEN * width,
            16 * width * width + 40 * tokens * width,
        ),
        name="attention_backward",
    )(place.table, dx, x, mods, a, h, qkv, p, o, *buffers)
    return out[:4], out[4:]


def final_step(x, mods, head, bias, noise, mask):
    tokens, width = x.shape
    vmem = pl.BlockSpec(memory_space=pltpu.VMEM)
    return pl.pallas_call(
        final_body,
        in_specs=[vmem] * 6,
        out_specs=[vmem] * 5,
        out_shape=[
            shaped((tokens, width), F32),
            shaped((1, PATCH), F32),
            shaped((PATCH, width), F32),
            shaped((1, PATCH), F32),
            shaped(mods.shape, F32),
        ],
        scratch_shapes=[pltpu.VMEM((tokens, width), BF16), pltpu.VMEM((tokens, width), F32)],
        compiler_params=pltpu.CompilerParams(vmem_limit_bytes=32 * MIB),
        cost_estimate=cost(6 * tokens * width * PATCH, 12 * tokens * width),
        name="final_step",
    )(x, mods, head, bias, noise, mask)


def pack_body(in_ref, out_ref, block_ref, mode_ref):
    blocks = out_ref.shape[1] - 1
    for k in range(6):
        mode_ref[0, k] = in_ref[0, k].astype(BF16)
    attn = [in_ref[0, 6 + k] for k in range(3)] + [out_ref[0, 0].T]
    block_ref[0] = jnp.concatenate(attn, axis=1).astype(BF16)
    first = [in_ref[0, 9 + k] for k in range(blocks)]
    block_ref[1] = jnp.concatenate(first, axis=1).astype(BF16)
    second = [out_ref[0, 1 + k].T for k in range(blocks)]
    block_ref[2] = jnp.concatenate(second, axis=1).astype(BF16)


def pack_weights(weights_in, weights_out):
    layers, kinds, block, narrow = weights_in.shape
    outs = [
        shaped((3 * layers, block, 4 * narrow), BF16),
        shaped((layers, 6, block, narrow), BF16),
    ]
    return pl.pallas_call(
        pack_body,
        grid=(layers,),
        in_specs=[block_of(weights_in.shape), block_of(weights_out.shape)],
        out_specs=[
            pl.BlockSpec((3, block, 4 * narrow), lambda c: (c, 0, 0)),
            block_of(outs[1].shape),
        ],
        out_shape=outs,
        compiler_params=params(32),
        name="pack_weights",
    )(weights_in, weights_out)


def embed_body(base, noisy_ref, shared_ref, table_ref, out_ref):
    patch = jnp.concatenate(
        [
            shared_ref[c, base + 3 : base + 3 + PATCH, :]
            for c in range(shared_ref.shape[0])
        ],
        axis=1,
    ).astype(BF16)
    constant = row_of(shared_ref, base + 2) + table_ref[...]
    for s in range(noisy_ref.shape[0] // LEN):
        rows = pl.ds(s * LEN, LEN)
        out_ref[rows, :] = dot_nn(noisy_ref[rows, :], patch) + constant


def embed_tokens(base, noisy, shared, table):
    vmem = pl.BlockSpec(memory_space=pltpu.VMEM)
    return pl.pallas_call(
        functools.partial(embed_body, base),
        in_specs=[vmem] * 3,
        out_specs=vmem,
        out_shape=shaped((noisy.shape[0], table.shape[1]), F32),
        compiler_params=pltpu.CompilerParams(vmem_limit_bytes=32 * MIB),
        name="embed_tokens",
    )(noisy, shared, table)


def silu_slope(values):
    sigmoid_part = jax.nn.sigmoid(values)
    return sigmoid_part * (1.0 + values * (1.0 - sigmoid_part))


TIME_BLOCK = 128
CLASS_AT, FREQ_AT, LABEL_AT = 192, 208, 224


def condition_body(base, found, near_ref, shared_ref, *refs):
    cond_ref, act_ref, first_ref, first_act_ref, freq_ref, label_ref, class_ref, wave_ref = refs
    cols, _, narrow = shared_ref.shape
    rows = near_ref.shape[0] // cols
    steps = FREQ // TIME_BLOCK
    for r in range(rows):
        at = slice(r * 8, r * 8 + 8)
        for c in range(cols):
            block = near_ref[found[r * cols + c], CLASS_AT:, :].astype(F32)
            joined = jnp.concatenate([block[:8], block[8:16, : narrow - 128]], axis=1)
            class_ref[at, c * narrow : (c + 1) * narrow] = joined
            if c == 0:
                wave_ref[at, :TIME_BLOCK] = block[16:24]
                wave_ref[at, TIME_BLOCK:] = block[24:32]
                label_ref[at, :] = block[32:40] * 32.0 + block[40:48]
    freq = wave_ref[...].astype(BF16)
    freq_ref[...] = freq

    def product(left, first_row, count):
        parts = []
        for c in range(cols):
            total = None
            for k in range(count):
                block = near_ref[found[(first_row + k) * cols + c], :CLASS_AT, :]
                part = dot_nt(left[:, k * TIME_BLOCK : (k + 1) * TIME_BLOCK], block)
                total = part if total is None else total + part
            parts.append(total)
        return jnp.concatenate(parts, axis=1)

    first = product(freq, 0, steps) + row_of(shared_ref, base)
    first_ref[...] = first
    first_act = (first * jax.nn.sigmoid(first)).astype(BF16)
    first_act_ref[...] = first_act
    cond = product(first_act, steps, rows - steps) + row_of(shared_ref, base + 1)
    cond = cond + class_ref[...]
    cond_ref[...] = cond
    act_ref[...] = (cond * jax.nn.sigmoid(cond)).astype(BF16)


def condition_step(base, found, near, shared, samples, width):
    vmem = pl.BlockSpec(memory_space=pltpu.VMEM)
    outs = [
        shaped((samples, width), F32),
        shaped((samples, width), BF16),
        shaped((samples, width), F32),
        shaped((samples, width), BF16),
        shaped((samples, FREQ), BF16),
        shaped((samples, 128), F32),
    ]
    return pl.pallas_call(
        functools.partial(condition_body, base),
        in_specs=[SMEM, vmem, vmem],
        out_specs=[vmem] * len(outs),
        out_shape=outs,
        scratch_shapes=[pltpu.VMEM((samples, width), F32), pltpu.VMEM((samples, FREQ), F32)],
        compiler_params=pltpu.CompilerParams(vmem_limit_bytes=32 * MIB),
        name="condition_step",
    )(found, near, shared)


def condition_back_body(
    layers, blocks, found, spot, small_ref, part_ref, final_ref, square_ref, cond_ref, first_ref,
    input_ref, label_ref, pick_ref, near_ref, time_ref, embed_ref, bias_ref, own_ref, shared_ref,
    grad_ref,
):
    row, col = spot[0], spot[1]
    samples, width = cond_ref.shape
    narrow = pick_ref.shape[1]
    cols = width // narrow
    rows = near_ref.shape[0] // cols
    steps = FREQ // TIME_BLOCK
    start = 16 * layers + 2 * PATCH
    pick = pick_ref[...]
    pick_wide = pick.astype(F32)

    def own_cols(v):
        return jnp.dot(v, pick_wide, precision=HIGHEST, preferred_element_type=F32)

    def squares(v):
        return jnp.sum(v * v, keepdims=True)

    block_rows = part_ref.shape[2]
    for r in range(rows):
        part = part_ref[found[r * cols + col]]
        grad_ref[:, r * block_rows : (r + 1) * block_rows] = part
    grad_cond = (grad_ref[...] + final_ref[...]) * silu_slope(cond_ref[...])
    low = grad_cond.astype(BF16)
    parts = []
    for r in range(steps, rows):
        total = None
        for c in range(cols):
            block = near_ref[found[r * cols + c], :CLASS_AT, :]
            part = dot_nn(low[:, c * narrow : (c + 1) * narrow], block)
            total = part if total is None else total + part
        parts.append(total)
    grad_first = jnp.concatenate(parts, axis=1) * silu_slope(first_ref[...])
    is_first = (row < steps).astype(F32)
    outputs = grad_first.astype(BF16).astype(F32) * is_first + low.astype(F32) * (1.0 - is_first)
    outputs = dot_nn(outputs.astype(BF16), pick).astype(BF16)
    time_grad = dot_tn(outputs, input_ref[...])
    time_ref[...] = time_grad
    hot = lax.broadcasted_iota(jnp.int32, (samples, CLASSES), 1).astype(F32)
    hot = (hot == label_ref[:, 0:1]).astype(F32)
    class_grad = lax.dot_general(
        own_cols(grad_cond), hot, TN, precision=HIGHEST, preferred_element_type=F32
    )
    patch = own_cols(small_ref[start - PATCH : start, :])
    embed_ref[...] = jnp.concatenate([class_grad, patch.T], axis=1)
    own_ref[...] = squares(time_grad) + squares(class_grad) * (1.0 / rows)
    time_bias = jnp.concatenate(
        [jnp.sum(grad_first, axis=0, keepdims=True), jnp.sum(grad_cond, axis=0, keepdims=True)],
        axis=0,
    )
    total = square_ref[...] + squares(time_bias) + squares(small_ref[start - 2 * PATCH : start + 3, :])
    total = total + squares(small_ref[start + 3 : start + 4, :PATCH])
    own = own_cols(small_ref[: start + 16, :])
    lines = []
    for layer in range(layers):
        at = 16 * layer
        total = total + squares(small_ref[at : at + 6 + cols, :])
        total = total + squares(small_ref[at + 10 : at + 10 + cols, :narrow])
        total = total + squares(small_ref[at + 10 : at + 10 + cols, 2 * narrow : 3 * narrow])
        total = total + squares(small_ref[at + 14 : at + 16, :])
        attn = small_ref[pl.ds(at + 10 + col, 1), :]
        mlp = small_ref[pl.ds(at + 6 + col, 1), :]
        lines += [own[at : at + 6], attn[:, :narrow], attn[:, 2 * narrow : 3 * narrow]]
        lines += [mlp[:, k * narrow : (k + 1) * narrow] for k in range(blocks)]
        lines += [own[at + 14 : at + 16]]
    lines += [own_cols(time_bias), own[start : start + 1]]
    bias_ref[...] = jnp.concatenate(lines, axis=0)
    shared_ref[...] = total


def condition_back(
    layers, blocks, found, spot, small, part, final, squares, cond, first, inputs, labels, pick, near
):
    vmem = pl.BlockSpec(memory_space=pltpu.VMEM)
    narrow = pick.shape[1]
    outs = [
        shaped((narrow, TIME_BLOCK), F32),
        shaped((narrow, CLASSES + PATCH), F32),
        shaped((14 * layers + 3, narrow), F32),
        shaped((1, 1), F32),
        shaped((1, 1), F32),
    ]
    operands = [small, part, final, squares, cond, first, inputs, labels, pick, near]
    return pl.pallas_call(
        functools.partial(condition_back_body, layers, blocks),
        in_specs=[SMEM, SMEM] + [vmem] * len(operands),
        out_specs=[vmem] * len(outs),
        out_shape=outs,
        scratch_shapes=[pltpu.VMEM(cond.shape, F32)],
        compiler_params=pltpu.CompilerParams(vmem_limit_bytes=48 * MIB),
        name="condition_back",
    )(found, spot, *operands)


def modes_backward_body(
    layers, near_ref, at_ref, rows_ref, pick_ref, mode_ref, act_ref, final_ref,
    block_ref, part_ref, square_ref, grad_ref, cond_ref, shared_ref,
):
    near = near_ref[...]
    at = at_ref[...]
    samples = at.shape[0]
    where = lax.broadcasted_iota(jnp.int32, (samples, near.shape[0]), 1)
    cols, narrow = mode_ref.shape[0], mode_ref.shape[4]
    spreads = []
    for layer in range(layers):
        for k in range(6):
            offset = 12 * layer + 6 * (k // 3) + k % 3
            spreads.append((where == at[:, 0:1] + at[:, 1:2] * 3 + offset).astype(BF16))
    for k in range(2):
        spreads.append((where == at[:, 0:1] + at[:, 1:2] * 2 + 12 * layers + k).astype(BF16))
    rows = dot_nn(jnp.concatenate(spreads, axis=0), near).astype(BF16)
    mine = dot_nn(rows[: 6 * layers * samples], pick_ref[...]).astype(BF16)

    total = None
    squares = jnp.zeros((1, 1), F32)
    for layer in range(layers):
        for k in range(6):
            at_row = (6 * layer + k) * samples
            low = rows[at_row : at_row + samples]
            grad = dot_tn(rows_ref[...], mine[at_row : at_row + samples])
            block_ref[layer, k] = grad
            squares = squares + jnp.sum(grad * grad, keepdims=True)
            full = jnp.concatenate([mode_ref[c, layer, k] for c in range(cols)], axis=1)
            part = dot_nt(low, full)
            total = part if total is None else total + part
    part_ref[...] = total
    square_ref[...] = squares
    width = act_ref.shape[1]
    at_row = 6 * layers * samples
    shift, scale = rows[at_row : at_row + samples], rows[at_row + samples :]
    squares = jnp.zeros((1, 1), F32)
    for k, low in enumerate((shift, scale)):
        grad = dot_tn(low, act_ref[...])
        grad_ref[k * width : (k + 1) * width, :] = grad
        squares = squares + jnp.sum(grad * grad, keepdims=True)
    cond_ref[...] = dot_nn(shift, final_ref[:width, :]) + dot_nn(
        scale, final_ref[width : 2 * width, :]
    )
    shared_ref[...] = squares


def modes_backward(near, at, cond_rows, pick, mode_full, act, final):
    vmem = pl.BlockSpec(memory_space=pltpu.VMEM)
    samples, block = cond_rows.shape
    width = near.shape[2]
    layers, narrow = mode_full.shape[1], mode_full.shape[4]
    outs = [
        shaped((layers, 6, block, narrow), F32),
        shaped((samples, block), F32),
        shaped((1, 1), F32),
        shaped((2 * width, width), F32),
        shaped((samples, width), F32),
        shaped((1, 1), F32),
    ]
    operands = [near.reshape(-1, width), at, cond_rows, pick, mode_full, act, final]
    return pl.pallas_call(
        functools.partial(modes_backward_body, layers),
        in_specs=[vmem] * len(operands),
        out_specs=[vmem] * len(outs),
        out_shape=outs,
        compiler_params=pltpu.CompilerParams(vmem_limit_bytes=40 * MIB),
        name="modes_backward",
    )(*operands)


def modes_backward_plain(near, cond_rows, mode_full, act, final, col):
    layers, narrow, width = mode_full.shape[1], mode_full.shape[4], near.shape[2]
    devices = near.shape[0]
    samples = act.shape[0] // devices
    low = near[:, : 12 * layers].reshape(devices, layers, 2, samples, 3, width)
    low = jnp.transpose(low, (1, 2, 4, 0, 3, 5)).reshape(layers, 6, devices * samples, width)
    mine = lax.dynamic_slice_in_dim(low, col * narrow, narrow, 3)
    block = jnp.einsum("sd,lkse->lkde", cond_rows, mine, preferred_element_type=F32)
    full = jnp.transpose(mode_full, (1, 2, 3, 0, 4)).reshape(layers, 6, -1, width)
    part = jnp.einsum("lkse,lkde->sd", low, full, preferred_element_type=F32)
    ends = near[:, 12 * layers : 12 * layers + 2 * samples].reshape(-1, 2, width)
    grad = jnp.einsum("ske,sd->ked", ends, act, preferred_element_type=F32)
    cond = jnp.einsum(
        "ske,ked->sd", ends, final[: 2 * width].reshape(2, width, width), preferred_element_type=F32
    )
    grad = grad.reshape(2 * width, width)
    return block, part, squared(block)[None, None], grad, cond, squared(grad)[None, None]


def collect_body(layers, *refs):
    out_ref = refs[-1]
    at = 0
    out_ref[...] = jnp.zeros_like(out_ref)
    take = list(refs[:-1])
    for _ in range(layers):
        dmod_a, dmod_b, dbias_a, dbias_b, dtail_a, dtail_b = [take.pop(0) for _ in range(6)]
        for k, source in enumerate((dmod_a, dmod_b)):
            total = source[0]
            for s in range(1, source.shape[0]):
                total = total + source[s]
            out_ref[at + 3 * k : at + 3 * k + 3, :] = total
        for c in range(dbias_b.shape[0]):
            out_ref[at + 6 + c : at + 7 + c, : dbias_b.shape[2]] = dbias_b[c]
            out_ref[at + 10 + c : at + 11 + c, : dbias_a.shape[2]] = dbias_a[c]
        out_ref[at + 14 : at + 15, :] = dtail_a[...]
        out_ref[at + 15 : at + 16, :] = dtail_b[...]
        at += 16
    head, head_bias, loss, mask, dfinal, dx, noisy = take
    out_ref[at : at + PATCH, :] = head[...]
    out_ref[at + PATCH : at + 2 * PATCH, :] = dot_tn(noisy[...], dx[...].astype(BF16))
    at += 2 * PATCH
    out_ref[at : at + 1, :] = jnp.sum(dx[...], axis=0, keepdims=True)
    total = dfinal[0]
    for s in range(1, dfinal.shape[0]):
        total = total + dfinal[s]
    out_ref[at + 1 : at + 3, :] = total
    out_ref[at + 3 : at + 4, 0:PATCH] = head_bias[...]
    out_ref[at + 4 : at + 5, 0:PATCH] = loss[...]
    out_ref[at + 5 : at + 6, 0:1] = jnp.sum(mask[...], keepdims=True)


def collect(layers, parts, height, width):
    vmem = pl.BlockSpec(memory_space=pltpu.VMEM)
    return pl.pallas_call(
        functools.partial(collect_body, layers),
        in_specs=[vmem] * len(parts),
        out_specs=vmem,
        out_shape=shaped((height, width), F32),
        compiler_params=pltpu.CompilerParams(vmem_limit_bytes=48 * MIB),
        name="collect_small",
    )(*parts)


def adam(weight, gradient, moment, second, clip, rate):
    gradient = gradient * clip
    moment = BETA_ONE * moment + (1.0 - BETA_ONE) * gradient
    second = BETA_TWO * second + (1.0 - BETA_TWO) * gradient * gradient
    update = (
        moment / (1.0 - BETA_ONE**STEP) / (jnp.sqrt(second / (1.0 - BETA_TWO**STEP)) + ADAM_EPS)
    )
    return weight - rate * (update + DECAY * weight), moment, second


def adam_blocks_body(layers, halves, clip_ref, spot, *refs):
    clip = clip_ref[0]
    per = 5 if halves else 3
    sums = [refs[per * layer : per * layer + per] for layer in range(layers)]
    refs = refs[per * layers :]
    wi, mi, vi, wo, mo, vo = refs[:6]
    out_i, out_o = refs[6:9], refs[9:12]
    total_ref = refs[12]
    narrow = wi.shape[3]

    def fill(layer):
        group = sums[layer]
        for k in range(3):
            if not halves:
                total_ref[k] = group[1][0] if k == 0 else group[2][k - 1]
                continue
            half = total_ref.shape[1] // 2
            mine, other = group[1:3] if k == 0 else group[3:5]
            at = 0 if k == 0 else k - 1
            core = spot[1] % 2
            total_ref[k, pl.ds(pl.multiple_of(core * half, 8), half), :] = mine[0, at]
            total_ref[k, pl.ds(pl.multiple_of((1 - core) * half, 8), half), :] = other[at]

    def update(layer, mode_ref):
        for k in range(wi.shape[1]):
            if k < 6:
                grad = mode_ref[layer, k]
            elif k < 9:
                grad = total_ref[0, :, (k - 6) * narrow : (k - 5) * narrow]
            else:
                grad = total_ref[1, :, (k - 9) * narrow : (k - 8) * narrow]
            new = adam(wi[0, k], grad, mi[0, k], vi[0, k], clip, RATE)
            for ref, value in zip(out_i, new):
                ref[0, k] = value
        for k in range(wo.shape[1]):
            if k == 0:
                grad = total_ref[0, :, 3 * narrow :]
            else:
                grad = total_ref[2, :, (k - 1) * narrow : k * narrow]
            new = adam(wo[0, k], grad.T, mo[0, k], vo[0, k], clip, RATE)
            for ref, value in zip(out_o, new):
                ref[0, k] = value

    for layer in range(layers):

        @pl.when(pl.program_id(0) == layer)
        def _(layer=layer):
            fill(layer)
            update(layer, sums[layer][0])


def adam_blocks(clip, spot, sums, ins, outs):
    arrays = list(ins) + list(outs)
    grads = [v for group in sums for v in group]
    halves = len(sums[0]) == 5
    results = [shaped(v.shape, F32) for v in arrays]
    block, narrow = ins[0].shape[2:]
    return pl.pallas_call(
        functools.partial(adam_blocks_body, len(sums), halves),
        grid=(ins[0].shape[0],),
        in_specs=[SMEM, SMEM]
        + [whole_block(v.shape) for v in grads]
        + [block_of(v.shape) for v in arrays],
        out_specs=[block_of(v.shape) for v in results],
        out_shape=results,
        scratch_shapes=[pltpu.VMEM((3, block, 4 * narrow), F32)],
        compiler_params=params(58),
        name="adam_blocks",
    )(clip, spot, *grads, *arrays)


def adam_final_body(clip_ref, grad_ref, head_ref, w, m, v, *outs):
    clip = clip_ref[0]
    step = pl.program_id(0)
    last = pl.num_programs(0) - 1

    @pl.when(step < last)
    def _():
        new = adam(w[...], grad_ref[...], m[...], v[...], clip, RATE)
        for ref, value in zip(outs, new):
            ref[...] = value

    @pl.when(step == last)
    def _():
        rows = slice(0, PATCH)
        new = adam(w[rows, :], head_ref[...], m[rows, :], v[rows, :], clip, RATE)
        for ref, value in zip(outs, new):
            ref[rows, :] = value


def adam_final(clip, grad, head, w, m, v):
    width = w.shape[1]
    height = 256
    steps = grad.shape[0] // height
    part = pl.BlockSpec((height, width), lambda c: (c, 0))
    grad_part = pl.BlockSpec((height, width), lambda c: (jnp.minimum(c, steps - 1), 0))
    return pl.pallas_call(
        adam_final_body,
        grid=(steps + 1,),
        in_specs=[SMEM, grad_part, whole_block(head.shape)] + [part] * 3,
        out_specs=[part] * 3,
        out_shape=[shaped(w.shape, F32)] * 3,
        compiler_params=params(58),
        name="adam_final",
    )(clip, grad, head, w, m, v)


def adam_rest_body(rates, clip_ref, *refs):
    clip = clip_ref[0]
    count = len(rates)
    ins, outs = refs[: 4 * count], refs[4 * count :]
    for k, rate in enumerate(rates):
        w, g, m, v = [r[...] for r in ins[4 * k : 4 * k + 4]]
        for ref, value in zip(outs[3 * k : 3 * k + 3], adam(w, g, m, v, clip, rate)):
            ref[...] = value


def adam_rest(clip, groups):
    vmem = pl.BlockSpec(memory_space=pltpu.VMEM)
    arrays, results, rates = [], [], []
    for w, g, m, v, rate in groups:
        arrays += [w, g, m, v]
        results += [shaped(w.shape, F32)] * 3
        rates.append(rate)
    return pl.pallas_call(
        functools.partial(adam_rest_body, tuple(rates)),
        in_specs=[SMEM] + [vmem] * len(arrays),
        out_specs=[vmem] * len(results),
        out_shape=results,
        compiler_params=pltpu.CompilerParams(vmem_limit_bytes=58 * MIB),
        name="adam_rest",
    )(clip, *arrays)


def squared(values):
    return jnp.sum(values * values)


def position_table(width):
    half = width // 2
    rate = np.exp(-math.log(10000.0) * (np.arange(width) % half) / half)
    angle = np.arange(LEN)[:, None] * rate[None, :]
    table = np.where(np.arange(width)[None, :] < half, np.sin(angle), np.cos(angle))
    return table.astype(np.float32)


def on_device(
    latents,
    noise,
    timesteps,
    labels,
    loss_mask,
    weights_in,
    weights_out,
    time_mlp,
    embed_table,
    final_layer,
    bias_table,
    final_bias,
    momentum_in,
    momentum_out,
    momentum_time,
    momentum_embed,
    momentum_final,
    momentum_bias,
    momentum_final_bias,
    variance_in,
    variance_out,
    variance_time,
    variance_embed,
    variance_final,
    variance_bias,
    variance_final_bias,
):
    layers, block, _, narrow = weights_in.shape
    place = Place(block)
    rows, cols = place.rows, place.cols
    width = final_layer.shape[0]
    row_samples = timesteps.shape[0]
    samples = row_samples // cols
    every_sample = row_samples * rows
    tokens = samples * LEN
    base = layers * 14
    hidden_blocks = weights_out.shape[1] - 1

    def my_cols(v, axis):
        return lax.dynamic_slice_in_dim(v, place.col * narrow, narrow, axis)

    in_view = [jnp.transpose(v, (0, 2, 1, 3)) for v in (weights_in, momentum_in, variance_in)]
    packed, mode_low = pack_weights(in_view[0], weights_out)

    embed_low = embed_table.astype(BF16)
    one_hot_row = (labels[:, None] == jnp.arange(CLASSES, dtype=jnp.int32)[None, :]).astype(BF16)
    class_rows = jnp.dot(
        one_hot_row, embed_low[:CLASSES], preferred_element_type=F32
    ).astype(BF16)
    half_freq = FREQ // 2
    freq_rate = jnp.asarray(
        np.exp(-math.log(10000.0) * np.arange(half_freq) / half_freq).astype(np.float32)
    )
    angle_grid = timesteps.astype(F32)[:, None] * freq_rate[None, :]
    freq_row = jnp.concatenate([jnp.cos(angle_grid), jnp.sin(angle_grid)], axis=1).astype(BF16)
    time_rows = time_mlp.shape[0]
    mine = jnp.concatenate([bias_table, embed_low[CLASSES:].astype(F32)], axis=0)
    final_view = [v.T for v in (final_layer, momentum_final, variance_final)]
    found = place.found_at()
    sample = jnp.arange(every_sample, dtype=jnp.int32)
    mode_height = -(-(12 * layers + 4) // 16) * 16
    at = jnp.stack([found[sample // samples] * mode_height, sample % samples], axis=1)
    feature = jnp.arange(width, dtype=jnp.int32)[:, None]
    picked = jnp.arange(narrow, dtype=jnp.int32)[None, :] + place.col * narrow
    pick = (feature == picked).astype(BF16)
    spot = jnp.stack([place.row, place.col]).astype(jnp.int32)

    def partial_modes(cond_act):
        cond_rows = lax.dynamic_slice_in_dim(cond_act, place.row * block, block, 1)
        partial = jnp.einsum("sd,lkde->slke", cond_rows, mode_low, preferred_element_type=F32)
        return cond_rows, partial.reshape(every_sample, layers * 6, narrow)

    def own_modes(total, shared, cond_act, final_low):
        bias_full = jnp.swapaxes(shared, 0, 1).reshape(-1, width)
        modes = total.reshape(samples, layers, 6, width) + jnp.stack(
            [bias_full[14 * layer : 14 * layer + 6] for layer in range(layers)]
        )
        own_start = place.row * row_samples + place.col * samples
        cond_own = lax.dynamic_slice_in_dim(cond_act, own_start, samples, 0)
        final_mod = (
            jnp.einsum("sd,ed->se", cond_own, final_low[: 2 * width], preferred_element_type=F32)
            + final_bias[: 2 * width]
        ).reshape(samples, 2, width)
        mods_a = [modes[:, layer, 0:3] for layer in range(layers)]
        mods_b = [modes[:, layer, 3:6] for layer in range(layers)]
        return mods_a, mods_b, final_mod

    own_tokens = place.col * tokens
    latents = lax.dynamic_slice_in_dim(latents, own_tokens, tokens, 0)
    noise = lax.dynamic_slice_in_dim(noise, own_tokens, tokens, 0)
    mask = lax.dynamic_slice_in_dim(loss_mask, own_tokens, tokens, 0).astype(F32)
    steps_own = lax.dynamic_slice_in_dim(timesteps, place.col * samples, samples, 0).astype(F32)
    alpha_bar = jnp.cos((steps_own / STEPS_T + 0.008) / 1.008 * (math.pi / 2)) ** 2
    keep_part = jnp.repeat(jnp.sqrt(alpha_bar), LEN)[:, None]
    noise_part = jnp.repeat(jnp.sqrt(1.0 - alpha_bar), LEN)[:, None]
    noisy = (keep_part * latents + noise_part * noise).astype(BF16)
    position = jnp.asarray(position_table(width))

    def attn_step(layer):
        def work(buffers, x, mods, shared):
            return attention_forward(place, 14 * layer, buffers, x, mods, shared)

        return work

    def mlp_step(layer):
        def work(buffers, x, mods, shared):
            return mlp_forward(place, 14 * layer, buffers, x, mods, shared)

        return work

    def attn_back(buffers, *operands):
        return attention_backward(place, buffers, *operands)

    def mlp_back(buffers, *operands):
        return mlp_backward(place, buffers, *operands)

    def last_step(x, final_mod, final_low):
        return final_step(
            x, final_mod, final_low[2 * width :], final_bias[2 * width :][None], noise, mask[:, None]
        )

    def mode_parts(back_a, back_b, grad_final_mod):
        parts = []
        for layer in range(layers):
            parts += [back_a[layer][1], back_b[layer][1]]
        parts = [v.reshape(-1, width) for v in parts + [grad_final_mod]]
        spare = mode_height - sum(v.shape[0] for v in parts)
        return jnp.concatenate(parts + [jnp.zeros((spare, width), F32)], axis=0).astype(BF16)

    start = 16 * layers + 2 * PATCH
    height = -(-(start + 16) // 32) * 32

    def collected(back_a, back_b, last):
        small = []
        for layer in range(layers):
            _, dmod_a, dbias_a, dtail_a = back_a[layer]
            _, dmod_b, dbias_b, dtail_b = back_b[layer]
            small += [dmod_a, dmod_b, dbias_a, dbias_b, dtail_a, dtail_b]
        _, loss_parts, grad_head, grad_head_bias, grad_final_mod = last
        small += [grad_head, grad_head_bias, loss_parts, mask[:, None], grad_final_mod]
        small += [back_a[0][0], noisy]
        return collect(layers, small, height, width)

    buffers = [None] * (2 * layers)
    fore_a, fore_b = [None] * layers, [None] * layers
    entry = [None] * layers
    back_a, back_b = [None] * layers, [None] * layers
    summed = [None] * (2 * layers)
    if place.direct and layers == 2:
        stages = Stages()
        halves = packed.reshape(3 * layers, 2, place.half, packed.shape[2])
        kept = lax.dynamic_index_in_dim(halves, place.core, 1, False)
        sent = lax.dynamic_index_in_dim(halves, 1 - place.core, 1, False)
        (got,), _ = stages.run([(swap_core, sent)])
        a0, b0, a1, b1 = [
            Spread(kept[k : k + n], got[k : k + n]) for k, n in ((0, 1), (1, 2), (3, 1), (4, 2))
        ]
        wide = jnp.broadcast_to
        own_block = jnp.concatenate(
            [
                time_mlp.astype(BF16).T,
                class_rows[:, :128],
                jnp.pad(class_rows[:, 128:], ((0, 0), (0, 256 - narrow))),
                freq_row[:, :128],
                freq_row[:, 128:],
                wide((labels // 32).astype(BF16)[:, None], (row_samples, 128)),
                wide((labels % 32).astype(BF16)[:, None], (row_samples, 128)),
            ],
            axis=0,
        )
        got, (near, shared) = stages.run(
            a0.at_once(),
            [
                (near_rows, own_block),
                (functools.partial(gather_cols, place), mine),
            ],
        )
        a0.along_at_once(got)
        got, (near, residual) = stages.run(
            a0.first() + b0.far(),
            [
                (near_x, near),
                (functools.partial(embed_tokens, base), noisy, shared, position),
            ],
        )

        def condition_work(near, shared, found):
            near = near_core(near)
            got = condition_step(base, found, near, shared, every_sample, width)
            return near, got, partial_modes(got[1])

        got, ((near, conditions, (cond_rows, partial)),) = stages.run(
            a0.second(got[0]) + b0.near(got[1]),
            [(condition_work, near, shared, found)],
            a0.core(),
        )
        b0.along(got[1])
        condition, cond_act, first_time, first_act, freq_low, all_labels = conditions
        core = got[2]
        got, (total,) = stages.run(
            b0.first() + a1.far() + a0.late_core(got[0]),
            [(functools.partial(scatter_y, place), partial)],
        )
        buffers[0] = a0.buffers(core, got[2])

        two = a1.near(got[1])[0][1]

        def scatter_work(total, two):
            blocks = swap_near(two)
            total, blocks = lax.optimization_barrier((scatter_z(place, total), blocks))
            return blocks, scatter_x(place, total, samples)

        got, ((blocks, total), final_low) = stages.run(
            b0.second(got[0]) + b0.core(),
            [(scatter_work, total, two), (lambda v: v.astype(BF16), final_view[0])],
        )
        a1.along(blocks)
        core = got[1]

        def modes_work(total, shared, cond_act):
            return own_modes(scatter_core(place, total), shared, cond_act, final_low)

        got, ((mods_a, mods_b, final_mod),) = stages.run(
            b1.far() + b0.late_core(got[0]),
            [(modes_work, total, shared, cond_act)],
            a1.first(),
        )
        buffers[1] = b0.buffers(core, got[1])
        got = [got[2], got[0]]
        got, (fore_a[0],) = stages.run(
            a1.second(got[0]) + b1.near(got[1]) + a1.core(),
            [(attn_step(0), buffers[0], residual, mods_a[0], shared)],
        )
        b1.along(got[1])
        core = got[2]
        got, (fore_b[0],) = stages.run(
            b1.first() + a1.late_core(got[0]),
            [(mlp_step(0), buffers[1], fore_a[0][0], mods_b[0], shared)],
        )
        buffers[2] = a1.buffers(core, got[1])
        got, (fore_a[1],) = stages.run(
            b1.second(got[0]) + b1.core(),
            [(attn_step(1), buffers[2], fore_b[0][0], mods_a[1], shared)],
        )
        core = got[1]
        got, _ = stages.run(b1.late_core(got[0]))
        buffers[3] = b1.buffers(core, got[0])
        got, (fore_b[1],) = stages.run(
            [(swap_x, mode_low)], [(mlp_step(1), buffers[3], fore_a[1][0], mods_b[1], shared)]
        )
        mode_half = pair(place.x, mode_low, got[0])
        entry = [residual, fore_b[0][0]]
        last = last_step(fore_b[1][0], final_mod, final_low)

        def back_b_work(layer, grad):
            out, h, u, m = fore_b[layer]
            return (mlp_back, buffers[2 * layer + 1], grad, fore_a[layer][0], mods_b[layer], m, h, u)

        def back_a_work(layer, grad):
            out, h, qkv, p, o, a = fore_a[layer]
            return (
                attn_back, buffers[2 * layer], grad, entry[layer], mods_a[layer], a, h, qkv, p, o,
            )

        got, ((back_b[1], grads),) = stages.run(
            [(swap_core, mode_half)], [back_b_work(1, last[0])]
        )
        mode_full = jnp.swapaxes(pair(place.core, mode_half, got[0]), 0, 1)
        mode_full = mode_full.reshape((4,) + mode_low.shape)
        gb1 = Gathered(grads)
        got, ((back_a[1], grads),) = stages.run(gb1.core, [back_a_work(1, back_b[1][0])])
        ga1 = Gathered(grads)
        got, ((back_b[0], grads),) = stages.run(
            gb1.first(got[0]) + ga1.core, [back_b_work(0, back_a[1][0])]
        )
        core_a1 = got[1]
        gb0 = Gathered(grads)
        got, ((back_a[0], grads),) = stages.run(
            gb1.second(got[0]) + ga1.first(core_a1) + gb0.core, [back_a_work(0, back_b[0][0])]
        )
        zn_b1 = gb1.near(got[0])
        ga0 = Gathered(grads)

        def sum_work(back_a, back_b, last):
            return sum_along_z(place, collected(back_a, back_b, last))

        moded = mode_parts(back_a, back_b, last[4])
        t2_a1 = ga1.second(got[1])
        got, (near_modes, small) = stages.run(
            gb0.first(got[2]) + ga0.core,
            [(near_z, moded), (sum_work, back_a, back_b, last)],
            zn_b1,
        )
        got = [got[0], got[2], got[1]]
        t2_b0 = gb0.second(got[0])
        got, (near_modes, small) = stages.run(
            ga0.first(got[2]) + t2_a1 + gb1.far(got[1]),
            [(near_y, near_modes), (sum_with(swap_core), small)],
        )
        total_b1 = gb1.total(got[2])
        t2_a0 = ga0.second(got[0])
        got, (near_modes, small) = stages.run(
            t2_b0 + ga1.near(got[1]), [(near_x, near_modes), (sum_with(swap_x), small)]
        )
        got, (near_modes, small) = stages.run(
            gb0.near(got[0]) + ga1.far(got[1]),
            [(near_core, near_modes), (sum_with(swap_y), small)],
            t2_a0,
        )
        got = [got[2], got[1], got[0]]
        total_a1 = ga1.total(got[1])

        def modes_back_work(near):
            return modes_backward(near, at, cond_rows, pick, mode_full, cond_act, final_low)

        got, (moded, small) = stages.run(
            gb0.far(got[2]) + ga0.near(got[0]),
            [(modes_back_work, near_modes), (functools.partial(sum_spread, place), small)],
        )
        total_b0 = gb0.total(got[0])
        time_inputs = lax.dynamic_slice_in_dim(
            jnp.concatenate([freq_low, first_act], axis=1), place.row * time_rows, time_rows, 1
        )
        got, (part,) = stages.run(ga0.far(got[1]), [(near_z_at_once, moded[1])])
        total_a0 = ga0.total(got[0])
        part = near_y(part)
        ends = condition_back(
            layers, hidden_blocks, found, spot, small, part, moded[4], moded[5], condition,
            first_time, time_inputs, all_labels, pick, near,
        )
        late = swap_core(
            jnp.concatenate([total_b1[1], total_b0[1], total_a1[1], total_a0[1]])
        )
        summed = [total_a0, total_b0, total_a1, total_b1]
        sums = [
            (moded[0], total_a0, late[5:6], total_b0, late[2:4]),
            (moded[0], total_a1, late[4:5], total_b1, late[0:2]),
        ]
        time_grad, embed_grad, bias_grad, own_part, shared_part = ends
        own_squares = own_part[0, 0] + moded[2][0, 0]
        shared_squares = shared_part[0, 0]
        final_grad = moded[3]
    else:
        final_low = final_view[0].astype(BF16)
        shared = gather_cols(place, mine)
        time_full = lax.all_gather(time_mlp.astype(BF16), "row", axis=0, tiled=True)
        time_full = lax.all_gather(time_full, "col", axis=1, tiled=True)
        class_full = lax.all_gather(class_rows, "col", axis=1, tiled=True)
        class_full = lax.all_gather(class_full, "row", axis=0, tiled=True).astype(F32)
        freq_low = lax.all_gather(freq_row, "row", axis=0, tiled=True)
        all_labels = lax.all_gather(labels, "row", axis=0, tiled=True)
        bias_full = jnp.swapaxes(shared, 0, 1).reshape(-1, width)
        first_time = (
            jnp.dot(freq_low, time_full[:FREQ], preferred_element_type=F32) + bias_full[base]
        )
        first_act = jax.nn.silu(first_time).astype(BF16)
        condition = (
            jnp.dot(first_act, time_full[FREQ:], preferred_element_type=F32)
            + bias_full[base + 1]
            + class_full
        )
        cond_act = jax.nn.silu(condition).astype(BF16)
        cond_rows, partial = partial_modes(cond_act)
        mods_a, mods_b, final_mod = own_modes(
            scatter_plain(place, partial, samples), shared, cond_act, final_low
        )
        grad = embed_tokens(base, noisy, shared, position)
        for layer in range(layers):
            buffers[2 * layer] = [plain_gather(packed[3 * layer : 3 * layer + 1])]
            buffers[2 * layer + 1] = [plain_gather(packed[3 * layer + 1 : 3 * layer + 3])]
            entry[layer] = grad
            fore_a[layer] = attn_step(layer)(buffers[2 * layer], grad, mods_a[layer], shared)
            grad = fore_a[layer][0]
            fore_b[layer] = mlp_step(layer)(buffers[2 * layer + 1], grad, mods_b[layer], shared)
            grad = fore_b[layer][0]
        last = last_step(grad, final_mod, final_low)
        grad = last[0]
        for layer in reversed(range(layers)):
            out, h, u, m = fore_b[layer]
            back_b[layer], grads = mlp_back(
                buffers[2 * layer + 1], grad, fore_a[layer][0], mods_b[layer], m, h, u
            )
            summed[2 * layer + 1] = plain_scatter(grads[0])
            grad = back_b[layer][0]
            out, h, qkv, p, o, a = fore_a[layer]
            back_a[layer], grads = attn_back(
                buffers[2 * layer], grad, entry[layer], mods_a[layer], a, h, qkv, p, o
            )
            summed[2 * layer] = plain_scatter(grads[0])
            grad = back_a[layer][0]
        mode_full = lax.all_gather(mode_low, "col")
        near = gather_near(place, mode_parts(back_a, back_b, last[4]))
        moded = modes_backward_plain(
            near, cond_rows, mode_full, cond_act, final_low, place.col
        )
        mode_blocks, part, square, final_grad, cond_final, final_squares = moded
        own_squares = square[0, 0]
        small = lax.psum(collected(back_a, back_b, last), ("row", "col"))
        grad_cond = lax.all_gather(part, "row", axis=1, tiled=True) + cond_final
        grad_condition = grad_cond * silu_slope(condition)
        one_hot = (all_labels[:, None] == jnp.arange(CLASSES, dtype=jnp.int32)[None, :]).astype(F32)
        grad_classes = jnp.einsum(
            "sd,sc->dc", my_cols(grad_condition, 1), one_hot, precision=HIGHEST
        )
        condition_low = grad_condition.astype(BF16)
        grad_first = jnp.einsum(
            "se,de->sd", condition_low, time_full[FREQ:], preferred_element_type=F32
        ) * silu_slope(first_time)
        time_inputs = lax.dynamic_slice_in_dim(
            jnp.concatenate([freq_low, first_act], axis=1), place.row * time_rows, time_rows, 1
        )
        time_outputs = jnp.where(
            (place.row + 1) * time_rows <= FREQ, grad_first.astype(BF16), condition_low
        )
        time_grad = jnp.einsum(
            "sd,se->ed", time_inputs, my_cols(time_outputs, 1), preferred_element_type=F32
        )
        own_rows, shared_squares = [], jnp.zeros((), F32)
        for layer in range(layers):
            rows_at = small[16 * layer : 16 * layer + 16]
            own = my_cols(rows_at, 1)
            mlp_rows = lax.dynamic_index_in_dim(rows_at[6:10], place.col, 0, False)
            attn_rows = lax.dynamic_index_in_dim(rows_at[10:14], place.col, 0, False)
            attn_rows = attn_rows[: 3 * narrow].reshape(3, narrow)
            own_rows += [own[:6], attn_rows[0:1], attn_rows[2:3]]
            own_rows += [mlp_rows.reshape(hidden_blocks, narrow), own[14:16]]
            counted = rows_at[10:14, : 3 * narrow].reshape(4, 3, narrow)[:, 0::2]
            shared_squares = (
                shared_squares + squared(rows_at[:10]) + squared(counted) + squared(rows_at[14:])
            )
        time_bias = jnp.stack([jnp.sum(grad_first, axis=0), jnp.sum(grad_condition, axis=0)])
        own_rows += [my_cols(time_bias, 1), my_cols(small[start : start + 1], 1)]
        bias_grad = jnp.concatenate(own_rows, axis=0)
        shared_squares = (
            shared_squares
            + squared(time_bias)
            + squared(small[start - 2 * PATCH : start + 3])
            + squared(small[start + 3, :PATCH])
            + final_squares[0, 0]
        )
        own_squares = own_squares + squared(time_grad) + squared(grad_classes) / rows
        sums = [(mode_blocks, summed[2 * k], summed[2 * k + 1]) for k in range(layers)]
        patch_grad = my_cols(small[start - PATCH : start], 1)
        embed_grad = jnp.concatenate([grad_classes, patch_grad.T], axis=1)

    head_grad = small[start - 2 * PATCH : start - PATCH]
    final_bias_grad = jnp.concatenate(
        [small[start + 1], small[start + 2], small[start + 3, :PATCH]]
    )
    loss_total = jnp.sum(small[start + 4, :PATCH])
    count_total = small[start + 5, 0]
    for value in summed:
        own_squares = own_squares + squared(value)
    grad_norm = jnp.sqrt(sum_scalar(place, own_squares) + shared_squares)
    clip_factor = jnp.minimum(1.0, CLIP_NORM / (grad_norm + 1e-06))
    clip = clip_factor[None]

    results = [loss_total, count_total, grad_norm]
    new_blocks = adam_blocks(clip, spot, sums, in_view, [weights_out, momentum_out, variance_out])
    results += [jnp.transpose(v, (0, 2, 1, 3)) for v in new_blocks[:3]] + list(new_blocks[3:])
    rest = adam_rest(
        clip,
        [
            (time_mlp.T, time_grad, momentum_time.T, variance_time.T, RATE),
            (embed_table.T, embed_grad, momentum_embed.T, variance_embed.T, RATE),
            (bias_table, bias_grad, momentum_bias, variance_bias, RATE_BIAS),
        ],
    )
    results += [v.T for v in rest[:6]]
    results += [v.T for v in adam_final(clip, final_grad, head_grad, *final_view)]
    results += list(rest[6:9])
    results += adam(
        final_bias, final_bias_grad, momentum_final_bias, variance_final_bias, clip_factor,
        RATE_BIAS,
    )
    return tuple(results)


def solution(mesh):
    tokens, latents = P("row", None), P("row")
    weights = (
        P(None, "row", None, "col"),
        P(None, None, "col", "row"),
        P("row", "col"),
        P(None, "col"),
        P(),
        P(None, "col"),
        P(),
    )
    updated = []
    for spec in weights:
        updated += [spec] * 3
    return jax.shard_map(
        on_device,
        mesh=mesh,
        in_specs=(tokens, tokens, latents, latents, latents) + weights * 3,
        out_specs=(P(), P(), P()) + tuple(updated),
        check_vma=False,
    )
```
